32 devices in a mesh: dp: 2 (over x), dep: 4 (over z), hgt: 4 (over y, core).
Axes of the slice: x: 2, y: 2, z: 4, core: 2. Of those that a mesh axis runs over, the one named last changes fastest.
Arguments:
- volume: bfloat16 [2, 32, 8, 32, 128], P('dp', None, 'dep', 'hgt'), may hold values from -6 to 6
- kernel_first: bfloat16 [27, 64, 32], replicated, may hold values from -0.21875 to 0.21875
- kernel_second: bfloat16 [27, 128, 64], replicated, may hold values from -0.15625 to 0.15625
- cotangent: bfloat16 [2, 128, 8, 32, 128], P('dp', None, 'dep', 'hgt'), may hold values from -0.03125 to 0.03125
Outputs:
- features: bfloat16 [2, 128, 8, 32, 128], P('dp', None, 'dep', 'hgt')
- grad_first: float32 [27, 64, 32], P(None, 'dp')
- grad_second: float32 [27, 128, 64], P(None, 'dp')
The draws below stay inside these ranges and needn't reach their ends.
All inputs are finite; a program needn't handle non-finite values.
Results may differ from the reference program's by a relative error of at most 0.0049.
Values may be sent and summed in bfloat16 or wider, within the bound.
No kernel may reach another device: no remote copies, remote signals or barrier semaphores. Data moves between devices by JAX's collectives and lax.ppermute only.
A program may use at most 64 MiB of HBM per device.

```python
import jax
import jax.numpy as jnp

CH_IN = 32
CH_MID = 64
CH_OUT = 128
WIDTH = 128
VOLUMES = 2
DEPTH = 8
HEIGHT = 32


def with_spikes(drawn, stream_key, source, target, blocks, factor):
    owner, partner = [(jnp.arange(drawn.shape[position]) // (drawn.shape[position] // blocks)).reshape([-1 if axis == position else 1 for axis in range(drawn.ndim)]) for position in (source, target)]
    chosen = jax.random.permutation(stream_key, blocks)[partner]
    strong = (owner == chosen) | (owner == (partner + blocks // 2) % blocks)
    return jnp.where(strong, factor * drawn, drawn)


def level_of(stream_key, shape, split, least, largest):
    loudness, own = 1.0, jax.random.fold_in(stream_key, 6)
    for dim, shards_of in split:
        steps = jnp.exp(jax.random.uniform(jax.random.fold_in(own, dim), (shards_of,), jnp.float32, least / len(split), largest / len(split)))
        loudness = loudness * jnp.repeat(steps, shape[dim] // shards_of).reshape([-1 if axis == dim else 1 for axis in range(len(shape))])
    return loudness


def noise(key, dims, deviation, most, split=(), kind=jnp.bfloat16):
    drawn = jax.random.normal(key, dims, jnp.float32) * deviation
    if len(split) > 0:
        drawn = level_of(key, dims, split, -0.22, 0.18) * drawn
    return jnp.clip(drawn, min=-most, max=most).astype(kind)


def gaussian_with(key, extent, spread, most, split, heavy, dtype=jnp.bfloat16):
    values = spread * jax.random.normal(key, extent, jnp.float32)
    if split:
        values = values * level_of(key, extent, split, -0.22, 0.18)
    return jnp.clip(with_spikes(values, jax.random.fold_in(key, 3), *heavy), -most, most).astype(dtype)


def setup_inputs(seed: int = 0) -> dict:
    arg_keys = jax.random.split(jax.random.key(seed), 5)
    return {
        "volume": noise(arg_keys[0], (VOLUMES, CH_IN, DEPTH, HEIGHT, WIDTH), 1.0, 6.0, ((0, 2), (2, 4), (3, 4))),
        "kernel_first": noise(arg_keys[1], (27, CH_MID, CH_IN), (27 * CH_IN) ** -0.5, 0.21875),
        "kernel_second": noise(arg_keys[2], (27, CH_OUT, CH_MID), (27 * CH_MID) ** -0.5, 0.15625),
        "cotangent": gaussian_with(arg_keys[3], (VOLUMES, CH_OUT, DEPTH, HEIGHT, WIDTH), ((VOLUMES * DEPTH * HEIGHT * WIDTH) ** -0.5), 0.03125, ((0, 2), (2, 4), (3, 4)), (0, 1, 2, 2.0)),
    }


OFFSETS = [(first, second, third) for first in (-1, 0, 1) for second in (-1, 0, 1) for third in (-1, 0, 1)]

def pad_all(field):
    return jnp.pad(field, ((0, 0), (0, 0), (1, 1), (1, 1), (1, 1)))

def window(padded, shift_d, shift_h, shift_w, depth, height, width):
    return padded[:, :, 1 + shift_d:1 + shift_d + depth, 1 + shift_h:1 + shift_h + height, 1 + shift_w:1 + shift_w + width]

def reference(volume, kernel_first, kernel_second, cotangent):
    depth, height, width = (volume.shape[2], volume.shape[3], volume.shape[4])

    def convolve(field, kernel):
        padded = pad_all(field).astype(jnp.float32)
        total = jnp.zeros((field.shape[0], kernel.shape[1], depth, height, width), jnp.float32)
        for number, shift in enumerate(OFFSETS):
            piece = window(padded, shift[0], shift[1], shift[2], depth, height, width)
            total = total + jnp.einsum('oi,bidhw->bodhw', kernel[number].astype(jnp.float32), piece)
        return total

    def kernel_grad(upstream, field):
        padded = pad_all(field).astype(jnp.float32)
        upper = upstream.astype(jnp.float32)
        parts = []
        for shift in OFFSETS:
            piece = window(padded, shift[0], shift[1], shift[2], depth, height, width)
            parts.append(jnp.einsum('bodhw,bidhw->oi', upper, piece))
        return jnp.stack(parts)
    pre = convolve(volume, kernel_first)
    hidden = jax.nn.silu(pre).astype(jnp.bfloat16)
    features = convolve(hidden, kernel_second).astype(jnp.bfloat16)
    grad_second = kernel_grad(cotangent, hidden)
    padded_cot = pad_all(cotangent).astype(jnp.float32)
    back = jnp.zeros(pre.shape, jnp.float32)
    for number, shift in enumerate(OFFSETS):
        piece = window(padded_cot, -shift[0], -shift[1], -shift[2], depth, height, width)
        back = back + jnp.einsum('oi,bodhw->bidhw', kernel_second[number].astype(jnp.float32), piece)
    sigma = jax.nn.sigmoid(pre)
    delta = (back * (sigma * (1.0 + pre * (1.0 - sigma)))).astype(jnp.bfloat16)
    grad_first = kernel_grad(delta, volume)
    return (features, grad_first, grad_second)
```

```python
import functools

import jax
import jax.numpy as jnp
from jax import lax
from jax.experimental import pallas as pl
from jax.experimental.pallas import tpu as pltpu
from jax.sharding import PartitionSpec as P

BF, F32 = jnp.bfloat16, jnp.float32
LANES = 128
VMEM_BYTES = 48 * 2**20


def call(body, outs, args, scratch=(), flops=0):
    moved = sum(x.size * x.dtype.itemsize for x in (*outs, *args))
    return pl.pallas_call(
        body,
        out_shape=outs,
        in_specs=[pl.BlockSpec(memory_space=pltpu.VMEM)] * len(args),
        out_specs=[pl.BlockSpec(memory_space=pltpu.VMEM)] * len(outs),
        scratch_shapes=list(scratch),
        compiler_params=pltpu.CompilerParams(vmem_limit_bytes=VMEM_BYTES),
        cost_estimate=pl.CostEstimate(flops=flops, bytes_accessed=moved, transcendentals=0),
    )(*args)


def shape(dims, dtype):
    return jax.ShapeDtypeStruct(dims, dtype)


def moved_along_width(x, c):
    if c == 0:
        return x
    pieces = []
    for start in range(0, x.shape[1], LANES):
        piece = x[:, start : start + LANES]
        lane = lax.broadcasted_iota(jnp.int32, piece.shape, 1)
        rolled = pltpu.roll(piece, c % LANES, 1)
        pieces.append(jnp.where(lane == (0 if c == 1 else LANES - 1), 0.0, rolled))
    return pieces[0] if len(pieces) == 1 else jnp.concatenate(pieces, axis=1)


def by_rows(ref, scratch, store):
    channels, depth, height, width = ref.shape
    rows = depth * height
    scratch[...] = ref[...].astype(F32).reshape(channels * rows, width)
    for d in range(depth):
        for h in range(height):
            store(d, h, scratch[pl.ds(d * height + h, channels, stride=rows), :])


def volume_kernel(vol_ref, out_ref, scratch):
    def store(d, h, row):
        out_ref[d, :, h * LANES : (h + 1) * LANES] = row.astype(BF)

    by_rows(vol_ref, scratch, store)


def cotangent_kernel(cot_ref, k1_ref, k2_ref, lo_ref, hi_ref, moved_ref, w1_ref, w2_ref, scratch):
    def store(d, h, row):
        lanes = slice(h * LANES, (h + 1) * LANES)
        (lo_ref, hi_ref)[d][:, lanes] = row.astype(BF)
        channels = row.shape[0]
        for n, c in enumerate((-1, 0, 1)):
            moved_ref[d, n * channels : (n + 1) * channels, lanes] = moved_along_width(row, c).astype(BF)

    by_rows(cot_ref, scratch, store)
    mid, out = k1_ref.shape[2], k2_ref.shape[2]
    for c in range(3):
        one = jnp.concatenate([k1_ref[3 * ab + c] for ab in range(9)], axis=0)
        w1_ref[c * mid : (c + 1) * mid, :] = one.astype(F32).T.astype(BF)
        two = jnp.concatenate([k2_ref[3 * ab + c] for ab in range(9)], axis=0)
        w2_ref[c * out : (c + 1) * out, :] = two.astype(F32).T.astype(BF)


def rim_kernel(own_ref, before_ref, after_ref, first_ref, last_ref):
    n = first_ref.shape[2]
    rows = [before_ref[0], before_ref[1], own_ref[0], own_ref[1], after_ref[0], after_ref[1]]
    for d, row in enumerate(rows):
        first_ref[d] = row[:, :n]
        last_ref[d] = row[:, row.shape[1] - n :]


def cot_rim_kernel(lo_ref, hi_ref, before_ref, after_ref, first_ref, last_ref):
    n = first_ref.shape[2]
    for d, ref in enumerate((before_ref, lo_ref, hi_ref, after_ref)):
        first_ref[d] = ref[:, :n]
        last_ref[d] = ref[:, ref.shape[1] - n :]


def volume_rows(own_ref, before_ref, after_ref, left_ref, right_ref):
    middle = [before_ref[0], before_ref[1], own_ref[0], own_ref[1], after_ref[0], after_ref[1]]
    return [
        jnp.concatenate([left_ref[d], middle[d], right_ref[d]], axis=1) for d in range(len(middle))
    ]


def hidden_kernel(
    own_ref, before_ref, after_ref, left_ref, right_ref, w1_ref, moved_ref, hidden_ref, slope_ref, g2_ref
):
    rows = volume_rows(own_ref, before_ref, after_ref, left_ref, right_ref)
    mid = w1_ref.shape[0] // 3
    dep, deps = lax.axis_index("dep"), lax.axis_size("dep")
    hgt, hgts = lax.axis_index("hgt"), lax.axis_size("hgt")
    depth, height = hidden_ref.shape[0], hidden_ref.shape[2] // LANES
    w1 = w1_ref[...]
    for d in range(depth):
        for h in range(0, height, 2):
            rhs = jnp.concatenate(
                [rows[d + a][:, (h + b) * LANES : (h + b + 2) * LANES] for a in range(3) for b in range(3)], axis=0
            )
            y = jnp.dot(w1, rhs, preferred_element_type=F32)
            pre = sum(moved_along_width(y[n * mid : (n + 1) * mid], 1 - n) for n in range(3))
            s = 1.0 / (1.0 + jnp.exp(-pre))
            for r in range(2):
                lanes = slice(r * LANES, (r + 1) * LANES)
                p, q = pre[:, lanes], s[:, lanes]
                value = (p * q).astype(BF)
                outside = []
                if d == 0:
                    outside.append(dep == 0)
                if d == depth - 1:
                    outside.append(dep == deps - 1)
                if h + r == 0:
                    outside.append(hgt == 0)
                if h + r == height - 1:
                    outside.append(hgt == hgts - 1)
                for far in outside:
                    value = jnp.where(far, jnp.zeros_like(value), value)
                hidden_ref[d, :, (h + r) * LANES : (h + r + 1) * LANES] = value
                if 0 < d < depth - 1 and 0 < h + r < height - 1:
                    at = (h + r - 1) * LANES
                    slope_ref[d - 1, :, at : at + LANES] = q * (1.0 + p * (1.0 - q))
    cells = (height - 2) * LANES
    own = depth - 2
    out = moved_ref.shape[1] // 3
    left = jnp.concatenate([moved_ref[d] for d in range(own)], axis=1)
    tails = []
    for first in (0, 4, 8):
        group = range(first, min(first + 4, 9))
        right = jnp.concatenate(
            [
                jnp.concatenate(
                    [hidden_ref[d + ab // 3, :, (ab % 3) * LANES : (ab % 3) * LANES + cells] for ab in group], axis=0
                )
                for d in range(own)
            ],
            axis=1,
        )
        g = lax.dot_general(left, right, (((1,), (1,)), ((), ())), preferred_element_type=F32)
        for n in range(3):
            part = g[n * out : (n + 1) * out]
            if first < 8:
                for m in range(2):
                    g2_ref[4 * n + first // 2 + m] = part[:, m * LANES : (m + 1) * LANES].astype(BF)
            else:
                tails.append(part)
    tails.append(jnp.zeros_like(tails[0]))
    for m in range(2):
        g2_ref[12 + m] = jnp.concatenate(tails[2 * m : 2 * m + 2], axis=1).astype(BF)


def features_kernel(hidden_ref, w2_ref, out_ref, scratch):
    out = w2_ref.shape[0] // 3
    _, depth, height, _ = out_ref.shape
    w2 = w2_ref[...]
    for d in range(depth):
        for h in range(0, height, 2):
            rhs = jnp.concatenate(
                [
                    hidden_ref[d + a, :, (h + b) * LANES : (h + b + 2) * LANES]
                    for a in range(3)
                    for b in range(3)
                ],
                axis=0,
            )
            y = jnp.dot(w2, rhs, preferred_element_type=F32)
            total = sum(moved_along_width(y[n * out : (n + 1) * out], 1 - n) for n in range(3))
            for r in range(2):
                row = total[:, r * LANES : (r + 1) * LANES]
                scratch[pl.ds(d * height + h + r, out, stride=depth * height), :] = row
    out_ref[...] = scratch[...].reshape(out_ref.shape).astype(BF)


def delta_kernel(
    direct, own_ref, before_ref, after_ref, left_ref, right_ref,
    lo_ref, hi_ref, cot_before_ref, cot_after_ref, cot_left_ref, cot_right_ref,
    k2_ref, slope_ref, g2_ref, *outs_and_scratch,
):
    *out_refs, delta_ref = outs_and_scratch
    rows = volume_rows(own_ref, before_ref, after_ref, left_ref, right_ref)
    middle = (cot_before_ref, lo_ref, hi_ref, cot_after_ref)
    cots = [
        jnp.concatenate([cot_left_ref[d], middle[d][...], cot_right_ref[d]], axis=1) for d in range(len(middle))
    ]
    mid = k2_ref.shape[1]
    own, cells = slope_ref.shape[0], slope_ref.shape[2]
    w = jnp.concatenate([k2_ref[3 * ab : 3 * ab + 3].reshape(3 * mid, k2_ref.shape[2]) for ab in range(9)], axis=1)
    for d in range(own):
        for at in range(0, cells, 2 * LANES):
            rhs = jnp.concatenate(
                [
                    cots[d + 2 - a][:, at + (2 - b) * LANES : at + (4 - b) * LANES]
                    for a in range(3)
                    for b in range(3)
                ],
                axis=0,
            )
            y = jnp.dot(w, rhs, preferred_element_type=F32)
            back = sum(moved_along_width(y[n * mid : (n + 1) * mid], n - 1) for n in range(3))
            delta = back * slope_ref[d, :, at : at + 2 * LANES]
            for n in range(3):
                delta_ref[n * mid : (n + 1) * mid, d * cells + at : d * cells + at + 2 * LANES] = moved_along_width(
                    delta, n - 1
                ).astype(BF)
    left = delta_ref[...]
    blocks, tails = [None] * 6, []
    inner = own_ref.shape[1]
    for first in (0, 8):
        group = range(first, min(first + 8, 9))
        right = jnp.concatenate(
            [
                jnp.concatenate(
                    [rows[d + 1 + ab // 3][:, (1 + ab % 3) * LANES : (1 + ab % 3) * LANES + cells] for ab in group],
                    axis=0,
                )
                for d in range(own)
            ],
            axis=1,
        )
        g = lax.dot_general(left, right, (((1,), (1,)), ((), ())), preferred_element_type=F32)
        for n in range(3):
            part = g[n * mid : (n + 1) * mid]
            if first == 0:
                for m in range(2):
                    blocks[2 * n + m] = part[:, m * LANES : (m + 1) * LANES]
            else:
                tails.append(part)
    tails.append(jnp.zeros((mid, LANES - 3 * inner), F32))
    blocks.append(jnp.concatenate(tails, axis=1))
    if not direct:
        for j, block in enumerate(blocks):
            out_refs[0][j] = block.astype(BF)
        return
    packed_ref = out_refs[0]
    parts, quarters, units, size, _ = packed_ref.shape

    def put(part, unit, value):
        packed_ref[part, unit // units, unit % units] = value

    for part in range(parts):
        for j in range(14):
            for half in range(2):
                start = (2 * part + half) * size
                put(part, 2 * j + half, g2_ref[j, start : start + size, :])
        for j, block in enumerate(blocks):
            put(part, 28 + j, block[part * size : (part + 1) * size].astype(BF))
        for unit in range(35, quarters * units):
            put(part, unit, jnp.zeros((size, LANES), BF))


def sum_kernel(in_ref, out_ref):
    total = in_ref[0].astype(F32)
    for n in range(1, in_ref.shape[0]):
        total = total + in_ref[n].astype(F32)
    out_ref[...] = total.astype(out_ref.dtype)


def sum_four_kernel(a_ref, b_ref, c_ref, d_ref, out_ref):
    one = a_ref[...].astype(F32) + b_ref[...].astype(F32)
    two = c_ref[...].astype(F32) + d_ref[...].astype(F32)
    out_ref[...] = (one + two).astype(out_ref.dtype)


def unpack_kernel(in_ref, g1_ref, g2_ref):
    quarters, units, size, _ = in_ref.shape

    def get(unit):
        return in_ref[unit // units, unit % units].astype(F32)

    for j in range(14):
        for half in range(2):
            rows = slice(half * size, (half + 1) * size)
            value = get(2 * j + half)
            for m in range(2):
                if j < 12:
                    c, ab = j // 4, 2 * (j % 4) + m
                else:
                    c, ab = 2 * (j - 12) + m, 8
                if c < 3:
                    g2_ref[3 * ab + c, rows, :] = value[:, m * 64 : (m + 1) * 64]
    for j in range(7):
        value = get(28 + j)
        for m in range(4):
            c, ab = (j // 2, 4 * (j % 2) + m) if j < 6 else (m, 8)
            if c < 3:
                g1_ref[3 * ab + c] = value[:, m * 32 : (m + 1) * 32]


def exchange(up, down, axis):
    size = lax.axis_size(axis)
    rising = [(i, i + 1) for i in range(size - 1)]
    falling = [(j, i) for i, j in rising]
    return lax.ppermute(up, axis, rising), lax.ppermute(down, axis, falling)


def gathered_by_xor(x, axis):
    size = lax.axis_size(axis)
    return [x] + [lax.ppermute(x, axis, [(i, i ^ k) for i in range(size)]) for k in range(1, size)]


def per_device(volume, kernel_first, kernel_second, cotangent):
    _, inner, depth, height, width = volume.shape
    mid, out = kernel_first.shape[1], kernel_second.shape[1]
    cells = height * width
    parts, quarters = lax.axis_size("dp"), lax.axis_size("hgt")
    k1, k2 = jnp.swapaxes(kernel_first, 1, 2), jnp.swapaxes(kernel_second, 1, 2)
    rows = depth * height

    (vol,) = call(
        volume_kernel, [shape((depth, inner, cells), BF)], [volume[0]], [pltpu.VMEM((inner * rows, width), F32)]
    )
    before, after = exchange(vol, vol, "dep")
    lo, hi, moved, w1, w2 = call(
        cotangent_kernel,
        [shape((out, cells), BF)] * 2
        + [shape((depth, 3 * out, cells), BF), shape((3 * mid, 9 * inner), BF), shape((3 * out, 9 * mid), BF)],
        [cotangent[0], k1, k2],
        [pltpu.VMEM((out * rows, width), F32)],
    )
    first, last = call(rim_kernel, [shape((depth + 4, inner, 2 * width), BF)] * 2, [vol, before, after])
    left, right = exchange(last, first, "hgt")
    cot_before, cot_after = exchange(hi, lo, "dep")
    cot_first, cot_last = call(
        cot_rim_kernel, [shape((depth + 2, out, width), BF)] * 2, [lo, hi, cot_before, cot_after]
    )
    cot_left, cot_right = exchange(cot_last, cot_first, "hgt")

    volumes = [vol, before, after, left, right]
    hidden, slope, g2 = call(
        hidden_kernel,
        [
            shape((depth + 2, mid, cells + 2 * width), BF),
            shape((depth, mid, cells), F32),
            shape((14, out, LANES), BF),
        ],
        [*volumes, w1, moved],
        flops=1_500_000_000,
    )
    size = mid // parts
    direct = size % 16 == 0
    packed = (parts, quarters, 9, size, LANES)
    (grads,) = call(
        functools.partial(delta_kernel, direct),
        [shape(packed if direct else (7, mid, LANES), BF)],
        [*volumes, lo, hi, cot_before, cot_after, cot_left, cot_right, k2, slope, g2],
        [pltpu.VMEM((3 * mid, depth * cells), BF)],
        flops=1_100_000_000,
    )
    if not direct:
        one = jnp.swapaxes(grads.reshape(7, parts, size, LANES), 0, 1)
        two = jnp.swapaxes(g2.reshape(14, parts, 2, size, LANES), 0, 1).reshape(parts, 28, size, LANES)
        grads = jnp.pad(jnp.concatenate([two, one], axis=1), ((0, 0), (0, quarters * 9 - 35), (0, 0), (0, 0)))
        grads = grads.reshape(packed)
    grads = grads.reshape(parts * quarters, 9 * size, LANES)
    swapped = lax.all_to_all(grads, ("dp", "hgt"), 0, 0, tiled=True)
    (features,) = call(
        features_kernel, [shape(cotangent.shape[1:], BF)], [hidden, w2], [pltpu.VMEM((out * rows, width), F32)],
        flops=900_000_000,
    )
    (share,) = call(sum_kernel, [shape(grads.shape[1:], BF)], [swapped])
    (share,) = call(sum_four_kernel, [shape(grads.shape[1:], BF)], gathered_by_xor(share, "dep"))
    near = jnp.stack(gathered_by_xor(share, "hgt"))
    me = lax.axis_index("hgt")
    whole = jnp.stack([lax.dynamic_index_in_dim(near, me ^ q, 0, False) for q in range(quarters)])
    grad_first, grad_second = call(
        unpack_kernel,
        [shape((27, size, inner), F32), shape((27, 2 * size, mid), F32)],
        [whole.reshape(quarters, 9, size, LANES)],
    )
    return features[None], grad_first, grad_second


def solution(mesh):
    placed = (P("dp", None, "dep", "hgt", None), P(), P(), P("dp", None, "dep", "hgt", None))
    return jax.shard_map(
        per_device,
        mesh=mesh,
        in_specs=placed,
        out_specs=(P("dp", None, "dep", "hgt", None), P(None, "dp", None), P(None, "dp", None)),
        check_vma=False,
    )
```

```python
import functools

import jax
import jax.numpy as jnp
from jax import lax
from jax.experimental import pallas as pl
from jax.experimental.pallas import tpu as pltpu
from jax.sharding import PartitionSpec as P

BF, F32 = jnp.bfloat16, jnp.float32
LANES = 128
VMEM_BYTES = 48 * 2**20


def call(body, outs, args, scratch=(), flops=0, far=()):
    moved = sum(x.size * x.dtype.itemsize for x in (*outs, *args))
    return pl.pallas_call(
        body,
        out_shape=outs,
        in_specs=[pl.BlockSpec(memory_space=pl.ANY if n in far else pltpu.VMEM) for n in range(len(args))],
        out_specs=[pl.BlockSpec(memory_space=pltpu.VMEM)] * len(outs),
        scratch_shapes=list(scratch),
        compiler_params=pltpu.CompilerParams(vmem_limit_bytes=VMEM_BYTES),
        cost_estimate=pl.CostEstimate(flops=flops, bytes_accessed=moved, transcendentals=0),
    )(*args)


def shape(dims, dtype):
    return jax.ShapeDtypeStruct(dims, dtype)


def moved_along_width(x, c):
    if c == 0:
        return x
    pieces = []
    for start in range(0, x.shape[1], LANES):
        piece = x[:, start : start + LANES]
        lane = lax.broadcasted_iota(jnp.int32, piece.shape, 1)
        rolled = pltpu.roll(piece, c % LANES, 1)
        pieces.append(jnp.where(lane == (0 if c == 1 else LANES - 1), 0.0, rolled))
    return pieces[0] if len(pieces) == 1 else jnp.concatenate(pieces, axis=1)


def by_rows(ref, scratch, store):
    channels, depth, height, width = ref.shape
    rows = depth * height
    scratch[...] = ref[...].astype(F32).reshape(channels * rows, width)
    for d in range(depth):
        for h in range(height):
            store(d, h, scratch[pl.ds(d * height + h, channels, stride=rows), :])


def odd(axis):
    return lax.rem(lax.axis_index(axis), 2) == 1


def begin_copies(pairs, sems):
    copies = [pltpu.make_async_copy(src, dst, sems.at[n]) for n, (src, dst) in enumerate(pairs)]
    for copy in copies:
        copy.start()
    return copies


def volume_kernel(vol_ref, out_ref, held, scratch, sems):
    (copy,) = begin_copies([(vol_ref, held)], sems)
    copy.wait()

    def store(d, h, row):
        out_ref[d, :, h * LANES : (h + 1) * LANES] = row.astype(BF)

    by_rows(held, scratch, store)


def cotangent_kernel(
    _, cot_ref, k1_ref, k2_ref, own_ref, one_ref, two_ref, moved_ref, w1_ref, w2_ref, held, k1, k2, scratch, sems
):
    copies = begin_copies([(cot_ref, held), (k1_ref, k1), (k2_ref, k2)], sems)
    copies[0].wait()

    def store(d, h, row):
        lanes = slice(h * LANES, (h + 1) * LANES)
        own_ref[d, :, lanes] = row.astype(BF)
        channels = row.shape[0]
        for n, c in enumerate((-1, 0, 1)):
            moved_ref[d, n * channels : (n + 1) * channels, lanes] = moved_along_width(row, c).astype(BF)

    by_rows(held, scratch, store)
    is_odd = odd("dep")
    one_ref[...] = jnp.where(is_odd, own_ref[0], own_ref[own_ref.shape[0] - 1])
    two_ref[...] = jnp.where(is_odd, own_ref[own_ref.shape[0] - 1], own_ref[0])
    copies[1].wait()
    copies[2].wait()
    mid, out = k1.shape[2], k2.shape[2]
    for c in range(3):
        one = jnp.concatenate([k1[3 * ab + c] for ab in range(9)], axis=0)
        w1_ref[c * mid : (c + 1) * mid, :] = one.astype(F32).T.astype(BF)
        two = jnp.concatenate([k2[3 * ab + c] for ab in range(9)], axis=0)
        w2_ref[c * out : (c + 1) * out, :] = two.astype(F32).T.astype(BF)


def sides(axis, one, two):
    me, size = lax.axis_index(axis), lax.axis_size(axis)
    is_odd = odd(axis)
    none = jnp.zeros_like(one)
    before = jnp.where(me == 0, none, jnp.where(is_odd, one, two))
    after = jnp.where(me == size - 1, none, jnp.where(is_odd, two, one))
    return before, after


def rim_kernel(own_ref, one_ref, two_ref, deep_ref, send_one_ref, send_two_ref):
    before, after = sides("dep", one_ref[...], two_ref[...])
    edge, own = one_ref.shape[0], own_ref.shape[0]
    deep_ref[:edge] = before
    deep_ref[edge : edge + own] = own_ref[...]
    deep_ref[edge + own :] = after
    n, cells = send_one_ref.shape[2], deep_ref.shape[2]
    first, last = deep_ref[:, :, :n], deep_ref[:, :, cells - n :]
    is_odd = odd("hgt")
    send_one_ref[...] = jnp.where(is_odd, first, last)
    send_two_ref[...] = jnp.where(is_odd, last, first)


def widened(deep_ref, one_ref, two_ref):
    left, right = sides("hgt", one_ref[...], two_ref[...])
    return [jnp.concatenate([left[d], deep_ref[d], right[d]], axis=1) for d in range(deep_ref.shape[0])]


def hidden_kernel(deep_ref, one_ref, two_ref, w1_ref, moved_ref, hidden_ref, slope_ref, g2_ref, rows_ref):
    for d, row in enumerate(widened(deep_ref, one_ref, two_ref)):
        rows_ref[d] = row
    rows = rows_ref
    mid = w1_ref.shape[0] // 3
    dep, deps = lax.axis_index("dep"), lax.axis_size("dep")
    hgt, hgts = lax.axis_index("hgt"), lax.axis_size("hgt")
    depth, height = hidden_ref.shape[0], hidden_ref.shape[2] // LANES
    w1 = w1_ref[...]
    for d in range(depth):
        for h in range(0, height, 2):
            rhs = jnp.concatenate(
                [rows[d + a, :, (h + b) * LANES : (h + b + 2) * LANES] for a in range(3) for b in range(3)], axis=0
            )
            y = jnp.dot(w1, rhs, preferred_element_type=F32)
            pre = sum(moved_along_width(y[n * mid : (n + 1) * mid], 1 - n) for n in range(3))
            s = 1.0 / (1.0 + jnp.exp(-pre))
            for r in range(2):
                lanes = slice(r * LANES, (r + 1) * LANES)
                p, q = pre[:, lanes], s[:, lanes]
                value = (p * q).astype(BF)
                outside = []
                if d == 0:
                    outside.append(dep == 0)
                if d == depth - 1:
                    outside.append(dep == deps - 1)
                if h + r == 0:
                    outside.append(hgt == 0)
                if h + r == height - 1:
                    outside.append(hgt == hgts - 1)
                for far in outside:
                    value = jnp.where(far, jnp.zeros_like(value), value)
                hidden_ref[d, :, (h + r) * LANES : (h + r + 1) * LANES] = value
                if 0 < d < depth - 1 and 0 < h + r < height - 1:
                    at = (h + r - 1) * LANES
                    slope_ref[d - 1, :, at : at + LANES] = q * (1.0 + p * (1.0 - q))
    cells = (height - 2) * LANES
    own = depth - 2
    out = moved_ref.shape[1] // 3
    left = jnp.concatenate([moved_ref[d] for d in range(own)], axis=1)
    tails = []
    for first in (0, 4, 8):
        group = range(first, min(first + 4, 9))
        right = jnp.concatenate(
            [
                jnp.concatenate(
                    [hidden_ref[d + ab // 3, :, (ab % 3) * LANES : (ab % 3) * LANES + cells] for ab in group], axis=0
                )
                for d in range(own)
            ],
            axis=1,
        )
        g = lax.dot_general(left, right, (((1,), (1,)), ((), ())), preferred_element_type=F32)
        for n in range(3):
            part = g[n * out : (n + 1) * out]
            if first < 8:
                for m in range(2):
                    g2_ref[4 * n + first // 2 + m] = part[:, m * LANES : (m + 1) * LANES]
            else:
                tails.append(part)
    tails.append(jnp.zeros_like(tails[0]))
    for m in range(2):
        g2_ref[12 + m] = jnp.concatenate(tails[2 * m : 2 * m + 2], axis=1)


def features_kernel(hidden_ref, w2_ref, out_ref, scratch):
    out = w2_ref.shape[0] // 3
    _, depth, height, _ = out_ref.shape
    w2 = w2_ref[...]
    for d in range(depth):
        for h in range(0, height, 2):
            rhs = jnp.concatenate(
                [
                    hidden_ref[d + a, :, (h + b) * LANES : (h + b + 2) * LANES]
                    for a in range(3)
                    for b in range(3)
                ],
                axis=0,
            )
            y = jnp.dot(w2, rhs, preferred_element_type=F32)
            total = sum(moved_along_width(y[n * out : (n + 1) * out], 1 - n) for n in range(3))
            for r in range(2):
                row = total[:, r * LANES : (r + 1) * LANES]
                scratch[pl.ds(d * height + h + r, out, stride=depth * height), :] = row
    out_ref[...] = scratch[...].reshape(out_ref.shape).astype(BF)


def delta_kernel(direct, rows_ref, cot_ref, one_ref, two_ref, k2_ref, slope_ref, g2_ref, *outs_and_scratch):
    *out_refs, delta_ref = outs_and_scratch
    cots = widened(cot_ref, one_ref, two_ref)
    mid = k2_ref.shape[1]
    own, cells = slope_ref.shape[0], slope_ref.shape[2]
    w = jnp.concatenate([k2_ref[3 * ab : 3 * ab + 3].reshape(3 * mid, k2_ref.shape[2]) for ab in range(9)], axis=1)
    for d in range(own):
        for at in range(0, cells, 2 * LANES):
            rhs = jnp.concatenate(
                [
                    cots[d + 2 - a][:, at + (2 - b) * LANES : at + (4 - b) * LANES]
                    for a in range(3)
                    for b in range(3)
                ],
                axis=0,
            )
            y = jnp.dot(w, rhs, preferred_element_type=F32)
            back = sum(moved_along_width(y[n * mid : (n + 1) * mid], n - 1) for n in range(3))
            delta = back * slope_ref[d, :, at : at + 2 * LANES]
            for n in range(3):
                delta_ref[n * mid : (n + 1) * mid, d * cells + at : d * cells + at + 2 * LANES] = moved_along_width(
                    delta, n - 1
                ).astype(BF)
    left = delta_ref[...]
    blocks, tails = [None] * 6, []
    inner = rows_ref.shape[1]
    for first in (0, 8):
        group = range(first, min(first + 8, 9))
        right = jnp.concatenate(
            [
                jnp.concatenate(
                    [
                        rows_ref[d + 1 + ab // 3, :, (1 + ab % 3) * LANES : (1 + ab % 3) * LANES + cells]
                        for ab in group
                    ],
                    axis=0,
                )
                for d in range(own)
            ],
            axis=1,
        )
        g = lax.dot_general(left, right, (((1,), (1,)), ((), ())), preferred_element_type=F32)
        for n in range(3):
            part = g[n * mid : (n + 1) * mid]
            if first == 0:
                for m in range(2):
                    blocks[2 * n + m] = part[:, m * LANES : (m + 1) * LANES]
            else:
                tails.append(part)
    tails.append(jnp.zeros((mid, LANES - 3 * inner), F32))
    blocks.append(jnp.concatenate(tails, axis=1))
    if not direct:
        for j, block in enumerate(blocks):
            out_refs[0][j] = block
        return
    keep_ref, send_ref = out_refs
    parts, halves, units, size, _ = keep_ref.shape
    core = odd("hgt")

    def value(part, unit):
        if unit < 28:
            start = (2 * part + unit % 2) * size
            return g2_ref[unit // 2, start : start + size, :]
        if unit < 35:
            return blocks[unit - 28][part * size : (part + 1) * size]
        return jnp.zeros((size, LANES), F32)

    for part in range(parts):
        for half in range(halves):
            for unit in range(units):
                one, two = (value(part, (2 * half + c) * units + unit) for c in range(2))
                keep_ref[part, half, unit] = jnp.where(core, two, one)
                send_ref[part, half, unit] = jnp.where(core, one, two).astype(BF)


def halve_kernel(axis, bit, keep_ref, got_ref, kept_ref, send_ref):
    mine = lax.rem(lax.div(lax.axis_index(axis), bit), 2)
    kept_ref[...] = keep_ref[mine] + got_ref[mine].astype(F32)
    send_ref[...] = (keep_ref[1 - mine] + got_ref[1 - mine].astype(F32)).astype(BF)


def add_kernel(one_ref, two_ref, out_ref):
    out_ref[...] = (one_ref[...].astype(F32) + two_ref[...].astype(F32)).astype(BF)


def order_kernel(axis, bit, own_ref, got_ref, out_ref):
    mine = lax.rem(lax.div(lax.axis_index(axis), bit), 2)
    out_ref[mine] = own_ref[...]
    out_ref[1 - mine] = got_ref[...]


def unpack_kernel(own_ref, got_ref, g1_ref, g2_ref):
    _, units, size, _ = own_ref.shape
    core = odd("hgt")

    def get(unit):
        quarter = unit // units
        at = quarter // 2, unit % units
        one, two = (got_ref, own_ref) if quarter % 2 else (own_ref, got_ref)
        return jnp.where(core, two[at], one[at]).astype(F32)

    for j in range(14):
        for half in range(2):
            rows = slice(half * size, (half + 1) * size)
            value = get(2 * j + half)
            for m in range(2):
                if j < 12:
                    c, ab = j // 4, 2 * (j % 4) + m
                else:
                    c, ab = 2 * (j - 12) + m, 8
                if c < 3:
                    g2_ref[3 * ab + c, rows, :] = value[:, m * 64 : (m + 1) * 64]
    for j in range(7):
        value = get(28 + j)
        for m in range(4):
            c, ab = (j // 2, 4 * (j % 2) + m) if j < 6 else (m, 8)
            if c < 3:
                g1_ref[3 * ab + c] = value[:, m * 32 : (m + 1) * 32]


def swapped(x, axis, pattern):
    size = lax.axis_size(axis)
    first = {"one": 0, "two": 1, "inner": 1}[pattern]
    pairs = [(i, (i + 1) % size) for i in range(first, size, 2)]
    if pattern == "inner":
        pairs = pairs[:-1]
    return lax.ppermute(x, axis, pairs + [(j, i) for i, j in pairs])


def across(x, axis, bit):
    return lax.ppermute(x, axis, [(i, i ^ bit) for i in range(lax.axis_size(axis))])


def per_device(volume, kernel_first, kernel_second, cotangent):
    _, inner, depth, height, width = volume.shape
    mid, out = kernel_first.shape[1], kernel_second.shape[1]
    cells = height * width
    parts, quarters = lax.axis_size("dp"), lax.axis_size("hgt")
    k1, k2 = jnp.swapaxes(kernel_first, 1, 2), jnp.swapaxes(kernel_second, 1, 2)
    rows = depth * height

    (vol,) = call(
        volume_kernel,
        [shape((depth, inner, cells), BF)],
        [volume[0]],
        [
            pltpu.VMEM(volume.shape[1:], BF),
            pltpu.VMEM((inner * rows, width), F32),
            pltpu.SemaphoreType.DMA((1,)),
        ],
        far=(0,),
    )
    one, two = swapped(vol, "dep", "one"), swapped(vol, "dep", "two")
    cot, cot_one, cot_two, moved, w1, w2 = call(
        cotangent_kernel,
        [
            shape((depth, out, cells), BF),
            shape((out, cells), BF),
            shape((out, cells), BF),
            shape((depth, 3 * out, cells), BF),
            shape((3 * mid, 9 * inner), BF),
            shape((3 * out, 9 * mid), BF),
        ],
        [vol, cotangent[0], k1, k2],
        [
            pltpu.VMEM(cotangent.shape[1:], BF),
            pltpu.VMEM(k1.shape, BF),
            pltpu.VMEM(k2.shape, BF),
            pltpu.VMEM((out * rows, width), F32),
            pltpu.SemaphoreType.DMA((3,)),
        ],
        far=(0, 1, 2, 3),
    )
    deep, one, two = call(
        rim_kernel,
        [shape((depth + 4, inner, cells), BF)] + [shape((depth + 4, inner, 2 * width), BF)] * 2,
        [vol, one, two],
    )
    one, two = swapped(one, "hgt", "one"), swapped(two, "hgt", "two")
    cot_one, cot_two = swapped(cot_one, "dep", "one"), swapped(cot_two, "dep", "inner")
    cot_deep, cot_one, cot_two = call(
        rim_kernel,
        [shape((depth + 2, out, cells), BF)] + [shape((depth + 2, out, width), BF)] * 2,
        [cot, cot_one[None], cot_two[None]],
    )
    cot_one, cot_two = swapped(cot_one, "hgt", "one"), swapped(cot_two, "hgt", "inner")

    hidden, slope, g2, wide = call(
        hidden_kernel,
        [
            shape((depth + 2, mid, cells + 2 * width), BF),
            shape((depth, mid, cells), F32),
            shape((14, out, LANES), F32),
            shape((depth + 4, inner, cells + 4 * width), BF),
        ],
        [deep, one, two, w1, moved],
        flops=1_500_000_000,
    )
    size = mid // parts
    direct = parts == 2 and size % 16 == 0
    half = (parts, quarters // 2, 9, size, LANES)
    grads = call(
        functools.partial(delta_kernel, direct),
        [shape(half, F32), shape(half, BF)] if direct else [shape((7, mid, LANES), F32)],
        [wide, cot_deep, cot_one, cot_two, k2, slope, g2],
        [pltpu.VMEM((3 * mid, depth * cells), BF)],
        flops=1_100_000_000,
    )
    if direct:
        keep, send = grads
    else:
        grad = jnp.swapaxes(grads[0].reshape(7, parts, size, LANES), 0, 1)
        grad2 = jnp.swapaxes(g2.reshape(14, parts, 2, size, LANES), 0, 1).reshape(parts, 28, size, LANES)
        grad = jnp.pad(jnp.concatenate([grad2, grad], axis=1), ((0, 0), (0, quarters * 9 - 35), (0, 0), (0, 0)))
        grad = lax.psum_scatter(grad, "dp", scatter_dimension=0, tiled=True)
        grad = grad.reshape(quarters // 2, 2, 9, size, LANES)
        core = lax.rem(lax.axis_index("hgt"), 2)
        keep = lax.dynamic_index_in_dim(grad, core, 1, False)
        send = lax.dynamic_index_in_dim(grad, 1 - core, 1, False).astype(BF)
    (features,) = call(
        features_kernel, [shape(cotangent.shape[1:], BF)], [hidden, w2], [pltpu.VMEM((out * rows, width), F32)],
        flops=900_000_000,
    )
    got = across(send, "hgt", 1)
    if direct:
        keep, send = call(
            functools.partial(halve_kernel, "dp", 1), [shape(half[1:], F32), shape(half[1:], BF)], [keep, got]
        )
        got = across(send, "dp", 1)
    keep, send = call(
        functools.partial(halve_kernel, "hgt", 2), [shape(half[2:], F32), shape(half[2:], BF)], [keep, got]
    )
    got = across(send, "hgt", 2)
    (share,) = call(add_kernel, [shape(half[2:], BF)], [keep, got])
    (share,) = call(add_kernel, [shape(half[2:], BF)], [share, across(share, "dep", 1)])
    (share,) = call(add_kernel, [shape(half[2:], BF)], [share, across(share, "dep", 3)])
    (pair,) = call(
        functools.partial(order_kernel, "hgt", 2), [shape(half[1:], BF)], [share, across(share, "hgt", 2)]
    )
    grad_first, grad_second = call(
        unpack_kernel,
        [shape((27, size, inner), F32), shape((27, 2 * size, mid), F32)],
        [pair, across(pair, "hgt", 1)],
    )
    return features[None], grad_first, grad_second


def solution(mesh):
    placed = (P("dp", None, "dep", "hgt", None), P(), P(), P("dp", None, "dep", "hgt", None))
    return jax.shard_map(
        per_device,
        mesh=mesh,
        in_specs=placed,
        out_specs=(P("dp", None, "dep", "hgt", None), P(None, "dp", None), P(None, "dp", None)),
        check_vma=False,
    )
```

```python
import functools

import jax
import jax.numpy as jnp
from jax import lax
from jax.experimental import pallas as pl
from jax.experimental.pallas import tpu as pltpu
from jax.sharding import PartitionSpec as P

BF, F32 = jnp.bfloat16, jnp.float32
LANES = 128
VMEM_BYTES = 48 * 2**20


def call(body, outs, args, scratch=(), flops=0, far=()):
    moved = sum(x.size * x.dtype.itemsize for x in (*outs, *args))
    return pl.pallas_call(
        body,
        out_shape=outs,
        in_specs=[pl.BlockSpec(memory_space=pltpu.HBM if n in far else pltpu.VMEM) for n in range(len(args))],
        out_specs=[pl.BlockSpec(memory_space=pltpu.VMEM)] * len(outs),
        scratch_shapes=list(scratch),
        compiler_params=pltpu.CompilerParams(vmem_limit_bytes=VMEM_BYTES),
        cost_estimate=pl.CostEstimate(flops=flops, bytes_accessed=moved, transcendentals=0),
    )(*args)


def shape(dims, dtype):
    return jax.ShapeDtypeStruct(dims, dtype)


def moved_along_width(x, c):
    if c == 0:
        return x
    pieces = []
    for start in range(0, x.shape[1], LANES):
        piece = x[:, start : start + LANES]
        lane = lax.broadcasted_iota(jnp.int32, piece.shape, 1)
        rolled = pltpu.roll(piece, c % LANES, 1)
        pieces.append(jnp.where(lane == (0 if c == 1 else LANES - 1), 0.0, rolled))
    return pieces[0] if len(pieces) == 1 else jnp.concatenate(pieces, axis=1)


def by_rows(ref, scratch, store):
    channels, depth, height, width = ref.shape
    rows = depth * height
    scratch[...] = ref[...].astype(F32).reshape(channels * rows, width)
    for d in range(depth):
        for h in range(height):
            store(d, h, scratch[pl.ds(d * height + h, channels, stride=rows), :])


def odd(axis):
    return lax.rem(lax.axis_index(axis), 2) == 1


def begin_copies(pairs, sems):
    copies = [pltpu.make_async_copy(src, dst, sems.at[n]) for n, (src, dst) in enumerate(pairs)]
    for copy in copies:
        copy.start()
    return copies


def prepare_kernel(
    vol_ref, cot_ref, k1_ref, k2_ref, own_ref, moved_ref, w1_ref, w2_ref, back_ref, one_ref, two_ref,
    vol, cot, k1, k2, vol_scratch, cot_scratch, sems,
):
    copies = begin_copies([(cot_ref, cot), (k2_ref, k2), (vol_ref, vol), (k1_ref, k1)], sems)
    copies[0].wait()
    out, depth, height, _ = cot.shape
    rows = [[None] * height for _ in range(depth)]

    def store(d, h, row):
        lanes = slice(h * LANES, (h + 1) * LANES)
        rows[d][h] = row.astype(BF)
        for n, c in enumerate((-1, 0, 1)):
            moved_ref[d, n * out : (n + 1) * out, lanes] = moved_along_width(row, c).astype(BF)

    by_rows(cot, cot_scratch, store)
    copies[1].wait()
    mid = k2.shape[1]
    none = jnp.zeros((out, 2 * LANES), BF)
    padded = [jnp.concatenate([none, *rows[d], none], axis=1) for d in range(depth)]
    is_odd = odd("dep")
    faces = [[], []]
    for e in range(depth + 2):
        reached = [(d, e - 1 - d) for d in range(depth) if abs(e - 1 - d) <= 1]
        w = jnp.concatenate(
            [
                k2[9 * (a + 1) + 3 * b : 9 * (a + 1) + 3 * b + 3].reshape(3 * mid, out)
                for _, a in reached
                for b in range(3)
            ],
            axis=1,
        )
        for j in range(0, height + 2, 2):
            rhs = jnp.concatenate(
                [padded[d][:, (j + 2 - b) * LANES : (j + 4 - b) * LANES] for d, _ in reached for b in range(3)], axis=0
            )
            y = jnp.dot(w, rhs, preferred_element_type=F32)
            back = sum(moved_along_width(y[n * mid : (n + 1) * mid], n - 1) for n in range(3))
            if 0 < e < depth + 1:
                back_ref[e - 1, :, j * LANES : (j + 2) * LANES] = back
            else:
                faces[e > 0].append(back.astype(BF))
    low, high = (jnp.concatenate(face, axis=1) for face in faces)
    one_ref[...] = jnp.where(is_odd, low, high)
    two_ref[...] = jnp.where(is_odd, high, low)
    copies[3].wait()
    for c in range(3):
        one = jnp.concatenate([k1[3 * ab + c] for ab in range(9)], axis=0)
        w1_ref[c * mid : (c + 1) * mid, :] = one.astype(F32).T.astype(BF)
        two = jnp.concatenate([k2[3 * ab + c] for ab in range(9)], axis=0)
        w2_ref[c * out : (c + 1) * out, :] = two.astype(F32).T.astype(BF)
    copies[2].wait()

    def store_own(d, h, row):
        own_ref[d, :, h * LANES : (h + 1) * LANES] = row.astype(BF)

    by_rows(vol, vol_scratch, store_own)


def sides(axis, one, two):
    me, size = lax.axis_index(axis), lax.axis_size(axis)
    is_odd = odd(axis)
    none = jnp.zeros_like(one)
    before = jnp.where(me == 0, none, jnp.where(is_odd, one, two))
    after = jnp.where(me == size - 1, none, jnp.where(is_odd, two, one))
    return before, after


def rim_kernel(own_ref, one_ref, two_ref, deep_ref, send_one_ref, send_two_ref, scratch):
    depth = own_ref.shape[0]
    deep_ref[depth : 2 * depth] = own_ref[...]
    for at, side in zip((0, 2 * depth), sides("dep", one_ref[...], two_ref[...]), strict=True):

        def store(d, h, row, at=at):
            deep_ref[at + d, :, h * LANES : (h + 1) * LANES] = row.astype(BF)

        by_rows(side, scratch, store)
    n, cells = send_one_ref.shape[2], deep_ref.shape[2]
    first, last = deep_ref[:, :, :n], deep_ref[:, :, cells - n :]
    is_odd = odd("hgt")
    send_one_ref[...] = jnp.where(is_odd, first, last)
    send_two_ref[...] = jnp.where(is_odd, last, first)


def back_rim_kernel(own_ref, one_ref, two_ref, back_ref, send_one_ref, send_two_ref):
    before, after = sides("dep", one_ref[...], two_ref[...])
    last = own_ref.shape[0] - 1
    cells = back_ref.shape[2]
    ends = []
    for d in range(last + 1):
        total = own_ref[d]
        if d == 0:
            total = total + before.astype(F32)
        if d == last:
            total = total + after.astype(F32)
        back_ref[d] = total[:, LANES : LANES + cells]
        ends.append((total[:, :LANES].astype(BF), total[:, LANES + cells :].astype(BF)))
    is_odd = odd("hgt")
    for d, (low, high) in enumerate(ends):
        send_one_ref[d] = jnp.where(is_odd, low, high)
        send_two_ref[d] = jnp.where(is_odd, high, low)


def widened(deep_ref, one_ref, two_ref):
    left, right = sides("hgt", one_ref[...], two_ref[...])
    return [jnp.concatenate([left[d], deep_ref[d], right[d]], axis=1) for d in range(deep_ref.shape[0])]


def hidden_kernel(deep_ref, one_ref, two_ref, w1_ref, moved_ref, hidden_ref, slope_ref, g2_ref, rows_ref):
    for d, row in enumerate(widened(deep_ref, one_ref, two_ref)):
        rows_ref[d] = row
    rows = rows_ref
    mid = w1_ref.shape[0] // 3
    dep, deps = lax.axis_index("dep"), lax.axis_size("dep")
    hgt, hgts = lax.axis_index("hgt"), lax.axis_size("hgt")
    depth, height = hidden_ref.shape[0], hidden_ref.shape[2] // LANES
    w1 = w1_ref[...]
    for d in range(depth):
        for h in range(0, height, 2):
            rhs = jnp.concatenate(
                [rows[d + a, :, (h + b) * LANES : (h + b + 2) * LANES] for a in range(3) for b in range(3)], axis=0
            )
            y = jnp.dot(w1, rhs, preferred_element_type=F32)
            pre = sum(moved_along_width(y[n * mid : (n + 1) * mid], 1 - n) for n in range(3))
            s = 1.0 / (1.0 + jnp.exp(-pre))
            for r in range(2):
                lanes = slice(r * LANES, (r + 1) * LANES)
                p, q = pre[:, lanes], s[:, lanes]
                value = (p * q).astype(BF)
                outside = []
                if d == 0:
                    outside.append(dep == 0)
                if d == depth - 1:
                    outside.append(dep == deps - 1)
                if h + r == 0:
                    outside.append(hgt == 0)
                if h + r == height - 1:
                    outside.append(hgt == hgts - 1)
                for far in outside:
                    value = jnp.where(far, jnp.zeros_like(value), value)
                hidden_ref[d, :, (h + r) * LANES : (h + r + 1) * LANES] = value
                if 0 < d < depth - 1 and 0 < h + r < height - 1:
                    at = (h + r - 1) * LANES
                    slope_ref[d - 1, :, at : at + LANES] = q * (1.0 + p * (1.0 - q))
    cells = (height - 2) * LANES
    own = depth - 2
    out = moved_ref.shape[1] // 3
    left = jnp.concatenate([moved_ref[d] for d in range(own)], axis=1)
    tails = []
    for first in (0, 4, 8):
        group = range(first, min(first + 4, 9))
        right = jnp.concatenate(
            [
                jnp.concatenate(
                    [hidden_ref[d + ab // 3, :, (ab % 3) * LANES : (ab % 3) * LANES + cells] for ab in group], axis=0
                )
                for d in range(own)
            ],
            axis=1,
        )
        g = lax.dot_general(left, right, (((1,), (1,)), ((), ())), preferred_element_type=F32)
        for n in range(3):
            part = g[n * out : (n + 1) * out]
            if first < 8:
                for m in range(2):
                    g2_ref[4 * n + first // 2 + m] = part[:, m * LANES : (m + 1) * LANES]
            else:
                tails.append(part)
    tails.append(jnp.zeros_like(tails[0]))
    for m in range(2):
        g2_ref[12 + m] = jnp.concatenate(tails[2 * m : 2 * m + 2], axis=1)


def features_kernel(hidden_ref, w2_ref, out_ref, scratch):
    out = w2_ref.shape[0] // 3
    _, depth, height, _ = out_ref.shape
    w2 = w2_ref[...]
    for d in range(depth):
        for h in range(0, height, 2):
            rhs = jnp.concatenate(
                [
                    hidden_ref[d + a, :, (h + b) * LANES : (h + b + 2) * LANES]
                    for a in range(3)
                    for b in range(3)
                ],
                axis=0,
            )
            y = jnp.dot(w2, rhs, preferred_element_type=F32)
            total = sum(moved_along_width(y[n * out : (n + 1) * out], 1 - n) for n in range(3))
            for r in range(2):
                row = total[:, r * LANES : (r + 1) * LANES]
                scratch[pl.ds(d * height + h + r, out, stride=depth * height), :] = row
    out_ref[...] = scratch[...].reshape(out_ref.shape).astype(BF)


def delta_kernel(direct, rows_ref, back_ref, one_ref, two_ref, slope_ref, g2_ref, *outs_and_scratch):
    *out_refs, delta_ref = outs_and_scratch
    before, after = sides("hgt", one_ref[...], two_ref[...])
    own, mid, cells = slope_ref.shape
    for d in range(own):
        for at in range(0, cells, LANES):
            back = back_ref[d, :, at : at + LANES]
            if at == 0:
                back = back + before[d].astype(F32)
            if at == cells - LANES:
                back = back + after[d].astype(F32)
            delta = back * slope_ref[d, :, at : at + LANES]
            for n in range(3):
                delta_ref[n * mid : (n + 1) * mid, d * cells + at : d * cells + at + LANES] = moved_along_width(
                    delta, n - 1
                ).astype(BF)
    left = delta_ref[...]
    blocks, tails = [None] * 6, []
    inner = rows_ref.shape[1]
    for first in (0, 8):
        group = range(first, min(first + 8, 9))
        right = jnp.concatenate(
            [
                jnp.concatenate(
                    [
                        rows_ref[d + 1 + ab // 3, :, (1 + ab % 3) * LANES : (1 + ab % 3) * LANES + cells]
                        for ab in group
                    ],
                    axis=0,
                )
                for d in range(own)
            ],
            axis=1,
        )
        g = lax.dot_general(left, right, (((1,), (1,)), ((), ())), preferred_element_type=F32)
        for n in range(3):
            part = g[n * mid : (n + 1) * mid]
            if first == 0:
                for m in range(2):
                    blocks[2 * n + m] = part[:, m * LANES : (m + 1) * LANES]
            else:
                tails.append(part)
    tails.append(jnp.zeros((mid, LANES - 3 * inner), F32))
    blocks.append(jnp.concatenate(tails, axis=1))
    if not direct:
        for j, block in enumerate(blocks):
            out_refs[0][j] = block
        return
    keep_ref, send_ref = out_refs
    parts, halves, deps, units, size, _ = keep_ref.shape
    each = mid // parts
    core = odd("hgt")

    def value(part, number):
        unit, start = divmod(number * size, each)
        if unit < 28:
            start += (2 * part + unit % 2) * each
            return g2_ref[unit // 2, start : start + size, :]
        if unit < 35:
            start += part * each
            return blocks[unit - 28][start : start + size]
        return jnp.zeros((size, LANES), F32)

    for part in range(parts):
        for half in range(halves):
            for dep in range(deps):
                for unit in range(units):
                    one, two = (value(part, ((2 * half + c) * deps + dep) * units + unit) for c in range(2))
                    keep_ref[part, half, dep, unit] = jnp.where(core, two, one)
                    send_ref[part, half, dep, unit] = jnp.where(core, one, two).astype(BF)


def plane_kernel(moves, keep_ref, got_ref, kept_ref, *send_refs):
    part = lax.rem(lax.axis_index("dp"), keep_ref.shape[0])
    half = lax.div(lax.axis_index("hgt"), 2)
    kept_ref[...] = keep_ref[part, half] + got_ref[part, half].astype(F32)
    for (x, y), send_ref in zip(moves, send_refs, strict=True):
        p = 1 - part if x else part
        h = 1 - half if y else half
        send_ref[...] = (keep_ref[p, h] + got_ref[p, h].astype(F32)).astype(BF)


def depth_kernel(n_got, *refs):
    kept_ref, got_refs, (_, out_ref, *send_refs) = refs[0], refs[1 : 1 + n_got], refs[1 + n_got :]
    me = lax.axis_index("dep")

    def total(at):
        value = kept_ref[at]
        for ref in got_refs:
            value = value + ref[at].astype(F32)
        return value

    out_ref[...] = total(me)
    for n, ref in enumerate(send_refs):
        ref[...] = total(lax.bitwise_xor(me, n + 1)).astype(BF)


def finish_kernel(kept_ref, *refs):
    *got_refs, out_ref = refs
    value = kept_ref[...]
    for ref in got_refs:
        value = value + ref[...].astype(F32)
    out_ref[...] = value.astype(BF)


def order_kernel(axis, bit, own_ref, *refs):
    *got_refs, out_ref = refs
    me = lax.div(lax.axis_index(axis), bit)
    out_ref[me] = own_ref[...]
    for n, ref in enumerate(got_refs):
        out_ref[lax.bitwise_xor(me, n + 1)] = ref[...]


def unpack_kernel(own_ref, got_ref, g1_ref, g2_ref):
    _, deps, units, block, _ = own_ref.shape
    size = g1_ref.shape[1]
    core = odd("hgt")

    def block_at(number):
        quarter, number = divmod(number, deps * units)
        at = quarter // 2, number // units, number % units
        one, two = (got_ref, own_ref) if quarter % 2 else (own_ref, got_ref)
        return jnp.where(core, two[at], one[at]).astype(F32)

    def get(unit):
        first, start = divmod(unit * size, block)
        if size < block:
            return block_at(first)[start : start + size]
        return jnp.concatenate([block_at(first + n) for n in range(size // block)], axis=0)

    for j in range(14):
        for half in range(2):
            rows = slice(half * size, (half + 1) * size)
            value = get(2 * j + half)
            for m in range(2):
                if j < 12:
                    c, ab = j // 4, 2 * (j % 4) + m
                else:
                    c, ab = 2 * (j - 12) + m, 8
                if c < 3:
                    g2_ref[3 * ab + c, rows, :] = value[:, m * 64 : (m + 1) * 64]
    for j in range(7):
        value = get(28 + j)
        for m in range(4):
            c, ab = (j // 2, 4 * (j % 2) + m) if j < 6 else (m, 8)
            if c < 3:
                g1_ref[3 * ab + c] = value[:, m * 32 : (m + 1) * 32]


def swapped(x, axis, pattern):
    size = lax.axis_size(axis)
    first = {"one": 0, "two": 1, "inner": 1}[pattern]
    pairs = [(i, (i + 1) % size) for i in range(first, size, 2)]
    if pattern == "inner":
        pairs = pairs[:-1]
    return lax.ppermute(x, axis, pairs + [(j, i) for i, j in pairs])


def across(x, axis, bit):
    return lax.ppermute(x, axis, [(i, i ^ bit) for i in range(lax.axis_size(axis))])


def across_plane(x, moves):
    dp, hgt = moves
    if not dp:
        return across(x, "hgt", 2)
    if not hgt:
        return across(x, "dp", 1)
    size = lax.axis_size("dp") * lax.axis_size("hgt")
    flip = lax.axis_size("hgt") + 2
    return lax.ppermute(x, ("dp", "hgt"), [(i, i ^ flip) for i in range(size)])


def per_device(volume, kernel_first, kernel_second, cotangent):
    _, inner, depth, height, width = volume.shape
    mid, out = kernel_first.shape[1], kernel_second.shape[1]
    cells = height * width
    parts, quarters, deps = lax.axis_size("dp"), lax.axis_size("hgt"), lax.axis_size("dep")
    k1, k2 = jnp.swapaxes(kernel_first, 1, 2), jnp.swapaxes(kernel_second, 1, 2)
    rows = depth * height

    one, two = swapped(volume[0], "dep", "one"), swapped(volume[0], "dep", "inner")
    vol, moved, w1, w2, back, back_one, back_two = call(
        prepare_kernel,
        [
            shape((depth, inner, cells), BF),
            shape((depth, 3 * out, cells), BF),
            shape((3 * mid, 9 * inner), BF),
            shape((3 * out, 9 * mid), BF),
            shape((depth, mid, cells + 2 * width), F32),
            shape((mid, cells + 2 * width), BF),
            shape((mid, cells + 2 * width), BF),
        ],
        [volume[0], cotangent[0], k1, k2],
        [
            pltpu.VMEM(volume.shape[1:], BF),
            pltpu.VMEM(cotangent.shape[1:], BF),
            pltpu.VMEM(k1.shape, BF),
            pltpu.VMEM(k2.shape, BF),
            pltpu.VMEM((inner * rows, width), F32),
            pltpu.VMEM((out * rows, width), F32),
            pltpu.SemaphoreType.DMA((4,)),
        ],
        far=(0, 1, 2, 3),
        flops=1_100_000_000,
    )
    deep, one, two = call(
        rim_kernel,
        [shape((3 * depth, inner, cells), BF)] + [shape((3 * depth, inner, 2 * width), BF)] * 2,
        [vol, one, two],
        [pltpu.VMEM((inner * rows, width), F32)],
    )
    one, two = swapped(one, "hgt", "one"), swapped(two, "hgt", "inner")
    back_one, back_two = swapped(back_one, "dep", "one"), swapped(back_two, "dep", "inner")
    back, back_one, back_two = call(
        back_rim_kernel,
        [shape((depth, mid, cells), F32)] + [shape((depth, mid, width), BF)] * 2,
        [back, back_one, back_two],
    )
    back_one, back_two = swapped(back_one, "hgt", "one"), swapped(back_two, "hgt", "inner")

    hidden, slope, g2, wide = call(
        hidden_kernel,
        [
            shape((depth + 2, mid, cells + 2 * width), BF),
            shape((depth, mid, cells), F32),
            shape((14, out, LANES), F32),
            shape((3 * depth, inner, cells + 4 * width), BF),
        ],
        [deep, one, two, w1, moved],
        flops=1_500_000_000,
    )
    size = mid // parts
    direct = parts == 2 and size % 16 == 0
    units = -(-35 * size // (16 * deps * quarters))
    block = (units, 16, width)
    packed = (parts if direct else 1, quarters // 2, deps, *block)
    grads = call(
        functools.partial(delta_kernel, direct),
        [shape(packed, F32), shape(packed, BF)] if direct else [shape((7, mid, LANES), F32)],
        [wide, back, back_one, back_two, slope, g2],
        [pltpu.VMEM((3 * mid, depth * cells), BF)],
        flops=300_000_000,
    )
    if direct:
        keep, send = grads
        moves = [(1, 0), (0, 1), (1, 1)]
    else:
        grad = jnp.swapaxes(grads[0].reshape(7, parts, size, LANES), 0, 1)
        grad2 = jnp.swapaxes(g2.reshape(14, parts, 2, size, LANES), 0, 1).reshape(parts, 28, size, LANES)
        grad = jnp.concatenate([grad2, grad], axis=1).reshape(parts, 35 * size, LANES)
        grad = jnp.pad(grad, ((0, 0), (0, quarters * deps * units * 16 - 35 * size), (0, 0)))
        grad = lax.psum_scatter(grad, "dp", scatter_dimension=0, tiled=True)
        grad = grad.reshape(1, quarters // 2, 2, deps, *block)
        core = lax.rem(lax.axis_index("hgt"), 2)
        keep = lax.dynamic_index_in_dim(grad, core, 2, False)
        send = lax.dynamic_index_in_dim(grad, 1 - core, 2, False).astype(BF)
        moves = [(0, 1)]
    (features,) = call(
        features_kernel, [shape(cotangent.shape[1:], BF)], [hidden, w2], [pltpu.VMEM((out * rows, width), F32)],
        flops=900_000_000,
    )
    got = across(send, "hgt", 1)
    kept, *sends = call(
        functools.partial(plane_kernel, moves),
        [shape((deps, *block), F32)] + [shape((deps, *block), BF)] * len(moves),
        [keep, got],
    )
    gots = [across_plane(send, move) for send, move in zip(sends, moves, strict=True)]
    kept, *sends = call(
        functools.partial(depth_kernel, len(gots)),
        [shape(block, F32)] + [shape(block, BF)] * (deps - 1),
        [kept, *gots, features],
        far=(1 + len(gots),),
    )
    (share,) = call(
        finish_kernel, [shape(block, BF)], [kept, *(across(send, "dep", n + 1) for n, send in enumerate(sends))]
    )
    (share,) = call(
        functools.partial(order_kernel, "dep", 1),
        [shape((deps, *block), BF)],
        [share, *(across(share, "dep", n) for n in range(1, deps))],
    )
    (share,) = call(
        functools.partial(order_kernel, "hgt", 2),
        [shape((quarters // 2, deps, *block), BF)],
        [share, across(share, "hgt", 2)],
    )
    grad_first, grad_second = call(
        unpack_kernel,
        [shape((27, size, inner), F32), shape((27, 2 * size, mid), F32)],
        [share, across(share, "hgt", 1)],
    )
    return features[None], grad_first, grad_second


def solution(mesh):
    placed = (P("dp", None, "dep", "hgt", None), P(), P(), P("dp", None, "dep", "hgt", None))
    return jax.shard_map(
        per_device,
        mesh=mesh,
        in_specs=placed,
        out_specs=(P("dp", None, "dep", "hgt", None), P(None, "dp", None), P(None, "dp", None)),
        check_vma=False,
    )
```

```python
import functools

import jax
import jax.numpy as jnp
from jax import lax
from jax.experimental import pallas as pl
from jax.experimental.pallas import tpu as pltpu
from jax.sharding import PartitionSpec as P

BF, F32 = jnp.bfloat16, jnp.float32
LANES = 128
HGT = ("y", "core")
VMEM_BYTES = 48 * 2**20


def call(body, outs, args, scratch=(), flops=0, far=()):
    moved = sum(x.size * x.dtype.itemsize for x in (*outs, *args))
    return pl.pallas_call(
        body,
        out_shape=outs,
        in_specs=[pl.BlockSpec(memory_space=pl.ANY if n in far else pltpu.VMEM) for n in range(len(args))],
        out_specs=[pl.BlockSpec(memory_space=pltpu.VMEM)] * len(outs),
        scratch_shapes=list(scratch),
        compiler_params=pltpu.CompilerParams(vmem_limit_bytes=VMEM_BYTES),
        cost_estimate=pl.CostEstimate(flops=flops, bytes_accessed=moved, transcendentals=0),
    )(*args)


def shape(dims, dtype):
    return jax.ShapeDtypeStruct(dims, dtype)


def moved_along_width(x, c):
    if c == 0:
        return x
    pieces = []
    for start in range(0, x.shape[1], LANES):
        piece = x[:, start : start + LANES]
        lane = lax.broadcasted_iota(jnp.int32, piece.shape, 1)
        rolled = pltpu.roll(piece, c % LANES, 1)
        pieces.append(jnp.where(lane == (0 if c == 1 else LANES - 1), 0.0, rolled))
    return pieces[0] if len(pieces) == 1 else jnp.concatenate(pieces, axis=1)


def by_rows(ref, scratch, store):
    channels, depth, height, width = ref.shape
    rows = depth * height
    scratch[...] = ref[...].astype(F32).reshape(channels * rows, width)
    for d in range(depth):
        for h in range(height):
            store(d, h, scratch[pl.ds(d * height + h, channels, stride=rows), :])


def odd(axis):
    return lax.rem(lax.axis_index(axis), 2) == 1


def spread_kernel(cot_ref, k2_ref, cot_rows_ref, back_ref, one_ref, two_ref, scratch):
    out, depth, height, _ = cot_ref.shape
    rows = [[None] * height for _ in range(depth)]

    def store(d, h, row):
        rows[d][h] = row.astype(BF)
        cot_rows_ref[d, :, h * LANES : (h + 1) * LANES] = rows[d][h]

    by_rows(cot_ref, scratch, store)
    mid = k2_ref.shape[1]
    none = jnp.zeros((out, 2 * LANES), BF)
    padded = [jnp.concatenate([none, *rows[d], none], axis=1) for d in range(depth)]
    is_odd = odd("dep")
    faces = [[], []]
    for e in range(depth + 2):
        reached = [(d, e - 1 - d) for d in range(depth) if abs(e - 1 - d) <= 1]
        w = jnp.concatenate(
            [
                k2_ref[9 * (a + 1) + 3 * b : 9 * (a + 1) + 3 * b + 3].reshape(3 * mid, out)
                for _, a in reached
                for b in range(3)
            ],
            axis=1,
        )
        for j in range(0, height + 2, 2):
            rhs = jnp.concatenate(
                [padded[d][:, (j + 2 - b) * LANES : (j + 4 - b) * LANES] for d, _ in reached for b in range(3)], axis=0
            )
            y = jnp.dot(w, rhs, preferred_element_type=F32)
            back = sum(moved_along_width(y[n * mid : (n + 1) * mid], n - 1) for n in range(3))
            if 0 < e < depth + 1:
                back_ref[e - 1, :, j * LANES : (j + 2) * LANES] = back
            else:
                faces[e > 0].append(back.astype(BF))
    low, high = (jnp.concatenate(face, axis=1) for face in faces)
    one_ref[...] = jnp.where(is_odd, low, high)
    two_ref[...] = jnp.where(is_odd, high, low)


def arrange_kernel(cot_rows_ref, k1_ref, k2_ref, _, moved_ref, w1_ref, w2_ref):
    depth, out, cells = cot_rows_ref.shape
    for d in range(depth):
        for h in range(0, cells, LANES):
            row = cot_rows_ref[d, :, h : h + LANES]
            for n, c in enumerate((-1, 0, 1)):
                value = row if c == 0 else moved_along_width(row.astype(F32), c).astype(BF)
                moved_ref[d, n * out : (n + 1) * out, h : h + LANES] = value
    mid = k1_ref.shape[2]
    for c in range(3):
        one = jnp.concatenate([k1_ref[3 * ab + c] for ab in range(9)], axis=0)
        w1_ref[c * mid : (c + 1) * mid, :] = one.astype(F32).T.astype(BF)
        two = jnp.concatenate([k2_ref[3 * ab + c] for ab in range(9)], axis=0)
        w2_ref[c * out : (c + 1) * out, :] = two.astype(F32).T.astype(BF)


def sides(axis, one, two):
    me, size = lax.axis_index(axis), lax.axis_size(axis)
    is_odd = odd(axis)
    none = jnp.zeros_like(one)
    before = jnp.where(me == 0, none, jnp.where(is_odd, one, two))
    after = jnp.where(me == size - 1, none, jnp.where(is_odd, two, one))
    return before, after


def rim_kernel(own_ref, one_ref, two_ref, _, deep_ref, send_one_ref, send_two_ref, scratch):
    depth = own_ref.shape[1]
    before, after = sides("dep", one_ref[...], two_ref[...])
    for n, part in enumerate((before, own_ref[...], after)):

        def store(d, h, row, at=n * depth):
            deep_ref[at + d, :, h * LANES : (h + 1) * LANES] = row.astype(BF)

        by_rows(part, scratch, store)
    n, cells = send_one_ref.shape[2], deep_ref.shape[2]
    first, last = deep_ref[:, :, :n], deep_ref[:, :, cells - n :]
    is_odd = odd(HGT)
    send_one_ref[...] = jnp.where(is_odd, first, last)
    send_two_ref[...] = jnp.where(is_odd, last, first)


def back_rim_kernel(own_ref, one_ref, two_ref, back_ref, send_one_ref, send_two_ref):
    before, after = sides("dep", one_ref[...], two_ref[...])
    last = own_ref.shape[0] - 1
    cells = back_ref.shape[2]
    ends = []
    for d in range(last + 1):
        total = own_ref[d]
        if d == 0:
            total = total + before.astype(F32)
        if d == last:
            total = total + after.astype(F32)
        back_ref[d] = total[:, LANES : LANES + cells]
        ends.append((total[:, :LANES].astype(BF), total[:, LANES + cells :].astype(BF)))
    is_odd = odd(HGT)
    for d, (low, high) in enumerate(ends):
        send_one_ref[d] = jnp.where(is_odd, low, high)
        send_two_ref[d] = jnp.where(is_odd, high, low)


def widened(deep_ref, one_ref, two_ref):
    left, right = sides(HGT, one_ref[...], two_ref[...])
    return [jnp.concatenate([left[d], deep_ref[d], right[d]], axis=1) for d in range(deep_ref.shape[0])]


def hidden_kernel(deep_ref, one_ref, two_ref, w1_ref, moved_ref, _, hidden_ref, slope_ref, g2_ref, rows_ref):
    for d, row in enumerate(widened(deep_ref, one_ref, two_ref)):
        rows_ref[d] = row
    rows = rows_ref
    mid = w1_ref.shape[0] // 3
    dep, deps = lax.axis_index("dep"), lax.axis_size("dep")
    hgt, hgts = lax.axis_index(HGT), lax.axis_size(HGT)
    depth, height = hidden_ref.shape[0], hidden_ref.shape[2] // LANES
    w1 = w1_ref[...]
    for d in range(depth):
        for h in range(0, height, 2):
            rhs = jnp.concatenate(
                [rows[d + a, :, (h + b) * LANES : (h + b + 2) * LANES] for a in range(3) for b in range(3)], axis=0
            )
            y = jnp.dot(w1, rhs, preferred_element_type=F32)
            pre = sum(moved_along_width(y[n * mid : (n + 1) * mid], 1 - n) for n in range(3))
            s = 1.0 / (1.0 + jnp.exp(-pre))
            for r in range(2):
                lanes = slice(r * LANES, (r + 1) * LANES)
                p, q = pre[:, lanes], s[:, lanes]
                value = (p * q).astype(BF)
                outside = []
                if d == 0:
                    outside.append(dep == 0)
                if d == depth - 1:
                    outside.append(dep == deps - 1)
                if h + r == 0:
                    outside.append(hgt == 0)
                if h + r == height - 1:
                    outside.append(hgt == hgts - 1)
                for far in outside:
                    value = jnp.where(far, jnp.zeros_like(value), value)
                hidden_ref[d, :, (h + r) * LANES : (h + r + 1) * LANES] = value
                if 0 < d < depth - 1 and 0 < h + r < height - 1:
                    at = (h + r - 1) * LANES
                    slope_ref[d - 1, :, at : at + LANES] = q * (1.0 + p * (1.0 - q))
    cells = (height - 2) * LANES
    own = depth - 2
    out = moved_ref.shape[1] // 3
    left = jnp.concatenate([moved_ref[d] for d in range(own)], axis=1)
    tails = []
    for first in (0, 4, 8):
        group = range(first, min(first + 4, 9))
        right = jnp.concatenate(
            [
                jnp.concatenate(
                    [hidden_ref[d + ab // 3, :, (ab % 3) * LANES : (ab % 3) * LANES + cells] for ab in group], axis=0
                )
                for d in range(own)
            ],
            axis=1,
        )
        g = lax.dot_general(left, right, (((1,), (1,)), ((), ())), preferred_element_type=F32)
        for n in range(3):
            part = g[n * out : (n + 1) * out]
            if first < 8:
                for m in range(2):
                    g2_ref[4 * n + first // 2 + m] = part[:, m * LANES : (m + 1) * LANES]
            else:
                tails.append(part)
    tails.append(jnp.zeros_like(tails[0]))
    for m in range(2):
        g2_ref[12 + m] = jnp.concatenate(tails[2 * m : 2 * m + 2], axis=1)


def features_kernel(hidden_ref, w2_ref, out_ref, token_ref, scratch):
    out = w2_ref.shape[0] // 3
    _, depth, height, _ = out_ref.shape
    w2 = w2_ref[...]
    for d in range(depth):
        for h in range(0, height, 2):
            rhs = jnp.concatenate(
                [
                    hidden_ref[d + a, :, (h + b) * LANES : (h + b + 2) * LANES]
                    for a in range(3)
                    for b in range(3)
                ],
                axis=0,
            )
            y = jnp.dot(w2, rhs, preferred_element_type=F32)
            total = sum(moved_along_width(y[n * out : (n + 1) * out], 1 - n) for n in range(3))
            for r in range(2):
                row = total[:, r * LANES : (r + 1) * LANES]
                scratch[pl.ds(d * height + h + r, out, stride=depth * height), :] = row
    out_ref[...] = scratch[...].reshape(out_ref.shape).astype(BF)
    token_ref[...] = scratch[:8]


def delta_kernel(direct, rows_ref, back_ref, one_ref, two_ref, slope_ref, g2_ref, *outs_and_scratch):
    *out_refs, delta_ref = outs_and_scratch
    before, after = sides(HGT, one_ref[...], two_ref[...])
    own, mid, cells = slope_ref.shape
    for d in range(own):
        for at in range(0, cells, LANES):
            back = back_ref[d, :, at : at + LANES]
            if at == 0:
                back = back + before[d].astype(F32)
            if at == cells - LANES:
                back = back + after[d].astype(F32)
            delta = back * slope_ref[d, :, at : at + LANES]
            for n in range(3):
                delta_ref[n * mid : (n + 1) * mid, d * cells + at : d * cells + at + LANES] = moved_along_width(
                    delta, n - 1
                ).astype(BF)
    left = delta_ref[...]
    blocks, tails = [None] * 6, []
    inner = rows_ref.shape[1]
    for first in (0, 8):
        group = range(first, min(first + 8, 9))
        right = jnp.concatenate(
            [
                jnp.concatenate(
                    [
                        rows_ref[d + 1 + ab // 3, :, (1 + ab % 3) * LANES : (1 + ab % 3) * LANES + cells]
                        for ab in group
                    ],
                    axis=0,
                )
                for d in range(own)
            ],
            axis=1,
        )
        g = lax.dot_general(left, right, (((1,), (1,)), ((), ())), preferred_element_type=F32)
        for n in range(3):
            part = g[n * mid : (n + 1) * mid]
            if first == 0:
                for m in range(2):
                    blocks[2 * n + m] = part[:, m * LANES : (m + 1) * LANES]
            else:
                tails.append(part)
    tails.append(jnp.zeros((mid, LANES - 3 * inner), F32))
    blocks.append(jnp.concatenate(tails, axis=1))
    if not direct:
        for j, block in enumerate(blocks):
            out_refs[0][j] = block
        return
    keep_ref, send_ref = out_refs
    parts, deps, halves, length, _ = keep_ref.shape
    size = mid // parts
    core = lax.axis_index("core") == 1

    def piece(part, number):
        values, row = [], number * length
        while row < (number + 1) * length:
            unit, start = divmod(row, size)
            stop = min(size, start + (number + 1) * length - row)
            if unit < 28:
                first = (2 * part + unit % 2) * size
                values.append(g2_ref[unit // 2, first + start : first + stop, :])
            elif unit < 35:
                values.append(blocks[unit - 28][part * size + start : part * size + stop])
            else:
                values.append(jnp.zeros((stop - start, LANES), F32))
            row += stop - start
        return jnp.concatenate(values, axis=0)

    for part in range(parts):
        for dep in range(deps):
            for half in range(halves):
                one, two = (piece(part, 2 * (dep * halves + half) + c) for c in range(2))
                keep_ref[part, dep, half] = jnp.where(core, two, one)
                send_ref[part, dep, half] = jnp.where(core, one, two).astype(BF)


def join_kernel(keep_ref, got_ref, _, out_ref):
    out_ref[...] = (keep_ref[...] + got_ref[...].astype(F32)).astype(BF)


def total_kernel(in_ref, out_ref):
    value = in_ref[0].astype(F32)
    for n in range(1, in_ref.shape[0]):
        value = value + in_ref[n].astype(F32)
    for n in range(out_ref.shape[0]):
        out_ref[n] = value.astype(BF)


def unpack_kernel(own_ref, got_ref, g1_ref, g2_ref):
    pieces, length, _ = own_ref.shape
    size, inner = g1_ref.shape[1:]
    mid = g2_ref.shape[2]
    core = lax.axis_index("core") == 1
    whole = []
    for n in range(pieces):
        own, got = own_ref[n].astype(F32), got_ref[n].astype(F32)
        whole += [jnp.where(core, got, own), jnp.where(core, own, got)]

    def get(unit):
        values, row = [], unit * size
        while row < (unit + 1) * size:
            number, start = divmod(row, length)
            stop = min(length, start + (unit + 1) * size - row)
            values.append(whole[number][start:stop])
            row += stop - start
        return values[0] if len(values) == 1 else jnp.concatenate(values, axis=0)

    for j in range(14):
        for half in range(2):
            value = get(2 * j + half)
            for m in range(2):
                c, ab = (j // 4, 2 * (j % 4) + m) if j < 12 else (2 * (j - 12) + m, 8)
                if c < 3:
                    g2_ref[3 * ab + c, half * size : (half + 1) * size, :] = value[:, m * mid : (m + 1) * mid]
    for j in range(7):
        value = get(28 + j)
        for m in range(4):
            c, ab = (j // 2, 4 * (j % 2) + m) if j < 6 else (m, 8)
            if c < 3:
                g1_ref[3 * ab + c] = value[:, m * inner : (m + 1) * inner]


def swapped(x, axis, first):
    size = lax.axis_size(axis)
    partner = list(range(size))
    for i in range(first, size - 1, 2):
        partner[i], partner[i + 1] = i + 1, i
    return lax.ppermute(x, axis, list(enumerate(partner)))


def from_other_core(x):
    return lax.ppermute(x, "core", [(0, 1), (1, 0)])


def per_device(volume, kernel_first, kernel_second, cotangent):
    _, inner, depth, height, width = volume.shape
    mid, out = kernel_first.shape[1], kernel_second.shape[1]
    cells = height * width
    parts = lax.axis_size("dp")
    k1, k2 = jnp.swapaxes(kernel_first, 1, 2), jnp.swapaxes(kernel_second, 1, 2)
    rows = depth * height

    one, two = swapped(volume[0], "dep", 0), swapped(volume[0], "dep", 1)
    cot_rows, back, back_one, back_two = call(
        spread_kernel,
        [
            shape((depth, out, cells), BF),
            shape((depth, mid, cells + 2 * width), F32),
            shape((mid, cells + 2 * width), BF),
            shape((mid, cells + 2 * width), BF),
        ],
        [cotangent[0], k2],
        [pltpu.VMEM((out * rows, width), F32)],
        flops=1_100_000_000,
    )
    deep, one, two = call(
        rim_kernel,
        [shape((3 * depth, inner, cells), BF)] + [shape((3 * depth, inner, 2 * width), BF)] * 2,
        [volume[0], one, two, cot_rows],
        [pltpu.VMEM((inner * rows, width), F32)],
    )
    one, two = swapped(one, HGT, 0), swapped(two, HGT, 1)
    moved, w1, w2 = call(
        arrange_kernel,
        [shape((depth, 3 * out, cells), BF), shape((3 * mid, 9 * inner), BF), shape((3 * out, 9 * mid), BF)],
        [cot_rows, k1, k2, deep],
        flops=500_000_000,
    )
    back_one, back_two = swapped(back_one, "dep", 0), swapped(back_two, "dep", 1)
    back, back_one, back_two = call(
        back_rim_kernel,
        [shape((depth, mid, cells), F32)] + [shape((depth, mid, width), BF)] * 2,
        [back, back_one, back_two],
    )
    back_one, back_two = swapped(back_one, HGT, 0), swapped(back_two, HGT, 1)

    hidden, slope, g2, wide = call(
        hidden_kernel,
        [
            shape((depth + 2, mid, cells + 2 * width), BF),
            shape((depth, mid, cells), F32),
            shape((14, out, LANES), F32),
            shape((3 * depth, inner, cells + 4 * width), BF),
        ],
        [deep, one, two, w1, moved, back],
        flops=1_500_000_000,
    )
    size = mid // parts
    direct = parts == 2 and size % 16 == 0
    deps, halves = lax.axis_size("dep"), lax.axis_size("y")
    pieces = deps * halves
    length = -(-35 * size // (16 * pieces)) * 8
    packed = (parts, deps, halves, length, width)
    grads = call(
        functools.partial(delta_kernel, direct),
        [shape(packed, F32), shape(packed, BF)] if direct else [shape((7, mid, LANES), F32)],
        [wide, back, back_one, back_two, slope, g2],
        [pltpu.VMEM((3 * mid, depth * cells), BF)],
        flops=300_000_000,
    )
    if direct:
        keep, send = grads
        group = ("dp", "dep", "y")
    else:
        grad = jnp.swapaxes(grads[0].reshape(7, parts, size, LANES), 0, 1)
        grad2 = jnp.swapaxes(g2.reshape(14, parts, 2, size, LANES), 0, 1).reshape(parts, 28, size, LANES)
        grad = jnp.concatenate([grad2, grad], axis=1).reshape(parts, 35 * size, LANES)
        grad = jnp.pad(grad, ((0, 0), (0, 2 * pieces * length - 35 * size), (0, 0)))
        grad = lax.psum_scatter(grad, "dp", scatter_dimension=0, tiled=True)
        grad = grad.reshape(1, deps, halves, 2, length, LANES)
        core = lax.axis_index("core")
        keep = lax.dynamic_index_in_dim(grad, core, 3, False)
        send = lax.dynamic_index_in_dim(grad, 1 - core, 3, False).astype(BF)
        group = ("dep", "y")
    features, token = call(
        features_kernel,
        [shape(cotangent.shape[1:], BF), shape((8, width), F32)],
        [hidden, w2],
        [pltpu.VMEM((out * rows, width), F32)],
        flops=900_000_000,
    )
    (joined,) = call(join_kernel, [shape(keep.shape, BF)], [keep, from_other_core(send), token])
    arrived = lax.all_to_all(joined.reshape(-1, length, width), group, 0, 0, tiled=True)
    (share,) = call(total_kernel, [shape((pieces, length, width), BF)], [arrived])
    own = lax.all_to_all(share, ("dep", "y"), 0, 0, tiled=True)
    grad_first, grad_second = call(
        unpack_kernel,
        [shape((27, size, inner), F32), shape((27, 2 * size, mid), F32)],
        [own, from_other_core(own)],
    )
    return features[None], grad_first, grad_second


def solution(mesh):
    dp, dep, hgt = (mesh.shape[axis] for axis in ("dp", "dep", "hgt"))
    split = jax.sharding.Mesh(mesh.devices.reshape(dp, dep, hgt // 2, 2), ("dp", "dep", *HGT))
    block = P("dp", None, "dep", HGT, None)
    return jax.shard_map(
        per_device,
        mesh=split,
        in_specs=(block, P(), P(), block),
        out_specs=(block, P(None, "dp", None), P(None, "dp", None)),
        check_vma=False,
    )
```

```python
import functools

import jax
import jax.numpy as jnp
from jax import lax
from jax.experimental import pallas as pl
from jax.experimental.pallas import tpu as pltpu
from jax.sharding import PartitionSpec as P

BF, F32 = jnp.bfloat16, jnp.float32
LANES = 128
HGT = ("y", "core")
VMEM_BYTES = 48 * 2**20


def call(body, outs, args, scratch=(), flops=0, far=()):
    moved = sum(x.size * x.dtype.itemsize for x in (*outs, *args))
    return pl.pallas_call(
        body,
        out_shape=outs,
        in_specs=[pl.BlockSpec(memory_space=pl.ANY if n in far else pltpu.VMEM) for n in range(len(args))],
        out_specs=[pl.BlockSpec(memory_space=pltpu.VMEM)] * len(outs),
        scratch_shapes=list(scratch),
        compiler_params=pltpu.CompilerParams(vmem_limit_bytes=VMEM_BYTES),
        cost_estimate=pl.CostEstimate(flops=flops, bytes_accessed=moved, transcendentals=0),
    )(*args)


def shape(dims, dtype):
    return jax.ShapeDtypeStruct(dims, dtype)


def moved_along_width(x, c):
    if c == 0:
        return x
    pieces = []
    for start in range(0, x.shape[1], LANES):
        piece = x[:, start : start + LANES]
        lane = lax.broadcasted_iota(jnp.int32, piece.shape, 1)
        rolled = pltpu.roll(piece, c % LANES, 1)
        pieces.append(jnp.where(lane == (0 if c == 1 else LANES - 1), 0.0, rolled))
    return pieces[0] if len(pieces) == 1 else jnp.concatenate(pieces, axis=1)


def by_rows(ref, scratch, store):
    channels, depth, height, width = ref.shape
    rows = depth * height
    scratch[...] = ref[...].astype(F32).reshape(channels * rows, width)
    for d in range(depth):
        for h in range(height):
            store(d, h, scratch[pl.ds(d * height + h, channels, stride=rows), :])


def odd(axis):
    return lax.rem(lax.axis_index(axis), 2) == 1


def spread_kernel(cot_ref, k2_ref, cot_rows_ref, back_ref, one_ref, two_ref, scratch):
    out, depth, height, _ = cot_ref.shape
    rows = [[None] * height for _ in range(depth)]

    def store(d, h, row):
        rows[d][h] = row.astype(BF)
        cot_rows_ref[d, :, h * LANES : (h + 1) * LANES] = rows[d][h]

    by_rows(cot_ref, scratch, store)
    mid = k2_ref.shape[1]
    none = jnp.zeros((out, 2 * LANES), BF)
    padded = [jnp.concatenate([none, *rows[d], none], axis=1) for d in range(depth)]
    is_odd = odd("dep")
    faces = [[], []]
    for e in range(depth + 2):
        reached = [(d, e - 1 - d) for d in range(depth) if abs(e - 1 - d) <= 1]
        w = jnp.concatenate(
            [
                k2_ref[9 * (a + 1) + 3 * b : 9 * (a + 1) + 3 * b + 3].reshape(3 * mid, out)
                for _, a in reached
                for b in range(3)
            ],
            axis=1,
        )
        for j in range(0, height + 2, 2):
            rhs = jnp.concatenate(
                [padded[d][:, (j + 2 - b) * LANES : (j + 4 - b) * LANES] for d, _ in reached for b in range(3)], axis=0
            )
            y = jnp.dot(w, rhs, preferred_element_type=F32)
            back = sum(moved_along_width(y[n * mid : (n + 1) * mid], n - 1) for n in range(3))
            if 0 < e < depth + 1:
                back_ref[e - 1, :, j * LANES : (j + 2) * LANES] = back
            else:
                faces[e > 0].append(back.astype(BF))
    low, high = (jnp.concatenate(face, axis=1) for face in faces)
    one_ref[...] = jnp.where(is_odd, low, high)
    two_ref[...] = jnp.where(is_odd, high, low)


def arrange_kernel(cot_rows_ref, k1_ref, k2_ref, _, moved_ref, w1_ref, w2_ref):
    depth, out, cells = cot_rows_ref.shape
    for d in range(depth):
        for h in range(0, cells, LANES):
            row = cot_rows_ref[d, :, h : h + LANES]
            for n, c in enumerate((-1, 0, 1)):
                value = row if c == 0 else moved_along_width(row.astype(F32), c).astype(BF)
                moved_ref[d, n * out : (n + 1) * out, h : h + LANES] = value
    mid = k1_ref.shape[2]
    for c in range(3):
        one = jnp.concatenate([k1_ref[3 * ab + c] for ab in range(9)], axis=0)
        w1_ref[c * mid : (c + 1) * mid, :] = one.astype(F32).T.astype(BF)
        two = jnp.concatenate([k2_ref[3 * ab + c] for ab in range(9)], axis=0)
        w2_ref[c * out : (c + 1) * out, :] = two.astype(F32).T.astype(BF)


def sides(axis, one, two):
    me, size = lax.axis_index(axis), lax.axis_size(axis)
    is_odd = odd(axis)
    none = jnp.zeros_like(one)
    before = jnp.where(me == 0, none, jnp.where(is_odd, one, two))
    after = jnp.where(me == size - 1, none, jnp.where(is_odd, two, one))
    return before, after


def rim_kernel(own_ref, one_ref, two_ref, _, deep_ref, send_one_ref, send_two_ref, scratch):
    depth = own_ref.shape[1]
    before, after = sides("dep", one_ref[...], two_ref[...])
    for n, part in enumerate((before, own_ref[...], after)):

        def store(d, h, row, at=n * depth):
            deep_ref[at + d, :, h * LANES : (h + 1) * LANES] = row.astype(BF)

        by_rows(part, scratch, store)
    n, cells = send_one_ref.shape[2], deep_ref.shape[2]
    first, last = deep_ref[:, :, :n], deep_ref[:, :, cells - n :]
    is_odd = odd(HGT)
    send_one_ref[...] = jnp.where(is_odd, first, last)
    send_two_ref[...] = jnp.where(is_odd, last, first)


def back_rim_kernel(own_ref, one_ref, two_ref, back_ref, send_one_ref, send_two_ref):
    before, after = sides("dep", one_ref[...], two_ref[...])
    last = own_ref.shape[0] - 1
    cells = back_ref.shape[2]
    ends = []
    for d in range(last + 1):
        total = own_ref[d]
        if d == 0:
            total = total + before.astype(F32)
        if d == last:
            total = total + after.astype(F32)
        back_ref[d] = total[:, LANES : LANES + cells]
        ends.append((total[:, :LANES].astype(BF), total[:, LANES + cells :].astype(BF)))
    is_odd = odd(HGT)
    for d, (low, high) in enumerate(ends):
        send_one_ref[d] = jnp.where(is_odd, low, high)
        send_two_ref[d] = jnp.where(is_odd, high, low)


def widened(deep_ref, one_ref, two_ref):
    left, right = sides(HGT, one_ref[...], two_ref[...])
    return [jnp.concatenate([left[d], deep_ref[d], right[d]], axis=1) for d in range(deep_ref.shape[0])]


def hidden_kernel(deep_ref, one_ref, two_ref, w1_ref, moved_ref, _, hidden_ref, slope_ref, g2_ref, rows_ref):
    for d, row in enumerate(widened(deep_ref, one_ref, two_ref)):
        rows_ref[d] = row
    rows = rows_ref
    mid = w1_ref.shape[0] // 3
    dep, deps = lax.axis_index("dep"), lax.axis_size("dep")
    hgt, hgts = lax.axis_index(HGT), lax.axis_size(HGT)
    depth, height = hidden_ref.shape[0], hidden_ref.shape[2] // LANES
    w1 = w1_ref[...]
    for d in range(depth):
        for h in range(0, height, 2):
            rhs = jnp.concatenate(
                [rows[d + a, :, (h + b) * LANES : (h + b + 2) * LANES] for a in range(3) for b in range(3)], axis=0
            )
            y = jnp.dot(w1, rhs, preferred_element_type=F32)
            pre = sum(moved_along_width(y[n * mid : (n + 1) * mid], 1 - n) for n in range(3))
            s = 1.0 / (1.0 + jnp.exp(-pre))
            for r in range(2):
                lanes = slice(r * LANES, (r + 1) * LANES)
                p, q = pre[:, lanes], s[:, lanes]
                value = (p * q).astype(BF)
                outside = []
                if d == 0:
                    outside.append(dep == 0)
                if d == depth - 1:
                    outside.append(dep == deps - 1)
                if h + r == 0:
                    outside.append(hgt == 0)
                if h + r == height - 1:
                    outside.append(hgt == hgts - 1)
                for far in outside:
                    value = jnp.where(far, jnp.zeros_like(value), value)
                hidden_ref[d, :, (h + r) * LANES : (h + r + 1) * LANES] = value
                if 0 < d < depth - 1 and 0 < h + r < height - 1:
                    at = (h + r - 1) * LANES
                    slope_ref[d - 1, :, at : at + LANES] = q * (1.0 + p * (1.0 - q))
    cells = (height - 2) * LANES
    own = depth - 2
    out = moved_ref.shape[1] // 3
    left = jnp.concatenate([moved_ref[d] for d in range(own)], axis=1)
    tails = []
    for first in (0, 4, 8):
        group = range(first, min(first + 4, 9))
        right = jnp.concatenate(
            [
                jnp.concatenate(
                    [hidden_ref[d + ab // 3, :, (ab % 3) * LANES : (ab % 3) * LANES + cells] for ab in group], axis=0
                )
                for d in range(own)
            ],
            axis=1,
        )
        g = lax.dot_general(left, right, (((1,), (1,)), ((), ())), preferred_element_type=F32)
        for n in range(3):
            part = g[n * out : (n + 1) * out]
            if first < 8:
                for m in range(2):
                    g2_ref[4 * n + first // 2 + m] = part[:, m * LANES : (m + 1) * LANES]
            else:
                tails.append(part)
    tails.append(jnp.zeros_like(tails[0]))
    for m in range(2):
        g2_ref[12 + m] = jnp.concatenate(tails[2 * m : 2 * m + 2], axis=1)


def features_kernel(hidden_ref, w2_ref, out_ref, token_ref, scratch):
    out = w2_ref.shape[0] // 3
    _, depth, height, _ = out_ref.shape
    w2 = w2_ref[...]
    for d in range(depth):
        for h in range(0, height, 2):
            rhs = jnp.concatenate(
                [
                    hidden_ref[d + a, :, (h + b) * LANES : (h + b + 2) * LANES]
                    for a in range(3)
                    for b in range(3)
                ],
                axis=0,
            )
            y = jnp.dot(w2, rhs, preferred_element_type=F32)
            total = sum(moved_along_width(y[n * out : (n + 1) * out], 1 - n) for n in range(3))
            for r in range(2):
                row = total[:, r * LANES : (r + 1) * LANES]
                scratch[pl.ds(d * height + h + r, out, stride=depth * height), :] = row
    out_ref[...] = scratch[...].reshape(out_ref.shape).astype(BF)
    token_ref[...] = scratch[:8]


def delta_kernel(direct, rows_ref, back_ref, one_ref, two_ref, slope_ref, g2_ref, *outs_and_scratch):
    *out_refs, delta_ref = outs_and_scratch
    before, after = sides(HGT, one_ref[...], two_ref[...])
    own, mid, cells = slope_ref.shape
    for d in range(own):
        for at in range(0, cells, LANES):
            back = back_ref[d, :, at : at + LANES]
            if at == 0:
                back = back + before[d].astype(F32)
            if at == cells - LANES:
                back = back + after[d].astype(F32)
            delta = back * slope_ref[d, :, at : at + LANES]
            for n in range(3):
                delta_ref[n * mid : (n + 1) * mid, d * cells + at : d * cells + at + LANES] = moved_along_width(
                    delta, n - 1
                ).astype(BF)
    left = delta_ref[...]
    blocks, tails = [None] * 6, []
    inner = rows_ref.shape[1]
    for first in (0, 8):
        group = range(first, min(first + 8, 9))
        right = jnp.concatenate(
            [
                jnp.concatenate(
                    [
                        rows_ref[d + 1 + ab // 3, :, (1 + ab % 3) * LANES : (1 + ab % 3) * LANES + cells]
                        for ab in group
                    ],
                    axis=0,
                )
                for d in range(own)
            ],
            axis=1,
        )
        g = lax.dot_general(left, right, (((1,), (1,)), ((), ())), preferred_element_type=F32)
        for n in range(3):
            part = g[n * mid : (n + 1) * mid]
            if first == 0:
                for m in range(2):
                    blocks[2 * n + m] = part[:, m * LANES : (m + 1) * LANES]
            else:
                tails.append(part)
    tails.append(jnp.zeros((mid, LANES - 3 * inner), F32))
    blocks.append(jnp.concatenate(tails, axis=1))
    if not direct:
        for j, block in enumerate(blocks):
            out_refs[0][j] = block
        return
    keep_ref, send_ref = out_refs
    parts, halves, length, _ = keep_ref.shape
    size = mid // parts
    core = lax.axis_index("core") == 1

    def piece(part, number):
        values, row = [], number * length
        while row < (number + 1) * length:
            unit, start = divmod(row, size)
            stop = min(size, start + (number + 1) * length - row)
            if unit < 28:
                first = (2 * part + unit % 2) * size
                values.append(g2_ref[unit // 2, first + start : first + stop, :])
            elif unit < 35:
                values.append(blocks[unit - 28][part * size + start : part * size + stop])
            else:
                values.append(jnp.zeros((stop - start, LANES), F32))
            row += stop - start
        return jnp.concatenate(values, axis=0)

    for part in range(parts):
        for half in range(halves):
            one, two = (piece(part, 2 * half + c) for c in range(2))
            keep_ref[part, half] = jnp.where(core, two, one)
            send_ref[part, half] = jnp.where(core, one, two).astype(BF)


def plane_kernel(moves, keep_ref, got_ref, kept_ref, *send_refs):
    part = lax.rem(lax.axis_index("dp"), keep_ref.shape[0])
    half = lax.axis_index("y")
    kept_ref[...] = keep_ref[part, half] + got_ref[part, half].astype(F32)
    for (x, y), send_ref in zip(moves, send_refs, strict=True):
        p = 1 - part if x else part
        h = 1 - half if y else half
        send_ref[...] = (keep_ref[p, h] + got_ref[p, h].astype(F32)).astype(BF)


def total_kernel(kept_ref, *refs):
    *got_refs, _, out_ref = refs
    value = kept_ref[...]
    for ref in got_refs:
        value = value + ref[...].astype(F32)
    out_ref[...] = value.astype(BF)


def add_kernel(one_ref, two_ref, out_ref):
    out_ref[...] = (one_ref[...].astype(F32) + two_ref[...].astype(F32)).astype(BF)


def order_kernel(own_ref, got_ref, out_ref):
    mine = lax.axis_index("y")
    out_ref[mine] = own_ref[...]
    out_ref[1 - mine] = got_ref[...]


def unpack_kernel(own_ref, got_ref, g1_ref, g2_ref):
    pieces, length, _ = own_ref.shape
    size, inner = g1_ref.shape[1:]
    mid = g2_ref.shape[2]
    core = lax.axis_index("core") == 1
    whole = []
    for n in range(pieces):
        own, got = own_ref[n].astype(F32), got_ref[n].astype(F32)
        whole += [jnp.where(core, got, own), jnp.where(core, own, got)]

    def get(unit):
        values, row = [], unit * size
        while row < (unit + 1) * size:
            number, start = divmod(row, length)
            stop = min(length, start + (unit + 1) * size - row)
            values.append(whole[number][start:stop])
            row += stop - start
        return values[0] if len(values) == 1 else jnp.concatenate(values, axis=0)

    for j in range(14):
        for half in range(2):
            value = get(2 * j + half)
            for m in range(2):
                c, ab = (j // 4, 2 * (j % 4) + m) if j < 12 else (2 * (j - 12) + m, 8)
                if c < 3:
                    g2_ref[3 * ab + c, half * size : (half + 1) * size, :] = value[:, m * mid : (m + 1) * mid]
    for j in range(7):
        value = get(28 + j)
        for m in range(4):
            c, ab = (j // 2, 4 * (j % 2) + m) if j < 6 else (m, 8)
            if c < 3:
                g1_ref[3 * ab + c] = value[:, m * inner : (m + 1) * inner]


def swapped(x, axis, first):
    axes = (axis,) if isinstance(axis, str) else axis
    parts, size = lax.axis_size("dp"), lax.axis_size(axis)
    partner = list(range(parts * size))
    for i in partner:
        part, at = divmod(i, size)
        if first <= at < size - (size - first) % 2:
            partner[i] = part * size + (at - first ^ 1) + first
        elif parts % 2 == 0:
            partner[i] = (part ^ 1) * size + at
    return lax.ppermute(x, ("dp", *axes), list(enumerate(partner)))


def across(x, *moves):
    axes = tuple(axis for axis, _ in moves)
    flip = 0
    for axis, bit in moves:
        flip = flip * lax.axis_size(axis) + bit
    return lax.ppermute(x, axes, [(i, i ^ flip) for i in range(lax.axis_size(axes))])


def per_device(volume, kernel_first, kernel_second, cotangent):
    _, inner, depth, height, width = volume.shape
    mid, out = kernel_first.shape[1], kernel_second.shape[1]
    cells = height * width
    parts = lax.axis_size("dp")
    k1, k2 = jnp.swapaxes(kernel_first, 1, 2), jnp.swapaxes(kernel_second, 1, 2)
    rows = depth * height

    one, two = swapped(volume[0], "dep", 0), swapped(volume[0], "dep", 1)
    cot_rows, back, back_one, back_two = call(
        spread_kernel,
        [
            shape((depth, out, cells), BF),
            shape((depth, mid, cells + 2 * width), F32),
            shape((mid, cells + 2 * width), BF),
            shape((mid, cells + 2 * width), BF),
        ],
        [cotangent[0], k2],
        [pltpu.VMEM((out * rows, width), F32)],
        flops=1_100_000_000,
    )
    deep, one, two = call(
        rim_kernel,
        [shape((3 * depth, inner, cells), BF)] + [shape((3 * depth, inner, 2 * width), BF)] * 2,
        [volume[0], one, two, cot_rows],
        [pltpu.VMEM((inner * rows, width), F32)],
    )
    one, two = swapped(one, HGT, 0), swapped(two, HGT, 1)
    moved, w1, w2 = call(
        arrange_kernel,
        [shape((depth, 3 * out, cells), BF), shape((3 * mid, 9 * inner), BF), shape((3 * out, 9 * mid), BF)],
        [cot_rows, k1, k2, deep],
        flops=500_000_000,
    )
    back_one, back_two = swapped(back_one, "dep", 0), swapped(back_two, "dep", 1)
    back, back_one, back_two = call(
        back_rim_kernel,
        [shape((depth, mid, cells), F32)] + [shape((depth, mid, width), BF)] * 2,
        [back, back_one, back_two],
    )
    back_one, back_two = swapped(back_one, HGT, 0), swapped(back_two, HGT, 1)

    hidden, slope, g2, wide = call(
        hidden_kernel,
        [
            shape((depth + 2, mid, cells + 2 * width), BF),
            shape((depth, mid, cells), F32),
            shape((14, out, LANES), F32),
            shape((3 * depth, inner, cells + 4 * width), BF),
        ],
        [deep, one, two, w1, moved, back],
        flops=1_500_000_000,
    )
    size = mid // parts
    direct = parts == 2 and size % 16 == 0
    halves = lax.axis_size("y")
    length = -(-35 * size // (32 * halves)) * 16
    packed = (parts, halves, length, width)
    grads = call(
        functools.partial(delta_kernel, direct),
        [shape(packed, F32), shape(packed, BF)] if direct else [shape((7, mid, LANES), F32)],
        [wide, back, back_one, back_two, slope, g2],
        [pltpu.VMEM((3 * mid, depth * cells), BF)],
        flops=300_000_000,
    )
    if direct:
        keep, send = grads
        moves = [(1, 0), (0, 1), (1, 1)]
    else:
        grad = jnp.swapaxes(grads[0].reshape(7, parts, size, LANES), 0, 1)
        grad2 = jnp.swapaxes(g2.reshape(14, parts, 2, size, LANES), 0, 1).reshape(parts, 28, size, LANES)
        grad = jnp.concatenate([grad2, grad], axis=1).reshape(parts, 35 * size, LANES)
        grad = jnp.pad(grad, ((0, 0), (0, 2 * halves * length - 35 * size), (0, 0)))
        grad = lax.psum_scatter(grad, "dp", scatter_dimension=0, tiled=True)
        grad = grad.reshape(1, halves, 2, length, LANES)
        core = lax.axis_index("core")
        keep = lax.dynamic_index_in_dim(grad, core, 2, False)
        send = lax.dynamic_index_in_dim(grad, 1 - core, 2, False).astype(BF)
        moves = [(0, 1)]
    features, token = call(
        features_kernel,
        [shape(cotangent.shape[1:], BF), shape((8, width), F32)],
        [hidden, w2],
        [pltpu.VMEM((out * rows, width), F32)],
        flops=900_000_000,
    )
    kept, *sends = call(
        functools.partial(plane_kernel, moves),
        [shape((length, width), F32)] + [shape((length, width), BF)] * len(moves),
        [keep, across(send, ("core", 1))],
    )
    gots = [across(send, ("dp", x), ("y", y)) for send, (x, y) in zip(sends, moves, strict=True)]
    (share,) = call(total_kernel, [shape((length, width), BF)], [kept, *gots, token])
    for bit in (1, 2):
        (share,) = call(add_kernel, [shape((length, width), BF)], [share, across(share, ("dep", bit))])
    (own,) = call(order_kernel, [shape((halves, length, width), BF)], [share, across(share, ("y", 1))])
    grad_first, grad_second = call(
        unpack_kernel,
        [shape((27, size, inner), F32), shape((27, 2 * size, mid), F32)],
        [own, across(own, ("core", 1))],
    )
    return features[None], grad_first, grad_second


def solution(mesh):
    dp, dep, hgt = (mesh.shape[axis] for axis in ("dp", "dep", "hgt"))
    split = jax.sharding.Mesh(mesh.devices.reshape(dp, dep, hgt // 2, 2), ("dp", "dep", *HGT))
    block = P("dp", None, "dep", HGT, None)
    return jax.shard_map(
        per_device,
        mesh=split,
        in_specs=(block, P(), P(), block),
        out_specs=(block, P(None, "dp", None), P(None, "dp", None)),
        check_vma=False,
    )
```

```python
import functools

import jax
import jax.numpy as jnp
from jax import lax
from jax.experimental import pallas as pl
from jax.experimental.pallas import tpu as pltpu
from jax.sharding import PartitionSpec as P

BF, F32 = jnp.bfloat16, jnp.float32
LANES = 128
HGT = ("y", "core")
VMEM_BYTES = 48 * 2**20


def call(body, outs, args, scratch=(), flops=0, far=()):
    moved = sum(x.size * x.dtype.itemsize for x in (*outs, *args))
    return pl.pallas_call(
        body,
        out_shape=outs,
        in_specs=[pl.BlockSpec(memory_space=pl.ANY if n in far else pltpu.VMEM) for n in range(len(args))],
        out_specs=[pl.BlockSpec(memory_space=pltpu.VMEM)] * len(outs),
        scratch_shapes=list(scratch),
        compiler_params=pltpu.CompilerParams(vmem_limit_bytes=VMEM_BYTES),
        cost_estimate=pl.CostEstimate(flops=flops, bytes_accessed=moved, transcendentals=0),
    )(*args)


def shape(dims, dtype):
    return jax.ShapeDtypeStruct(dims, dtype)


def moved_along_width(x, c):
    if c == 0:
        return x
    pieces = []
    for start in range(0, x.shape[1], LANES):
        piece = x[:, start : start + LANES]
        lane = lax.broadcasted_iota(jnp.int32, piece.shape, 1)
        rolled = pltpu.roll(piece, c % LANES, 1)
        pieces.append(jnp.where(lane == (0 if c == 1 else LANES - 1), 0.0, rolled))
    return pieces[0] if len(pieces) == 1 else jnp.concatenate(pieces, axis=1)


def by_rows(ref, scratch, store):
    channels, depth, height, width = ref.shape
    rows = depth * height
    scratch[...] = ref[...].astype(F32).reshape(channels * rows, width)
    for d in range(depth):
        for h in range(height):
            store(d, h, scratch[pl.ds(d * height + h, channels, stride=rows), :])


def odd(axis):
    return lax.rem(lax.axis_index(axis), 2) == 1


def blank_kernel(out_ref):
    out_ref[...] = jnp.zeros(out_ref.shape, BF)


def spread_kernel(cot_ref, k2_ref, blank_ref, cot_rows_ref, back_ref, one_ref, two_ref, scratch):
    out, depth, height, _ = cot_ref.shape
    rows = [[None] * height for _ in range(depth)]

    def store(d, h, row):
        rows[d][h] = row.astype(BF)
        cot_rows_ref[d, :, h * LANES : (h + 1) * LANES] = rows[d][h]

    by_rows(cot_ref, scratch, store)
    mid = k2_ref.shape[1]
    none = blank_ref[...]
    padded = [jnp.concatenate([none, *rows[d], none], axis=1) for d in range(depth)]
    is_odd = odd("dep")
    faces = [[], []]
    for e in range(depth + 2):
        reached = [(d, e - 1 - d) for d in range(depth) if abs(e - 1 - d) <= 1]
        w = jnp.concatenate(
            [
                k2_ref[9 * (a + 1) + 3 * b : 9 * (a + 1) + 3 * b + 3].reshape(3 * mid, out)
                for _, a in reached
                for b in range(3)
            ],
            axis=1,
        )
        for j in range(0, height + 2, 2):
            rhs = jnp.concatenate(
                [padded[d][:, (j + 2 - b) * LANES : (j + 4 - b) * LANES] for d, _ in reached for b in range(3)], axis=0
            )
            y = jnp.dot(w, rhs, preferred_element_type=F32)
            back = sum(moved_along_width(y[n * mid : (n + 1) * mid], n - 1) for n in range(3))
            if 0 < e < depth + 1:
                back_ref[e - 1, :, j * LANES : (j + 2) * LANES] = back
            else:
                faces[e > 0].append(back.astype(BF))
    low, high = (jnp.concatenate(face, axis=1) for face in faces)
    one_ref[...] = jnp.where(is_odd, low, high)
    two_ref[...] = jnp.where(is_odd, high, low)


def arrange_kernel(cot_rows_ref, k1_ref, k2_ref, _, moved_ref, w1_ref, w2_ref):
    depth, out, cells = cot_rows_ref.shape
    for d in range(depth):
        for h in range(0, cells, LANES):
            row = cot_rows_ref[d, :, h : h + LANES]
            for n, c in enumerate((-1, 0, 1)):
                value = row if c == 0 else moved_along_width(row.astype(F32), c).astype(BF)
                moved_ref[d, n * out : (n + 1) * out, h : h + LANES] = value
    mid = k1_ref.shape[2]
    for c in range(3):
        one = jnp.concatenate([k1_ref[3 * ab + c] for ab in range(9)], axis=0)
        w1_ref[c * mid : (c + 1) * mid, :] = one.astype(F32).T.astype(BF)
        two = jnp.concatenate([k2_ref[3 * ab + c] for ab in range(9)], axis=0)
        w2_ref[c * out : (c + 1) * out, :] = two.astype(F32).T.astype(BF)


def sides(axis, one, two):
    me, size = lax.axis_index(axis), lax.axis_size(axis)
    is_odd = odd(axis)
    none = jnp.zeros_like(one)
    before = jnp.where(me == 0, none, jnp.where(is_odd, one, two))
    after = jnp.where(me == size - 1, none, jnp.where(is_odd, two, one))
    return before, after


def rim_kernel(own_ref, one_ref, two_ref, _, deep_ref, send_one_ref, send_two_ref, scratch):
    depth = own_ref.shape[1]
    before, after = sides("dep", one_ref[...], two_ref[...])
    for n, part in enumerate((before, own_ref[...], after)):

        def store(d, h, row, at=n * depth):
            deep_ref[at + d, :, h * LANES : (h + 1) * LANES] = row.astype(BF)

        by_rows(part, scratch, store)
    n, cells = send_one_ref.shape[2], deep_ref.shape[2]
    first, last = deep_ref[:, :, :n], deep_ref[:, :, cells - n :]
    is_odd = odd(HGT)
    send_one_ref[...] = jnp.where(is_odd, first, last)
    send_two_ref[...] = jnp.where(is_odd, last, first)


def back_rim_kernel(own_ref, one_ref, two_ref, back_ref, send_one_ref, send_two_ref):
    before, after = sides("dep", one_ref[...], two_ref[...])
    last = own_ref.shape[0] - 1
    cells = back_ref.shape[2]
    ends = []
    for d in range(last + 1):
        total = own_ref[d]
        if d == 0:
            total = total + before.astype(F32)
        if d == last:
            total = total + after.astype(F32)
        back_ref[d] = total[:, LANES : LANES + cells]
        ends.append((total[:, :LANES].astype(BF), total[:, LANES + cells :].astype(BF)))
    is_odd = odd(HGT)
    for d, (low, high) in enumerate(ends):
        send_one_ref[d] = jnp.where(is_odd, low, high)
        send_two_ref[d] = jnp.where(is_odd, high, low)


def widened(deep_ref, one_ref, two_ref):
    left, right = sides(HGT, one_ref[...], two_ref[...])
    return [jnp.concatenate([left[d], deep_ref[d], right[d]], axis=1) for d in range(deep_ref.shape[0])]


def pack(direct, blocks, size, refs):
    if not direct:
        for j, block in enumerate(blocks):
            refs[0][j] = block
        return
    keep_ref, send_ref = refs
    parts, halves, length, _ = keep_ref.shape
    fold = blocks[0].shape[0] // (parts * size)
    core = lax.axis_index("core") == 1

    def quarter(part, number):
        values, row = [], number * length
        while row < (number + 1) * length:
            unit, start = divmod(row, size)
            if unit < fold * len(blocks):
                stop = min(size, start + (number + 1) * length - row)
                first = (fold * part + unit % fold) * size
                values.append(blocks[unit // fold][first + start : first + stop])
                row += stop - start
            else:
                values.append(jnp.zeros(((number + 1) * length - row, LANES), F32))
                row = (number + 1) * length
        return jnp.concatenate(values, axis=0)

    for part in range(parts):
        for half in range(halves):
            one, two = (quarter(part, 2 * half + c) for c in range(2))
            keep_ref[part, half] = jnp.where(core, two, one)
            send_ref[part, half] = jnp.where(core, one, two).astype(BF)


def hidden_kernel(
    direct, deep_ref, one_ref, two_ref, w1_ref, moved_ref, _, hidden_ref, slope_ref, rows_ref, *grad_refs
):
    for d, row in enumerate(widened(deep_ref, one_ref, two_ref)):
        rows_ref[d] = row
    rows = rows_ref
    mid = w1_ref.shape[0] // 3
    dep, deps = lax.axis_index("dep"), lax.axis_size("dep")
    hgt, hgts = lax.axis_index(HGT), lax.axis_size(HGT)
    depth, height = hidden_ref.shape[0], hidden_ref.shape[2] // LANES
    w1 = w1_ref[...]
    for d in range(depth):
        for h in range(0, height, 2):
            rhs = jnp.concatenate(
                [rows[d + a, :, (h + b) * LANES : (h + b + 2) * LANES] for a in range(3) for b in range(3)], axis=0
            )
            y = jnp.dot(w1, rhs, preferred_element_type=F32)
            pre = sum(moved_along_width(y[n * mid : (n + 1) * mid], 1 - n) for n in range(3))
            s = 1.0 / (1.0 + jnp.exp(-pre))
            for r in range(2):
                lanes = slice(r * LANES, (r + 1) * LANES)
                p, q = pre[:, lanes], s[:, lanes]
                value = (p * q).astype(BF)
                outside = []
                if d == 0:
                    outside.append(dep == 0)
                if d == depth - 1:
                    outside.append(dep == deps - 1)
                if h + r == 0:
                    outside.append(hgt == 0)
                if h + r == height - 1:
                    outside.append(hgt == hgts - 1)
                for far in outside:
                    value = jnp.where(far, jnp.zeros_like(value), value)
                hidden_ref[d, :, (h + r) * LANES : (h + r + 1) * LANES] = value
                if 0 < d < depth - 1 and 0 < h + r < height - 1:
                    at = (h + r - 1) * LANES
                    slope_ref[d - 1, :, at : at + LANES] = q * (1.0 + p * (1.0 - q))
    cells = (height - 2) * LANES
    own = depth - 2
    out = moved_ref.shape[1] // 3
    left = jnp.concatenate([moved_ref[d] for d in range(own)], axis=1)
    blocks, tails = [None] * 12, []
    for first in (0, 4, 8):
        group = range(first, min(first + 4, 9))
        right = jnp.concatenate(
            [
                jnp.concatenate(
                    [hidden_ref[d + ab // 3, :, (ab % 3) * LANES : (ab % 3) * LANES + cells] for ab in group], axis=0
                )
                for d in range(own)
            ],
            axis=1,
        )
        g = lax.dot_general(left, right, (((1,), (1,)), ((), ())), preferred_element_type=F32)
        for n in range(3):
            part = g[n * out : (n + 1) * out]
            if first < 8:
                for m in range(2):
                    blocks[4 * n + first // 2 + m] = part[:, m * LANES : (m + 1) * LANES]
            else:
                tails.append(part)
    tails.append(jnp.zeros_like(tails[0]))
    blocks += [jnp.concatenate(tails[2 * m : 2 * m + 2], axis=1) for m in range(2)]
    pack(direct, blocks, mid // lax.axis_size("dp"), grad_refs)


def features_kernel(hidden_ref, w2_ref, out_ref, token_ref, scratch):
    out = w2_ref.shape[0] // 3
    _, depth, height, _ = out_ref.shape
    w2 = w2_ref[...]
    for d in range(depth):
        for h in range(0, height, 2):
            rhs = jnp.concatenate(
                [
                    hidden_ref[d + a, :, (h + b) * LANES : (h + b + 2) * LANES]
                    for a in range(3)
                    for b in range(3)
                ],
                axis=0,
            )
            y = jnp.dot(w2, rhs, preferred_element_type=F32)
            total = sum(moved_along_width(y[n * out : (n + 1) * out], 1 - n) for n in range(3))
            for r in range(2):
                row = total[:, r * LANES : (r + 1) * LANES]
                scratch[pl.ds(d * height + h + r, out, stride=depth * height), :] = row
    out_ref[...] = scratch[...].reshape(out_ref.shape).astype(BF)
    token_ref[...] = scratch[:8]


def delta_kernel(direct, rows_ref, back_ref, one_ref, two_ref, slope_ref, *outs_and_scratch):
    *grad_refs, delta_ref = outs_and_scratch
    before, after = sides(HGT, one_ref[...], two_ref[...])
    own, mid, cells = slope_ref.shape
    for d in range(own):
        for at in range(0, cells, LANES):
            back = back_ref[d, :, at : at + LANES]
            if at == 0:
                back = back + before[d].astype(F32)
            if at == cells - LANES:
                back = back + after[d].astype(F32)
            delta = back * slope_ref[d, :, at : at + LANES]
            for n in range(3):
                delta_ref[n * mid : (n + 1) * mid, d * cells + at : d * cells + at + LANES] = moved_along_width(
                    delta, n - 1
                ).astype(BF)
    left = delta_ref[...]
    blocks, tails = [None] * 6, []
    inner = rows_ref.shape[1]
    for first in (0, 8):
        group = range(first, min(first + 8, 9))
        right = jnp.concatenate(
            [
                jnp.concatenate(
                    [
                        rows_ref[d + 1 + ab // 3, :, (1 + ab % 3) * LANES : (1 + ab % 3) * LANES + cells]
                        for ab in group
                    ],
                    axis=0,
                )
                for d in range(own)
            ],
            axis=1,
        )
        g = lax.dot_general(left, right, (((1,), (1,)), ((), ())), preferred_element_type=F32)
        for n in range(3):
            part = g[n * mid : (n + 1) * mid]
            if first == 0:
                for m in range(2):
                    blocks[2 * n + m] = part[:, m * LANES : (m + 1) * LANES]
            else:
                tails.append(part)
    tails.append(jnp.zeros((mid, LANES - 3 * inner), F32))
    blocks.append(jnp.concatenate(tails, axis=1))
    pack(direct, blocks, mid // lax.axis_size("dp"), grad_refs)


def plane_kernel(moves, *refs):
    keep_second, got_second, keep_first, got_first, kept_ref, *send_refs = refs
    part = lax.rem(lax.axis_index("dp"), keep_first.shape[0])
    half = lax.axis_index("y")

    def total(x, y):
        p = 1 - part if x else part
        h = 1 - half if y else half
        second = keep_second[p, h] + got_second[p, h].astype(F32)
        first = keep_first[p, h] + got_first[p, h].astype(F32)
        return jnp.concatenate([second, first], axis=0).reshape(kept_ref.shape)

    kept_ref[...] = total(0, 0)
    for (x, y), send_ref in zip(moves, send_refs, strict=True):
        send_ref[...] = total(x, y).astype(BF)


def depth_kernel(kept_ref, *refs):
    *got_refs, _, own_ref, send_ref = refs
    mine = lax.rem(lax.axis_index("dep"), 2)

    def total(at):
        value = kept_ref[at]
        for ref in got_refs:
            value = value + ref[at].astype(F32)
        return value

    own_ref[...] = total(mine)
    send_ref[...] = total(1 - mine).astype(BF)


def add_kernel(one_ref, two_ref, out_ref):
    out_ref[...] = (one_ref[...].astype(F32) + two_ref[...].astype(F32)).astype(BF)


def order_kernel(own_ref, depth_ref, height_ref, both_ref, out_ref):
    y, z = lax.axis_index("y"), lax.rem(lax.axis_index("dep"), 2)
    out_ref[y, z] = own_ref[...]
    out_ref[y, 1 - z] = depth_ref[...]
    out_ref[1 - y, z] = height_ref[...]
    out_ref[1 - y, 1 - z] = both_ref[...]


def unpack_kernel(length_second, own_ref, got_ref, g1_ref, g2_ref):
    halves, _, half, _ = own_ref.shape
    size, inner = g1_ref.shape[1:]
    mid = g2_ref.shape[2]
    core = lax.axis_index("core") == 1
    quarters = []
    for n in range(halves):
        own, got = (ref[n].astype(F32).reshape(2 * half, LANES) for ref in (own_ref, got_ref))
        quarters += [jnp.where(core, got, own), jnp.where(core, own, got)]
    second = [quarter[:length_second] for quarter in quarters]
    first = [quarter[length_second:] for quarter in quarters]

    def get(unit, whole=second):
        length = whole[0].shape[0]
        values, row = [], unit * size
        while row < (unit + 1) * size:
            number, start = divmod(row, length)
            stop = min(length, start + (unit + 1) * size - row)
            values.append(whole[number][start:stop])
            row += stop - start
        return values[0] if len(values) == 1 else jnp.concatenate(values, axis=0)

    for j in range(14):
        for half in range(2):
            value = get(2 * j + half)
            for m in range(2):
                c, ab = (j // 4, 2 * (j % 4) + m) if j < 12 else (2 * (j - 12) + m, 8)
                if c < 3:
                    g2_ref[3 * ab + c, half * size : (half + 1) * size, :] = value[:, m * mid : (m + 1) * mid]
    for j in range(7):
        value = get(j, first)
        for m in range(4):
            c, ab = (j // 2, 4 * (j % 2) + m) if j < 6 else (m, 8)
            if c < 3:
                g1_ref[3 * ab + c] = value[:, m * inner : (m + 1) * inner]


def swapped(x, axis, first):
    axes = (axis,) if isinstance(axis, str) else axis
    parts, size = lax.axis_size("dp"), lax.axis_size(axis)
    partner = list(range(parts * size))
    for i in partner:
        part, at = divmod(i, size)
        if first <= at < size - (size - first) % 2:
            partner[i] = part * size + (at - first ^ 1) + first
        elif parts % 2 == 0:
            partner[i] = (part ^ 1) * size + at
    return lax.ppermute(x, ("dp", *axes), list(enumerate(partner)))


def across(x, *moves):
    axes = tuple(axis for axis, _ in moves)
    flip = 0
    for axis, bit in moves:
        flip = flip * lax.axis_size(axis) + bit
    return lax.ppermute(x, axes, [(i, i ^ flip) for i in range(lax.axis_size(axes))])


def scattered(grad, parts, halves, size, length):
    grad = jnp.swapaxes(grad.reshape(grad.shape[0], parts, -1, LANES), 0, 1).reshape(parts, -1, LANES)
    grad = jnp.pad(grad, ((0, 0), (0, 2 * halves * length - grad.shape[1]), (0, 0)))
    grad = lax.psum_scatter(grad, "dp", scatter_dimension=0, tiled=True).reshape(1, halves, 2, length, LANES)
    core = lax.axis_index("core")
    keep, send = (lax.dynamic_index_in_dim(grad, at, 2, False) for at in (core, 1 - core))
    return keep, send.astype(BF)


def per_device(volume, kernel_first, kernel_second, cotangent):
    _, inner, depth, height, width = volume.shape
    mid, out = kernel_first.shape[1], kernel_second.shape[1]
    cells = height * width
    parts = lax.axis_size("dp")
    k1, k2 = jnp.swapaxes(kernel_first, 1, 2), jnp.swapaxes(kernel_second, 1, 2)
    rows = depth * height

    one, two = swapped(volume[0], "dep", 0), swapped(volume[0], "dep", 1)
    (blank,) = call(blank_kernel, [shape((out, 2 * width), BF)], [], flops=3_000_000_000)
    cot_rows, back, back_one, back_two = call(
        spread_kernel,
        [
            shape((depth, out, cells), BF),
            shape((depth, mid, cells + 2 * width), F32),
            shape((mid, cells + 2 * width), BF),
            shape((mid, cells + 2 * width), BF),
        ],
        [cotangent[0], k2, blank],
        [pltpu.VMEM((out * rows, width), F32)],
        flops=1_100_000_000,
    )
    deep, one, two = call(
        rim_kernel,
        [shape((3 * depth, inner, cells), BF)] + [shape((3 * depth, inner, 2 * width), BF)] * 2,
        [volume[0], one, two, cot_rows],
        [pltpu.VMEM((inner * rows, width), F32)],
    )
    one, two = swapped(one, HGT, 0), swapped(two, HGT, 1)
    moved, w1, w2 = call(
        arrange_kernel,
        [shape((depth, 3 * out, cells), BF), shape((3 * mid, 9 * inner), BF), shape((3 * out, 9 * mid), BF)],
        [cot_rows, k1, k2, deep],
        flops=500_000_000,
    )
    back_one, back_two = swapped(back_one, "dep", 0), swapped(back_two, "dep", 1)
    back, back_one, back_two = call(
        back_rim_kernel,
        [shape((depth, mid, cells), F32)] + [shape((depth, mid, width), BF)] * 2,
        [back, back_one, back_two],
    )
    back_one, back_two = swapped(back_one, HGT, 0), swapped(back_two, HGT, 1)

    size = mid // parts
    direct = parts == 2 and size % 16 == 0
    halves = lax.axis_size("y")
    length_second, length_first = (-(-units * size // (32 * halves)) * 16 for units in (28, 7))
    length = length_second + length_first
    hidden, slope, wide, *second = call(
        functools.partial(hidden_kernel, direct),
        [
            shape((depth + 2, mid, cells + 2 * width), BF),
            shape((depth, mid, cells), F32),
            shape((3 * depth, inner, cells + 4 * width), BF),
        ]
        + (
            [shape((parts, halves, length_second, width), kind) for kind in (F32, BF)]
            if direct
            else [shape((14, out, LANES), F32)]
        ),
        [deep, one, two, w1, moved, back],
        flops=1_500_000_000,
    )
    first = call(
        functools.partial(delta_kernel, direct),
        [shape((parts, halves, length_first, width), kind) for kind in (F32, BF)]
        if direct
        else [shape((7, mid, LANES), F32)],
        [wide, back, back_one, back_two, slope],
        [pltpu.VMEM((3 * mid, depth * cells), BF)],
        flops=4_000_000_000,
    )
    if direct:
        moves = [(1, 0), (0, 1), (1, 1)]
    else:
        moves = [(0, 1)]
        first, second = (
            scattered(grad[0], parts, halves, size, rows)
            for grad, rows in ((first, length_first), (second, length_second))
        )
    got_second, got_first = (across(send, ("core", 1)) for _, send in (second, first))
    features, token = call(
        features_kernel,
        [shape(cotangent.shape[1:], BF), shape((8, width), F32)],
        [hidden, w2],
        [pltpu.VMEM((out * rows, width), F32)],
        flops=900_000_000,
    )
    block = (2, length // 2, width)
    kept, *sends = call(
        functools.partial(plane_kernel, moves),
        [shape(block, F32)] + [shape(block, BF)] * len(moves),
        [second[0], got_second, first[0], got_first],
    )
    gots = [across(send, ("dp", x), ("y", y)) for send, (x, y) in zip(sends, moves, strict=True)]
    own, send = call(depth_kernel, [shape(block[1:], F32), shape(block[1:], BF)], [kept, *gots, token])
    (share,) = call(add_kernel, [shape(block[1:], BF)], [own, across(send, ("dep", 1))])
    (share,) = call(add_kernel, [shape(block[1:], BF)], [share, across(share, ("dep", 2))])
    (own,) = call(
        order_kernel,
        [shape((halves, *block), BF)],
        [share, *(across(share, ("dep", z), ("y", y)) for z, y in ((1, 0), (0, 1), (1, 1)))],
    )
    grad_first, grad_second = call(
        functools.partial(unpack_kernel, length_second),
        [shape((27, size, inner), F32), shape((27, 2 * size, mid), F32)],
        [own, across(own, ("core", 1))],
    )
    return features[None], grad_first, grad_second


def solution(mesh):
    dp, dep, hgt = (mesh.shape[axis] for axis in ("dp", "dep", "hgt"))
    split = jax.sharding.Mesh(mesh.devices.reshape(dp, dep, hgt // 2, 2), ("dp", "dep", *HGT))
    block = P("dp", None, "dep", HGT, None)
    return jax.shard_map(
        per_device,
        mesh=split,
        in_specs=(block, P(), P(), block),
        out_specs=(block, P(None, "dp", None), P(None, "dp", None)),
        check_vma=False,
    )
```

```python
import functools

import jax
import jax.numpy as jnp
from jax import lax
from jax.experimental import pallas as pl
from jax.experimental.pallas import tpu as pltpu
from jax.sharding import PartitionSpec as P

BF, F32 = jnp.bfloat16, jnp.float32
LANES = 128
HGT = ("y", "core")
VMEM_BYTES = 48 * 2**20


def call(body, outs, args, scratch=(), flops=0, far=()):
    moved = sum(x.size * x.dtype.itemsize for x in (*outs, *args))
    return pl.pallas_call(
        body,
        out_shape=outs,
        in_specs=[pl.BlockSpec(memory_space=pl.ANY if n in far else pltpu.VMEM) for n in range(len(args))],
        out_specs=[pl.BlockSpec(memory_space=pltpu.VMEM)] * len(outs),
        scratch_shapes=list(scratch),
        compiler_params=pltpu.CompilerParams(vmem_limit_bytes=VMEM_BYTES),
        cost_estimate=pl.CostEstimate(flops=flops, bytes_accessed=moved, transcendentals=0),
    )(*args)


def shape(dims, dtype):
    return jax.ShapeDtypeStruct(dims, dtype)


def moved_along_width(x, c):
    if c == 0:
        return x
    pieces = []
    for start in range(0, x.shape[1], LANES):
        piece = x[:, start : start + LANES]
        lane = lax.broadcasted_iota(jnp.int32, piece.shape, 1)
        rolled = pltpu.roll(piece, c % LANES, 1)
        pieces.append(jnp.where(lane == (0 if c == 1 else LANES - 1), 0.0, rolled))
    return pieces[0] if len(pieces) == 1 else jnp.concatenate(pieces, axis=1)


def by_rows(ref, scratch, store):
    channels, depth, height, width = ref.shape
    rows = depth * height
    scratch[...] = ref[...].astype(F32).reshape(channels * rows, width)
    for d in range(depth):
        for h in range(height):
            store(d, h, scratch[pl.ds(d * height + h, channels, stride=rows), :])


def odd(axis):
    return lax.rem(lax.axis_index(axis), 2) == 1


def blank_kernel(out_ref):
    out_ref[...] = jnp.zeros(out_ref.shape, BF)


def spread_kernel(cot_ref, k2_ref, blank_ref, cot_rows_ref, back_ref, one_ref, two_ref, scratch):
    out, depth, height, _ = cot_ref.shape
    rows = [[None] * height for _ in range(depth)]

    def store(d, h, row):
        rows[d][h] = row.astype(BF)
        cot_rows_ref[d, :, h * LANES : (h + 1) * LANES] = rows[d][h]

    by_rows(cot_ref, scratch, store)
    mid = k2_ref.shape[1]
    none = blank_ref[...]
    padded = [jnp.concatenate([none, *rows[d], none], axis=1) for d in range(depth)]
    is_odd = odd("dep")
    faces = [[], []]
    for e in range(depth + 2):
        reached = [(d, e - 1 - d) for d in range(depth) if abs(e - 1 - d) <= 1]
        w = jnp.concatenate(
            [
                k2_ref[9 * (a + 1) + 3 * b : 9 * (a + 1) + 3 * b + 3].reshape(3 * mid, out)
                for _, a in reached
                for b in range(3)
            ],
            axis=1,
        )
        for j in range(0, height + 2, 2):
            rhs = jnp.concatenate(
                [padded[d][:, (j + 2 - b) * LANES : (j + 4 - b) * LANES] for d, _ in reached for b in range(3)], axis=0
            )
            y = jnp.dot(w, rhs, preferred_element_type=F32)
            back = sum(moved_along_width(y[n * mid : (n + 1) * mid], n - 1) for n in range(3))
            if 0 < e < depth + 1:
                back_ref[e - 1, :, j * LANES : (j + 2) * LANES] = back
            else:
                faces[e > 0].append(back.astype(BF))
    low, high = (jnp.concatenate(face, axis=1) for face in faces)
    one_ref[...] = jnp.where(is_odd, low, high)
    two_ref[...] = jnp.where(is_odd, high, low)


def as_matrix(ref, c):
    stacked = jnp.concatenate([ref[3 * ab + c] for ab in range(9)], axis=0)
    return stacked.astype(F32).T.astype(BF)


def arrange_kernel(cot_rows_ref, k1_ref, _, moved_ref, w1_ref):
    depth, out, cells = cot_rows_ref.shape
    for d in range(depth):
        for h in range(0, cells, LANES):
            row = cot_rows_ref[d, :, h : h + LANES]
            for n, c in enumerate((-1, 0, 1)):
                value = row if c == 0 else moved_along_width(row.astype(F32), c).astype(BF)
                moved_ref[d, n * out : (n + 1) * out, h : h + LANES] = value
    mid = k1_ref.shape[2]
    for c in range(3):
        w1_ref[c * mid : (c + 1) * mid, :] = as_matrix(k1_ref, c)


def sides(axis, one, two):
    me, size = lax.axis_index(axis), lax.axis_size(axis)
    is_odd = odd(axis)
    none = jnp.zeros_like(one)
    before = jnp.where(me == 0, none, jnp.where(is_odd, one, two))
    after = jnp.where(me == size - 1, none, jnp.where(is_odd, two, one))
    return before, after


def rim_kernel(own_ref, one_ref, two_ref, _, deep_ref, send_one_ref, send_two_ref, scratch):
    depth = own_ref.shape[1]
    before, after = sides("dep", one_ref[...], two_ref[...])
    for n, part in enumerate((before, own_ref[...], after)):

        def store(d, h, row, at=n * depth):
            deep_ref[at + d, :, h * LANES : (h + 1) * LANES] = row.astype(BF)

        by_rows(part, scratch, store)
    n, cells = send_one_ref.shape[2], deep_ref.shape[2]
    first, last = deep_ref[:, :, :n], deep_ref[:, :, cells - n :]
    is_odd = odd(HGT)
    send_one_ref[...] = jnp.where(is_odd, first, last)
    send_two_ref[...] = jnp.where(is_odd, last, first)


def back_rim_kernel(own_ref, one_ref, two_ref, back_ref, send_one_ref, send_two_ref):
    before, after = sides("dep", one_ref[...], two_ref[...])
    last = own_ref.shape[0] - 1
    cells = back_ref.shape[2]
    ends = []
    for d in range(last + 1):
        total = own_ref[d]
        if d == 0:
            total = total + before.astype(F32)
        if d == last:
            total = total + after.astype(F32)
        back_ref[d] = total[:, LANES : LANES + cells]
        ends.append((total[:, :LANES].astype(BF), total[:, LANES + cells :].astype(BF)))
    is_odd = odd(HGT)
    for d, (low, high) in enumerate(ends):
        send_one_ref[d] = jnp.where(is_odd, low, high)
        send_two_ref[d] = jnp.where(is_odd, high, low)


def widened(deep_ref, one_ref, two_ref):
    left, right = sides(HGT, one_ref[...], two_ref[...])
    return [jnp.concatenate([left[d], deep_ref[d], right[d]], axis=1) for d in range(deep_ref.shape[0])]


def pack(direct, blocks, size, refs):
    if not direct:
        for j, block in enumerate(blocks):
            refs[0][j] = block
        return
    keep_ref, send_ref = refs
    parts, halves, length, _ = keep_ref.shape
    fold = blocks[0].shape[0] // (parts * size)
    core = lax.axis_index("core") == 1

    def quarter(part, number):
        values, row = [], number * length
        while row < (number + 1) * length:
            unit, start = divmod(row, size)
            if unit < fold * len(blocks):
                stop = min(size, start + (number + 1) * length - row)
                first = (fold * part + unit % fold) * size
                values.append(blocks[unit // fold][first + start : first + stop])
                row += stop - start
            else:
                values.append(jnp.zeros(((number + 1) * length - row, LANES), F32))
                row = (number + 1) * length
        return jnp.concatenate(values, axis=0)

    for part in range(parts):
        for half in range(halves):
            one, two = (quarter(part, 2 * half + c) for c in range(2))
            keep_ref[part, half] = jnp.where(core, two, one)
            send_ref[part, half] = jnp.where(core, one, two).astype(BF)


def hidden_kernel(
    direct, deep_ref, one_ref, two_ref, w1_ref, moved_ref, _, hidden_ref, slope_ref, rows_ref, *grad_refs
):
    for d, row in enumerate(widened(deep_ref, one_ref, two_ref)):
        rows_ref[d] = row
    rows = rows_ref
    mid = w1_ref.shape[0] // 3
    dep, deps = lax.axis_index("dep"), lax.axis_size("dep")
    hgt, hgts = lax.axis_index(HGT), lax.axis_size(HGT)
    depth, height = hidden_ref.shape[0], hidden_ref.shape[2] // LANES
    w1 = w1_ref[...]
    for d in range(depth):
        for h in range(0, height, 2):
            rhs = jnp.concatenate(
                [rows[d + a, :, (h + b) * LANES : (h + b + 2) * LANES] for a in range(3) for b in range(3)], axis=0
            )
            y = jnp.dot(w1, rhs, preferred_element_type=F32)
            pre = sum(moved_along_width(y[n * mid : (n + 1) * mid], 1 - n) for n in range(3))
            s = 1.0 / (1.0 + jnp.exp(-pre))
            for r in range(2):
                lanes = slice(r * LANES, (r + 1) * LANES)
                p, q = pre[:, lanes], s[:, lanes]
                value = (p * q).astype(BF)
                outside = []
                if d == 0:
                    outside.append(dep == 0)
                if d == depth - 1:
                    outside.append(dep == deps - 1)
                if h + r == 0:
                    outside.append(hgt == 0)
                if h + r == height - 1:
                    outside.append(hgt == hgts - 1)
                for far in outside:
                    value = jnp.where(far, jnp.zeros_like(value), value)
                hidden_ref[d, :, (h + r) * LANES : (h + r + 1) * LANES] = value
                if 0 < d < depth - 1 and 0 < h + r < height - 1:
                    at = (h + r - 1) * LANES
                    slope_ref[d - 1, :, at : at + LANES] = q * (1.0 + p * (1.0 - q))
    cells = (height - 2) * LANES
    own = depth - 2
    out = moved_ref.shape[1] // 3
    left = jnp.concatenate([moved_ref[d] for d in range(own)], axis=1)
    blocks, tails = [None] * 12, []
    for first in (0, 4, 8):
        group = range(first, min(first + 4, 9))
        right = jnp.concatenate(
            [
                jnp.concatenate(
                    [hidden_ref[d + ab // 3, :, (ab % 3) * LANES : (ab % 3) * LANES + cells] for ab in group], axis=0
                )
                for d in range(own)
            ],
            axis=1,
        )
        g = lax.dot_general(left, right, (((1,), (1,)), ((), ())), preferred_element_type=F32)
        for n in range(3):
            part = g[n * out : (n + 1) * out]
            if first < 8:
                for m in range(2):
                    blocks[4 * n + first // 2 + m] = part[:, m * LANES : (m + 1) * LANES]
            else:
                tails.append(part)
    tails.append(jnp.zeros_like(tails[0]))
    blocks += [jnp.concatenate(tails[2 * m : 2 * m + 2], axis=1) for m in range(2)]
    pack(direct, blocks, mid // lax.axis_size("dp"), grad_refs)


def features_kernel(hidden_ref, k2_ref, out_ref, token_ref, scratch):
    out, depth, height, _ = out_ref.shape
    w2 = jnp.concatenate([as_matrix(k2_ref, c) for c in range(3)], axis=0)
    for d in range(depth):
        for h in range(0, height, 2):
            rhs = jnp.concatenate(
                [
                    hidden_ref[d + a, :, (h + b) * LANES : (h + b + 2) * LANES]
                    for a in range(3)
                    for b in range(3)
                ],
                axis=0,
            )
            y = jnp.dot(w2, rhs, preferred_element_type=F32)
            total = sum(moved_along_width(y[n * out : (n + 1) * out], 1 - n) for n in range(3))
            for r in range(2):
                row = total[:, r * LANES : (r + 1) * LANES]
                scratch[pl.ds(d * height + h + r, out, stride=depth * height), :] = row
    out_ref[...] = scratch[...].reshape(out_ref.shape).astype(BF)
    token_ref[...] = scratch[:8]


def delta_kernel(direct, rows_ref, back_ref, one_ref, two_ref, slope_ref, *outs_and_scratch):
    *grad_refs, delta_ref = outs_and_scratch
    before, after = sides(HGT, one_ref[...], two_ref[...])
    own, mid, cells = slope_ref.shape
    for d in range(own):
        for at in range(0, cells, LANES):
            back = back_ref[d, :, at : at + LANES]
            if at == 0:
                back = back + before[d].astype(F32)
            if at == cells - LANES:
                back = back + after[d].astype(F32)
            delta = back * slope_ref[d, :, at : at + LANES]
            for n in range(3):
                delta_ref[n * mid : (n + 1) * mid, d * cells + at : d * cells + at + LANES] = moved_along_width(
                    delta, n - 1
                ).astype(BF)
    left = delta_ref[...]
    blocks, tails = [None] * 6, []
    inner = rows_ref.shape[1]
    for first in (0, 8):
        group = range(first, min(first + 8, 9))
        right = jnp.concatenate(
            [
                jnp.concatenate(
                    [
                        rows_ref[d + 1 + ab // 3, :, (1 + ab % 3) * LANES : (1 + ab % 3) * LANES + cells]
                        for ab in group
                    ],
                    axis=0,
                )
                for d in range(own)
            ],
            axis=1,
        )
        g = lax.dot_general(left, right, (((1,), (1,)), ((), ())), preferred_element_type=F32)
        for n in range(3):
            part = g[n * mid : (n + 1) * mid]
            if first == 0:
                for m in range(2):
                    blocks[2 * n + m] = part[:, m * LANES : (m + 1) * LANES]
            else:
                tails.append(part)
    tails.append(jnp.zeros((mid, LANES - 3 * inner), F32))
    blocks.append(jnp.concatenate(tails, axis=1))
    pack(direct, blocks, mid // lax.axis_size("dp"), grad_refs)


def plane_kernel(moves, *refs):
    keep_second, got_second, keep_first, got_first, kept_ref, *send_refs = refs
    part = lax.rem(lax.axis_index("dp"), keep_first.shape[0])
    half = lax.axis_index("y")

    def total(x, y):
        p = 1 - part if x else part
        h = 1 - half if y else half
        second = keep_second[p, h] + got_second[p, h].astype(F32)
        first = keep_first[p, h] + got_first[p, h].astype(F32)
        return jnp.concatenate([second, first], axis=0)

    kept_ref[...] = total(0, 0)
    for (x, y), send_ref in zip(moves, send_refs, strict=True):
        send_ref[...] = total(x, y).astype(BF)


def total_kernel(kept_ref, *refs):
    *got_refs, out_ref = refs
    value = kept_ref[...]
    for ref in got_refs:
        value = value + ref[...].astype(F32)
    out_ref[...] = value.astype(BF)


def depth_kernel(a_ref, b_ref, c_ref, d_ref, _, out_ref):
    one = a_ref[...].astype(F32) + b_ref[...].astype(F32)
    two = c_ref[...].astype(F32) + d_ref[...].astype(F32)
    out_ref[...] = (one + two).astype(BF)


def order_kernel(own_ref, got_ref, out_ref):
    mine = lax.axis_index("y")
    out_ref[mine] = own_ref[...]
    out_ref[1 - mine] = got_ref[...]


def unpack_kernel(length_second, own_ref, got_ref, g1_ref, g2_ref):
    halves = own_ref.shape[0]
    size, inner = g1_ref.shape[1:]
    mid = g2_ref.shape[2]
    core = lax.axis_index("core") == 1
    quarters = []
    for n in range(halves):
        own, got = (ref[n].astype(F32) for ref in (own_ref, got_ref))
        quarters += [jnp.where(core, got, own), jnp.where(core, own, got)]
    second = [quarter[:length_second] for quarter in quarters]
    first = [quarter[length_second:] for quarter in quarters]

    def get(unit, whole=second):
        length = whole[0].shape[0]
        values, row = [], unit * size
        while row < (unit + 1) * size:
            number, start = divmod(row, length)
            stop = min(length, start + (unit + 1) * size - row)
            values.append(whole[number][start:stop])
            row += stop - start
        return values[0] if len(values) == 1 else jnp.concatenate(values, axis=0)

    for j in range(14):
        for half in range(2):
            value = get(2 * j + half)
            for m in range(2):
                c, ab = (j // 4, 2 * (j % 4) + m) if j < 12 else (2 * (j - 12) + m, 8)
                if c < 3:
                    g2_ref[3 * ab + c, half * size : (half + 1) * size, :] = value[:, m * mid : (m + 1) * mid]
    for j in range(7):
        value = get(j, first)
        for m in range(4):
            c, ab = (j // 2, 4 * (j % 2) + m) if j < 6 else (m, 8)
            if c < 3:
                g1_ref[3 * ab + c] = value[:, m * inner : (m + 1) * inner]


def swapped(x, axis, first):
    axes = (axis,) if isinstance(axis, str) else axis
    parts, size = lax.axis_size("dp"), lax.axis_size(axis)
    partner = list(range(parts * size))
    for i in partner:
        part, at = divmod(i, size)
        if first <= at < size - (size - first) % 2:
            partner[i] = part * size + (at - first ^ 1) + first
        elif parts % 2 == 0:
            partner[i] = (part ^ 1) * size + at
    return lax.ppermute(x, ("dp", *axes), list(enumerate(partner)))


def across(x, *moves):
    axes = tuple(axis for axis, _ in moves)
    flip = 0
    for axis, bit in moves:
        flip = flip * lax.axis_size(axis) + bit
    return lax.ppermute(x, axes, [(i, i ^ flip) for i in range(lax.axis_size(axes))])


def scattered(grad, parts, halves, size, length):
    grad = jnp.swapaxes(grad.reshape(grad.shape[0], parts, -1, LANES), 0, 1).reshape(parts, -1, LANES)
    grad = jnp.pad(grad, ((0, 0), (0, 2 * halves * length - grad.shape[1]), (0, 0)))
    grad = lax.psum_scatter(grad, "dp", scatter_dimension=0, tiled=True).reshape(1, halves, 2, length, LANES)
    core = lax.axis_index("core")
    keep, send = (lax.dynamic_index_in_dim(grad, at, 2, False) for at in (core, 1 - core))
    return keep, send.astype(BF)


def per_device(volume, kernel_first, kernel_second, cotangent):
    _, inner, depth, height, width = volume.shape
    mid, out = kernel_first.shape[1], kernel_second.shape[1]
    cells = height * width
    parts = lax.axis_size("dp")
    k1, k2 = jnp.swapaxes(kernel_first, 1, 2), jnp.swapaxes(kernel_second, 1, 2)
    rows = depth * height

    one, two = swapped(volume[0], "dep", 0), swapped(volume[0], "dep", 1)
    (blank,) = call(blank_kernel, [shape((out, 2 * width), BF)], [], flops=3_000_000_000)
    cot_rows, back, back_one, back_two = call(
        spread_kernel,
        [
            shape((depth, out, cells), BF),
            shape((depth, mid, cells + 2 * width), F32),
            shape((mid, cells + 2 * width), BF),
            shape((mid, cells + 2 * width), BF),
        ],
        [cotangent[0], k2, blank],
        [pltpu.VMEM((out * rows, width), F32)],
        flops=1_100_000_000,
    )
    deep, one, two = call(
        rim_kernel,
        [shape((3 * depth, inner, cells), BF)] + [shape((3 * depth, inner, 2 * width), BF)] * 2,
        [volume[0], one, two, cot_rows],
        [pltpu.VMEM((inner * rows, width), F32)],
    )
    one, two = swapped(one, HGT, 0), swapped(two, HGT, 1)
    moved, w1 = call(
        arrange_kernel,
        [shape((depth, 3 * out, cells), BF), shape((3 * mid, 9 * inner), BF)],
        [cot_rows, k1, deep],
        flops=500_000_000,
    )
    back_one, back_two = swapped(back_one, "dep", 0), swapped(back_two, "dep", 1)
    back, back_one, back_two = call(
        back_rim_kernel,
        [shape((depth, mid, cells), F32)] + [shape((depth, mid, width), BF)] * 2,
        [back, back_one, back_two],
    )
    back_one, back_two = swapped(back_one, HGT, 0), swapped(back_two, HGT, 1)

    size = mid // parts
    direct = parts == 2 and size % 16 == 0
    halves = lax.axis_size("y")
    length_second, length_first = (-(-units * size // (32 * halves)) * 16 for units in (28, 7))
    length = length_second + length_first
    hidden, slope, wide, *second = call(
        functools.partial(hidden_kernel, direct),
        [
            shape((depth + 2, mid, cells + 2 * width), BF),
            shape((depth, mid, cells), F32),
            shape((3 * depth, inner, cells + 4 * width), BF),
        ]
        + (
            [shape((parts, halves, length_second, width), kind) for kind in (F32, BF)]
            if direct
            else [shape((14, out, LANES), F32)]
        ),
        [deep, one, two, w1, moved, back],
        flops=1_500_000_000,
    )
    first = call(
        functools.partial(delta_kernel, direct),
        [shape((parts, halves, length_first, width), kind) for kind in (F32, BF)]
        if direct
        else [shape((7, mid, LANES), F32)],
        [wide, back, back_one, back_two, slope],
        [pltpu.VMEM((3 * mid, depth * cells), BF)],
        flops=4_000_000_000,
    )
    if direct:
        moves = [(1, 0), (0, 1), (1, 1)]
    else:
        moves = [(0, 1)]
        first, second = (
            scattered(grad[0], parts, halves, size, rows)
            for grad, rows in ((first, length_first), (second, length_second))
        )
    got_second, got_first = (across(send, ("core", 1)) for _, send in (second, first))
    features, token = call(
        features_kernel,
        [shape(cotangent.shape[1:], BF), shape((8, width), F32)],
        [hidden, k2],
        [pltpu.VMEM((out * rows, width), F32)],
        flops=900_000_000,
    )
    block = (length, width)
    kept, *sends = call(
        functools.partial(plane_kernel, moves),
        [shape(block, F32)] + [shape(block, BF)] * len(moves),
        [second[0], got_second, first[0], got_first],
    )
    gots = [across(send, ("dp", x), ("y", y)) for send, (x, y) in zip(sends, moves, strict=True)]
    (share,) = call(total_kernel, [shape(block, BF)], [kept, *gots])
    gots = [across(share, ("dep", bits)) for bits in (1, 2, 3)]
    (share,) = call(depth_kernel, [shape(block, BF)], [share, *gots, token])
    (own,) = call(order_kernel, [shape((halves, *block), BF)], [share, across(share, ("y", 1))])
    grad_first, grad_second = call(
        functools.partial(unpack_kernel, length_second),
        [shape((27, size, inner), F32), shape((27, 2 * size, mid), F32)],
        [own, across(own, ("core", 1))],
    )
    return features[None], grad_first, grad_second


def solution(mesh):
    dp, dep, hgt = (mesh.shape[axis] for axis in ("dp", "dep", "hgt"))
    split = jax.sharding.Mesh(mesh.devices.reshape(dp, dep, hgt // 2, 2), ("dp", "dep", *HGT))
    block = P("dp", None, "dep", HGT, None)
    return jax.shard_map(
        per_device,
        mesh=split,
        in_specs=(block, P(), P(), block),
        out_specs=(block, P(None, "dp", None), P(None, "dp", None)),
        check_vma=False,
    )
```

```python
import functools

import jax
import jax.numpy as jnp
from jax import lax
from jax.experimental import pallas as pl
from jax.experimental.pallas import tpu as pltpu
from jax.sharding import PartitionSpec as P

BF, F32 = jnp.bfloat16, jnp.float32
LANES = 128
HGT = ("y", "core")
VMEM_BYTES = 48 * 2**20


def call(body, outs, args, scratch=(), flops=0, far=()):
    moved = sum(x.size * x.dtype.itemsize for x in (*outs, *args))
    return pl.pallas_call(
        body,
        out_shape=outs,
        in_specs=[pl.BlockSpec(memory_space=pl.ANY if n in far else pltpu.VMEM) for n in range(len(args))],
        out_specs=[pl.BlockSpec(memory_space=pltpu.VMEM)] * len(outs),
        scratch_shapes=list(scratch),
        compiler_params=pltpu.CompilerParams(vmem_limit_bytes=VMEM_BYTES),
        cost_estimate=pl.CostEstimate(flops=flops, bytes_accessed=moved, transcendentals=0),
    )(*args)


def shape(dims, dtype):
    return jax.ShapeDtypeStruct(dims, dtype)


def moved_along_width(x, c):
    if c == 0:
        return x
    pieces = []
    for start in range(0, x.shape[1], LANES):
        piece = x[:, start : start + LANES]
        lane = lax.broadcasted_iota(jnp.int32, piece.shape, 1)
        rolled = pltpu.roll(piece, c % LANES, 1)
        pieces.append(jnp.where(lane == (0 if c == 1 else LANES - 1), 0.0, rolled))
    return pieces[0] if len(pieces) == 1 else jnp.concatenate(pieces, axis=1)


def by_rows(ref, scratch, store):
    channels, depth, height, width = ref.shape
    rows = depth * height
    scratch[...] = ref[...].astype(F32).reshape(channels * rows, width)
    for d in range(depth):
        for h in range(height):
            store(d, h, scratch[pl.ds(d * height + h, channels, stride=rows), :])


def odd(axis):
    return lax.rem(lax.axis_index(axis), 2) == 1


def blank_kernel(out_ref):
    out_ref[...] = jnp.zeros(out_ref.shape, BF)


def spread_kernel(cot_ref, k2_ref, blank_ref, cot_rows_ref, back_ref, one_ref, two_ref, scratch):
    out, depth, height, _ = cot_ref.shape
    rows = [[None] * height for _ in range(depth)]

    def store(d, h, row):
        rows[d][h] = row.astype(BF)
        cot_rows_ref[d, :, h * LANES : (h + 1) * LANES] = rows[d][h]

    by_rows(cot_ref, scratch, store)
    mid = k2_ref.shape[1]
    none = blank_ref[...]
    padded = [jnp.concatenate([none, *rows[d], none], axis=1) for d in range(depth)]
    is_odd = odd("dep")
    faces = [[], []]
    for e in range(depth + 2):
        reached = [(d, e - 1 - d) for d in range(depth) if abs(e - 1 - d) <= 1]
        w = jnp.concatenate(
            [
                k2_ref[9 * (a + 1) + 3 * b : 9 * (a + 1) + 3 * b + 3].reshape(3 * mid, out)
                for _, a in reached
                for b in range(3)
            ],
            axis=1,
        )
        for j in range(0, height + 2, 2):
            rhs = jnp.concatenate(
                [padded[d][:, (j + 2 - b) * LANES : (j + 4 - b) * LANES] for d, _ in reached for b in range(3)], axis=0
            )
            y = jnp.dot(w, rhs, preferred_element_type=F32)
            back = sum(moved_along_width(y[n * mid : (n + 1) * mid], n - 1) for n in range(3))
            if 0 < e < depth + 1:
                back_ref[e - 1, :, j * LANES : (j + 2) * LANES] = back
            else:
                faces[e > 0].append(back.astype(BF))
    low, high = (jnp.concatenate(face, axis=1) for face in faces)
    one_ref[...] = jnp.where(is_odd, low, high)
    two_ref[...] = jnp.where(is_odd, high, low)


def as_matrix(ref, c):
    stacked = jnp.concatenate([ref[3 * ab + c] for ab in range(9)], axis=0)
    return stacked.astype(F32).T.astype(BF)


def arrange_kernel(cot_rows_ref, k1_ref, _, moved_ref, w1_ref):
    depth, out, cells = cot_rows_ref.shape
    for d in range(depth):
        for h in range(0, cells, LANES):
            row = cot_rows_ref[d, :, h : h + LANES]
            for n, c in enumerate((-1, 0, 1)):
                value = row if c == 0 else moved_along_width(row.astype(F32), c).astype(BF)
                moved_ref[d, n * out : (n + 1) * out, h : h + LANES] = value
    mid = k1_ref.shape[2]
    for c in range(3):
        w1_ref[c * mid : (c + 1) * mid, :] = as_matrix(k1_ref, c)


def sides(axis, one, two):
    me, size = lax.axis_index(axis), lax.axis_size(axis)
    is_odd = odd(axis)
    none = jnp.zeros_like(one)
    before = jnp.where(me == 0, none, jnp.where(is_odd, one, two))
    after = jnp.where(me == size - 1, none, jnp.where(is_odd, two, one))
    return before, after


def rim_kernel(own_ref, one_ref, two_ref, _, deep_ref, send_one_ref, send_two_ref, scratch):
    depth = own_ref.shape[1]
    before, after = sides("dep", one_ref[...], two_ref[...])
    for n, part in enumerate((before, own_ref[...], after)):

        def store(d, h, row, at=n * depth):
            deep_ref[at + d, :, h * LANES : (h + 1) * LANES] = row.astype(BF)

        by_rows(part, scratch, store)
    n, cells = send_one_ref.shape[2], deep_ref.shape[2]
    first, last = deep_ref[:, :, :n], deep_ref[:, :, cells - n :]
    is_odd = odd(HGT)
    send_one_ref[...] = jnp.where(is_odd, first, last)
    send_two_ref[...] = jnp.where(is_odd, last, first)


def back_rim_kernel(own_ref, one_ref, two_ref, back_ref, send_one_ref, send_two_ref):
    before, after = sides("dep", one_ref[...], two_ref[...])
    last = own_ref.shape[0] - 1
    cells = back_ref.shape[2]
    ends = []
    for d in range(last + 1):
        total = own_ref[d]
        if d == 0:
            total = total + before.astype(F32)
        if d == last:
            total = total + after.astype(F32)
        back_ref[d] = total[:, LANES : LANES + cells]
        ends.append((total[:, :LANES].astype(BF), total[:, LANES + cells :].astype(BF)))
    is_odd = odd(HGT)
    for d, (low, high) in enumerate(ends):
        send_one_ref[d] = jnp.where(is_odd, low, high)
        send_two_ref[d] = jnp.where(is_odd, high, low)


def widened(deep_ref, one_ref, two_ref):
    left, right = sides(HGT, one_ref[...], two_ref[...])
    return [jnp.concatenate([left[d], deep_ref[d], right[d]], axis=1) for d in range(deep_ref.shape[0])]


def pack(direct, blocks, refs, units_of):
    if not direct:
        for j, block in enumerate(blocks):
            refs[0][j] = block
        return
    keep_ref, send_ref = refs
    parts, halves, length, _ = keep_ref.shape
    core = lax.axis_index("core") == 1
    for part in range(parts):
        whole = units_of(part)
        size = whole[0].shape[0]

        def quarter(number, whole=whole, size=size):
            values, row = [], number * length
            while row < (number + 1) * length:
                unit, start = divmod(row, size)
                stop = min(size, start + (number + 1) * length - row)
                values.append(whole[unit][start:stop])
                row += stop - start
            return jnp.concatenate(values, axis=0)

        for half in range(halves):
            one, two = (quarter(2 * half + c) for c in range(2))
            keep_ref[part, half] = jnp.where(core, two, one)
            send_ref[part, half] = jnp.where(core, one, two).astype(BF)


def hidden_kernel(
    direct, deep_ref, one_ref, two_ref, w1_ref, moved_ref, _, hidden_ref, slope_ref, rows_ref, *grad_refs
):
    for d, row in enumerate(widened(deep_ref, one_ref, two_ref)):
        rows_ref[d] = row
    rows = rows_ref
    mid = w1_ref.shape[0] // 3
    dep, deps = lax.axis_index("dep"), lax.axis_size("dep")
    hgt, hgts = lax.axis_index(HGT), lax.axis_size(HGT)
    depth, height = hidden_ref.shape[0], hidden_ref.shape[2] // LANES
    w1 = w1_ref[...]
    for d in range(depth):
        for h in range(0, height, 2):
            rhs = jnp.concatenate(
                [rows[d + a, :, (h + b) * LANES : (h + b + 2) * LANES] for a in range(3) for b in range(3)], axis=0
            )
            y = jnp.dot(w1, rhs, preferred_element_type=F32)
            pre = sum(moved_along_width(y[n * mid : (n + 1) * mid], 1 - n) for n in range(3))
            s = 1.0 / (1.0 + jnp.exp(-pre))
            for r in range(2):
                lanes = slice(r * LANES, (r + 1) * LANES)
                p, q = pre[:, lanes], s[:, lanes]
                value = (p * q).astype(BF)
                outside = []
                if d == 0:
                    outside.append(dep == 0)
                if d == depth - 1:
                    outside.append(dep == deps - 1)
                if h + r == 0:
                    outside.append(hgt == 0)
                if h + r == height - 1:
                    outside.append(hgt == hgts - 1)
                for far in outside:
                    value = jnp.where(far, jnp.zeros_like(value), value)
                hidden_ref[d, :, (h + r) * LANES : (h + r + 1) * LANES] = value
                if 0 < d < depth - 1 and 0 < h + r < height - 1:
                    at = (h + r - 1) * LANES
                    slope_ref[d - 1, :, at : at + LANES] = q * (1.0 + p * (1.0 - q))
    cells = (height - 2) * LANES
    own = depth - 2
    out = moved_ref.shape[1] // 3
    left = jnp.concatenate([moved_ref[d] for d in range(own)], axis=1)
    blocks, tails = [None] * 12, []
    for first in (0, 4, 8):
        group = range(first, min(first + 4, 9))
        right = jnp.concatenate(
            [
                jnp.concatenate(
                    [hidden_ref[d + ab // 3, :, (ab % 3) * LANES : (ab % 3) * LANES + cells] for ab in group], axis=0
                )
                for d in range(own)
            ],
            axis=1,
        )
        g = lax.dot_general(left, right, (((1,), (1,)), ((), ())), preferred_element_type=F32)
        for n in range(3):
            part = g[n * out : (n + 1) * out]
            if first < 8:
                for m in range(2):
                    blocks[4 * n + first // 2 + m] = part[:, m * LANES : (m + 1) * LANES]
            else:
                tails.append(part)
    tails.append(jnp.zeros_like(tails[0]))
    blocks += [jnp.concatenate(tails[2 * m : 2 * m + 2], axis=1) for m in range(2)]
    size = mid // lax.axis_size("dp")

    def units_of(part):
        rows = [slice((2 * part + half) * size, (2 * part + half + 1) * size) for half in range(2)]
        return [block[at] for block in blocks[:13] for at in rows] + [
            jnp.concatenate([tails[2][at] for at in rows], axis=1)
        ]

    pack(direct, blocks, grad_refs, units_of)


def features_kernel(hidden_ref, k2_ref, _, out_ref, token_ref, scratch):
    out, depth, height, _ = out_ref.shape
    w2 = jnp.concatenate([as_matrix(k2_ref, c) for c in range(3)], axis=0)
    for d in range(depth):
        for h in range(0, height, 2):
            rhs = jnp.concatenate(
                [
                    hidden_ref[d + a, :, (h + b) * LANES : (h + b + 2) * LANES]
                    for a in range(3)
                    for b in range(3)
                ],
                axis=0,
            )
            y = jnp.dot(w2, rhs, preferred_element_type=F32)
            total = sum(moved_along_width(y[n * out : (n + 1) * out], 1 - n) for n in range(3))
            for r in range(2):
                row = total[:, r * LANES : (r + 1) * LANES]
                scratch[pl.ds(d * height + h + r, out, stride=depth * height), :] = row
    out_ref[...] = scratch[...].reshape(out_ref.shape).astype(BF)
    token_ref[...] = scratch[:8]


def delta_kernel(direct, rows_ref, back_ref, one_ref, two_ref, slope_ref, *outs_and_scratch):
    *grad_refs, delta_ref = outs_and_scratch
    before, after = sides(HGT, one_ref[...], two_ref[...])
    own, mid, cells = slope_ref.shape
    for d in range(own):
        for at in range(0, cells, LANES):
            back = back_ref[d, :, at : at + LANES]
            if at == 0:
                back = back + before[d].astype(F32)
            if at == cells - LANES:
                back = back + after[d].astype(F32)
            delta = back * slope_ref[d, :, at : at + LANES]
            for n in range(3):
                delta_ref[n * mid : (n + 1) * mid, d * cells + at : d * cells + at + LANES] = moved_along_width(
                    delta, n - 1
                ).astype(BF)
    left = delta_ref[...]
    blocks, tails = [None] * 6, []
    inner = rows_ref.shape[1]
    for first in (0, 8):
        group = range(first, min(first + 8, 9))
        right = jnp.concatenate(
            [
                jnp.concatenate(
                    [
                        rows_ref[d + 1 + ab // 3, :, (1 + ab % 3) * LANES : (1 + ab % 3) * LANES + cells]
                        for ab in group
                    ],
                    axis=0,
                )
                for d in range(own)
            ],
            axis=1,
        )
        g = lax.dot_general(left, right, (((1,), (1,)), ((), ())), preferred_element_type=F32)
        for n in range(3):
            part = g[n * mid : (n + 1) * mid]
            if first == 0:
                for m in range(2):
                    blocks[2 * n + m] = part[:, m * LANES : (m + 1) * LANES]
            else:
                tails.append(part)
    tails.append(jnp.zeros((mid, LANES - 3 * inner), F32))
    blocks.append(jnp.concatenate(tails, axis=1))
    size = mid // lax.axis_size("dp")
    pack(direct, blocks, grad_refs, lambda part: [block[part * size : (part + 1) * size] for block in blocks])


def plane_kernel(moves, keep_ref, got_ref, _, kept_ref, *send_refs):
    part = lax.rem(lax.axis_index("dp"), keep_ref.shape[0])
    half = lax.axis_index("y")

    def total(x, y):
        at = 1 - part if x else part, 1 - half if y else half
        return keep_ref[at] + got_ref[at].astype(F32)

    kept_ref[...] = total(0, 0)
    for (x, y), send_ref in zip(moves, send_refs, strict=True):
        send_ref[...] = total(x, y).astype(BF)


def total_kernel(kept_ref, *refs):
    *got_refs, _, out_ref = refs
    value = kept_ref[...]
    for ref in got_refs:
        value = value + ref[...].astype(F32)
    out_ref[...] = value.astype(BF)


def depth_kernel(*refs):
    *in_refs, out_ref = refs
    sums = []
    for n in range(0, len(in_refs), 4):
        a, b, c, d = (ref[...].astype(F32) for ref in in_refs[n : n + 4])
        sums.append((a + b) + (c + d))
    out_ref[...] = jnp.concatenate(sums, axis=0).astype(BF)


def order_kernel(own_ref, got_ref, _, out_ref):
    mine = lax.axis_index("y")
    out_ref[mine] = own_ref[...]
    out_ref[1 - mine] = got_ref[...]


def quarters_of(own_ref, got_ref):
    core = lax.axis_index("core") == 1
    quarters = []
    for n in range(own_ref.shape[0]):
        own, got = (ref[n].astype(F32) for ref in (own_ref, got_ref))
        quarters += [jnp.where(core, got, own), jnp.where(core, own, got)]
    return quarters


def units_in(quarters, size):
    length = quarters[0].shape[0]

    def get(unit):
        values, row = [], unit * size
        while row < (unit + 1) * size:
            number, start = divmod(row, length)
            stop = min(length, start + (unit + 1) * size - row)
            values.append(quarters[number][start:stop])
            row += stop - start
        return values[0] if len(values) == 1 else jnp.concatenate(values, axis=0)

    return get


def unpack_kernel(length, own_ref, got_ref, first_ref, second_ref):
    quarters = quarters_of(own_ref, got_ref)
    size, inner = first_ref.shape[1:]
    mid = second_ref.shape[2]
    get = units_in([quarter[:length] for quarter in quarters], size)
    for j in range(13):
        for half in range(2):
            value = get(2 * j + half)
            for m in range(2):
                c, ab = (j // 4, 2 * (j % 4) + m) if j < 12 else (m, 8)
                second_ref[3 * ab + c, half * size : (half + 1) * size, :] = value[:, m * mid : (m + 1) * mid]
    value = get(26)
    for half in range(2):
        second_ref[26, half * size : (half + 1) * size, :] = value[:, half * mid : (half + 1) * mid]
    get = units_in([quarter[length:] for quarter in quarters], size)
    for j in range(7):
        value = get(j)
        for m in range(4):
            c, ab = (j // 2, 4 * (j % 2) + m) if j < 6 else (m, 8)
            if c < 3:
                first_ref[3 * ab + c] = value[:, m * inner : (m + 1) * inner]


def swapped(x, axis, first):
    axes = (axis,) if isinstance(axis, str) else axis
    parts, size = lax.axis_size("dp"), lax.axis_size(axis)
    partner = list(range(parts * size))
    for i in partner:
        part, at = divmod(i, size)
        if first <= at < size - (size - first) % 2:
            partner[i] = part * size + (at - first ^ 1) + first
        elif parts % 2 == 0:
            partner[i] = (part ^ 1) * size + at
    return lax.ppermute(x, ("dp", *axes), list(enumerate(partner)))


def across(x, *moves):
    axes = tuple(axis for axis, _ in moves)
    flip = 0
    for axis, bit in moves:
        flip = flip * lax.axis_size(axis) + bit
    return lax.ppermute(x, axes, [(i, i ^ flip) for i in range(lax.axis_size(axes))])


def scattered(units, length):
    parts, halves = units.shape[0], lax.axis_size("y")
    grad = units.reshape(parts, -1, LANES)
    grad = jnp.pad(grad, ((0, 0), (0, 2 * halves * length - grad.shape[1]), (0, 0)))
    grad = lax.psum_scatter(grad, "dp", scatter_dimension=0, tiled=True).reshape(1, halves, 2, length, LANES)
    core = lax.axis_index("core")
    keep, send = (lax.dynamic_index_in_dim(grad, at, 2, False) for at in (core, 1 - core))
    return keep, send.astype(BF)


def per_device(volume, kernel_first, kernel_second, cotangent):
    _, inner, depth, height, width = volume.shape
    mid, out = kernel_first.shape[1], kernel_second.shape[1]
    cells = height * width
    parts = lax.axis_size("dp")
    k1, k2 = jnp.swapaxes(kernel_first, 1, 2), jnp.swapaxes(kernel_second, 1, 2)
    rows = depth * height

    one, two = swapped(volume[0], "dep", 0), swapped(volume[0], "dep", 1)
    (blank,) = call(blank_kernel, [shape((out, 2 * width), BF)], [], flops=3_000_000_000)
    cot_rows, back, back_one, back_two = call(
        spread_kernel,
        [
            shape((depth, out, cells), BF),
            shape((depth, mid, cells + 2 * width), F32),
            shape((mid, cells + 2 * width), BF),
            shape((mid, cells + 2 * width), BF),
        ],
        [cotangent[0], k2, blank],
        [pltpu.VMEM((out * rows, width), F32)],
        flops=1_100_000_000,
    )
    deep, one, two = call(
        rim_kernel,
        [shape((3 * depth, inner, cells), BF)] + [shape((3 * depth, inner, 2 * width), BF)] * 2,
        [volume[0], one, two, cot_rows],
        [pltpu.VMEM((inner * rows, width), F32)],
    )
    one, two = swapped(one, HGT, 0), swapped(two, HGT, 1)
    moved, w1 = call(
        arrange_kernel,
        [shape((depth, 3 * out, cells), BF), shape((3 * mid, 9 * inner), BF)],
        [cot_rows, k1, deep],
        flops=500_000_000,
    )
    back_one, back_two = swapped(back_one, "dep", 0), swapped(back_two, "dep", 1)
    back, back_one, back_two = call(
        back_rim_kernel,
        [shape((depth, mid, cells), F32)] + [shape((depth, mid, width), BF)] * 2,
        [back, back_one, back_two],
    )
    back_one, back_two = swapped(back_one, HGT, 0), swapped(back_two, HGT, 1)

    size = mid // parts
    direct = parts == 2 and size % 16 == 0
    halves = lax.axis_size("y")
    length_second, length_first = (-(-units * size // (16 * halves)) * 8 for units in (27, 7))
    hidden, slope, wide, *second = call(
        functools.partial(hidden_kernel, direct),
        [
            shape((depth + 2, mid, cells + 2 * width), BF),
            shape((depth, mid, cells), F32),
            shape((3 * depth, inner, cells + 4 * width), BF),
        ]
        + (
            [shape((parts, halves, length_second, width), kind) for kind in (F32, BF)]
            if direct
            else [shape((14, out, LANES), F32)]
        ),
        [deep, one, two, w1, moved, back],
        flops=1_500_000_000,
    )
    first = call(
        functools.partial(delta_kernel, direct),
        [shape((parts, halves, length_first, width), kind) for kind in (F32, BF)]
        if direct
        else [shape((7, mid, LANES), F32)],
        [wide, back, back_one, back_two, slope],
        [pltpu.VMEM((3 * mid, depth * cells), BF)],
        flops=4_000_000_000,
    )
    if direct:
        moves = [(1, 0), (0, 1), (1, 1)]
    else:
        moves = [(0, 1)]
        blocks = jnp.swapaxes(second[0].reshape(14, parts, 2, size, LANES), 0, 1)
        tail = jnp.concatenate([blocks[:, 13, half, :, :mid] for half in range(2)], axis=-1)
        units = jnp.concatenate([blocks[:, :13].reshape(parts, 26, size, LANES), tail[:, None]], axis=1)
        second = scattered(units, length_second)
        first = scattered(jnp.swapaxes(first[0].reshape(7, parts, size, LANES), 0, 1), length_first)
    grads = []
    after = slope
    for keep, send in (second, first):
        block = keep.shape[2:]
        kept, *sends = call(
            functools.partial(plane_kernel, moves),
            [shape(block, F32)] + [shape(block, BF)] * len(moves),
            [keep, across(send, ("core", 1)), after],
        )
        after = kept
        grads.append((kept, [across(send, ("dp", x), ("y", y)) for send, (x, y) in zip(sends, moves, strict=True)]))
    shares, weights, orders = [], (0, 4_000_000_000), ((1, 3, 2), (3, 2, 1))
    for (kept, gots), weight, order in zip(grads, weights, orders, strict=True):
        (share,) = call(total_kernel, [shape(kept.shape, BF)], [kept, *gots, after], flops=weight)
        after = share
        shares.append((share, [across(share, ("dep", bits)) for bits in order]))
    (share,) = call(
        depth_kernel,
        [shape((length_second + length_first, width), BF)],
        [x for share, gots in shares for x in (share, *gots)],
    )
    features, token = call(
        features_kernel,
        [shape(cotangent.shape[1:], BF), shape((8, width), F32)],
        [hidden, k2, share],
        [pltpu.VMEM((out * rows, width), F32)],
        flops=900_000_000,
    )
    (own,) = call(order_kernel, [shape((halves, *share.shape), BF)], [share, across(share, ("y", 1)), token])
    grad_first, grad_second = call(
        functools.partial(unpack_kernel, length_second),
        [shape((27, size, inner), F32), shape((27, 2 * size, mid), F32)],
        [own, across(own, ("core", 1))],
    )
    return features[None], grad_first, grad_second


def solution(mesh):
    dp, dep, hgt = (mesh.shape[axis] for axis in ("dp", "dep", "hgt"))
    split = jax.sharding.Mesh(mesh.devices.reshape(dp, dep, hgt // 2, 2), ("dp", "dep", *HGT))
    block = P("dp", None, "dep", HGT, None)
    return jax.shard_map(
        per_device,
        mesh=split,
        in_specs=(block, P(), P(), block),
        out_specs=(block, P(None, "dp", None), P(None, "dp", None)),
        check_vma=False,
    )
```

```python
import functools

import jax
import jax.numpy as jnp
from jax import lax
from jax.experimental import pallas as pl
from jax.experimental.pallas import tpu as pltpu
from jax.sharding import PartitionSpec as P

BF, F32 = jnp.bfloat16, jnp.float32
LANES = 128
HGT = ("y", "core")
VMEM_BYTES = 48 * 2**20


def call(body, outs, args, scratch=(), flops=0, far=()):
    moved = sum(x.size * x.dtype.itemsize for x in (*outs, *args))
    return pl.pallas_call(
        body,
        out_shape=outs,
        in_specs=[pl.BlockSpec(memory_space=pl.ANY if n in far else pltpu.VMEM) for n in range(len(args))],
        out_specs=[pl.BlockSpec(memory_space=pltpu.VMEM)] * len(outs),
        scratch_shapes=list(scratch),
        compiler_params=pltpu.CompilerParams(vmem_limit_bytes=VMEM_BYTES),
        cost_estimate=pl.CostEstimate(flops=flops, bytes_accessed=moved, transcendentals=0),
    )(*args)


def shape(dims, dtype):
    return jax.ShapeDtypeStruct(dims, dtype)


def moved_along_width(x, c):
    if c == 0:
        return x
    pieces = []
    for start in range(0, x.shape[1], LANES):
        piece = x[:, start : start + LANES]
        lane = lax.broadcasted_iota(jnp.int32, piece.shape, 1)
        rolled = pltpu.roll(piece, c % LANES, 1)
        pieces.append(jnp.where(lane == (0 if c == 1 else LANES - 1), 0.0, rolled))
    return pieces[0] if len(pieces) == 1 else jnp.concatenate(pieces, axis=1)


def by_rows(ref, scratch, store):
    channels, depth, height, width = ref.shape
    rows = depth * height
    scratch[...] = ref[...].astype(F32).reshape(channels * rows, width)
    for d in range(depth):
        for h in range(height):
            store(d, h, scratch[pl.ds(d * height + h, channels, stride=rows), :])


def odd(axis):
    return lax.rem(lax.axis_index(axis), 2) == 1


def blank_kernel(out_ref):
    out_ref[...] = jnp.zeros(out_ref.shape, BF)


def spread_kernel(cot_ref, k2_ref, blank_ref, cot_rows_ref, back_ref, scratch):
    out, depth, height, _ = cot_ref.shape
    rows = [[None] * height for _ in range(depth)]

    def store(d, h, row):
        rows[d][h] = row.astype(BF)
        cot_rows_ref[d, :, h * LANES : (h + 1) * LANES] = rows[d][h]

    by_rows(cot_ref, scratch, store)
    mid = k2_ref.shape[1]
    none = blank_ref[...]
    padded = [jnp.concatenate([none, *rows[d], none], axis=1) for d in range(depth)]
    for e in range(depth + 2):
        reached = [(d, e - 1 - d) for d in range(depth) if abs(e - 1 - d) <= 1]
        w = jnp.concatenate(
            [
                k2_ref[9 * (a + 1) + 3 * b : 9 * (a + 1) + 3 * b + 3].reshape(3 * mid, out)
                for _, a in reached
                for b in range(3)
            ],
            axis=1,
        )
        for j in range(0, height + 2, 2):
            rhs = jnp.concatenate(
                [padded[d][:, (j + 2 - b) * LANES : (j + 4 - b) * LANES] for d, _ in reached for b in range(3)], axis=0
            )
            y = jnp.dot(w, rhs, preferred_element_type=F32)
            back = sum(moved_along_width(y[n * mid : (n + 1) * mid], n - 1) for n in range(3))
            back_ref[e, :, j * LANES : (j + 2) * LANES] = back


def as_matrix(ref, c):
    stacked = jnp.concatenate([ref[3 * ab + c] for ab in range(9)], axis=0)
    return stacked.astype(F32).T.astype(BF)


def arrange_kernel(cot_rows_ref, k1_ref, _, moved_ref, w1_ref):
    depth, out, cells = cot_rows_ref.shape
    for d in range(depth):
        for h in range(0, cells, LANES):
            row = cot_rows_ref[d, :, h : h + LANES]
            for n, c in enumerate((-1, 0, 1)):
                value = row if c == 0 else moved_along_width(row.astype(F32), c).astype(BF)
                moved_ref[d, n * out : (n + 1) * out, h : h + LANES] = value
    mid = k1_ref.shape[2]
    for c in range(3):
        w1_ref[c * mid : (c + 1) * mid, :] = as_matrix(k1_ref, c)


def sides(axis, one, two):
    me, size = lax.axis_index(axis), lax.axis_size(axis)
    is_odd = odd(axis)
    none = jnp.zeros_like(one)
    before = jnp.where(me == 0, none, jnp.where(is_odd, one, two))
    after = jnp.where(me == size - 1, none, jnp.where(is_odd, two, one))
    return before, after


def rim_kernel(own_ref, one_ref, two_ref, _, deep_ref, send_one_ref, send_two_ref, scratch):
    depth = own_ref.shape[1]
    before, after = sides("dep", one_ref[...], two_ref[...])
    for n, part in enumerate((before, own_ref[...], after)):

        def store(d, h, row, at=n * depth):
            deep_ref[at + d, :, h * LANES : (h + 1) * LANES] = row.astype(BF)

        by_rows(part, scratch, store)
    n, cells = send_one_ref.shape[2], deep_ref.shape[2]
    first, last = deep_ref[:, :, :n], deep_ref[:, :, cells - n :]
    is_odd = odd(HGT)
    send_one_ref[...] = jnp.where(is_odd, first, last)
    send_two_ref[...] = jnp.where(is_odd, last, first)


def widened(deep_ref, one_ref, two_ref):
    left, right = sides(HGT, one_ref[...], two_ref[...])
    return [jnp.concatenate([left[d], deep_ref[d], right[d]], axis=1) for d in range(deep_ref.shape[0])]


def pack(direct, blocks, refs, units_of):
    if not direct:
        for j, block in enumerate(blocks):
            refs[0][j] = block
        return
    keep_ref, send_ref = refs
    parts, halves, length, _ = keep_ref.shape
    core = lax.axis_index("core") == 1
    for part in range(parts):
        whole = units_of(part)
        size = whole[0].shape[0]

        def quarter(number, whole=whole, size=size):
            values, row = [], number * length
            while row < (number + 1) * length:
                unit, start = divmod(row, size)
                stop = min(size, start + (number + 1) * length - row)
                values.append(whole[unit][start:stop])
                row += stop - start
            return jnp.concatenate(values, axis=0)

        for half in range(halves):
            one, two = (quarter(2 * half + c) for c in range(2))
            keep_ref[part, half] = jnp.where(core, two, one)
            send_ref[part, half] = jnp.where(core, one, two)


def hidden_kernel(
    direct, deep_ref, one_ref, two_ref, w1_ref, moved_ref, hidden_ref, slope_ref, rows_ref, *grad_refs
):
    for d, row in enumerate(widened(deep_ref, one_ref, two_ref)):
        rows_ref[d] = row
    rows = rows_ref
    mid = w1_ref.shape[0] // 3
    dep, deps = lax.axis_index("dep"), lax.axis_size("dep")
    hgt, hgts = lax.axis_index(HGT), lax.axis_size(HGT)
    depth, height = hidden_ref.shape[0], hidden_ref.shape[2] // LANES
    w1 = w1_ref[...]
    for d in range(depth):
        for h in range(0, height, 2):
            rhs = jnp.concatenate(
                [rows[d + a, :, (h + b) * LANES : (h + b + 2) * LANES] for a in range(3) for b in range(3)], axis=0
            )
            y = jnp.dot(w1, rhs, preferred_element_type=F32)
            pre = sum(moved_along_width(y[n * mid : (n + 1) * mid], 1 - n) for n in range(3))
            s = 1.0 / (1.0 + jnp.exp(-pre))
            for r in range(2):
                lanes = slice(r * LANES, (r + 1) * LANES)
                p, q = pre[:, lanes], s[:, lanes]
                value = (p * q).astype(BF)
                slope = q * (1.0 + p * (1.0 - q))
                outside = []
                if d == 0:
                    outside.append(dep == 0)
                if d == depth - 1:
                    outside.append(dep == deps - 1)
                if h + r == 0:
                    outside.append(hgt == 0)
                if h + r == height - 1:
                    outside.append(hgt == hgts - 1)
                for far in outside:
                    value = jnp.where(far, jnp.zeros_like(value), value)
                    slope = jnp.where(far, jnp.zeros_like(slope), slope)
                at = slice((h + r) * LANES, (h + r + 1) * LANES)
                hidden_ref[d, :, at] = value
                slope_ref[d, :, at] = slope
    cells = (height - 2) * LANES
    own = depth - 2
    out = moved_ref.shape[1] // 3
    left = jnp.concatenate([moved_ref[d] for d in range(own)], axis=1)
    blocks, tails = [None] * 12, []
    for first in (0, 4, 8):
        group = range(first, min(first + 4, 9))
        right = jnp.concatenate(
            [
                jnp.concatenate(
                    [hidden_ref[d + ab // 3, :, (ab % 3) * LANES : (ab % 3) * LANES + cells] for ab in group], axis=0
                )
                for d in range(own)
            ],
            axis=1,
        )
        g = lax.dot_general(left, right, (((1,), (1,)), ((), ())), preferred_element_type=F32)
        for n in range(3):
            part = g[n * out : (n + 1) * out]
            if first < 8:
                for m in range(2):
                    blocks[4 * n + first // 2 + m] = part[:, m * LANES : (m + 1) * LANES]
            else:
                tails.append(part)
    tails.append(jnp.zeros_like(tails[0]))
    blocks += [jnp.concatenate(tails[2 * m : 2 * m + 2], axis=1) for m in range(2)]
    size = mid // lax.axis_size("dp")

    def units_of(part):
        rows = [slice((2 * part + half) * size, (2 * part + half + 1) * size) for half in range(2)]
        return [block[at] for block in blocks[:13] for at in rows] + [
            jnp.concatenate([tails[2][at] for at in rows], axis=1)
        ]

    pack(direct, blocks, grad_refs, units_of)


def features_kernel(hidden_ref, k2_ref, out_ref, token_ref, scratch):
    out, depth, height, _ = out_ref.shape
    w2 = jnp.concatenate([as_matrix(k2_ref, c) for c in range(3)], axis=0)
    for d in range(depth):
        for h in range(0, height, 2):
            rhs = jnp.concatenate(
                [
                    hidden_ref[d + a, :, (h + b) * LANES : (h + b + 2) * LANES]
                    for a in range(3)
                    for b in range(3)
                ],
                axis=0,
            )
            y = jnp.dot(w2, rhs, preferred_element_type=F32)
            total = sum(moved_along_width(y[n * out : (n + 1) * out], 1 - n) for n in range(3))
            for r in range(2):
                row = total[:, r * LANES : (r + 1) * LANES]
                scratch[pl.ds(d * height + h + r, out, stride=depth * height), :] = row
    out_ref[...] = scratch[...].reshape(out_ref.shape).astype(BF)
    token_ref[...] = scratch[:8]


def delta_kernel(direct, rows_ref, back_ref, slope_ref, *outs_and_scratch):
    *grad_refs, delta_ref = outs_and_scratch
    depth, mid, cells = slope_ref.shape
    for d in range(depth):
        for at in range(0, cells, LANES):
            delta = back_ref[d, :, at : at + LANES] * slope_ref[d, :, at : at + LANES]
            for n in range(3):
                delta_ref[n * mid : (n + 1) * mid, d * cells + at : d * cells + at + LANES] = moved_along_width(
                    delta, n - 1
                ).astype(BF)
    left = delta_ref[...]
    blocks, tails = [None] * 6, []
    inner = rows_ref.shape[1]
    for first in (0, 8):
        group = range(first, min(first + 8, 9))
        right = jnp.concatenate(
            [
                jnp.concatenate(
                    [
                        rows_ref[d + ab // 3, :, (ab % 3) * LANES : (ab % 3) * LANES + cells]
                        for ab in group
                    ],
                    axis=0,
                )
                for d in range(depth)
            ],
            axis=1,
        )
        g = lax.dot_general(left, right, (((1,), (1,)), ((), ())), preferred_element_type=F32)
        for n in range(3):
            part = g[n * mid : (n + 1) * mid]
            if first == 0:
                for m in range(2):
                    blocks[2 * n + m] = part[:, m * LANES : (m + 1) * LANES]
            else:
                tails.append(part)
    tails.append(jnp.zeros((mid, LANES - 3 * inner), F32))
    blocks.append(jnp.concatenate(tails, axis=1))
    size = mid // lax.axis_size("dp")
    pack(direct, blocks, grad_refs, lambda part: [block[part * size : (part + 1) * size] for block in blocks])


def plane_kernel(moves, *refs):
    keep_second, got_second, keep_first, got_first, kept_ref, *send_refs = refs
    part = lax.rem(lax.axis_index("dp"), keep_first.shape[0])
    half = lax.axis_index("y")

    def total(x, y):
        at = 1 - part if x else part, 1 - half if y else half
        return jnp.concatenate([keep_second[at] + got_second[at], keep_first[at] + got_first[at]], axis=0)

    kept_ref[...] = total(0, 0)
    for (x, y), send_ref in zip(moves, send_refs, strict=True):
        send_ref[...] = total(x, y).astype(BF)


def total_kernel(kept_ref, *refs):
    *got_refs, out_ref = refs
    value = kept_ref[...]
    for ref in got_refs:
        value = value + ref[...].astype(F32)
    out_ref[...] = value.astype(BF)


def depth_kernel(a_ref, b_ref, c_ref, d_ref, _, out_ref):
    one = a_ref[...].astype(F32) + b_ref[...].astype(F32)
    two = c_ref[...].astype(F32) + d_ref[...].astype(F32)
    out_ref[...] = (one + two).astype(BF)


def order_kernel(own_ref, got_ref, out_ref):
    mine = lax.axis_index("y")
    out_ref[mine] = own_ref[...]
    out_ref[1 - mine] = got_ref[...]


def quarters_of(own_ref, got_ref):
    core = lax.axis_index("core") == 1
    quarters = []
    for n in range(own_ref.shape[0]):
        own, got = (ref[n].astype(F32) for ref in (own_ref, got_ref))
        quarters += [jnp.where(core, got, own), jnp.where(core, own, got)]
    return quarters


def units_in(quarters, size):
    length = quarters[0].shape[0]

    def get(unit):
        values, row = [], unit * size
        while row < (unit + 1) * size:
            number, start = divmod(row, length)
            stop = min(length, start + (unit + 1) * size - row)
            values.append(quarters[number][start:stop])
            row += stop - start
        return values[0] if len(values) == 1 else jnp.concatenate(values, axis=0)

    return get


def unpack_kernel(length, own_ref, got_ref, first_ref, second_ref):
    quarters = quarters_of(own_ref, got_ref)
    size, inner = first_ref.shape[1:]
    mid = second_ref.shape[2]
    get = units_in([quarter[:length] for quarter in quarters], size)
    for j in range(13):
        for half in range(2):
            value = get(2 * j + half)
            for m in range(2):
                c, ab = (j // 4, 2 * (j % 4) + m) if j < 12 else (m, 8)
                second_ref[3 * ab + c, half * size : (half + 1) * size, :] = value[:, m * mid : (m + 1) * mid]
    value = get(26)
    for half in range(2):
        second_ref[26, half * size : (half + 1) * size, :] = value[:, half * mid : (half + 1) * mid]
    get = units_in([quarter[length:] for quarter in quarters], size)
    for j in range(7):
        value = get(j)
        for m in range(4):
            c, ab = (j // 2, 4 * (j % 2) + m) if j < 6 else (m, 8)
            if c < 3:
                first_ref[3 * ab + c] = value[:, m * inner : (m + 1) * inner]


def swapped(x, axis, first):
    axes = (axis,) if isinstance(axis, str) else axis
    parts, size = lax.axis_size("dp"), lax.axis_size(axis)
    partner = list(range(parts * size))
    for i in partner:
        part, at = divmod(i, size)
        if first <= at < size - (size - first) % 2:
            partner[i] = part * size + (at - first ^ 1) + first
        elif parts % 2 == 0:
            partner[i] = (part ^ 1) * size + at
    return lax.ppermute(x, ("dp", *axes), list(enumerate(partner)))


def across(x, *moves):
    axes = tuple(axis for axis, _ in moves)
    flip = 0
    for axis, bit in moves:
        flip = flip * lax.axis_size(axis) + bit
    return lax.ppermute(x, axes, [(i, i ^ flip) for i in range(lax.axis_size(axes))])


def scattered(units, length):
    parts, halves = units.shape[0], lax.axis_size("y")
    grad = units.reshape(parts, -1, LANES)
    grad = jnp.pad(grad, ((0, 0), (0, 2 * halves * length - grad.shape[1]), (0, 0)))
    grad = lax.psum_scatter(grad, "dp", scatter_dimension=0, tiled=True).reshape(1, halves, 2, length, LANES)
    core = lax.axis_index("core")
    keep, send = (lax.dynamic_index_in_dim(grad, at, 2, False) for at in (core, 1 - core))
    return keep, send


def per_device(volume, kernel_first, kernel_second, cotangent):
    _, inner, depth, height, width = volume.shape
    mid, out = kernel_first.shape[1], kernel_second.shape[1]
    cells = height * width
    parts = lax.axis_size("dp")
    k1, k2 = jnp.swapaxes(kernel_first, 1, 2), jnp.swapaxes(kernel_second, 1, 2)
    rows = depth * height

    one, two = swapped(volume[0], "dep", 0), swapped(volume[0], "dep", 1)
    (blank,) = call(blank_kernel, [shape((out, 2 * width), BF)], [], flops=3_000_000_000)
    cot_rows, back = call(
        spread_kernel,
        [
            shape((depth, out, cells), BF),
            shape((depth + 2, mid, cells + 2 * width), F32),
        ],
        [cotangent[0], k2, blank],
        [pltpu.VMEM((out * rows, width), F32)],
        flops=1_100_000_000,
    )
    deep, one, two = call(
        rim_kernel,
        [shape((3 * depth, inner, cells), BF)] + [shape((3 * depth, inner, 2 * width), BF)] * 2,
        [volume[0], one, two, cot_rows],
        [pltpu.VMEM((inner * rows, width), F32)],
    )
    one, two = swapped(one, HGT, 0), swapped(two, HGT, 1)
    moved, w1 = call(
        arrange_kernel,
        [shape((depth, 3 * out, cells), BF), shape((3 * mid, 9 * inner), BF)],
        [cot_rows, k1, deep],
        flops=500_000_000,
    )
    size = mid // parts
    direct = parts == 2 and size % 16 == 0
    halves = lax.axis_size("y")
    length_second, length_first = (-(-units * size // (16 * halves)) * 8 for units in (27, 7))
    hidden, slope, wide, *second = call(
        functools.partial(hidden_kernel, direct),
        [
            shape((depth + 2, mid, cells + 2 * width), BF),
            shape((depth + 2, mid, cells + 2 * width), F32),
            shape((3 * depth, inner, cells + 4 * width), BF),
        ]
        + (
            [shape((parts, halves, length_second, width), F32) for _ in range(2)]
            if direct
            else [shape((14, out, LANES), F32)]
        ),
        [deep, one, two, w1, moved],
        flops=1_500_000_000,
    )
    first = call(
        functools.partial(delta_kernel, direct),
        [shape((parts, halves, length_first, width), F32) for _ in range(2)]
        if direct
        else [shape((7, mid, LANES), F32)],
        [wide, back, slope],
        [pltpu.VMEM((3 * mid, (depth + 2) * (cells + 2 * width)), BF)],
        flops=4_000_000_000,
    )
    if direct:
        moves = [(1, 0), (0, 1), (1, 1)]
    else:
        moves = [(0, 1)]
        blocks = jnp.swapaxes(second[0].reshape(14, parts, 2, size, LANES), 0, 1)
        tail = jnp.concatenate([blocks[:, 13, half, :, :mid] for half in range(2)], axis=-1)
        units = jnp.concatenate([blocks[:, :13].reshape(parts, 26, size, LANES), tail[:, None]], axis=1)
        second = scattered(units, length_second)
        first = scattered(jnp.swapaxes(first[0].reshape(7, parts, size, LANES), 0, 1), length_first)
    block = (length_second + length_first, width)
    kept, *sends = call(
        functools.partial(plane_kernel, moves),
        [shape(block, F32)] + [shape(block, BF)] * len(moves),
        [x for keep, send in (second, first) for x in (keep, across(send, ("core", 1)))],
    )
    gots = [across(send, ("dp", x), ("y", y)) for send, (x, y) in zip(sends, moves, strict=True)]
    (share,) = call(total_kernel, [shape(block, BF)], [kept, *gots])
    features, token = call(
        features_kernel,
        [shape(cotangent.shape[1:], BF), shape((8, width), F32)],
        [hidden, k2],
        [pltpu.VMEM((out * rows, width), F32)],
        flops=900_000_000,
    )
    gots = [across(share, ("dep", bits)) for bits in (1, 2, 3)]
    (share,) = call(depth_kernel, [shape(block, BF)], [share, *gots, token])
    (own,) = call(order_kernel, [shape((halves, *block), BF)], [share, across(share, ("y", 1))])
    grad_first, grad_second = call(
        functools.partial(unpack_kernel, length_second),
        [shape((27, size, inner), F32), shape((27, 2 * size, mid), F32)],
        [own, across(own, ("core", 1))],
    )
    return features[None], grad_first, grad_second


def solution(mesh):
    dp, dep, hgt = (mesh.shape[axis] for axis in ("dp", "dep", "hgt"))
    split = jax.sharding.Mesh(mesh.devices.reshape(dp, dep, hgt // 2, 2), ("dp", "dep", *HGT))
    block = P("dp", None, "dep", HGT, None)
    return jax.shard_map(
        per_device,
        mesh=split,
        in_specs=(block, P(), P(), block),
        out_specs=(block, P(None, "dp", None), P(None, "dp", None)),
        check_vma=False,
    )
```

```python
import functools

import jax
import jax.numpy as jnp
from jax import lax
from jax.experimental import pallas as pl
from jax.experimental.pallas import tpu as pltpu
from jax.sharding import PartitionSpec as P

BF, F32 = jnp.bfloat16, jnp.float32
LANES = 128
HGT = ("y", "core")
VMEM_BYTES = 28 * 2**20


def call(body, outs, args, scratch=(), flops=0, far=()):
    moved = sum(x.size * x.dtype.itemsize for x in (*outs, *args))
    return pl.pallas_call(
        body,
        out_shape=outs,
        in_specs=[pl.BlockSpec(memory_space=pl.ANY if n in far else pltpu.VMEM) for n in range(len(args))],
        out_specs=[pl.BlockSpec(memory_space=pltpu.VMEM)] * len(outs),
        scratch_shapes=list(scratch),
        compiler_params=pltpu.CompilerParams(vmem_limit_bytes=VMEM_BYTES),
        cost_estimate=pl.CostEstimate(flops=flops, bytes_accessed=moved, transcendentals=0),
    )(*args)


def shape(dims, dtype):
    return jax.ShapeDtypeStruct(dims, dtype)


def moved_along_width(x, c):
    if c == 0:
        return x
    pieces = []
    for start in range(0, x.shape[1], LANES):
        piece = x[:, start : start + LANES]
        lane = lax.broadcasted_iota(jnp.int32, piece.shape, 1)
        rolled = pltpu.roll(piece, c % LANES, 1)
        pieces.append(jnp.where(lane == (0 if c == 1 else LANES - 1), 0.0, rolled))
    return pieces[0] if len(pieces) == 1 else jnp.concatenate(pieces, axis=1)


def by_rows(ref, scratch, store):
    channels, depth, height, width = ref.shape
    rows = depth * height
    scratch[...] = ref[...].astype(F32).reshape(channels * rows, width)
    for d in range(depth):
        for h in range(height):
            store(d, h, scratch[pl.ds(d * height + h, channels, stride=rows), :])


def odd(axis):
    return lax.rem(lax.axis_index(axis), 2) == 1


def blank_kernel(out_ref):
    out_ref[...] = jnp.zeros(out_ref.shape, BF)


def spread_kernel(cot_ref, k2_ref, blank_ref, cot_rows_ref, back_ref, scratch):
    out, depth, height, _ = cot_ref.shape
    rows = [[None] * height for _ in range(depth)]

    def store(d, h, row):
        rows[d][h] = row.astype(BF)
        cot_rows_ref[d, :, h * LANES : (h + 1) * LANES] = rows[d][h]

    by_rows(cot_ref, scratch, store)
    mid = k2_ref.shape[1]
    none = blank_ref[...]
    padded = [jnp.concatenate([none, *rows[d], none], axis=1) for d in range(depth)]
    for e in range(depth + 2):
        reached = [(d, e - 1 - d) for d in range(depth) if abs(e - 1 - d) <= 1]
        w = jnp.concatenate(
            [
                k2_ref[9 * (a + 1) + 3 * b : 9 * (a + 1) + 3 * b + 3].reshape(3 * mid, out)
                for _, a in reached
                for b in range(3)
            ],
            axis=1,
        )
        for j in range(0, height + 2, 2):
            rhs = jnp.concatenate(
                [padded[d][:, (j + 2 - b) * LANES : (j + 4 - b) * LANES] for d, _ in reached for b in range(3)], axis=0
            )
            y = jnp.dot(w, rhs, preferred_element_type=F32)
            back = sum(moved_along_width(y[n * mid : (n + 1) * mid], n - 1) for n in range(3))
            back_ref[e, :, j * LANES : (j + 2) * LANES] = back


def as_matrix(ref, c):
    stacked = jnp.concatenate([ref[3 * ab + c] for ab in range(9)], axis=0)
    return stacked.astype(F32).T.astype(BF)


def arrange_kernel(cot_rows_ref, k1_ref, moved_ref, w1_ref):
    depth, out, cells = cot_rows_ref.shape
    for d in range(depth):
        for h in range(0, cells, LANES):
            row = cot_rows_ref[d, :, h : h + LANES]
            for n, c in enumerate((-1, 0, 1)):
                value = row if c == 0 else moved_along_width(row.astype(F32), c).astype(BF)
                moved_ref[d, n * out : (n + 1) * out, h : h + LANES] = value
    mid = k1_ref.shape[2]
    for c in range(3):
        w1_ref[c * mid : (c + 1) * mid, :] = as_matrix(k1_ref, c)


def sides(axis, one, two):
    me, size = lax.axis_index(axis), lax.axis_size(axis)
    is_odd = odd(axis)
    none = jnp.zeros_like(one)
    before = jnp.where(me == 0, none, jnp.where(is_odd, one, two))
    after = jnp.where(me == size - 1, none, jnp.where(is_odd, two, one))
    return before, after


def rim_kernel(own_ref, one_ref, two_ref, _, deep_ref, send_one_ref, send_two_ref, scratch):
    depth = own_ref.shape[1]
    before, after = sides("dep", one_ref[...], two_ref[...])
    for n, part in enumerate((before, own_ref[...], after)):

        def store(d, h, row, at=n * depth):
            deep_ref[at + d, :, h * LANES : (h + 1) * LANES] = row.astype(BF)

        by_rows(part, scratch, store)
    n, cells = send_one_ref.shape[2], deep_ref.shape[2]
    first, last = deep_ref[:, :, :n], deep_ref[:, :, cells - n :]
    is_odd = odd(HGT)
    send_one_ref[...] = jnp.where(is_odd, first, last)
    send_two_ref[...] = jnp.where(is_odd, last, first)


def widened(deep_ref, one_ref, two_ref):
    left, right = sides(HGT, one_ref[...], two_ref[...])
    return [jnp.concatenate([left[d], deep_ref[d], right[d]], axis=1) for d in range(deep_ref.shape[0])]


def pack(direct, blocks, refs, units_of):
    if not direct:
        for j, block in enumerate(blocks):
            refs[0][j] = block
        return
    keep_ref, send_ref = refs
    parts, halves, length, _ = keep_ref.shape
    core = lax.axis_index("core") == 1
    for part in range(parts):
        whole = units_of(part)
        size = whole[0].shape[0]

        def quarter(number, whole=whole, size=size):
            values, row = [], number * length
            while row < (number + 1) * length:
                unit, start = divmod(row, size)
                stop = min(size, start + (number + 1) * length - row)
                values.append(whole[unit][start:stop])
                row += stop - start
            return jnp.concatenate(values, axis=0)

        for half in range(halves):
            one, two = (quarter(2 * half + c) for c in range(2))
            keep_ref[part, half] = jnp.where(core, two, one)
            send_ref[part, half] = jnp.where(core, one, two)


def activated(w1, rhs, d, depth, heights):
    mid = w1.shape[0] // 3
    y = jnp.dot(w1, rhs, preferred_element_type=F32)
    pre = sum(moved_along_width(y[n * mid : (n + 1) * mid], 1 - n) for n in range(3))
    s = 1.0 / (1.0 + jnp.exp(-pre))
    dep, deps = lax.axis_index("dep"), lax.axis_size("dep")
    hgt, hgts = lax.axis_index(HGT), lax.axis_size(HGT)
    results = []
    for n, side in enumerate(heights):
        p, q = (x[:, n * LANES : (n + 1) * LANES] for x in (pre, s))
        value, slope = (p * q).astype(BF), q * (1.0 + p * (1.0 - q))
        outside = []
        if d == 0:
            outside.append(dep == 0)
        if d == depth - 1:
            outside.append(dep == deps - 1)
        if side < 0:
            outside.append(hgt == 0)
        if side > 0:
            outside.append(hgt == hgts - 1)
        for far in outside:
            value = jnp.where(far, jnp.zeros_like(value), value)
            slope = jnp.where(far, jnp.zeros_like(slope), slope)
        results.append((value, slope))
    return results


def neighbours(ref, d, starts, count):
    return jnp.concatenate(
        [
            jnp.concatenate(
                [ref[d + a, :, (start + b) * LANES : (start + b + count) * LANES] for start in starts], axis=1
            )
            for a in range(3)
            for b in range(3)
        ],
        axis=0,
    )


def products(left, right):
    return lax.dot_general(left, right, (((1,), (1,)), ((), ())), preferred_element_type=F32)


def shares(delta, n_channels, ref, at):
    for n in range(3):
        ref[n * n_channels : (n + 1) * n_channels, at : at + LANES] = moved_along_width(delta, n - 1).astype(BF)


def inner_kernel(deep_ref, w1_ref, moved_ref, back_ref, hidden_ref, second_ref, first_ref, delta_ref):
    w1 = w1_ref[...]
    depth, mid, cells = hidden_ref.shape
    height = cells // LANES
    for d in range(depth):
        for h in range(0, height, 2):
            results = activated(w1, neighbours(deep_ref, d, [h], 2), d, depth, (0, 0))
            for n, (value, slope) in enumerate(results):
                at = (h + n) * LANES
                hidden_ref[d, :, at : at + LANES] = value
                back = back_ref[d, :, at + 2 * LANES : at + 3 * LANES]
                shares(back * slope, mid, delta_ref, d * cells + at)
    own = depth - 2
    count = height - 2
    left = jnp.concatenate([moved_ref[d, :, 2 * LANES : (2 + count) * LANES] for d in range(own)], axis=1)
    right = jnp.concatenate([neighbours(hidden_ref, d, [0], count) for d in range(own)], axis=1)
    second_ref[...] = products(left, right)
    right = jnp.concatenate([neighbours(deep_ref, d, [0], height) for d in range(depth)], axis=1)
    first_ref[...] = products(delta_ref[...], right)


def outer_kernel(
    direct, deep_ref, one_ref, two_ref, w1_ref, moved_ref, inner_ref, second_ref,
    hidden_ref, slope_ref, rows_ref, *grad_refs,
):
    for d, row in enumerate(widened(deep_ref, one_ref, two_ref)):
        rows_ref[d] = row
    w1 = w1_ref[...]
    depth, mid, cells = hidden_ref.shape
    height = cells // LANES
    for d in range(depth):
        hidden_ref[d, :, 2 * LANES : cells - 2 * LANES] = inner_ref[d]
        for h, sides_of in ((0, (-1, 0)), (height - 2, (0, 1))):
            results = activated(w1, neighbours(rows_ref, d, [h], 2), d, depth, sides_of)
            for n, (value, slope) in enumerate(results):
                hidden_ref[d, :, (h + n) * LANES : (h + n + 1) * LANES] = value
                at = ((2 if h else 0) + n) * LANES
                slope_ref[d, :, at : at + LANES] = slope
    own, last = depth - 2, height - 4
    left = jnp.concatenate(
        [moved_ref[d, :, at * LANES : (at + 2) * LANES] for d in range(own) for at in (0, last)], axis=1
    )
    right = jnp.concatenate([neighbours(hidden_ref, d, [0, last], 2) for d in range(own)], axis=1)
    total = second_ref[...] + products(left, right)
    out = left.shape[0] // 3
    blocks, tails = [], []
    for n in range(3):
        part = total[n * out : (n + 1) * out]
        blocks += [part[:, m * LANES : (m + 1) * LANES] for m in range(4)]
        tails.append(part[:, 4 * LANES :])
    blocks.append(jnp.concatenate(tails[:2], axis=1))
    blocks.append(jnp.concatenate([tails[2], jnp.zeros_like(tails[2])], axis=1))
    size = mid // lax.axis_size("dp")

    def units_of(part):
        rows = [slice((2 * part + half) * size, (2 * part + half + 1) * size) for half in range(2)]
        return [block[at] for block in blocks[:13] for at in rows] + [
            jnp.concatenate([tails[2][at] for at in rows], axis=1)
        ]

    pack(direct, blocks, grad_refs, units_of)


def features_kernel(hidden_ref, k2_ref, out_ref, token_ref, scratch):
    out, depth, height, _ = out_ref.shape
    w2 = jnp.concatenate([as_matrix(k2_ref, c) for c in range(3)], axis=0)
    for d in range(depth):
        for h in range(0, height, 2):
            rhs = jnp.concatenate(
                [
                    hidden_ref[d + a, :, (h + b) * LANES : (h + b + 2) * LANES]
                    for a in range(3)
                    for b in range(3)
                ],
                axis=0,
            )
            y = jnp.dot(w2, rhs, preferred_element_type=F32)
            total = sum(moved_along_width(y[n * out : (n + 1) * out], 1 - n) for n in range(3))
            for r in range(2):
                row = total[:, r * LANES : (r + 1) * LANES]
                scratch[pl.ds(d * height + h + r, out, stride=depth * height), :] = row
    out_ref[...] = scratch[...].reshape(out_ref.shape).astype(BF)
    token_ref[...] = scratch[:8]


def delta_kernel(direct, rows_ref, back_ref, slope_ref, first_ref, *outs_and_scratch):
    *grad_refs, delta_ref = outs_and_scratch
    depth, mid, cells = slope_ref.shape
    last = back_ref.shape[2] // LANES - 2
    for d in range(depth):
        for n, h in enumerate((0, 1, last, last + 1)):
            delta = back_ref[d, :, h * LANES : (h + 1) * LANES] * slope_ref[d, :, n * LANES : (n + 1) * LANES]
            shares(delta, mid, delta_ref, d * cells + n * LANES)
    right = jnp.concatenate([neighbours(rows_ref, d, [0, last], 2) for d in range(depth)], axis=1)
    total = first_ref[...] + products(delta_ref[...], right)
    inner = rows_ref.shape[1]
    blocks, tails = [], []
    for n in range(3):
        part = total[n * mid : (n + 1) * mid]
        blocks += [part[:, m * LANES : (m + 1) * LANES] for m in range(2)]
        tails.append(part[:, 2 * LANES :])
    tails.append(jnp.zeros((mid, LANES - 3 * inner), F32))
    blocks.append(jnp.concatenate(tails, axis=1))
    size = mid // lax.axis_size("dp")
    pack(direct, blocks, grad_refs, lambda part: [block[part * size : (part + 1) * size] for block in blocks])


def plane_kernel(moves, *refs):
    keep_second, got_second, keep_first, got_first, kept_ref, *send_refs = refs
    part = lax.rem(lax.axis_index("dp"), keep_first.shape[0])
    half = lax.axis_index("y")

    def total(x, y):
        at = 1 - part if x else part, 1 - half if y else half
        return jnp.concatenate([keep_second[at] + got_second[at], keep_first[at] + got_first[at]], axis=0)

    kept_ref[...] = total(0, 0)
    for (x, y), send_ref in zip(moves, send_refs, strict=True):
        send_ref[...] = total(x, y).astype(BF)


def total_kernel(kept_ref, *refs):
    *got_refs, out_ref = refs
    value = kept_ref[...]
    for ref in got_refs:
        value = value + ref[...].astype(F32)
    out_ref[...] = value.astype(BF)


def depth_kernel(a_ref, b_ref, c_ref, d_ref, _, out_ref):
    one = a_ref[...].astype(F32) + b_ref[...].astype(F32)
    two = c_ref[...].astype(F32) + d_ref[...].astype(F32)
    out_ref[...] = (one + two).astype(BF)


def order_kernel(own_ref, got_ref, out_ref):
    mine = lax.axis_index("y")
    out_ref[mine] = own_ref[...]
    out_ref[1 - mine] = got_ref[...]


def quarters_of(own_ref, got_ref):
    core = lax.axis_index("core") == 1
    quarters = []
    for n in range(own_ref.shape[0]):
        own, got = (ref[n].astype(F32) for ref in (own_ref, got_ref))
        quarters += [jnp.where(core, got, own), jnp.where(core, own, got)]
    return quarters


def units_in(quarters, size):
    length = quarters[0].shape[0]

    def get(unit):
        values, row = [], unit * size
        while row < (unit + 1) * size:
            number, start = divmod(row, length)
            stop = min(length, start + (unit + 1) * size - row)
            values.append(quarters[number][start:stop])
            row += stop - start
        return values[0] if len(values) == 1 else jnp.concatenate(values, axis=0)

    return get


def unpack_kernel(length, own_ref, got_ref, first_ref, second_ref):
    quarters = quarters_of(own_ref, got_ref)
    size, inner = first_ref.shape[1:]
    mid = second_ref.shape[2]
    get = units_in([quarter[:length] for quarter in quarters], size)
    for j in range(13):
        for half in range(2):
            value = get(2 * j + half)
            for m in range(2):
                c, ab = (j // 4, 2 * (j % 4) + m) if j < 12 else (m, 8)
                second_ref[3 * ab + c, half * size : (half + 1) * size, :] = value[:, m * mid : (m + 1) * mid]
    value = get(26)
    for half in range(2):
        second_ref[26, half * size : (half + 1) * size, :] = value[:, half * mid : (half + 1) * mid]
    get = units_in([quarter[length:] for quarter in quarters], size)
    for j in range(7):
        value = get(j)
        for m in range(4):
            c, ab = (j // 2, 4 * (j % 2) + m) if j < 6 else (m, 8)
            if c < 3:
                first_ref[3 * ab + c] = value[:, m * inner : (m + 1) * inner]


def swapped(x, axis, first):
    axes = (axis,) if isinstance(axis, str) else axis
    parts, size = lax.axis_size("dp"), lax.axis_size(axis)
    partner = list(range(parts * size))
    for i in partner:
        part, at = divmod(i, size)
        if first <= at < size - (size - first) % 2:
            partner[i] = part * size + (at - first ^ 1) + first
        elif parts % 2 == 0:
            partner[i] = (part ^ 1) * size + at
    return lax.ppermute(x, ("dp", *axes), list(enumerate(partner)))


def across(x, *moves):
    axes = tuple(axis for axis, _ in moves)
    flip = 0
    for axis, bit in moves:
        flip = flip * lax.axis_size(axis) + bit
    return lax.ppermute(x, axes, [(i, i ^ flip) for i in range(lax.axis_size(axes))])


def scattered(units, length):
    parts, halves = units.shape[0], lax.axis_size("y")
    grad = units.reshape(parts, -1, LANES)
    grad = jnp.pad(grad, ((0, 0), (0, 2 * halves * length - grad.shape[1]), (0, 0)))
    grad = lax.psum_scatter(grad, "dp", scatter_dimension=0, tiled=True).reshape(1, halves, 2, length, LANES)
    core = lax.axis_index("core")
    keep, send = (lax.dynamic_index_in_dim(grad, at, 2, False) for at in (core, 1 - core))
    return keep, send


def per_device(volume, kernel_first, kernel_second, cotangent):
    _, inner, depth, height, width = volume.shape
    mid, out = kernel_first.shape[1], kernel_second.shape[1]
    cells = height * width
    parts = lax.axis_size("dp")
    k1, k2 = jnp.swapaxes(kernel_first, 1, 2), jnp.swapaxes(kernel_second, 1, 2)
    rows = depth * height

    one, two = swapped(volume[0], "dep", 0), swapped(volume[0], "dep", 1)
    (blank,) = call(blank_kernel, [shape((out, 2 * width), BF)], [], flops=3_000_000_000)
    cot_rows, back = call(
        spread_kernel,
        [
            shape((depth, out, cells), BF),
            shape((depth + 2, mid, cells + 2 * width), F32),
        ],
        [cotangent[0], k2, blank],
        [pltpu.VMEM((out * rows, width), F32)],
        flops=1_100_000_000,
    )
    moved, w1 = call(
        arrange_kernel,
        [shape((depth, 3 * out, cells), BF), shape((3 * mid, 9 * inner), BF)],
        [cot_rows, k1],
        flops=500_000_000,
    )
    deep, one, two = call(
        rim_kernel,
        [shape((3 * depth, inner, cells), BF)] + [shape((3 * depth, inner, 2 * width), BF)] * 2,
        [volume[0], one, two, w1],
        [pltpu.VMEM((inner * rows, width), F32)],
    )
    one, two = swapped(one, HGT, 0), swapped(two, HGT, 1)
    size = mid // parts
    direct = parts == 2 and size % 16 == 0
    halves = lax.axis_size("y")
    length_second, length_first = (-(-units * size // (16 * halves)) * 8 for units in (27, 7))
    rows_in, rows_out = height - 2, 4
    inner_hidden, inner_second, inner_first = call(
        inner_kernel,
        [
            shape((depth + 2, mid, rows_in * width), BF),
            shape((3 * out, 9 * mid), F32),
            shape((3 * mid, 9 * inner), F32),
        ],
        [deep, w1, moved, back],
        [pltpu.VMEM((3 * mid, (depth + 2) * rows_in * width), BF)],
        flops=1_500_000_000,
    )
    hidden, slope, wide, *second = call(
        functools.partial(outer_kernel, direct),
        [
            shape((depth + 2, mid, cells + 2 * width), BF),
            shape((depth + 2, mid, rows_out * width), F32),
            shape((3 * depth, inner, cells + 4 * width), BF),
        ]
        + (
            [shape((parts, halves, length_second, width), F32)] * 2
            if direct
            else [shape((14, out, LANES), F32)]
        ),
        [deep, one, two, w1, moved, inner_hidden, inner_second],
        flops=1_000_000_000,
    )
    first = call(
        functools.partial(delta_kernel, direct),
        [shape((parts, halves, length_first, width), F32)] * 2 if direct else [shape((7, mid, LANES), F32)],
        [wide, back, slope, inner_first],
        [pltpu.VMEM((3 * mid, (depth + 2) * rows_out * width), BF)],
        flops=4_000_000_000,
    )
    if direct:
        moves = [(1, 0), (0, 1), (1, 1)]
    else:
        moves = [(0, 1)]
        blocks = jnp.swapaxes(second[0].reshape(14, parts, 2, size, LANES), 0, 1)
        tail = jnp.concatenate([blocks[:, 13, half, :, :mid] for half in range(2)], axis=-1)
        units = jnp.concatenate([blocks[:, :13].reshape(parts, 26, size, LANES), tail[:, None]], axis=1)
        second = scattered(units, length_second)
        first = scattered(jnp.swapaxes(first[0].reshape(7, parts, size, LANES), 0, 1), length_first)
    block = (length_second + length_first, width)
    kept, *sends = call(
        functools.partial(plane_kernel, moves),
        [shape(block, F32)] + [shape(block, BF)] * len(moves),
        [x for keep, send in (second, first) for x in (keep, across(send, ("core", 1)))],
    )
    gots = [across(send, ("dp", x), ("y", y)) for send, (x, y) in zip(sends, moves, strict=True)]
    (share,) = call(total_kernel, [shape(block, BF)], [kept, *gots])
    features, token = call(
        features_kernel,
        [shape(cotangent.shape[1:], BF), shape((8, width), F32)],
        [hidden, k2],
        [pltpu.VMEM((out * rows, width), F32)],
        flops=900_000_000,
    )
    gots = [across(share, ("dep", bits)) for bits in (1, 2, 3)]
    (share,) = call(depth_kernel, [shape(block, BF)], [share, *gots, token])
    (own,) = call(order_kernel, [shape((halves, *block), BF)], [share, across(share, ("y", 1))])
    grad_first, grad_second = call(
        functools.partial(unpack_kernel, length_second),
        [shape((27, size, inner), F32), shape((27, 2 * size, mid), F32)],
        [own, across(own, ("core", 1))],
    )
    return features[None], grad_first, grad_second


def solution(mesh):
    dp, dep, hgt = (mesh.shape[axis] for axis in ("dp", "dep", "hgt"))
    split = jax.sharding.Mesh(mesh.devices.reshape(dp, dep, hgt // 2, 2), ("dp", "dep", *HGT))
    block = P("dp", None, "dep", HGT, None)
    return jax.shard_map(
        per_device,
        mesh=split,
        in_specs=(block, P(), P(), block),
        out_specs=(block, P(None, "dp", None), P(None, "dp", None)),
        check_vma=False,
    )
```

```python
import functools

import jax
import jax.numpy as jnp
from jax import lax
from jax.experimental import pallas as pl
from jax.experimental.pallas import tpu as pltpu
from jax.sharding import PartitionSpec as P

BF, F32 = jnp.bfloat16, jnp.float32
LANES = 128
HGT = ("y", "core")
VMEM_BYTES = 28 * 2**20


def call(body, outs, args, scratch=(), flops=0, far=(), far_outs=False, aliases=None):
    moved = sum(x.size * x.dtype.itemsize for x in (*outs, *args))
    return pl.pallas_call(
        body,
        out_shape=outs,
        in_specs=[pl.BlockSpec(memory_space=pl.ANY if n in far else pltpu.VMEM) for n in range(len(args))],
        out_specs=[pl.BlockSpec(memory_space=pl.ANY if far_outs else pltpu.VMEM)] * len(outs),
        scratch_shapes=list(scratch),
        input_output_aliases=aliases or {},
        compiler_params=pltpu.CompilerParams(vmem_limit_bytes=VMEM_BYTES),
        cost_estimate=pl.CostEstimate(flops=flops, bytes_accessed=moved, transcendentals=0),
    )(*args)


def shape(dims, dtype):
    return jax.ShapeDtypeStruct(dims, dtype)


def moved_along_width(x, c):
    if c == 0:
        return x
    pieces = []
    for start in range(0, x.shape[1], LANES):
        piece = x[:, start : start + LANES]
        lane = lax.broadcasted_iota(jnp.int32, piece.shape, 1)
        rolled = pltpu.roll(piece, c % LANES, 1)
        pieces.append(jnp.where(lane == (0 if c == 1 else LANES - 1), 0.0, rolled))
    return pieces[0] if len(pieces) == 1 else jnp.concatenate(pieces, axis=1)


def by_rows(ref, scratch, store):
    channels, depth, height, width = ref.shape
    rows = depth * height
    scratch[...] = ref[...].astype(F32).reshape(channels * rows, width)
    for d in range(depth):
        for h in range(height):
            store(d, h, scratch[pl.ds(d * height + h, channels, stride=rows), :])


def odd(axis):
    return lax.rem(lax.axis_index(axis), 2) == 1


def blank_kernel(out_ref):
    out_ref[...] = jnp.zeros(out_ref.shape, BF)


def spread_kernel(cot_ref, k2_ref, blank_ref, cot_rows_ref, back_ref, scratch):
    out, depth, height, _ = cot_ref.shape
    rows = [[None] * height for _ in range(depth)]

    def store(d, h, row):
        rows[d][h] = row.astype(BF)
        cot_rows_ref[d, :, h * LANES : (h + 1) * LANES] = rows[d][h]

    by_rows(cot_ref, scratch, store)
    mid = k2_ref.shape[1]
    none = blank_ref[...]
    padded = [jnp.concatenate([none, *rows[d], none], axis=1) for d in range(depth)]
    for e in range(depth + 2):
        reached = [(d, e - 1 - d) for d in range(depth) if abs(e - 1 - d) <= 1]
        w = jnp.concatenate(
            [
                k2_ref[9 * (a + 1) + 3 * b : 9 * (a + 1) + 3 * b + 3].reshape(3 * mid, out)
                for _, a in reached
                for b in range(3)
            ],
            axis=1,
        )
        for j in range(0, height + 2, 2):
            rhs = jnp.concatenate(
                [padded[d][:, (j + 2 - b) * LANES : (j + 4 - b) * LANES] for d, _ in reached for b in range(3)], axis=0
            )
            y = jnp.dot(w, rhs, preferred_element_type=F32)
            back = sum(moved_along_width(y[n * mid : (n + 1) * mid], n - 1) for n in range(3))
            back_ref[e, :, j * LANES : (j + 2) * LANES] = back


def as_matrix(ref, c):
    stacked = jnp.concatenate([ref[3 * ab + c] for ab in range(9)], axis=0)
    return stacked.astype(F32).T.astype(BF)


def arrange_kernel(cot_rows_ref, k1_ref, moved_ref, w1_ref):
    depth, out, cells = cot_rows_ref.shape
    for d in range(depth):
        for h in range(0, cells, LANES):
            row = cot_rows_ref[d, :, h : h + LANES]
            for n, c in enumerate((-1, 0, 1)):
                value = row if c == 0 else moved_along_width(row.astype(F32), c).astype(BF)
                moved_ref[d, n * out : (n + 1) * out, h : h + LANES] = value
    mid = k1_ref.shape[2]
    for c in range(3):
        w1_ref[c * mid : (c + 1) * mid, :] = as_matrix(k1_ref, c)


def sides(axis, one, two):
    me, size = lax.axis_index(axis), lax.axis_size(axis)
    is_odd = odd(axis)
    none = jnp.zeros_like(one)
    before = jnp.where(me == 0, none, jnp.where(is_odd, one, two))
    after = jnp.where(me == size - 1, none, jnp.where(is_odd, two, one))
    return before, after


def rim_kernel(own_ref, one_ref, two_ref, _, deep_ref, send_one_ref, send_two_ref, scratch):
    depth = own_ref.shape[1]
    before, after = sides("dep", one_ref[...], two_ref[...])
    for n, part in enumerate((before, own_ref[...], after)):

        def store(d, h, row, at=n * depth):
            deep_ref[at + d, :, h * LANES : (h + 1) * LANES] = row.astype(BF)

        by_rows(part, scratch, store)
    n, cells = send_one_ref.shape[2], deep_ref.shape[2]
    first, last = deep_ref[:, :, :n], deep_ref[:, :, cells - n :]
    is_odd = odd(HGT)
    send_one_ref[...] = jnp.where(is_odd, first, last)
    send_two_ref[...] = jnp.where(is_odd, last, first)


def widened(deep_ref, one_ref, two_ref):
    left, right = sides(HGT, one_ref[...], two_ref[...])
    return [jnp.concatenate([left[d], deep_ref[d], right[d]], axis=1) for d in range(deep_ref.shape[0])]


def pack(direct, refs, rows_of, blocks):
    if not direct:
        for j, block in enumerate(blocks):
            refs[0][j] = block
        return
    keep_ref, send_ref = refs
    parts, halves, length, _ = keep_ref.shape
    core = lax.axis_index("core") == 1
    for part in range(parts):
        one, two = (jnp.concatenate(rows_of(part, c), axis=0) for c in range(2))
        for half in range(halves):
            at = slice(half * length, (half + 1) * length)
            keep_ref[part, half] = jnp.where(core, two[at], one[at])
            send_ref[part, half] = jnp.where(core, one[at], two[at])


def folded(tail):
    half = tail.shape[0] // 2
    return jnp.concatenate([tail[:half], tail[half:]], axis=1)


def activated(w1, rhs, d, depth, heights):
    mid = w1.shape[0] // 3
    y = jnp.dot(w1, rhs, preferred_element_type=F32)
    pre = sum(moved_along_width(y[n * mid : (n + 1) * mid], 1 - n) for n in range(3))
    s = 1.0 / (1.0 + jnp.exp(-pre))
    dep, deps = lax.axis_index("dep"), lax.axis_size("dep")
    hgt, hgts = lax.axis_index(HGT), lax.axis_size(HGT)
    results = []
    for n, side in enumerate(heights):
        p, q = (x[:, n * LANES : (n + 1) * LANES] for x in (pre, s))
        value, slope = (p * q).astype(BF), q * (1.0 + p * (1.0 - q))
        outside = []
        if d == 0:
            outside.append(dep == 0)
        if d == depth - 1:
            outside.append(dep == deps - 1)
        if side < 0:
            outside.append(hgt == 0)
        if side > 0:
            outside.append(hgt == hgts - 1)
        for far in outside:
            value = jnp.where(far, jnp.zeros_like(value), value)
            slope = jnp.where(far, jnp.zeros_like(slope), slope)
        results.append((value, slope))
    return results


def neighbours(ref, d, starts, count):
    return jnp.concatenate(
        [
            jnp.concatenate(
                [ref[d + a, :, (start + b) * LANES : (start + b + count) * LANES] for start in starts], axis=1
            )
            for a in range(3)
            for b in range(3)
        ],
        axis=0,
    )


def products(left, right):
    return lax.dot_general(left, right, (((1,), (1,)), ((), ())), preferred_element_type=F32)


def shares(delta, n_channels, ref, at):
    for n in range(3):
        ref[n * n_channels : (n + 1) * n_channels, at : at + LANES] = moved_along_width(delta, n - 1).astype(BF)


def inner_kernel(deep_ref, w1_ref, moved_ref, back_ref, hidden_ref, second_ref, first_ref, delta_ref):
    w1 = w1_ref[...]
    depth, mid, cells = hidden_ref.shape
    height = cells // LANES
    for d in range(depth):
        for h in range(0, height, 2):
            results = activated(w1, neighbours(deep_ref, d, [h], 2), d, depth, (0, 0))
            for n, (value, slope) in enumerate(results):
                at = (h + n) * LANES
                hidden_ref[d, :, at : at + LANES] = value
                back = back_ref[d, :, at + 2 * LANES : at + 3 * LANES]
                shares(back * slope, mid, delta_ref, d * cells + at)
    own = depth - 2
    left = jnp.concatenate(
        [
            jnp.concatenate([moved_ref[d, :, (2 - b) * LANES : (2 - b) * LANES + cells] for d in range(own)], axis=1)
            for b in range(3)
        ],
        axis=0,
    )
    right = jnp.concatenate(
        [jnp.concatenate([hidden_ref[d + a] for a in range(3)], axis=0) for d in range(own)], axis=1
    )
    second_ref[...] = products(left, right)
    right = jnp.concatenate([neighbours(deep_ref, d, [0], height) for d in range(depth)], axis=1)
    first_ref[...] = products(delta_ref[...], right)


def outer_kernel(
    direct, deep_ref, one_ref, two_ref, w1_ref, moved_ref, inner_ref, second_ref,
    hidden_ref, slope_ref, rows_ref, *grad_refs,
):
    for d, row in enumerate(widened(deep_ref, one_ref, two_ref)):
        rows_ref[d] = row
    w1 = w1_ref[...]
    depth, mid, cells = hidden_ref.shape
    height = cells // LANES
    for d in range(depth):
        hidden_ref[d, :, 2 * LANES : cells - 2 * LANES] = inner_ref[d]
        for h, sides_of in ((0, (-1, 0)), (height - 2, (0, 1))):
            results = activated(w1, neighbours(rows_ref, d, [h], 2), d, depth, sides_of)
            for n, (value, slope) in enumerate(results):
                hidden_ref[d, :, (h + n) * LANES : (h + n + 1) * LANES] = value
                at = ((2 if h else 0) + n) * LANES
                slope_ref[d, :, at : at + LANES] = slope
    own = depth - 2
    out = moved_ref.shape[1] // 3
    heads, tails = [], []
    for b in range(3):
        far = [h for h in range(height - 2) if not 2 <= h + b <= height - 3]
        left = jnp.concatenate(
            [moved_ref[d, :, h * LANES : (h + 1) * LANES] for d in range(own) for h in far], axis=1
        )
        right = jnp.concatenate(
            [
                jnp.concatenate([hidden_ref[d + a, :, (h + b) * LANES : (h + b + 1) * LANES] for a in range(3)], axis=0)
                for d in range(own)
                for h in far
            ],
            axis=1,
        )
        total = second_ref[3 * b * out : 3 * (b + 1) * out, :] + products(left, right)
        for c in range(3):
            part = total[c * out : (c + 1) * out]
            heads.append(part[:, :LANES])
            tails.append(part[:, LANES:])
    blocks = heads + [jnp.concatenate(tails[n : n + 2], axis=1) for n in range(0, 8, 2)]
    size = mid // lax.axis_size("dp")

    def rows_of(part, core):
        at = slice((2 * part + core) * size, (2 * part + core + 1) * size)
        return [block[at] for block in blocks] + [folded(tails[8][at])]

    pack(direct, grad_refs, rows_of, [*blocks, jnp.concatenate([tails[8], jnp.zeros_like(tails[8])], axis=1)])


def features_kernel(hidden_ref, k2_ref, out_ref, token_ref, scratch):
    out, depth, height, _ = out_ref.shape
    w2 = jnp.concatenate([as_matrix(k2_ref, c) for c in range(3)], axis=0)
    for d in range(depth):
        for h in range(0, height, 2):
            rhs = jnp.concatenate(
                [
                    hidden_ref[d + a, :, (h + b) * LANES : (h + b + 2) * LANES]
                    for a in range(3)
                    for b in range(3)
                ],
                axis=0,
            )
            y = jnp.dot(w2, rhs, preferred_element_type=F32)
            total = sum(moved_along_width(y[n * out : (n + 1) * out], 1 - n) for n in range(3))
            for r in range(2):
                row = total[:, r * LANES : (r + 1) * LANES]
                scratch[pl.ds(d * height + h + r, out, stride=depth * height), :] = row
    out_ref[...] = scratch[...].reshape(out_ref.shape).astype(BF)
    token_ref[...] = scratch[:8]


def delta_kernel(direct, rows_ref, back_ref, slope_ref, first_ref, *outs_and_scratch):
    *grad_refs, delta_ref = outs_and_scratch
    depth, mid, cells = slope_ref.shape
    last = back_ref.shape[2] // LANES - 2
    for d in range(depth):
        for n, h in enumerate((0, 1, last, last + 1)):
            delta = back_ref[d, :, h * LANES : (h + 1) * LANES] * slope_ref[d, :, n * LANES : (n + 1) * LANES]
            shares(delta, mid, delta_ref, d * cells + n * LANES)
    right = jnp.concatenate([neighbours(rows_ref, d, [0, last], 2) for d in range(depth)], axis=1)
    total = first_ref[...] + products(delta_ref[...], right)
    inner = rows_ref.shape[1]
    blocks, tails = [], []
    for n in range(3):
        part = total[n * mid : (n + 1) * mid]
        blocks += [part[:, m * LANES : (m + 1) * LANES] for m in range(2)]
        tails.append(part[:, 2 * LANES :])
    tails.append(jnp.zeros((mid, LANES - 3 * inner), F32))
    blocks.append(jnp.concatenate(tails, axis=1))
    size = mid // lax.axis_size("dp")
    half = size // 2

    def rows_of(part, core):
        return [block[part * size + core * half : part * size + (core + 1) * half] for block in blocks]

    pack(direct, grad_refs, rows_of, blocks)


def plane_kernel(moves, *refs):
    keep_second, got_second, keep_first, got_first, kept_ref, *send_refs = refs
    part = lax.rem(lax.axis_index("dp"), keep_first.shape[0])
    half = lax.axis_index("y")

    def total(x, y):
        at = 1 - part if x else part, 1 - half if y else half
        return jnp.concatenate([keep_second[at] + got_second[at], keep_first[at] + got_first[at]], axis=0)

    kept_ref[...] = total(0, 0)
    for (x, y), send_ref in zip(moves, send_refs, strict=True):
        send_ref[...] = total(x, y).astype(BF)


def total_kernel(kept_ref, *refs):
    *got_refs, out_ref = refs
    value = kept_ref[...]
    for ref in got_refs:
        value = value + ref[...].astype(F32)
    out_ref[...] = value.astype(BF)


def depth_kernel(a_ref, b_ref, c_ref, d_ref, _, out_ref):
    one = a_ref[...].astype(F32) + b_ref[...].astype(F32)
    two = c_ref[...].astype(F32) + d_ref[...].astype(F32)
    out_ref[...] = (one + two).astype(BF)


def order_kernel(own_ref, got_ref, out_ref):
    mine = lax.axis_index("y")
    out_ref[mine] = own_ref[...]
    out_ref[1 - mine] = got_ref[...]


def unpack_kernel(length, theirs, in_ref, *refs):
    first_ref, second_ref, first, second, sems = refs[-5:]
    core = lax.axis_index("core")
    at = 1 - core if theirs else core
    _, size, mid = second.shape
    whole = [in_ref[n].astype(F32) for n in range(in_ref.shape[0])]
    rows = jnp.concatenate([x[:length] for x in whole], axis=0)
    for j in range(13):
        value = rows[j * size : (j + 1) * size]
        for m, k in enumerate((j, 9 + j) if j < 9 else (2 * j, 2 * j + 1)):
            second[k] = value[:, m * mid : (m + 1) * mid]
    value = rows[13 * size : 13 * size + size // 2]
    second[26] = jnp.concatenate([value[:, :mid], value[:, mid:]], axis=0)
    copies = [pltpu.make_async_copy(second, second_ref.at[:, pl.ds(pl.multiple_of(at * size, size), size), :], sems.at[1])]
    copies[0].start()
    _, half, inner = first.shape
    rows = jnp.concatenate([x[length:] for x in whole], axis=0)
    for j in range(7):
        value = rows[j * half : (j + 1) * half]
        for m in range(4):
            c, ab = (j // 2, 4 * (j % 2) + m) if j < 6 else (m, 8)
            if c < 3:
                first[3 * ab + c] = value[:, m * inner : (m + 1) * inner]
    copies.append(
        pltpu.make_async_copy(first, first_ref.at[:, pl.ds(pl.multiple_of(at * half, half), half), :], sems.at[0])
    )
    copies[1].start()
    for copy in copies:
        copy.wait()


def swapped(x, axis, first):
    axes = (axis,) if isinstance(axis, str) else axis
    parts, size = lax.axis_size("dp"), lax.axis_size(axis)
    partner = list(range(parts * size))
    for i in partner:
        part, at = divmod(i, size)
        if first <= at < size - (size - first) % 2:
            partner[i] = part * size + (at - first ^ 1) + first
        elif parts % 2 == 0:
            partner[i] = (part ^ 1) * size + at
    return lax.ppermute(x, ("dp", *axes), list(enumerate(partner)))


def across(x, *moves):
    axes = tuple(axis for axis, _ in moves)
    flip = 0
    for axis, bit in moves:
        flip = flip * lax.axis_size(axis) + bit
    return lax.ppermute(x, axes, [(i, i ^ flip) for i in range(lax.axis_size(axes))])


def scattered(rows, length):
    halves = lax.axis_size("y")
    grad = jnp.pad(rows, ((0, 0), (0, 0), (0, halves * length - rows.shape[2]), (0, 0)))
    grad = lax.psum_scatter(grad, "dp", scatter_dimension=0, tiled=True)
    grad = grad.reshape(1, 2, halves, length, LANES)
    core = lax.axis_index("core")
    return tuple(lax.dynamic_index_in_dim(grad, at, 1, False) for at in (core, 1 - core))


def assembled(own, got, length, size, inner, mid):
    core = lax.axis_index("core")
    both = jnp.stack([own, got]).astype(F32)
    both = jnp.stack([lax.dynamic_index_in_dim(both, at, 0, False) for at in (core, 1 - core)])
    rows = both[:, :, :length].reshape(2, -1, LANES)
    second = [None] * 27
    for j in range(13):
        for m, k in enumerate((j, 9 + j) if j < 9 else (2 * j, 2 * j + 1)):
            second[k] = rows[:, j * size : (j + 1) * size, m * mid : (m + 1) * mid].reshape(2 * size, mid)
    tail = rows[:, 13 * size : 13 * size + size // 2]
    second[26] = jnp.concatenate([tail[:, :, :mid], tail[:, :, mid:]], axis=1).reshape(2 * size, mid)
    rows, half = both[:, :, length:].reshape(2, -1, LANES), size // 2
    first = [None] * 27
    for j in range(7):
        for m in range(4):
            c, ab = (j // 2, 4 * (j % 2) + m) if j < 6 else (m, 8)
            if c < 3:
                value = rows[:, j * half : (j + 1) * half, m * inner : (m + 1) * inner]
                first[3 * ab + c] = value.reshape(size, inner)
    return jnp.stack(first), jnp.stack(second)


def per_device(volume, kernel_first, kernel_second, cotangent):
    _, inner, depth, height, width = volume.shape
    mid, out = kernel_first.shape[1], kernel_second.shape[1]
    cells = height * width
    parts = lax.axis_size("dp")
    k1, k2 = jnp.swapaxes(kernel_first, 1, 2), jnp.swapaxes(kernel_second, 1, 2)
    rows = depth * height

    one, two = swapped(volume[0], "dep", 0), swapped(volume[0], "dep", 1)
    (blank,) = call(blank_kernel, [shape((out, 2 * width), BF)], [], flops=3_000_000_000)
    cot_rows, back = call(
        spread_kernel,
        [
            shape((depth, out, cells), BF),
            shape((depth + 2, mid, cells + 2 * width), F32),
        ],
        [cotangent[0], k2, blank],
        [pltpu.VMEM((out * rows, width), F32)],
        flops=1_100_000_000,
    )
    moved, w1 = call(
        arrange_kernel,
        [shape((depth, 3 * out, cells), BF), shape((3 * mid, 9 * inner), BF)],
        [cot_rows, k1],
        flops=500_000_000,
    )
    deep, one, two = call(
        rim_kernel,
        [shape((3 * depth, inner, cells), BF)] + [shape((3 * depth, inner, 2 * width), BF)] * 2,
        [volume[0], one, two, w1],
        [pltpu.VMEM((inner * rows, width), F32)],
    )
    one, two = swapped(one, HGT, 0), swapped(two, HGT, 1)
    size = mid // parts
    direct = parts == 2 and size % 16 == 0
    halves = lax.axis_size("y")
    length_second, length_first = (-(-units * size // (16 * halves)) * 8 for units in (27, 7))
    rows_in, rows_out = height - 2, 4
    inner_hidden, inner_second, inner_first = call(
        inner_kernel,
        [
            shape((depth + 2, mid, rows_in * width), BF),
            shape((9 * out, 3 * mid), F32),
            shape((3 * mid, 9 * inner), F32),
        ],
        [deep, w1, moved, back],
        [pltpu.VMEM((3 * mid, (depth + 2) * rows_in * width), BF)],
        flops=1_500_000_000,
    )
    hidden, slope, wide, *second = call(
        functools.partial(outer_kernel, direct),
        [
            shape((depth + 2, mid, cells + 2 * width), BF),
            shape((depth + 2, mid, rows_out * width), F32),
            shape((3 * depth, inner, cells + 4 * width), BF),
        ]
        + (
            [shape((parts, halves, length_second, width), F32)] * 2
            if direct
            else [shape((14, out, LANES), F32)]
        ),
        [deep, one, two, w1, moved, inner_hidden, inner_second],
        flops=1_000_000_000,
    )
    first = call(
        functools.partial(delta_kernel, direct),
        [shape((parts, halves, length_first, width), F32)] * 2 if direct else [shape((7, mid, LANES), F32)],
        [wide, back, slope, inner_first],
        [pltpu.VMEM((3 * mid, (depth + 2) * rows_out * width), BF)],
        flops=4_000_000_000,
    )
    if direct:
        moves = [(1, 1), (0, 1), (1, 0)]
    else:
        moves = [(0, 1)]
        blocks = second[0].reshape(14, parts, 2, size, LANES).transpose(1, 2, 0, 3, 4)
        tail = blocks[:, :, 13, :, :mid]
        tail = jnp.concatenate([tail[:, :, : size // 2], tail[:, :, size // 2 :]], axis=-1)
        rows_second = jnp.concatenate([blocks[:, :, :13].reshape(parts, 2, 13 * size, LANES), tail], axis=2)
        second = scattered(rows_second, length_second)
        blocks = first[0].reshape(7, parts, 2, size // 2, LANES).transpose(1, 2, 0, 3, 4)
        first = scattered(blocks.reshape(parts, 2, 7 * (size // 2), LANES), length_first)
    block = (length_second + length_first, width)
    kept, *sends = call(
        functools.partial(plane_kernel, moves),
        [shape(block, F32)] + [shape(block, BF)] * len(moves),
        [x for keep, send in (second, first) for x in (keep, across(send, ("core", 1)))],
    )
    gots = [across(send, ("dp", x), ("y", y)) for send, (x, y) in zip(sends, moves, strict=True)]
    (share,) = call(total_kernel, [shape(block, BF)], [kept, *gots])
    features, token = call(
        features_kernel,
        [shape(cotangent.shape[1:], BF), shape((8, width), F32)],
        [hidden, k2],
        [pltpu.VMEM((out * rows, width), F32)],
        flops=900_000_000,
    )
    gots = [across(share, ("dep", bits)) for bits in (1, 2, 3)]
    (share,) = call(depth_kernel, [shape(block, BF)], [share, *gots, token])
    (own,) = call(order_kernel, [shape((halves, *block), BF)], [share, across(share, ("y", 1))])
    got = across(own, ("core", 1))
    if size % 16 == 0:
        grads = [shape((27, size, inner), F32), shape((27, 2 * size, mid), F32)]
        scratch = [
            pltpu.VMEM((27, size // 2, inner), F32),
            pltpu.VMEM((27, size, mid), F32),
            pltpu.SemaphoreType.DMA((2,)),
        ]
        written = call(functools.partial(unpack_kernel, length_second, False), grads, [own], scratch, far_outs=True)
        grad_first, grad_second = call(
            functools.partial(unpack_kernel, length_second, True),
            grads,
            [got, *written],
            scratch,
            far=(1, 2),
            far_outs=True,
            aliases={1: 0, 2: 1},
        )
    else:
        grad_first, grad_second = assembled(own, got, length_second, size, inner, mid)
    return features[None], grad_first, grad_second


def solution(mesh):
    dp, dep, hgt = (mesh.shape[axis] for axis in ("dp", "dep", "hgt"))
    split = jax.sharding.Mesh(mesh.devices.reshape(dp, dep, hgt // 2, 2), ("dp", "dep", *HGT))
    block = P("dp", None, "dep", HGT, None)
    return jax.shard_map(
        per_device,
        mesh=split,
        in_specs=(block, P(), P(), block),
        out_specs=(block, P(None, "dp", None), P(None, "dp", None)),
        check_vma=False,
    )
```

```python
import functools

import jax
import jax.numpy as jnp
from jax import lax
from jax.experimental import pallas as pl
from jax.experimental.pallas import tpu as pltpu
from jax.sharding import PartitionSpec as P

BF, F32 = jnp.bfloat16, jnp.float32
LANES = 128
HGT = ("y", "core")
VMEM_BYTES = 28 * 2**20


def call(body, outs, args, scratch=(), flops=0, far=(), far_outs=False, aliases=None):
    moved = sum(x.size * x.dtype.itemsize for x in (*outs, *args))
    return pl.pallas_call(
        body,
        out_shape=outs,
        in_specs=[pl.BlockSpec(memory_space=pl.ANY if n in far else pltpu.VMEM) for n in range(len(args))],
        out_specs=[pl.BlockSpec(memory_space=pl.ANY if far_outs else pltpu.VMEM)] * len(outs),
        scratch_shapes=list(scratch),
        input_output_aliases=aliases or {},
        compiler_params=pltpu.CompilerParams(vmem_limit_bytes=VMEM_BYTES),
        cost_estimate=pl.CostEstimate(flops=flops, bytes_accessed=moved, transcendentals=0),
    )(*args)


def shape(dims, dtype):
    return jax.ShapeDtypeStruct(dims, dtype)


def moved_along_width(x, c):
    if c == 0:
        return x
    pieces = []
    for start in range(0, x.shape[1], LANES):
        piece = x[:, start : start + LANES]
        lane = lax.broadcasted_iota(jnp.int32, piece.shape, 1)
        rolled = pltpu.roll(piece, c % LANES, 1)
        pieces.append(jnp.where(lane == (0 if c == 1 else LANES - 1), 0.0, rolled))
    return pieces[0] if len(pieces) == 1 else jnp.concatenate(pieces, axis=1)


def by_rows(ref, scratch, store):
    channels, depth, height, width = ref.shape
    rows = depth * height
    scratch[...] = ref[...].astype(F32).reshape(channels * rows, width)
    for d in range(depth):
        for h in range(height):
            store(d, h, scratch[pl.ds(d * height + h, channels, stride=rows), :])


def odd(axis):
    return lax.rem(lax.axis_index(axis), 2) == 1


def blank_kernel(out_ref):
    out_ref[...] = jnp.zeros(out_ref.shape, BF)


def spread_kernel(cot_ref, k2_ref, blank_ref, cot_rows_ref, back_ref, scratch):
    out, depth, height, _ = cot_ref.shape
    rows = [[None] * height for _ in range(depth)]

    def store(d, h, row):
        rows[d][h] = row.astype(BF)
        cot_rows_ref[d, :, h * LANES : (h + 1) * LANES] = rows[d][h]

    by_rows(cot_ref, scratch, store)
    mid = k2_ref.shape[1]
    none = blank_ref[...]
    padded = [jnp.concatenate([none, *rows[d], none], axis=1) for d in range(depth)]
    for e in range(depth + 2):
        reached = [(d, e - 1 - d) for d in range(depth) if abs(e - 1 - d) <= 1]
        w = jnp.concatenate(
            [
                k2_ref[9 * (a + 1) + 3 * b : 9 * (a + 1) + 3 * b + 3].reshape(3 * mid, out)
                for _, a in reached
                for b in range(3)
            ],
            axis=1,
        )
        for j in range(0, height + 2, 2):
            rhs = jnp.concatenate(
                [padded[d][:, (j + 2 - b) * LANES : (j + 4 - b) * LANES] for d, _ in reached for b in range(3)], axis=0
            )
            y = jnp.dot(w, rhs, preferred_element_type=F32)
            back = sum(moved_along_width(y[n * mid : (n + 1) * mid], n - 1) for n in range(3))
            back_ref[e, :, j * LANES : (j + 2) * LANES] = back


def as_matrix(ref, c):
    stacked = jnp.concatenate([ref[3 * ab + c] for ab in range(9)], axis=0)
    return stacked.astype(F32).T.astype(BF)


def arrange_kernel(cot_rows_ref, k1_ref, moved_ref, w1_ref):
    depth, out, cells = cot_rows_ref.shape
    for d in range(depth):
        for h in range(0, cells, LANES):
            row = cot_rows_ref[d, :, h : h + LANES]
            for n, c in enumerate((-1, 0, 1)):
                value = row if c == 0 else moved_along_width(row.astype(F32), c).astype(BF)
                moved_ref[d, n * out : (n + 1) * out, h : h + LANES] = value
    mid = k1_ref.shape[2]
    for c in range(3):
        w1_ref[c * mid : (c + 1) * mid, :] = as_matrix(k1_ref, c)


def sides(axis, one, two):
    me, size = lax.axis_index(axis), lax.axis_size(axis)
    is_odd = odd(axis)
    none = jnp.zeros_like(one)
    before = jnp.where(me == 0, none, jnp.where(is_odd, one, two))
    after = jnp.where(me == size - 1, none, jnp.where(is_odd, two, one))
    return before, after


def rim_kernel(own_ref, one_ref, two_ref, _, deep_ref, send_one_ref, send_two_ref, scratch):
    depth = own_ref.shape[1]
    before, after = sides("dep", one_ref[...], two_ref[...])
    for n, part in enumerate((before, own_ref[...], after)):

        def store(d, h, row, at=n * depth):
            deep_ref[at + d, :, h * LANES : (h + 1) * LANES] = row.astype(BF)

        by_rows(part, scratch, store)
    n, cells = send_one_ref.shape[2], deep_ref.shape[2]
    first, last = deep_ref[:, :, :n], deep_ref[:, :, cells - n :]
    is_odd = odd(HGT)
    send_one_ref[...] = jnp.where(is_odd, first, last)
    send_two_ref[...] = jnp.where(is_odd, last, first)


def widened(deep_ref, one_ref, two_ref):
    left, right = sides(HGT, one_ref[...], two_ref[...])
    return [jnp.concatenate([left[d], deep_ref[d], right[d]], axis=1) for d in range(deep_ref.shape[0])]


def pack(direct, refs, rows_of, blocks):
    if not direct:
        for j, block in enumerate(blocks):
            refs[0][j] = block
        return
    keep_ref, send_ref = refs
    parts, halves, length, _ = keep_ref.shape
    core = lax.axis_index("core") == 1
    for part in range(parts):
        one, two = (jnp.concatenate(rows_of(part, c), axis=0) for c in range(2))
        for half in range(halves):
            at = slice(half * length, (half + 1) * length)
            keep_ref[part, half] = jnp.where(core, two[at], one[at])
            send_ref[part, half] = jnp.where(core, one[at], two[at])


def folded(tail):
    half = tail.shape[0] // 2
    return jnp.concatenate([tail[:half], tail[half:]], axis=1)


def activated(w1, rhs, d, depth, heights):
    mid = w1.shape[0] // 3
    y = jnp.dot(w1, rhs, preferred_element_type=F32)
    pre = sum(moved_along_width(y[n * mid : (n + 1) * mid], 1 - n) for n in range(3))
    s = 1.0 / (1.0 + jnp.exp(-pre))
    dep, deps = lax.axis_index("dep"), lax.axis_size("dep")
    hgt, hgts = lax.axis_index(HGT), lax.axis_size(HGT)
    results = []
    for n, side in enumerate(heights):
        p, q = (x[:, n * LANES : (n + 1) * LANES] for x in (pre, s))
        value, slope = (p * q).astype(BF), q * (1.0 + p * (1.0 - q))
        outside = []
        if d == 0:
            outside.append(dep == 0)
        if d == depth - 1:
            outside.append(dep == deps - 1)
        if side < 0:
            outside.append(hgt == 0)
        if side > 0:
            outside.append(hgt == hgts - 1)
        for far in outside:
            value = jnp.where(far, jnp.zeros_like(value), value)
            slope = jnp.where(far, jnp.zeros_like(slope), slope)
        results.append((value, slope))
    return results


def neighbours(ref, d, starts, count):
    return jnp.concatenate(
        [
            jnp.concatenate(
                [ref[d + a, :, (start + b) * LANES : (start + b + count) * LANES] for start in starts], axis=1
            )
            for a in range(3)
            for b in range(3)
        ],
        axis=0,
    )


def products(left, right):
    return lax.dot_general(left, right, (((1,), (1,)), ((), ())), preferred_element_type=F32)


def shares(delta, n_channels, ref, at):
    for n in range(3):
        ref[n * n_channels : (n + 1) * n_channels, at : at + LANES] = moved_along_width(delta, n - 1).astype(BF)


def inner_kernel(deep_ref, w1_ref, moved_ref, back_ref, hidden_ref, second_ref, first_ref, delta_ref):
    w1 = w1_ref[...]
    depth, mid, cells = hidden_ref.shape
    height = cells // LANES
    for d in range(depth):
        for h in range(0, height, 2):
            results = activated(w1, neighbours(deep_ref, d, [h], 2), d, depth, (0, 0))
            for n, (value, slope) in enumerate(results):
                at = (h + n) * LANES
                hidden_ref[d, :, at : at + LANES] = value
                back = back_ref[d, :, at + 2 * LANES : at + 3 * LANES]
                shares(back * slope, mid, delta_ref, d * cells + at)
    own = depth - 2
    left = jnp.concatenate(
        [
            jnp.concatenate([moved_ref[d, :, (2 - b) * LANES : (2 - b) * LANES + cells] for d in range(own)], axis=1)
            for b in range(3)
        ],
        axis=0,
    )
    right = jnp.concatenate(
        [jnp.concatenate([hidden_ref[d + a] for a in range(3)], axis=0) for d in range(own)], axis=1
    )
    second_ref[...] = products(left, right)
    right = jnp.concatenate([neighbours(deep_ref, d, [0], height) for d in range(depth)], axis=1)
    first_ref[...] = products(delta_ref[...], right)


def outer_kernel(
    direct, deep_ref, two_ref, one_ref, w1_ref, moved_ref, inner_ref, second_ref,
    hidden_ref, slope_ref, rows_ref, *grad_refs,
):
    for d, row in enumerate(widened(deep_ref, one_ref, two_ref)):
        rows_ref[d] = row
    w1 = w1_ref[...]
    depth, mid, cells = hidden_ref.shape
    height = cells // LANES
    for d in range(depth):
        hidden_ref[d, :, 2 * LANES : cells - 2 * LANES] = inner_ref[d]
        for h, sides_of in ((0, (-1, 0)), (height - 2, (0, 1))):
            results = activated(w1, neighbours(rows_ref, d, [h], 2), d, depth, sides_of)
            for n, (value, slope) in enumerate(results):
                hidden_ref[d, :, (h + n) * LANES : (h + n + 1) * LANES] = value
                at = ((2 if h else 0) + n) * LANES
                slope_ref[d, :, at : at + LANES] = slope
    own = depth - 2
    out = moved_ref.shape[1] // 3
    heads, tails = [], []
    for b in range(3):
        far = [h for h in range(height - 2) if not 2 <= h + b <= height - 3]
        left = jnp.concatenate(
            [moved_ref[d, :, h * LANES : (h + 1) * LANES] for d in range(own) for h in far], axis=1
        )
        right = jnp.concatenate(
            [
                jnp.concatenate([hidden_ref[d + a, :, (h + b) * LANES : (h + b + 1) * LANES] for a in range(3)], axis=0)
                for d in range(own)
                for h in far
            ],
            axis=1,
        )
        total = second_ref[3 * b * out : 3 * (b + 1) * out, :] + products(left, right)
        for c in range(3):
            part = total[c * out : (c + 1) * out]
            heads.append(part[:, :LANES])
            tails.append(part[:, LANES:])
    blocks = heads + [jnp.concatenate(tails[n : n + 2], axis=1) for n in range(0, 8, 2)]
    size = mid // lax.axis_size("dp")

    def rows_of(part, core):
        at = slice((2 * part + core) * size, (2 * part + core + 1) * size)
        return [block[at] for block in blocks] + [folded(tails[8][at])]

    pack(direct, grad_refs, rows_of, [*blocks, jnp.concatenate([tails[8], jnp.zeros_like(tails[8])], axis=1)])


def features_kernel(hidden_ref, k2_ref, out_ref, token_ref, scratch):
    out, depth, height, _ = out_ref.shape
    w2 = jnp.concatenate([as_matrix(k2_ref, c) for c in range(3)], axis=0)
    for d in range(depth):
        for h in range(0, height, 2):
            rhs = jnp.concatenate(
                [
                    hidden_ref[d + a, :, (h + b) * LANES : (h + b + 2) * LANES]
                    for a in range(3)
                    for b in range(3)
                ],
                axis=0,
            )
            y = jnp.dot(w2, rhs, preferred_element_type=F32)
            total = sum(moved_along_width(y[n * out : (n + 1) * out], 1 - n) for n in range(3))
            for r in range(2):
                row = total[:, r * LANES : (r + 1) * LANES]
                scratch[pl.ds(d * height + h + r, out, stride=depth * height), :] = row
    out_ref[...] = scratch[...].reshape(out_ref.shape).astype(BF)
    token_ref[...] = scratch[:8]


def delta_kernel(direct, rows_ref, back_ref, slope_ref, first_ref, *outs_and_scratch):
    *grad_refs, delta_ref = outs_and_scratch
    depth, mid, cells = slope_ref.shape
    last = back_ref.shape[2] // LANES - 2
    for d in range(depth):
        for n, h in enumerate((0, 1, last, last + 1)):
            delta = back_ref[d, :, h * LANES : (h + 1) * LANES] * slope_ref[d, :, n * LANES : (n + 1) * LANES]
            shares(delta, mid, delta_ref, d * cells + n * LANES)
    right = jnp.concatenate([neighbours(rows_ref, d, [0, last], 2) for d in range(depth)], axis=1)
    total = first_ref[...] + products(delta_ref[...], right)
    inner = rows_ref.shape[1]
    blocks, tails = [], []
    for n in range(3):
        part = total[n * mid : (n + 1) * mid]
        blocks += [part[:, m * LANES : (m + 1) * LANES] for m in range(2)]
        tails.append(part[:, 2 * LANES :])
    tails.append(jnp.zeros((mid, LANES - 3 * inner), F32))
    blocks.append(jnp.concatenate(tails, axis=1))
    size = mid // lax.axis_size("dp")
    half = size // 2

    def rows_of(part, core):
        return [block[part * size + core * half : part * size + (core + 1) * half] for block in blocks]

    pack(direct, grad_refs, rows_of, blocks)


def plane_kernel(moves, *refs):
    keep_second, got_second, keep_first, got_first, kept_ref, *send_refs = refs
    part = lax.rem(lax.axis_index("dp"), keep_first.shape[0])
    half = lax.axis_index("y")

    def total(x, y):
        at = 1 - part if x else part, 1 - half if y else half
        return jnp.concatenate([keep_second[at] + got_second[at], keep_first[at] + got_first[at]], axis=0)

    kept_ref[...] = total(0, 0)
    for (x, y), send_ref in zip(moves, send_refs, strict=True):
        send_ref[...] = total(x, y).astype(BF)


def total_kernel(kept_ref, *refs):
    *got_refs, out_ref = refs
    value = kept_ref[...]
    for ref in got_refs:
        value = value + ref[...].astype(F32)
    out_ref[...] = value.astype(BF)


def depth_kernel(a_ref, b_ref, c_ref, d_ref, _, out_ref):
    one = a_ref[...].astype(F32) + b_ref[...].astype(F32)
    two = c_ref[...].astype(F32) + d_ref[...].astype(F32)
    out_ref[...] = (one + two).astype(BF)


def order_kernel(own_ref, got_ref, out_ref):
    mine = lax.axis_index("y")
    out_ref[mine] = own_ref[...]
    out_ref[1 - mine] = got_ref[...]


def unpack_kernel(length, theirs, in_ref, *refs):
    first_ref, second_ref, first, second, sems = refs[-5:]
    core = lax.axis_index("core")
    at = 1 - core if theirs else core
    _, size, mid = second.shape
    whole = [in_ref[n].astype(F32) for n in range(in_ref.shape[0])]
    rows = jnp.concatenate([x[:length] for x in whole], axis=0)
    for j in range(13):
        value = rows[j * size : (j + 1) * size]
        for m, k in enumerate((j, 9 + j) if j < 9 else (2 * j, 2 * j + 1)):
            second[k] = value[:, m * mid : (m + 1) * mid]
    value = rows[13 * size : 13 * size + size // 2]
    second[26] = jnp.concatenate([value[:, :mid], value[:, mid:]], axis=0)
    copies = [pltpu.make_async_copy(second, second_ref.at[:, pl.ds(pl.multiple_of(at * size, size), size), :], sems.at[1])]
    copies[0].start()
    _, half, inner = first.shape
    rows = jnp.concatenate([x[length:] for x in whole], axis=0)
    for j in range(7):
        value = rows[j * half : (j + 1) * half]
        for m in range(4):
            c, ab = (j // 2, 4 * (j % 2) + m) if j < 6 else (m, 8)
            if c < 3:
                first[3 * ab + c] = value[:, m * inner : (m + 1) * inner]
    copies.append(
        pltpu.make_async_copy(first, first_ref.at[:, pl.ds(pl.multiple_of(at * half, half), half), :], sems.at[0])
    )
    copies[1].start()
    for copy in copies:
        copy.wait()


def swapped(x, axis, first):
    axes = (axis,) if isinstance(axis, str) else axis
    parts, size = lax.axis_size("dp"), lax.axis_size(axis)
    partner = list(range(parts * size))
    for i in partner:
        part, at = divmod(i, size)
        if first <= at < size - (size - first) % 2:
            partner[i] = part * size + (at - first ^ 1) + first
        elif parts % 2 == 0:
            partner[i] = (part ^ 1) * size + at
    return lax.ppermute(x, ("dp", *axes), list(enumerate(partner)))


def across(x, *moves):
    axes = tuple(axis for axis, _ in moves)
    flip = 0
    for axis, bit in moves:
        flip = flip * lax.axis_size(axis) + bit
    return lax.ppermute(x, axes, [(i, i ^ flip) for i in range(lax.axis_size(axes))])


def scattered(rows, length):
    halves = lax.axis_size("y")
    grad = jnp.pad(rows, ((0, 0), (0, 0), (0, halves * length - rows.shape[2]), (0, 0)))
    grad = lax.psum_scatter(grad, "dp", scatter_dimension=0, tiled=True)
    grad = grad.reshape(1, 2, halves, length, LANES)
    core = lax.axis_index("core")
    return tuple(lax.dynamic_index_in_dim(grad, at, 1, False) for at in (core, 1 - core))


def assembled(own, got, length, size, inner, mid):
    core = lax.axis_index("core")
    both = jnp.stack([own, got]).astype(F32)
    both = jnp.stack([lax.dynamic_index_in_dim(both, at, 0, False) for at in (core, 1 - core)])
    rows = both[:, :, :length].reshape(2, -1, LANES)
    second = [None] * 27
    for j in range(13):
        for m, k in enumerate((j, 9 + j) if j < 9 else (2 * j, 2 * j + 1)):
            second[k] = rows[:, j * size : (j + 1) * size, m * mid : (m + 1) * mid].reshape(2 * size, mid)
    tail = rows[:, 13 * size : 13 * size + size // 2]
    second[26] = jnp.concatenate([tail[:, :, :mid], tail[:, :, mid:]], axis=1).reshape(2 * size, mid)
    rows, half = both[:, :, length:].reshape(2, -1, LANES), size // 2
    first = [None] * 27
    for j in range(7):
        for m in range(4):
            c, ab = (j // 2, 4 * (j % 2) + m) if j < 6 else (m, 8)
            if c < 3:
                value = rows[:, j * half : (j + 1) * half, m * inner : (m + 1) * inner]
                first[3 * ab + c] = value.reshape(size, inner)
    return jnp.stack(first), jnp.stack(second)


def per_device(volume, kernel_first, kernel_second, cotangent):
    _, inner, depth, height, width = volume.shape
    mid, out = kernel_first.shape[1], kernel_second.shape[1]
    cells = height * width
    parts = lax.axis_size("dp")
    k1, k2 = jnp.swapaxes(kernel_first, 1, 2), jnp.swapaxes(kernel_second, 1, 2)
    rows = depth * height

    one, two = swapped(volume[0], "dep", 0), swapped(volume[0], "dep", 1)
    (blank,) = call(blank_kernel, [shape((out, 2 * width), BF)], [], flops=3_000_000_000)
    cot_rows, back = call(
        spread_kernel,
        [
            shape((depth, out, cells), BF),
            shape((depth + 2, mid, cells + 2 * width), F32),
        ],
        [cotangent[0], k2, blank],
        [pltpu.VMEM((out * rows, width), F32)],
        flops=1_100_000_000,
    )
    moved, w1 = call(
        arrange_kernel,
        [shape((depth, 3 * out, cells), BF), shape((3 * mid, 9 * inner), BF)],
        [cot_rows, k1],
        flops=500_000_000,
    )
    deep, one, two = call(
        rim_kernel,
        [shape((3 * depth, inner, cells), BF)] + [shape((3 * depth, inner, 2 * width), BF)] * 2,
        [volume[0], one, two, w1],
        [pltpu.VMEM((inner * rows, width), F32)],
    )
    one, two = swapped(one, HGT, 0), swapped(two, HGT, 1)
    size = mid // parts
    direct = parts == 2 and size % 16 == 0
    halves = lax.axis_size("y")
    length_second, length_first = (-(-units * size // (16 * halves)) * 8 for units in (27, 7))
    rows_in, rows_out = height - 2, 4
    inner_hidden, inner_second, inner_first = call(
        inner_kernel,
        [
            shape((depth + 2, mid, rows_in * width), BF),
            shape((9 * out, 3 * mid), F32),
            shape((3 * mid, 9 * inner), F32),
        ],
        [deep, w1, moved, back],
        [pltpu.VMEM((3 * mid, (depth + 2) * rows_in * width), BF)],
        flops=1_500_000_000,
    )
    hidden, slope, wide, *second = call(
        functools.partial(outer_kernel, direct),
        [
            shape((depth + 2, mid, cells + 2 * width), BF),
            shape((depth + 2, mid, rows_out * width), F32),
            shape((3 * depth, inner, cells + 4 * width), BF),
        ]
        + (
            [shape((parts, halves, length_second, width), F32)] * 2
            if direct
            else [shape((14, out, LANES), F32)]
        ),
        [deep, two, one, w1, moved, inner_hidden, inner_second],
        flops=1_000_000_000,
    )
    first = call(
        functools.partial(delta_kernel, direct),
        [shape((parts, halves, length_first, width), F32)] * 2 if direct else [shape((7, mid, LANES), F32)],
        [wide, back, slope, inner_first],
        [pltpu.VMEM((3 * mid, (depth + 2) * rows_out * width), BF)],
        flops=4_000_000_000,
    )
    if direct:
        moves = [(1, 0), (0, 1), (1, 1)]
    else:
        moves = [(0, 1)]
        blocks = second[0].reshape(14, parts, 2, size, LANES).transpose(1, 2, 0, 3, 4)
        tail = blocks[:, :, 13, :, :mid]
        tail = jnp.concatenate([tail[:, :, : size // 2], tail[:, :, size // 2 :]], axis=-1)
        rows_second = jnp.concatenate([blocks[:, :, :13].reshape(parts, 2, 13 * size, LANES), tail], axis=2)
        second = scattered(rows_second, length_second)
        blocks = first[0].reshape(7, parts, 2, size // 2, LANES).transpose(1, 2, 0, 3, 4)
        first = scattered(blocks.reshape(parts, 2, 7 * (size // 2), LANES), length_first)
    block = (length_second + length_first, width)
    kept, *sends = call(
        functools.partial(plane_kernel, moves),
        [shape(block, F32)] + [shape(block, BF)] * len(moves),
        [x for keep, send in (second, first) for x in (keep, across(send, ("core", 1)))],
    )
    gots = [across(send, ("dp", x), ("y", y)) for send, (x, y) in zip(sends, moves, strict=True)]
    (share,) = call(total_kernel, [shape(block, BF)], [kept, *gots])
    features, token = call(
        features_kernel,
        [shape(cotangent.shape[1:], BF), shape((8, width), F32)],
        [hidden, k2],
        [pltpu.VMEM((out * rows, width), F32)],
        flops=900_000_000,
    )
    gots = [across(share, ("dep", bits)) for bits in (1, 2, 3)]
    (share,) = call(depth_kernel, [shape(block, BF)], [share, *gots, token])
    (own,) = call(order_kernel, [shape((halves, *block), BF)], [share, across(share, ("y", 1))])
    got = across(own, ("core", 1))
    if size % 16 == 0:
        grads = [shape((27, size, inner), F32), shape((27, 2 * size, mid), F32)]
        scratch = [
            pltpu.VMEM((27, size // 2, inner), F32),
            pltpu.VMEM((27, size, mid), F32),
            pltpu.SemaphoreType.DMA((2,)),
        ]
        written = call(functools.partial(unpack_kernel, length_second, False), grads, [own], scratch, far_outs=True)
        grad_first, grad_second = call(
            functools.partial(unpack_kernel, length_second, True),
            grads,
            [got, *written],
            scratch,
            far=(1, 2),
            far_outs=True,
            aliases={1: 0, 2: 1},
        )
    else:
        grad_first, grad_second = assembled(own, got, length_second, size, inner, mid)
    return features[None], grad_first, grad_second


def solution(mesh):
    dp, dep, hgt = (mesh.shape[axis] for axis in ("dp", "dep", "hgt"))
    split = jax.sharding.Mesh(mesh.devices.reshape(dp, dep, hgt // 2, 2), ("dp", "dep", *HGT))
    block = P("dp", None, "dep", HGT, None)
    return jax.shard_map(
        per_device,
        mesh=split,
        in_specs=(block, P(), P(), block),
        out_specs=(block, P(None, "dp", None), P(None, "dp", None)),
        check_vma=False,
    )
```

```python
import functools

import jax
import jax.numpy as jnp
from jax import lax
from jax.experimental import pallas as pl
from jax.experimental.pallas import tpu as pltpu
from jax.sharding import PartitionSpec as P

BF, F32 = jnp.bfloat16, jnp.float32
LANES = 128
HGT = ("y", "core")
VMEM_BYTES = 28 * 2**20


def call(body, outs, args, scratch=(), flops=0, far=(), far_outs=False, aliases=None):
    moved = sum(x.size * x.dtype.itemsize for x in (*outs, *args))
    return pl.pallas_call(
        body,
        out_shape=outs,
        in_specs=[pl.BlockSpec(memory_space=pl.ANY if n in far else pltpu.VMEM) for n in range(len(args))],
        out_specs=[pl.BlockSpec(memory_space=pl.ANY if far_outs else pltpu.VMEM)] * len(outs),
        scratch_shapes=list(scratch),
        input_output_aliases=aliases or {},
        compiler_params=pltpu.CompilerParams(vmem_limit_bytes=VMEM_BYTES),
        cost_estimate=pl.CostEstimate(flops=flops, bytes_accessed=moved, transcendentals=0),
    )(*args)


def shape(dims, dtype):
    return jax.ShapeDtypeStruct(dims, dtype)


def moved_along_width(x, c):
    if c == 0:
        return x
    pieces = []
    for start in range(0, x.shape[1], LANES):
        piece = x[:, start : start + LANES]
        lane = lax.broadcasted_iota(jnp.int32, piece.shape, 1)
        rolled = pltpu.roll(piece, c % LANES, 1)
        pieces.append(jnp.where(lane == (0 if c == 1 else LANES - 1), 0.0, rolled))
    return pieces[0] if len(pieces) == 1 else jnp.concatenate(pieces, axis=1)


def by_rows(ref, scratch, store):
    channels, depth, height, width = ref.shape
    rows = depth * height
    scratch[...] = ref[...].astype(F32).reshape(channels * rows, width)
    for d in range(depth):
        for h in range(height):
            store(d, h, scratch[pl.ds(d * height + h, channels, stride=rows), :])


def odd(axis):
    return lax.rem(lax.axis_index(axis), 2) == 1


def blank_kernel(out_ref):
    out_ref[...] = jnp.zeros(out_ref.shape, BF)


def spread_kernel(cot_ref, k2_ref, blank_ref, cot_rows_ref, back_ref, scratch):
    out, depth, height, _ = cot_ref.shape
    rows = [[None] * height for _ in range(depth)]

    def store(d, h, row):
        rows[d][h] = row.astype(BF)
        cot_rows_ref[d, :, h * LANES : (h + 1) * LANES] = rows[d][h]

    by_rows(cot_ref, scratch, store)
    mid = k2_ref.shape[1]
    none = blank_ref[...]
    padded = [jnp.concatenate([none, *rows[d], none], axis=1) for d in range(depth)]
    for e in range(depth + 2):
        reached = [(d, e - 1 - d) for d in range(depth) if abs(e - 1 - d) <= 1]
        w = jnp.concatenate(
            [
                k2_ref[9 * (a + 1) + 3 * b : 9 * (a + 1) + 3 * b + 3].reshape(3 * mid, out)
                for _, a in reached
                for b in range(3)
            ],
            axis=1,
        )
        for j in range(0, height + 2, 2):
            rhs = jnp.concatenate(
                [padded[d][:, (j + 2 - b) * LANES : (j + 4 - b) * LANES] for d, _ in reached for b in range(3)], axis=0
            )
            y = jnp.dot(w, rhs, preferred_element_type=F32)
            back = sum(moved_along_width(y[n * mid : (n + 1) * mid], n - 1) for n in range(3))
            back_ref[e, :, j * LANES : (j + 2) * LANES] = back


def as_matrix(ref, c):
    stacked = jnp.concatenate([ref[3 * ab + c] for ab in range(9)], axis=0)
    return stacked.astype(F32).T.astype(BF)


def arrange_kernel(cot_rows_ref, k1_ref, vol_ref, moved_ref, w1_ref, own_ref, scratch):
    def store(d, h, row):
        own_ref[d, :, h * LANES : (h + 1) * LANES] = row.astype(BF)

    by_rows(vol_ref, scratch, store)
    depth, out, cells = cot_rows_ref.shape
    for d in range(depth):
        for h in range(0, cells, LANES):
            row = cot_rows_ref[d, :, h : h + LANES]
            for n, c in enumerate((-1, 0, 1)):
                value = row if c == 0 else moved_along_width(row.astype(F32), c).astype(BF)
                moved_ref[d, n * out : (n + 1) * out, h : h + LANES] = value
    mid = k1_ref.shape[2]
    for c in range(3):
        w1_ref[c * mid : (c + 1) * mid, :] = as_matrix(k1_ref, c)


def sides(axis, one, two):
    me, size = lax.axis_index(axis), lax.axis_size(axis)
    is_odd = odd(axis)
    none = jnp.zeros_like(one)
    before = jnp.where(me == 0, none, jnp.where(is_odd, one, two))
    after = jnp.where(me == size - 1, none, jnp.where(is_odd, two, one))
    return before, after


def rim_kernel(own_ref, one_ref, two_ref, deep_ref, send_one_ref, send_two_ref, scratch):
    depth = own_ref.shape[0]
    deep_ref[depth : 2 * depth] = own_ref[...]
    for at, part in zip((0, 2 * depth), sides("dep", one_ref[...], two_ref[...]), strict=True):

        def store(d, h, row, at=at):
            deep_ref[at + d, :, h * LANES : (h + 1) * LANES] = row.astype(BF)

        by_rows(part, scratch, store)
    n, cells = send_one_ref.shape[2], deep_ref.shape[2]
    first, last = deep_ref[:, :, :n], deep_ref[:, :, cells - n :]
    is_odd = odd(HGT)
    send_one_ref[...] = jnp.where(is_odd, first, last)
    send_two_ref[...] = jnp.where(is_odd, last, first)


def widened(deep_ref, one_ref, two_ref):
    left, right = sides(HGT, one_ref[...], two_ref[...])
    return [jnp.concatenate([left[d], deep_ref[d], right[d]], axis=1) for d in range(deep_ref.shape[0])]


def pack(direct, refs, rows_of, blocks):
    if not direct:
        for j, block in enumerate(blocks):
            refs[0][j] = block
        return
    keep_ref, send_ref = refs
    parts, halves, length, _ = keep_ref.shape
    core = lax.axis_index("core") == 1
    for part in range(parts):
        one, two = (jnp.concatenate(rows_of(part, c), axis=0) for c in range(2))
        for half in range(halves):
            at = slice(half * length, (half + 1) * length)
            keep_ref[part, half] = jnp.where(core, two[at], one[at])
            send_ref[part, half] = jnp.where(core, one[at], two[at]).astype(send_ref.dtype)


def folded(tail):
    half = tail.shape[0] // 2
    return jnp.concatenate([tail[:half], tail[half:]], axis=1)


def activated(w1, rhs, d, depth, heights):
    mid = w1.shape[0] // 3
    y = jnp.dot(w1, rhs, preferred_element_type=F32)
    pre = sum(moved_along_width(y[n * mid : (n + 1) * mid], 1 - n) for n in range(3))
    s = 1.0 / (1.0 + jnp.exp(-pre))
    dep, deps = lax.axis_index("dep"), lax.axis_size("dep")
    hgt, hgts = lax.axis_index(HGT), lax.axis_size(HGT)
    results = []
    for n, side in enumerate(heights):
        p, q = (x[:, n * LANES : (n + 1) * LANES] for x in (pre, s))
        value, slope = (p * q).astype(BF), q * (1.0 + p * (1.0 - q))
        outside = []
        if d == 0:
            outside.append(dep == 0)
        if d == depth - 1:
            outside.append(dep == deps - 1)
        if side < 0:
            outside.append(hgt == 0)
        if side > 0:
            outside.append(hgt == hgts - 1)
        for far in outside:
            value = jnp.where(far, jnp.zeros_like(value), value)
            slope = jnp.where(far, jnp.zeros_like(slope), slope)
        results.append((value, slope))
    return results


def neighbours(ref, d, starts, count):
    return jnp.concatenate(
        [
            jnp.concatenate(
                [ref[d + a, :, (start + b) * LANES : (start + b + count) * LANES] for start in starts], axis=1
            )
            for a in range(3)
            for b in range(3)
        ],
        axis=0,
    )


def products(left, right):
    return lax.dot_general(left, right, (((1,), (1,)), ((), ())), preferred_element_type=F32)


def shares(delta, n_channels, ref, at):
    for n in range(3):
        ref[n * n_channels : (n + 1) * n_channels, at : at + LANES] = moved_along_width(delta, n - 1).astype(BF)


def inner_kernel(deep_ref, w1_ref, moved_ref, back_ref, hidden_ref, second_ref, first_ref, delta_ref):
    w1 = w1_ref[...]
    depth, mid, cells = hidden_ref.shape
    height = cells // LANES
    for d in range(depth):
        for h in range(0, height, 2):
            results = activated(w1, neighbours(deep_ref, d, [h], 2), d, depth, (0, 0))
            for n, (value, slope) in enumerate(results):
                at = (h + n) * LANES
                hidden_ref[d, :, at : at + LANES] = value
                back = back_ref[d, :, at + 2 * LANES : at + 3 * LANES]
                shares(back * slope, mid, delta_ref, d * cells + at)
    own = depth - 2
    left = jnp.concatenate(
        [
            jnp.concatenate([moved_ref[d, :, (2 - b) * LANES : (2 - b) * LANES + cells] for d in range(own)], axis=1)
            for b in range(3)
        ],
        axis=0,
    )
    right = jnp.concatenate(
        [jnp.concatenate([hidden_ref[d + a] for a in range(3)], axis=0) for d in range(own)], axis=1
    )
    second_ref[...] = products(left, right)
    right = jnp.concatenate([neighbours(deep_ref, d, [0], height) for d in range(depth)], axis=1)
    first_ref[...] = products(delta_ref[...], right)


def outer_kernel(
    direct, deep_ref, two_ref, one_ref, w1_ref, back_ref, inner_ref, first_ref, hidden_ref, *grad_refs_and_scratch,
):
    *grad_refs, rows_ref, delta_ref = grad_refs_and_scratch
    for d, row in enumerate(widened(deep_ref, one_ref, two_ref)):
        rows_ref[d] = row
    w1 = w1_ref[...]
    depth, mid, cells = hidden_ref.shape
    last = cells // LANES - 2
    for d in range(depth):
        hidden_ref[d, :, 2 * LANES : last * LANES] = inner_ref[d]
        for h, sides_of in ((0, (-1, 0)), (last, (0, 1))):
            results = activated(w1, neighbours(rows_ref, d, [h], 2), d, depth, sides_of)
            for n, (value, slope) in enumerate(results):
                at = (h + n) * LANES
                hidden_ref[d, :, at : at + LANES] = value
                delta = back_ref[d, :, at : at + LANES] * slope
                shares(delta, mid, delta_ref, (4 * d + (2 if h else 0) + n) * LANES)
    right = jnp.concatenate([neighbours(rows_ref, d, [0, last], 2) for d in range(depth)], axis=1)
    total = first_ref[...] + products(delta_ref[...], right)
    inner = rows_ref.shape[1]
    blocks, tails = [], []
    for n in range(3):
        part = total[n * mid : (n + 1) * mid]
        blocks += [part[:, m * LANES : (m + 1) * LANES] for m in range(2)]
        tails.append(part[:, 2 * LANES :])
    tails.append(jnp.zeros((mid, LANES - 3 * inner), F32))
    blocks.append(jnp.concatenate(tails, axis=1))
    size = mid // lax.axis_size("dp")
    half = size // 2

    def rows_of(part, core):
        return [block[part * size + core * half : part * size + (core + 1) * half] for block in blocks]

    pack(direct, grad_refs, rows_of, blocks)


def second_kernel(direct, hidden_ref, moved_ref, second_ref, *grad_refs):
    depth, mid, cells = hidden_ref.shape
    height = cells // LANES
    own = depth - 2
    out = moved_ref.shape[1] // 3
    heads, tails = [], []
    for b in range(3):
        far = [h for h in range(height - 2) if not 2 <= h + b <= height - 3]
        left = jnp.concatenate(
            [moved_ref[d, :, h * LANES : (h + 1) * LANES] for d in range(own) for h in far], axis=1
        )
        right = jnp.concatenate(
            [
                jnp.concatenate([hidden_ref[d + a, :, (h + b) * LANES : (h + b + 1) * LANES] for a in range(3)], axis=0)
                for d in range(own)
                for h in far
            ],
            axis=1,
        )
        total = second_ref[3 * b * out : 3 * (b + 1) * out, :] + products(left, right)
        for c in range(3):
            part = total[c * out : (c + 1) * out]
            heads.append(part[:, :LANES])
            tails.append(part[:, LANES:])
    blocks = heads + [jnp.concatenate(tails[n : n + 2], axis=1) for n in range(0, 8, 2)]
    size = mid // lax.axis_size("dp")

    def rows_of(part, core):
        at = slice((2 * part + core) * size, (2 * part + core + 1) * size)
        return [block[at] for block in blocks] + [folded(tails[8][at])]

    pack(direct, grad_refs, rows_of, [*blocks, jnp.concatenate([tails[8], jnp.zeros_like(tails[8])], axis=1)])


def features_kernel(hidden_ref, k2_ref, out_ref, token_ref, scratch):
    out, depth, height, _ = out_ref.shape
    w2 = jnp.concatenate([as_matrix(k2_ref, c) for c in range(3)], axis=0)
    for d in range(depth):
        for h in range(0, height, 2):
            rhs = jnp.concatenate(
                [
                    hidden_ref[d + a, :, (h + b) * LANES : (h + b + 2) * LANES]
                    for a in range(3)
                    for b in range(3)
                ],
                axis=0,
            )
            y = jnp.dot(w2, rhs, preferred_element_type=F32)
            total = sum(moved_along_width(y[n * out : (n + 1) * out], 1 - n) for n in range(3))
            for r in range(2):
                row = total[:, r * LANES : (r + 1) * LANES]
                scratch[pl.ds(d * height + h + r, out, stride=depth * height), :] = row
    out_ref[...] = scratch[...].reshape(out_ref.shape).astype(BF)
    token_ref[...] = scratch[:8]


def plane_kernel(moves, *refs):
    keep_first, got_first, keep_second, got_second, kept_ref, *send_refs = refs
    part = lax.rem(lax.axis_index("dp"), keep_first.shape[0])
    half = lax.axis_index("y")

    def total(x, y):
        at = 1 - part if x else part, 1 - half if y else half
        return jnp.concatenate([keep_second[at] + got_second[at].astype(F32), keep_first[at] + got_first[at]], axis=0)

    kept_ref[...] = total(0, 0)
    for (x, y), send_ref in zip(moves, send_refs, strict=True):
        send_ref[...] = total(x, y).astype(BF)


def total_kernel(kept_ref, *refs):
    *got_refs, out_ref = refs
    value = kept_ref[...]
    for ref in got_refs:
        value = value + ref[...].astype(F32)
    out_ref[...] = value.astype(BF)


def depth_kernel(a_ref, b_ref, c_ref, d_ref, _, out_ref):
    one = a_ref[...].astype(F32) + b_ref[...].astype(F32)
    two = c_ref[...].astype(F32) + d_ref[...].astype(F32)
    out_ref[...] = (one + two).astype(BF)


def order_kernel(own_ref, got_ref, out_ref):
    mine = lax.axis_index("y")
    out_ref[mine] = own_ref[...]
    out_ref[1 - mine] = got_ref[...]


def unpack_kernel(length, theirs, in_ref, *refs):
    first_ref, second_ref, first, second, sems = refs[-5:]
    core = lax.axis_index("core")
    at = 1 - core if theirs else core
    _, size, mid = second.shape
    whole = [in_ref[n].astype(F32) for n in range(in_ref.shape[0])]
    rows = jnp.concatenate([x[:length] for x in whole], axis=0)
    for j in range(13):
        value = rows[j * size : (j + 1) * size]
        for m, k in enumerate((j, 9 + j) if j < 9 else (2 * j, 2 * j + 1)):
            second[k] = value[:, m * mid : (m + 1) * mid]
    value = rows[13 * size : 13 * size + size // 2]
    second[26] = jnp.concatenate([value[:, :mid], value[:, mid:]], axis=0)
    copies = [pltpu.make_async_copy(second, second_ref.at[:, pl.ds(pl.multiple_of(at * size, size), size), :], sems.at[1])]
    copies[0].start()
    _, half, inner = first.shape
    rows = jnp.concatenate([x[length:] for x in whole], axis=0)
    for j in range(7):
        value = rows[j * half : (j + 1) * half]
        for m in range(4):
            c, ab = (j // 2, 4 * (j % 2) + m) if j < 6 else (m, 8)
            if c < 3:
                first[3 * ab + c] = value[:, m * inner : (m + 1) * inner]
    copies.append(
        pltpu.make_async_copy(first, first_ref.at[:, pl.ds(pl.multiple_of(at * half, half), half), :], sems.at[0])
    )
    copies[1].start()
    for copy in copies:
        copy.wait()


def swapped(x, axis, first):
    axes = (axis,) if isinstance(axis, str) else axis
    parts, size = lax.axis_size("dp"), lax.axis_size(axis)
    partner = list(range(parts * size))
    for i in partner:
        part, at = divmod(i, size)
        if first <= at < size - (size - first) % 2:
            partner[i] = part * size + (at - first ^ 1) + first
        elif parts % 2 == 0:
            partner[i] = (part ^ 1) * size + at
    return lax.ppermute(x, ("dp", *axes), list(enumerate(partner)))


def across(x, *moves):
    axes = tuple(axis for axis, _ in moves)
    flip = 0
    for axis, bit in moves:
        flip = flip * lax.axis_size(axis) + bit
    return lax.ppermute(x, axes, [(i, i ^ flip) for i in range(lax.axis_size(axes))])


def scattered(rows, length):
    halves = lax.axis_size("y")
    grad = jnp.pad(rows, ((0, 0), (0, 0), (0, halves * length - rows.shape[2]), (0, 0)))
    grad = lax.psum_scatter(grad, "dp", scatter_dimension=0, tiled=True)
    grad = grad.reshape(1, 2, halves, length, LANES)
    core = lax.axis_index("core")
    return tuple(lax.dynamic_index_in_dim(grad, at, 1, False) for at in (core, 1 - core))


def assembled(own, got, length, size, inner, mid):
    core = lax.axis_index("core")
    both = jnp.stack([own, got]).astype(F32)
    both = jnp.stack([lax.dynamic_index_in_dim(both, at, 0, False) for at in (core, 1 - core)])
    rows = both[:, :, :length].reshape(2, -1, LANES)
    second = [None] * 27
    for j in range(13):
        for m, k in enumerate((j, 9 + j) if j < 9 else (2 * j, 2 * j + 1)):
            second[k] = rows[:, j * size : (j + 1) * size, m * mid : (m + 1) * mid].reshape(2 * size, mid)
    tail = rows[:, 13 * size : 13 * size + size // 2]
    second[26] = jnp.concatenate([tail[:, :, :mid], tail[:, :, mid:]], axis=1).reshape(2 * size, mid)
    rows, half = both[:, :, length:].reshape(2, -1, LANES), size // 2
    first = [None] * 27
    for j in range(7):
        for m in range(4):
            c, ab = (j // 2, 4 * (j % 2) + m) if j < 6 else (m, 8)
            if c < 3:
                value = rows[:, j * half : (j + 1) * half, m * inner : (m + 1) * inner]
                first[3 * ab + c] = value.reshape(size, inner)
    return jnp.stack(first), jnp.stack(second)


def per_device(volume, kernel_first, kernel_second, cotangent):
    _, inner, depth, height, width = volume.shape
    mid, out = kernel_first.shape[1], kernel_second.shape[1]
    cells = height * width
    parts = lax.axis_size("dp")
    k1, k2 = jnp.swapaxes(kernel_first, 1, 2), jnp.swapaxes(kernel_second, 1, 2)
    rows = depth * height

    one, two = swapped(volume[0], "dep", 0), swapped(volume[0], "dep", 1)
    (blank,) = call(blank_kernel, [shape((out, 2 * width), BF)], [], flops=3_000_000_000)
    cot_rows, back = call(
        spread_kernel,
        [
            shape((depth, out, cells), BF),
            shape((depth + 2, mid, cells + 2 * width), F32),
        ],
        [cotangent[0], k2, blank],
        [pltpu.VMEM((out * rows, width), F32)],
        flops=1_100_000_000,
    )
    moved, w1, vol = call(
        arrange_kernel,
        [
            shape((depth, 3 * out, cells), BF),
            shape((3 * mid, 9 * inner), BF),
            shape((depth, inner, cells), BF),
        ],
        [cot_rows, k1, volume[0]],
        [pltpu.VMEM((inner * rows, width), F32)],
        flops=500_000_000,
    )
    deep, one, two = call(
        rim_kernel,
        [shape((3 * depth, inner, cells), BF)] + [shape((3 * depth, inner, 2 * width), BF)] * 2,
        [vol, one, two],
        [pltpu.VMEM((inner * rows, width), F32)],
    )
    one, two = swapped(one, HGT, 0), swapped(two, HGT, 1)
    size = mid // parts
    direct = parts == 2 and size % 16 == 0
    halves = lax.axis_size("y")
    length_second, length_first = (-(-units * size // (16 * halves)) * 8 for units in (27, 7))
    rows_in, rows_out = height - 2, 4
    inner_hidden, inner_second, inner_first = call(
        inner_kernel,
        [
            shape((depth + 2, mid, rows_in * width), BF),
            shape((9 * out, 3 * mid), F32),
            shape((3 * mid, 9 * inner), F32),
        ],
        [deep, w1, moved, back],
        [pltpu.VMEM((3 * mid, (depth + 2) * rows_in * width), BF)],
        flops=1_500_000_000,
    )
    hidden, *first = call(
        functools.partial(outer_kernel, direct),
        [shape((depth + 2, mid, cells + 2 * width), BF)]
        + ([shape((parts, halves, length_first, width), F32)] * 2 if direct else [shape((7, mid, LANES), F32)]),
        [deep, two, one, w1, back, inner_hidden, inner_first],
        [
            pltpu.VMEM((3 * depth, inner, cells + 4 * width), BF),
            pltpu.VMEM((3 * mid, (depth + 2) * rows_out * width), BF),
        ],
        flops=1_000_000_000,
    )
    second = call(
        functools.partial(second_kernel, direct),
        [shape((parts, halves, length_second, width), kind) for kind in (F32, BF)]
        if direct
        else [shape((14, out, LANES), F32)],
        [hidden, moved, inner_second],
        flops=4_000_000_000,
    )
    if direct:
        moves = [(1, 0), (0, 1), (1, 1)]
    else:
        moves = [(0, 1)]
        blocks = second[0].reshape(14, parts, 2, size, LANES).transpose(1, 2, 0, 3, 4)
        tail = blocks[:, :, 13, :, :mid]
        tail = jnp.concatenate([tail[:, :, : size // 2], tail[:, :, size // 2 :]], axis=-1)
        rows_second = jnp.concatenate([blocks[:, :, :13].reshape(parts, 2, 13 * size, LANES), tail], axis=2)
        second = scattered(rows_second, length_second)
        blocks = first[0].reshape(7, parts, 2, size // 2, LANES).transpose(1, 2, 0, 3, 4)
        first = scattered(blocks.reshape(parts, 2, 7 * (size // 2), LANES), length_first)
    block = (length_second + length_first, width)
    kept, *sends = call(
        functools.partial(plane_kernel, moves),
        [shape(block, F32)] + [shape(block, BF)] * len(moves),
        [x for keep, send in (first, second) for x in (keep, across(send, ("core", 1)))],
    )
    gots = [across(send, ("dp", x), ("y", y)) for send, (x, y) in zip(sends, moves, strict=True)]
    (share,) = call(total_kernel, [shape(block, BF)], [kept, *gots])
    features, token = call(
        features_kernel,
        [shape(cotangent.shape[1:], BF), shape((8, width), F32)],
        [hidden, k2],
        [pltpu.VMEM((out * rows, width), F32)],
        flops=900_000_000,
    )
    gots = [across(share, ("dep", bits)) for bits in (1, 2, 3)]
    (share,) = call(depth_kernel, [shape(block, BF)], [share, *gots, token])
    (own,) = call(order_kernel, [shape((halves, *block), BF)], [share, across(share, ("y", 1))])
    got = across(own, ("core", 1))
    if size % 16 == 0:
        grads = [shape((27, size, inner), F32), shape((27, 2 * size, mid), F32)]
        scratch = [
            pltpu.VMEM((27, size // 2, inner), F32),
            pltpu.VMEM((27, size, mid), F32),
            pltpu.SemaphoreType.DMA((2,)),
        ]
        written = call(functools.partial(unpack_kernel, length_second, False), grads, [own], scratch, far_outs=True)
        grad_first, grad_second = call(
            functools.partial(unpack_kernel, length_second, True),
            grads,
            [got, *written],
            scratch,
            far=(1, 2),
            far_outs=True,
            aliases={1: 0, 2: 1},
        )
    else:
        grad_first, grad_second = assembled(own, got, length_second, size, inner, mid)
    return features[None], grad_first, grad_second


def solution(mesh):
    dp, dep, hgt = (mesh.shape[axis] for axis in ("dp", "dep", "hgt"))
    split = jax.sharding.Mesh(mesh.devices.reshape(dp, dep, hgt // 2, 2), ("dp", "dep", *HGT))
    block = P("dp", None, "dep", HGT, None)
    return jax.shard_map(
        per_device,
        mesh=split,
        in_specs=(block, P(), P(), block),
        out_specs=(block, P(None, "dp", None), P(None, "dp", None)),
        check_vma=False,
    )
```

```python
import functools

import jax
import jax.numpy as jnp
from jax import lax
from jax.experimental import pallas as pl
from jax.experimental.pallas import tpu as pltpu
from jax.sharding import PartitionSpec as P

BF, F32 = jnp.bfloat16, jnp.float32
LANES = 128
HGT = ("y", "core")
VMEM_BYTES = 28 * 2**20


def call(body, outs, args, scratch=(), flops=0, far=(), far_outs=(), aliases=None):
    moved = sum(x.size * x.dtype.itemsize for x in (*outs, *args))
    return pl.pallas_call(
        body,
        out_shape=outs,
        in_specs=[pl.BlockSpec(memory_space=pl.ANY if n in far else pltpu.VMEM) for n in range(len(args))],
        out_specs=[pl.BlockSpec(memory_space=pl.ANY if n in far_outs else pltpu.VMEM) for n in range(len(outs))],
        scratch_shapes=list(scratch),
        input_output_aliases=aliases or {},
        compiler_params=pltpu.CompilerParams(vmem_limit_bytes=VMEM_BYTES),
        cost_estimate=pl.CostEstimate(flops=flops, bytes_accessed=moved, transcendentals=0),
    )(*args)


def shape(dims, dtype):
    return jax.ShapeDtypeStruct(dims, dtype)


def moved_along_width(x, c):
    if c == 0:
        return x
    pieces = []
    for start in range(0, x.shape[1], LANES):
        piece = x[:, start : start + LANES]
        lane = lax.broadcasted_iota(jnp.int32, piece.shape, 1)
        rolled = pltpu.roll(piece, c % LANES, 1)
        pieces.append(jnp.where(lane == (0 if c == 1 else LANES - 1), 0.0, rolled))
    return pieces[0] if len(pieces) == 1 else jnp.concatenate(pieces, axis=1)


def by_rows(ref, scratch, store):
    channels, depth, height, width = ref.shape
    rows = depth * height
    scratch[...] = ref[...].astype(F32).reshape(channels * rows, width)
    for d in range(depth):
        for h in range(height):
            store(d, h, scratch[pl.ds(d * height + h, channels, stride=rows), :])


def odd(axis):
    return lax.rem(lax.axis_index(axis), 2) == 1


def blank_kernel(out_ref):
    out_ref[...] = jnp.zeros(out_ref.shape, BF)


def spread_kernel(cot_ref, k2_ref, blank_ref, cot_rows_ref, back_ref, scratch):
    out, depth, height, _ = cot_ref.shape
    rows = [[None] * height for _ in range(depth)]

    def store(d, h, row):
        rows[d][h] = row.astype(BF)
        cot_rows_ref[d, :, h * LANES : (h + 1) * LANES] = rows[d][h]

    by_rows(cot_ref, scratch, store)
    mid = k2_ref.shape[1]
    none = blank_ref[...]
    padded = [jnp.concatenate([none, *rows[d], none], axis=1) for d in range(depth)]
    for e in range(depth + 2):
        reached = [(d, e - 1 - d) for d in range(depth) if abs(e - 1 - d) <= 1]
        w = jnp.concatenate(
            [
                k2_ref[9 * (a + 1) + 3 * b : 9 * (a + 1) + 3 * b + 3].reshape(3 * mid, out)
                for _, a in reached
                for b in range(3)
            ],
            axis=1,
        )
        for j in range(0, height + 2, 2):
            rhs = jnp.concatenate(
                [padded[d][:, (j + 2 - b) * LANES : (j + 4 - b) * LANES] for d, _ in reached for b in range(3)], axis=0
            )
            y = jnp.dot(w, rhs, preferred_element_type=F32)
            back = sum(moved_along_width(y[n * mid : (n + 1) * mid], n - 1) for n in range(3))
            back_ref[e, :, j * LANES : (j + 2) * LANES] = back


def as_matrix(ref, c):
    stacked = jnp.concatenate([ref[3 * ab + c] for ab in range(9)], axis=0)
    return stacked.astype(F32).T.astype(BF)


def arrange_kernel(cot_rows_ref, k1_ref, vol_ref, moved_ref, w1_ref, own_ref, scratch):
    def store(d, h, row):
        own_ref[d, :, h * LANES : (h + 1) * LANES] = row.astype(BF)

    by_rows(vol_ref, scratch, store)
    depth, out, cells = cot_rows_ref.shape
    for d in range(depth):
        for h in range(0, cells, LANES):
            row = cot_rows_ref[d, :, h : h + LANES]
            for n, c in enumerate((-1, 0, 1)):
                value = row if c == 0 else moved_along_width(row.astype(F32), c).astype(BF)
                moved_ref[d, n * out : (n + 1) * out, h : h + LANES] = value
    mid = k1_ref.shape[2]
    for c in range(3):
        w1_ref[c * mid : (c + 1) * mid, :] = as_matrix(k1_ref, c)


def sides(axis, one, two):
    me, size = lax.axis_index(axis), lax.axis_size(axis)
    is_odd = odd(axis)
    none = jnp.zeros_like(one)
    before = jnp.where(me == 0, none, jnp.where(is_odd, one, two))
    after = jnp.where(me == size - 1, none, jnp.where(is_odd, two, one))
    return before, after


def rim_kernel(own_ref, one_ref, two_ref, deep_ref, send_one_ref, send_two_ref, scratch):
    depth = own_ref.shape[0]
    deep_ref[depth : 2 * depth] = own_ref[...]
    for at, part in zip((0, 2 * depth), sides("dep", one_ref[...], two_ref[...]), strict=True):

        def store(d, h, row, at=at):
            deep_ref[at + d, :, h * LANES : (h + 1) * LANES] = row.astype(BF)

        by_rows(part, scratch, store)
    n, cells = send_one_ref.shape[2], deep_ref.shape[2]
    first, last = deep_ref[:, :, :n], deep_ref[:, :, cells - n :]
    is_odd = odd(HGT)
    send_one_ref[...] = jnp.where(is_odd, first, last)
    send_two_ref[...] = jnp.where(is_odd, last, first)


def widened(deep_ref, one_ref, two_ref):
    left, right = sides(HGT, one_ref[...], two_ref[...])
    return [jnp.concatenate([left[d], deep_ref[d], right[d]], axis=1) for d in range(deep_ref.shape[0])]


def pack(direct, refs, rows_of, blocks):
    if not direct:
        for j, block in enumerate(blocks):
            refs[0][j] = block
        return
    keep_ref, send_ref = refs
    parts, halves, length, _ = keep_ref.shape
    core = lax.axis_index("core") == 1

    def filled(rows):
        rest = length - sum(x.shape[0] for x in rows)
        return jnp.concatenate([*rows, jnp.zeros((rest, LANES), F32)] if rest else rows, axis=0)

    for part in range(parts):
        for half in range(halves):
            one, two = (filled(rows_of(part, c)[half]) for c in range(2))
            keep_ref[part, half] = jnp.where(core, two, one)
            send_ref[part, half] = jnp.where(core, one, two).astype(send_ref.dtype)


def folded(tail):
    half = tail.shape[0] // 2
    return jnp.concatenate([tail[:half], tail[half:]], axis=1)


def activated(w1, rhs, d, depth, heights):
    mid = w1.shape[0] // 3
    y = jnp.dot(w1, rhs, preferred_element_type=F32)
    pre = sum(moved_along_width(y[n * mid : (n + 1) * mid], 1 - n) for n in range(3))
    s = 1.0 / (1.0 + jnp.exp(-pre))
    dep, deps = lax.axis_index("dep"), lax.axis_size("dep")
    hgt, hgts = lax.axis_index(HGT), lax.axis_size(HGT)
    results = []
    for n, side in enumerate(heights):
        p, q = (x[:, n * LANES : (n + 1) * LANES] for x in (pre, s))
        value, slope = (p * q).astype(BF), q * (1.0 + p * (1.0 - q))
        outside = []
        if d == 0:
            outside.append(dep == 0)
        if d == depth - 1:
            outside.append(dep == deps - 1)
        if side < 0:
            outside.append(hgt == 0)
        if side > 0:
            outside.append(hgt == hgts - 1)
        for far in outside:
            value = jnp.where(far, jnp.zeros_like(value), value)
            slope = jnp.where(far, jnp.zeros_like(slope), slope)
        results.append((value, slope))
    return results


def neighbours(ref, d, starts, count):
    return jnp.concatenate(
        [
            jnp.concatenate(
                [ref[d + a, :, (start + b) * LANES : (start + b + count) * LANES] for start in starts], axis=1
            )
            for a in range(3)
            for b in range(3)
        ],
        axis=0,
    )


def products(left, right):
    return lax.dot_general(left, right, (((1,), (1,)), ((), ())), preferred_element_type=F32)


def shares(delta, n_channels, ref, at):
    for n in range(3):
        ref[n * n_channels : (n + 1) * n_channels, at : at + LANES] = moved_along_width(delta, n - 1).astype(BF)


def inner_kernel(deep_ref, w1_ref, moved_ref, back_ref, hidden_ref, second_ref, first_ref, delta_ref):
    w1 = w1_ref[...]
    depth, mid, cells = hidden_ref.shape
    height = cells // LANES
    for d in range(depth):
        for h in range(0, height, 2):
            results = activated(w1, neighbours(deep_ref, d, [h], 2), d, depth, (0, 0))
            for n, (value, slope) in enumerate(results):
                at = (h + n) * LANES
                hidden_ref[d, :, at : at + LANES] = value
                back = back_ref[d, :, at + 2 * LANES : at + 3 * LANES]
                shares(back * slope, mid, delta_ref, d * cells + at)
    own = depth - 2
    left = jnp.concatenate(
        [
            jnp.concatenate([moved_ref[d, :, (2 - b) * LANES : (2 - b) * LANES + cells] for d in range(own)], axis=1)
            for b in range(3)
        ],
        axis=0,
    )
    right = jnp.concatenate(
        [jnp.concatenate([hidden_ref[d + a] for a in range(3)], axis=0) for d in range(own)], axis=1
    )
    second_ref[...] = products(left, right)
    right = jnp.concatenate([neighbours(deep_ref, d, [0], height) for d in range(depth)], axis=1)
    first_ref[...] = products(delta_ref[...], right)


def outer_kernel(
    direct, deep_ref, two_ref, one_ref, w1_ref, back_ref, inner_ref, first_ref, hidden_ref, *grad_refs_and_scratch,
):
    *grad_refs, rows_ref, delta_ref = grad_refs_and_scratch
    for d, row in enumerate(widened(deep_ref, one_ref, two_ref)):
        rows_ref[d] = row
    w1 = w1_ref[...]
    depth, mid, cells = hidden_ref.shape
    last = cells // LANES - 2
    for d in range(depth):
        hidden_ref[d, :, 2 * LANES : last * LANES] = inner_ref[d]
        for h, sides_of in ((0, (-1, 0)), (last, (0, 1))):
            results = activated(w1, neighbours(rows_ref, d, [h], 2), d, depth, sides_of)
            for n, (value, slope) in enumerate(results):
                at = (h + n) * LANES
                hidden_ref[d, :, at : at + LANES] = value
                delta = back_ref[d, :, at : at + LANES] * slope
                shares(delta, mid, delta_ref, (4 * d + (2 if h else 0) + n) * LANES)
    right = jnp.concatenate([neighbours(rows_ref, d, [0, last], 2) for d in range(depth)], axis=1)
    total = first_ref[...] + products(delta_ref[...], right)
    inner = rows_ref.shape[1]
    blocks, tails = [], []
    for n in range(3):
        part = total[n * mid : (n + 1) * mid]
        blocks += [part[:, m * LANES : (m + 1) * LANES] for m in range(2)]
        tails.append(part[:, 2 * LANES :])
    tails.append(jnp.zeros((mid, LANES - 3 * inner), F32))
    blocks.append(jnp.concatenate(tails, axis=1))
    size = mid // lax.axis_size("dp")
    half = size // 2

    def rows_of(part, core):
        rows = [block[part * size + core * half : part * size + (core + 1) * half] for block in blocks]
        return rows[:3], rows[3:]

    pack(direct, grad_refs, rows_of, blocks)


def second_kernel(direct, hidden_ref, moved_ref, second_ref, *grad_refs):
    depth, mid, cells = hidden_ref.shape
    height = cells // LANES
    own = depth - 2
    out = moved_ref.shape[1] // 3
    heads, tails = [], []
    for b in range(3):
        far = [h for h in range(height - 2) if not 2 <= h + b <= height - 3]
        left = jnp.concatenate(
            [moved_ref[d, :, h * LANES : (h + 1) * LANES] for d in range(own) for h in far], axis=1
        )
        right = jnp.concatenate(
            [
                jnp.concatenate([hidden_ref[d + a, :, (h + b) * LANES : (h + b + 1) * LANES] for a in range(3)], axis=0)
                for d in range(own)
                for h in far
            ],
            axis=1,
        )
        total = second_ref[3 * b * out : 3 * (b + 1) * out, :] + products(left, right)
        for c in range(3):
            part = total[c * out : (c + 1) * out]
            heads.append(part[:, :LANES])
            tails.append(part[:, LANES:])
    blocks = heads + [jnp.concatenate(tails[n : n + 2], axis=1) for n in range(0, 8, 2)]
    size = mid // lax.axis_size("dp")

    def rows_of(part, core):
        at = slice((2 * part + core) * size, (2 * part + core + 1) * size)
        rows = [block[at] for block in blocks] + [folded(tails[8][at])]
        return rows[:7], rows[7:]

    pack(direct, grad_refs, rows_of, [*blocks, jnp.concatenate([tails[8], jnp.zeros_like(tails[8])], axis=1)])


def features_kernel(hidden_ref, k2_ref, out_ref, token_ref, scratch):
    out, depth, height, _ = out_ref.shape
    w2 = jnp.concatenate([as_matrix(k2_ref, c) for c in range(3)], axis=0)
    for d in range(depth):
        for h in range(0, height, 2):
            rhs = jnp.concatenate(
                [
                    hidden_ref[d + a, :, (h + b) * LANES : (h + b + 2) * LANES]
                    for a in range(3)
                    for b in range(3)
                ],
                axis=0,
            )
            y = jnp.dot(w2, rhs, preferred_element_type=F32)
            total = sum(moved_along_width(y[n * out : (n + 1) * out], 1 - n) for n in range(3))
            for r in range(2):
                row = total[:, r * LANES : (r + 1) * LANES]
                scratch[pl.ds(d * height + h + r, out, stride=depth * height), :] = row
    out_ref[...] = scratch[...].reshape(out_ref.shape).astype(BF)
    token_ref[...] = scratch[:8]


def plane_kernel(moves, cuts, *refs):
    sums, (kept_ref, *send_refs) = refs[: -1 - len(moves)], refs[-1 - len(moves) :]
    part = lax.rem(lax.axis_index("dp"), sums[0].shape[0])
    half = lax.axis_index("y")

    def total(x, y):
        at = 1 - part if x else part, 1 - half if y else half
        values = [keep[at] + got[at].astype(F32) for keep, got in zip(sums[::2], sums[1::2], strict=True)]
        if len(values) == 1:
            return values[0]
        one, two = (jnp.concatenate([v[:n] for v, n in zip(values, cut, strict=True)], axis=0) for cut in cuts)
        return jnp.where(at[1] == 0, one, two)

    kept_ref[...] = total(0, 0)
    for (x, y), send_ref in zip(moves, send_refs, strict=True):
        send_ref[...] = total(x, y).astype(BF)


def total_kernel(kept_ref, *refs):
    *got_refs, out_ref = refs
    value = kept_ref[...]
    for ref in got_refs:
        value = value + ref[...].astype(F32)
    out_ref[...] = value.astype(BF)


def depth_kernel(a_ref, b_ref, c_ref, d_ref, _, out_ref, padded_ref):
    one = a_ref[...].astype(F32) + b_ref[...].astype(F32)
    two = c_ref[...].astype(F32) + d_ref[...].astype(F32)
    out_ref[...] = (one + two).astype(BF)
    rest = jnp.zeros((padded_ref.shape[0] - out_ref.shape[0], LANES), F32)
    padded_ref[...] = jnp.concatenate([one + two, rest], axis=0).astype(BF)


def after_kernel(in_ref, _, out_ref):
    out_ref[...] = in_ref[: out_ref.shape[0]]


def write_kernel(count, wheres, *refs):
    n_scratch = 6
    in_refs = refs[:count]
    first_ref, second_ref, token_ref = refs[-3 - n_scratch * count : -n_scratch * count]
    token_ref[...] = jnp.zeros(token_ref.shape, F32)
    scratch = refs[-n_scratch * count :]
    core, y = lax.axis_index("core"), lax.axis_index("y")

    def begun(n, half):
        wide, last, low, high, tail, sems = scratch[n_scratch * n : n_scratch * (n + 1)]
        own_core, _ = wheres[n]
        at = core if own_core else 1 - core
        rows = in_refs[n][...].astype(F32)
        _, _, size, mid = wide.shape
        _, small, inner = low.shape
        here = pl.ds(pl.multiple_of(at * size, size), size)
        count = 2 if half else 7
        for j in range(count):
            value = rows[j * size : (j + 1) * size]
            for m in range(2):
                wide[m, j] = value[:, m * mid : (m + 1) * mid]
        pairs = [(wide.at[:, :count], second_ref.at[0:2, 7 * half : 7 * half + count, here, :])]
        row = count * size
        if half:
            for j in range(4):
                value = rows[row : row + size]
                row += size
                for m in range(2):
                    last[2 * j + m] = value[:, m * mid : (m + 1) * mid]
            value = rows[row : row + size // 2]
            row += size // 2
            last[8] = jnp.concatenate([value[:, :mid], value[:, mid:]], axis=0)
            pairs.append((last, second_ref.at[2, :, here, :]))
        copies = [pltpu.make_async_copy(src, dst, sems.at[i]) for i, (src, dst) in enumerate(pairs)]
        for copy in copies:
            copy.start()
        here = pl.ds(pl.multiple_of(at * small, small), small)
        places = [(high, 0, 4), (low, 0, 4), (low, 4, 4), (tail, 0, 3)] if half else [(low, 0, 4), (low, 4, 4), (high, 0, 4)]
        for ref, start, number in places:
            value = rows[row : row + small]
            row += small
            for m in range(number):
                ref[start + m] = value[:, m * inner : (m + 1) * inner]
        if half:
            pairs = [
                (high, first_ref.at[4:8, 1, here, :]),
                (low, first_ref.at[0:8, 2, here, :]),
                (tail, first_ref.at[8, :, here, :]),
            ]
        else:
            pairs = [(low, first_ref.at[0:8, 0, here, :]), (high, first_ref.at[0:4, 1, here, :])]
        more = [pltpu.make_async_copy(src, dst, sems.at[2 + i]) for i, (src, dst) in enumerate(pairs)]
        for copy in more:
            copy.start()
        return copies + more

    for half in range(2):

        @pl.when(y == half)
        def _(half=half):
            copies = []
            for n, (_, own_y) in enumerate(wheres):
                copies += begun(n, half if own_y else 1 - half)
            for copy in copies:
                copy.wait()


def swapped(x, axis, first):
    axes = (axis,) if isinstance(axis, str) else axis
    parts, size = lax.axis_size("dp"), lax.axis_size(axis)
    partner = list(range(parts * size))
    for i in partner:
        part, at = divmod(i, size)
        if first <= at < size - (size - first) % 2:
            partner[i] = part * size + (at - first ^ 1) + first
        elif parts % 2 == 0:
            partner[i] = (part ^ 1) * size + at
    return lax.ppermute(x, ("dp", *axes), list(enumerate(partner)))


def across(x, *moves):
    axes = tuple(axis for axis, _ in moves)
    flip = 0
    for axis, bit in moves:
        flip = flip * lax.axis_size(axis) + bit
    return lax.ppermute(x, axes, [(i, i ^ flip) for i in range(lax.axis_size(axes))])


def scattered(rows, cuts):
    halves = [
        jnp.concatenate([x[:, :, :n] if at == 0 else x[:, :, x.shape[2] - n :] for x, n in zip(rows, cut)], axis=2)
        for at, cut in enumerate(cuts)
    ]
    grad = lax.psum_scatter(jnp.stack(halves, axis=2), "dp", scatter_dimension=0, tiled=True)
    core = lax.axis_index("core")
    return tuple(lax.dynamic_index_in_dim(grad, at, 1, False) for at in (core, 1 - core))


def assembled(quarters, size, inner, mid):
    first, second = ([[None, None] for _ in range(27)] for _ in range(2))
    half = size // 2
    for core in range(2):
        for y in range(2):
            rows, row = quarters[core][y].astype(F32), 0
            for j in range(7) if y == 0 else range(7, 13):
                for m, k in enumerate((j, 9 + j) if j < 9 else (2 * j, 2 * j + 1)):
                    second[k][core] = rows[row : row + size, m * mid : (m + 1) * mid]
                row += size
            if y == 1:
                tail = rows[row : row + half]
                second[26][core] = jnp.concatenate([tail[:, :mid], tail[:, mid:]], axis=0)
                row += half
            for j in range(3) if y == 0 else range(3, 7):
                for m in range(4):
                    c, ab = (j // 2, 4 * (j % 2) + m) if j < 6 else (m, 8)
                    if c < 3:
                        first[3 * ab + c][core] = rows[row : row + half, m * inner : (m + 1) * inner]
                row += half
    return tuple(jnp.stack([jnp.concatenate(both, axis=0) for both in grad]) for grad in (first, second))


def per_device(volume, kernel_first, kernel_second, cotangent):
    _, inner, depth, height, width = volume.shape
    mid, out = kernel_first.shape[1], kernel_second.shape[1]
    cells = height * width
    parts = lax.axis_size("dp")
    k1, k2 = jnp.swapaxes(kernel_first, 1, 2), jnp.swapaxes(kernel_second, 1, 2)
    rows = depth * height

    one, two = swapped(volume[0], "dep", 0), swapped(volume[0], "dep", 1)
    (blank,) = call(blank_kernel, [shape((out, 2 * width), BF)], [], flops=3_000_000_000)
    cot_rows, back = call(
        spread_kernel,
        [
            shape((depth, out, cells), BF),
            shape((depth + 2, mid, cells + 2 * width), F32),
        ],
        [cotangent[0], k2, blank],
        [pltpu.VMEM((out * rows, width), F32)],
        flops=1_100_000_000,
    )
    moved, w1, vol = call(
        arrange_kernel,
        [
            shape((depth, 3 * out, cells), BF),
            shape((3 * mid, 9 * inner), BF),
            shape((depth, inner, cells), BF),
        ],
        [cot_rows, k1, volume[0]],
        [pltpu.VMEM((inner * rows, width), F32)],
        flops=500_000_000,
    )
    deep, one, two = call(
        rim_kernel,
        [shape((3 * depth, inner, cells), BF)] + [shape((3 * depth, inner, 2 * width), BF)] * 2,
        [vol, one, two],
        [pltpu.VMEM((inner * rows, width), F32)],
    )
    one, two = swapped(one, HGT, 0), swapped(two, HGT, 1)
    size = mid // parts
    direct = parts == 2 and size % 16 == 0
    halves = lax.axis_size("y")
    cuts = ((7 * size, 3 * size // 2), (13 * size // 2, 2 * size))
    length_second, length_first = 7 * size, 2 * size
    rows_in, rows_out = height - 2, 4
    inner_hidden, inner_second, inner_first = call(
        inner_kernel,
        [
            shape((depth + 2, mid, rows_in * width), BF),
            shape((9 * out, 3 * mid), F32),
            shape((3 * mid, 9 * inner), F32),
        ],
        [deep, w1, moved, back],
        [pltpu.VMEM((3 * mid, (depth + 2) * rows_in * width), BF)],
        flops=1_500_000_000,
    )
    hidden, *first = call(
        functools.partial(outer_kernel, direct),
        [shape((depth + 2, mid, cells + 2 * width), BF)]
        + ([shape((parts, halves, length_first, width), F32)] * 2 if direct else [shape((7, mid, LANES), F32)]),
        [deep, two, one, w1, back, inner_hidden, inner_first],
        [
            pltpu.VMEM((3 * depth, inner, cells + 4 * width), BF),
            pltpu.VMEM((3 * mid, (depth + 2) * rows_out * width), BF),
        ],
        flops=1_000_000_000,
    )
    second = call(
        functools.partial(second_kernel, direct),
        [shape((parts, halves, length_second, width), kind) for kind in (F32, BF)]
        if direct
        else [shape((14, out, LANES), F32)],
        [hidden, moved, inner_second],
        flops=4_000_000_000,
    )
    if direct:
        moves = [(1, 0), (1, 1), (0, 1)]
        grads = [second, first]
    else:
        moves = [(0, 1)]
        blocks = second[0].reshape(14, parts, 2, size, LANES).transpose(1, 2, 0, 3, 4)
        tail = blocks[:, :, 13, :, :mid]
        tail = jnp.concatenate([tail[:, :, : size // 2], tail[:, :, size // 2 :]], axis=-1)
        rows_second = jnp.concatenate([blocks[:, :, :13].reshape(parts, 2, 13 * size, LANES), tail], axis=2)
        blocks = first[0].reshape(7, parts, 2, size // 2, LANES).transpose(1, 2, 0, 3, 4)
        rows_first = blocks.reshape(parts, 2, 7 * (size // 2), LANES)
        grads = [scattered([rows_second, rows_first], cuts)]
    block = (sum(cuts[0]), width)
    kept, *sends = call(
        functools.partial(plane_kernel, moves, cuts),
        [shape(block, F32)] + [shape(block, BF)] * len(moves),
        [x for keep, send in grads for x in (keep, across(send, ("core", 1)))],
    )
    gots = [across(send, ("dp", x), ("y", y)) for send, (x, y) in zip(sends, moves, strict=True)]
    (share,) = call(total_kernel, [shape(block, BF)], [kept, *gots])
    features, token = call(
        features_kernel,
        [shape(cotangent.shape[1:], BF), shape((8, width), F32)],
        [hidden, k2],
        [pltpu.VMEM((out * rows, width), F32)],
        flops=900_000_000,
    )
    gots = [across(share, ("dep", bits)) for bits in (1, 2, 3)]
    share, for_y = call(depth_kernel, [shape(block, BF), shape((block[0] + 16, width), BF)], [share, *gots, token])
    other, far = across(share, ("core", 1)), across(for_y, ("y", 1))
    if size % 16 == 0:
        outs = [shape((9, 3, size, inner), F32), shape((3, 9, 2 * size, mid), F32)]

        def written(quarters, wheres, before=()):
            scratch = [
                pltpu.VMEM((2, 7, size, mid), F32),
                pltpu.VMEM((9, size, mid), F32),
                pltpu.VMEM((8, size // 2, inner), F32),
                pltpu.VMEM((4, size // 2, inner), F32),
                pltpu.VMEM((3, size // 2, inner), F32),
                pltpu.SemaphoreType.DMA((5,)),
            ]
            count = len(quarters)
            return call(
                functools.partial(write_kernel, count, wheres),
                [*outs, shape((8, width), F32)],
                [*quarters, *before],
                scratch * count,
                far=range(count, count + len(before)),
                far_outs=(0, 1),
                aliases={count + n: n for n in range(len(before))},
            )

        *grads, token = written([share, other], [(True, True), (False, True)])
        (far,) = call(after_kernel, [shape(block, BF)], [far, token])
        *grads, _ = written([far], [(True, False)], grads)
        *grads, _ = written([across(far, ("core", 1))], [(False, False)], grads)
        grad_first, grad_second = (grad.reshape(27, *grad.shape[2:]) for grad in grads)
    else:
        core, y = lax.axis_index("core"), lax.axis_index("y")
        stacked = jnp.stack([jnp.stack([share, far[: block[0]]]), jnp.stack([other, across(far[: block[0]], ("core", 1))])])
        quarters = [
            [stacked[lax.bitwise_xor(core, c), lax.bitwise_xor(y, h)] for h in range(2)] for c in range(2)
        ]
        grad_first, grad_second = assembled(quarters, size, inner, mid)
    return features[None], grad_first, grad_second


def solution(mesh):
    dp, dep, hgt = (mesh.shape[axis] for axis in ("dp", "dep", "hgt"))
    split = jax.sharding.Mesh(mesh.devices.reshape(dp, dep, hgt // 2, 2), ("dp", "dep", *HGT))
    block = P("dp", None, "dep", HGT, None)
    return jax.shard_map(
        per_device,
        mesh=split,
        in_specs=(block, P(), P(), block),
        out_specs=(block, P(None, "dp", None), P(None, "dp", None)),
        check_vma=False,
    )
```

```python
import functools

import jax
import jax.numpy as jnp
from jax import lax
from jax.experimental import pallas as pl
from jax.experimental.pallas import tpu as pltpu
from jax.sharding import PartitionSpec as P

BF, F32 = jnp.bfloat16, jnp.float32
LANES = 128
HGT = ("y", "core")
VMEM_BYTES = 28 * 2**20


def call(body, outs, args, scratch=(), flops=0, far=(), far_outs=False, aliases=None):
    moved = sum(x.size * x.dtype.itemsize for x in (*outs, *args))
    return pl.pallas_call(
        body,
        out_shape=outs,
        in_specs=[pl.BlockSpec(memory_space=pl.ANY if n in far else pltpu.VMEM) for n in range(len(args))],
        out_specs=[pl.BlockSpec(memory_space=pl.ANY if far_outs else pltpu.VMEM)] * len(outs),
        scratch_shapes=list(scratch),
        input_output_aliases=aliases or {},
        compiler_params=pltpu.CompilerParams(vmem_limit_bytes=VMEM_BYTES),
        cost_estimate=pl.CostEstimate(flops=flops, bytes_accessed=moved, transcendentals=0),
    )(*args)


def shape(dims, dtype):
    return jax.ShapeDtypeStruct(dims, dtype)


def moved_along_width(x, c):
    if c == 0:
        return x
    pieces = []
    for start in range(0, x.shape[1], LANES):
        piece = x[:, start : start + LANES]
        lane = lax.broadcasted_iota(jnp.int32, piece.shape, 1)
        rolled = pltpu.roll(piece, c % LANES, 1)
        pieces.append(jnp.where(lane == (0 if c == 1 else LANES - 1), 0.0, rolled))
    return pieces[0] if len(pieces) == 1 else jnp.concatenate(pieces, axis=1)


def by_rows(ref, scratch, store):
    channels, depth, height, width = ref.shape
    rows = depth * height
    scratch[...] = ref[...].astype(F32).reshape(channels * rows, width)
    for d in range(depth):
        for h in range(height):
            store(d, h, scratch[pl.ds(d * height + h, channels, stride=rows), :])


def odd(axis):
    return lax.rem(lax.axis_index(axis), 2) == 1


def blank_kernel(out_ref):
    out_ref[...] = jnp.zeros(out_ref.shape, BF)


def spread_kernel(cot_ref, k2_ref, blank_ref, cot_rows_ref, back_ref, scratch):
    out, depth, height, _ = cot_ref.shape
    rows = [[None] * height for _ in range(depth)]

    def store(d, h, row):
        rows[d][h] = row.astype(BF)
        cot_rows_ref[d, :, h * LANES : (h + 1) * LANES] = rows[d][h]

    by_rows(cot_ref, scratch, store)
    mid = k2_ref.shape[1]
    none = blank_ref[...]
    padded = [jnp.concatenate([none, *rows[d], none], axis=1) for d in range(depth)]
    for e in range(depth + 2):
        reached = [(d, e - 1 - d) for d in range(depth) if abs(e - 1 - d) <= 1]
        w = jnp.concatenate(
            [
                k2_ref[9 * (a + 1) + 3 * b : 9 * (a + 1) + 3 * b + 3].reshape(3 * mid, out)
                for _, a in reached
                for b in range(3)
            ],
            axis=1,
        )
        for j in range(0, height + 2, 2):
            rhs = jnp.concatenate(
                [padded[d][:, (j + 2 - b) * LANES : (j + 4 - b) * LANES] for d, _ in reached for b in range(3)], axis=0
            )
            y = jnp.dot(w, rhs, preferred_element_type=F32)
            back = sum(moved_along_width(y[n * mid : (n + 1) * mid], n - 1) for n in range(3))
            back_ref[e, :, j * LANES : (j + 2) * LANES] = back


def as_matrix(ref, c):
    stacked = jnp.concatenate([ref[3 * ab + c] for ab in range(9)], axis=0)
    return stacked.astype(F32).T.astype(BF)


def arrange_kernel(cot_rows_ref, k1_ref, vol_ref, moved_ref, w1_ref, w1_last_ref, own_ref, scratch):
    def store(d, h, row):
        own_ref[d, :, h * LANES : (h + 1) * LANES] = row.astype(BF)

    by_rows(vol_ref, scratch, store)
    depth, out, cells = cot_rows_ref.shape
    for d in range(depth):
        for h in range(0, cells, LANES):
            row = cot_rows_ref[d, :, h : h + LANES]
            for n, c in enumerate((-1, 0, 1)):
                value = row if c == 0 else moved_along_width(row.astype(F32), c).astype(BF)
                moved_ref[d, n * out : (n + 1) * out, h : h + LANES] = value
    mid = k1_ref.shape[2]
    for c in range(3):
        w = as_matrix(k1_ref, c)
        split = w1_ref.shape[1]
        w1_ref[c * mid : (c + 1) * mid, :] = w[:, :split]
        w1_last_ref[:, c * (w.shape[1] - split) : (c + 1) * (w.shape[1] - split)] = w[:, split:]


def sides(axis, one, two):
    me, size = lax.axis_index(axis), lax.axis_size(axis)
    is_odd = odd(axis)
    none = jnp.zeros_like(one)
    before = jnp.where(me == 0, none, jnp.where(is_odd, one, two))
    after = jnp.where(me == size - 1, none, jnp.where(is_odd, two, one))
    return before, after


def rim_kernel(own_ref, one_ref, two_ref, deep_ref, send_one_ref, send_two_ref, scratch):
    depth = own_ref.shape[0]
    deep_ref[depth : 2 * depth] = own_ref[...]
    for at, part in zip((0, 2 * depth), sides("dep", one_ref[...], two_ref[...]), strict=True):

        def store(d, h, row, at=at):
            deep_ref[at + d, :, h * LANES : (h + 1) * LANES] = row.astype(BF)

        by_rows(part, scratch, store)
    n, cells = send_one_ref.shape[2], deep_ref.shape[2]
    first, last = deep_ref[:, :, :n], deep_ref[:, :, cells - n :]
    is_odd = odd(HGT)
    send_one_ref[...] = jnp.where(is_odd, first, last)
    send_two_ref[...] = jnp.where(is_odd, last, first)


def widened(deep_ref, one_ref, two_ref):
    left, right = sides(HGT, one_ref[...], two_ref[...])
    return [jnp.concatenate([left[d], deep_ref[d], right[d]], axis=1) for d in range(deep_ref.shape[0])]


def pack(keep_ref, send_ref, rows_of):
    parts, halves, _, _ = keep_ref.shape
    core = lax.axis_index("core") == 1
    for part in range(parts):
        one, two = ([jnp.concatenate(rows, axis=0) for rows in rows_of(part, c)] for c in range(2))
        for half in range(halves):

            def quarter(grads, half=half):
                lengths = [grad.shape[0] // halves for grad in grads]
                return jnp.concatenate(
                    [grad[half * n : (half + 1) * n] for grad, n in zip(grads, lengths, strict=True)], axis=0
                )

            a, b = quarter(one), quarter(two)
            keep_ref[part, half] = jnp.where(core, b, a)
            send_ref[part, half] = jnp.where(core, a, b).astype(BF)


def folded(tail):
    half = tail.shape[0] // 2
    return jnp.concatenate([tail[:half], tail[half:]], axis=1)


def activated(weights, ref, d, h, depth, heights):
    w1, w1_last = weights
    mid = w1_last.shape[0]
    rhs = neighbours(ref, d, [h], 2)
    n_last = ref.shape[1]
    y = jnp.dot(w1, rhs[: rhs.shape[0] - n_last], preferred_element_type=F32)
    last = rhs[rhs.shape[0] - n_last :].astype(F32)
    last = jnp.concatenate([moved_along_width(last, 1 - n).astype(BF) for n in range(3)], axis=0)
    pre = jnp.dot(w1_last, last, preferred_element_type=F32)
    pre = sum((moved_along_width(y[n * mid : (n + 1) * mid], 1 - n) for n in range(3)), pre)
    s = 1.0 / (1.0 + jnp.exp(-pre))
    dep, deps = lax.axis_index("dep"), lax.axis_size("dep")
    hgt, hgts = lax.axis_index(HGT), lax.axis_size(HGT)
    results = []
    for n, side in enumerate(heights):
        p, q = (x[:, n * LANES : (n + 1) * LANES] for x in (pre, s))
        value, slope = (p * q).astype(BF), q * (1.0 + p * (1.0 - q))
        outside = []
        if d == 0:
            outside.append(dep == 0)
        if d == depth - 1:
            outside.append(dep == deps - 1)
        if side < 0:
            outside.append(hgt == 0)
        if side > 0:
            outside.append(hgt == hgts - 1)
        for far in outside:
            value = jnp.where(far, jnp.zeros_like(value), value)
            slope = jnp.where(far, jnp.zeros_like(slope), slope)
        results.append((value, slope))
    return results


def neighbours(ref, d, starts, count):
    return jnp.concatenate(
        [
            jnp.concatenate(
                [ref[d + a, :, (start + b) * LANES : (start + b + count) * LANES] for start in starts], axis=1
            )
            for a in range(3)
            for b in range(3)
        ],
        axis=0,
    )


def products(left, right):
    return lax.dot_general(left, right, (((1,), (1,)), ((), ())), preferred_element_type=F32)


def shares(delta, n_channels, ref, at):
    for n in range(3):
        ref[n * n_channels : (n + 1) * n_channels, at : at + LANES] = moved_along_width(delta, n - 1).astype(BF)


def inner_kernel(deep_ref, w1_ref, w1_last_ref, moved_ref, back_ref, hidden_ref, second_ref, first_ref, delta_ref):
    weights = w1_ref[...], w1_last_ref[...]
    depth, mid, cells = hidden_ref.shape
    height = cells // LANES
    for d in range(depth):
        for h in range(0, height, 2):
            results = activated(weights, deep_ref, d, h, depth, (0, 0))
            for n, (value, slope) in enumerate(results):
                at = (h + n) * LANES
                hidden_ref[d, :, at : at + LANES] = value
                back = back_ref[d, :, at + 2 * LANES : at + 3 * LANES]
                shares(back * slope, mid, delta_ref, d * cells + at)
    own = depth - 2
    left = jnp.concatenate(
        [
            jnp.concatenate([moved_ref[d, :, (2 - b) * LANES : (2 - b) * LANES + cells] for d in range(own)], axis=1)
            for b in range(3)
        ],
        axis=0,
    )
    right = jnp.concatenate(
        [jnp.concatenate([hidden_ref[d + a] for a in range(3)], axis=0) for d in range(own)], axis=1
    )
    second_ref[...] = products(left, right)
    right = jnp.concatenate([neighbours(deep_ref, d, [0], height) for d in range(depth)], axis=1)
    first_ref[...] = products(right, delta_ref[...])


def outer_kernel(
    deep_ref, two_ref, one_ref, w1_ref, w1_last_ref, back_ref, inner_ref, first_ref, hidden_ref, blocks_ref, rows_ref, delta_ref,
):
    for d, row in enumerate(widened(deep_ref, one_ref, two_ref)):
        rows_ref[d] = row
    weights = w1_ref[...], w1_last_ref[...]
    depth, mid, cells = hidden_ref.shape
    last = cells // LANES - 2
    for d in range(depth):
        hidden_ref[d, :, 2 * LANES : last * LANES] = inner_ref[d]
        for h, sides_of in ((0, (-1, 0)), (last, (0, 1))):
            results = activated(weights, rows_ref, d, h, depth, sides_of)
            for n, (value, slope) in enumerate(results):
                at = (h + n) * LANES
                hidden_ref[d, :, at : at + LANES] = value
                delta = back_ref[d, :, at : at + LANES] * slope
                shares(delta, mid, delta_ref, (4 * d + (2 if h else 0) + n) * LANES)
    right = jnp.concatenate([neighbours(rows_ref, d, [0, last], 2) for d in range(depth)], axis=1)
    total = (first_ref[...] + products(right, delta_ref[...])).T
    inner = rows_ref.shape[1]
    tails = []
    for n in range(3):
        part = total[n * mid : (n + 1) * mid]
        for m in range(2):
            blocks_ref[2 * n + m] = part[:, m * LANES : (m + 1) * LANES]
        tails.append(part[:, 2 * LANES :])
    tails.append(jnp.zeros((mid, LANES - 3 * inner), F32))
    blocks_ref[6] = jnp.concatenate(tails, axis=1)


def second_kernel(direct, hidden_ref, moved_ref, second_ref, first_ref, *grad_refs):
    depth, mid, cells = hidden_ref.shape
    height = cells // LANES
    own = depth - 2
    out = moved_ref.shape[1] // 3
    heads, tails = [], []
    for b in range(3):
        far = [h for h in range(height - 2) if not 2 <= h + b <= height - 3]
        left = jnp.concatenate(
            [moved_ref[d, :, h * LANES : (h + 1) * LANES] for d in range(own) for h in far], axis=1
        )
        right = jnp.concatenate(
            [
                jnp.concatenate([hidden_ref[d + a, :, (h + b) * LANES : (h + b + 1) * LANES] for a in range(3)], axis=0)
                for d in range(own)
                for h in far
            ],
            axis=1,
        )
        total = second_ref[3 * b * out : 3 * (b + 1) * out, :] + products(left, right)
        for c in range(3):
            part = total[c * out : (c + 1) * out]
            heads.append(part[:, :LANES])
            tails.append(part[:, LANES:])
    blocks = heads + [jnp.concatenate(tails[n : n + 2], axis=1) for n in range(0, 8, 2)]
    size = mid // lax.axis_size("dp")

    if not direct:
        for j, block in enumerate([*blocks, jnp.concatenate([tails[8], jnp.zeros_like(tails[8])], axis=1)]):
            grad_refs[0][j] = block
        return

    def rows_of(part, core):
        at = slice((2 * part + core) * size, (2 * part + core + 1) * size)
        second = [block[at] for block in blocks] + [folded(tails[8][at])]
        start = part * size + core * (size // 2)
        return second, [first_ref[j, start : start + size // 2, :] for j in range(first_ref.shape[0])]

    pack(*grad_refs, rows_of)


def features_kernel(hidden_ref, k2_ref, out_ref, token_ref, scratch):
    out, depth, height, _ = out_ref.shape
    w2 = jnp.concatenate([as_matrix(k2_ref, c) for c in range(3)], axis=0)
    for d in range(depth):
        for h in range(0, height, 2):
            rhs = jnp.concatenate(
                [
                    hidden_ref[d + a, :, (h + b) * LANES : (h + b + 2) * LANES]
                    for a in range(3)
                    for b in range(3)
                ],
                axis=0,
            )
            y = jnp.dot(w2, rhs, preferred_element_type=F32)
            total = sum(moved_along_width(y[n * out : (n + 1) * out], 1 - n) for n in range(3))
            for r in range(2):
                row = total[:, r * LANES : (r + 1) * LANES]
                scratch[pl.ds(d * height + h + r, out, stride=depth * height), :] = row
    out_ref[...] = scratch[...].reshape(out_ref.shape).astype(BF)
    token_ref[...] = scratch[:8]


def plane_kernel(moves, keep_ref, got_ref, kept_ref, *send_refs):
    part = lax.rem(lax.axis_index("dp"), keep_ref.shape[0])
    half = lax.axis_index("y")

    def total(x, y):
        at = 1 - part if x else part, 1 - half if y else half
        return keep_ref[at] + got_ref[at].astype(F32)

    kept_ref[...] = total(0, 0)
    for (x, y), send_ref in zip(moves, send_refs, strict=True):
        send_ref[...] = total(x, y).astype(BF)


def total_kernel(kept_ref, *refs):
    *got_refs, out_ref = refs
    value = kept_ref[...]
    for ref in got_refs:
        value = value + ref[...].astype(F32)
    out_ref[...] = value.astype(BF)


def depth_kernel(a_ref, b_ref, c_ref, d_ref, _, out_ref):
    one = a_ref[...].astype(F32) + b_ref[...].astype(F32)
    two = c_ref[...].astype(F32) + d_ref[...].astype(F32)
    out_ref[...] = (one + two).astype(BF)


def order_kernel(own_ref, got_ref, out_ref):
    mine = lax.axis_index("y")
    out_ref[mine] = own_ref[...]
    out_ref[1 - mine] = got_ref[...]


def unpack_kernel(length, theirs, in_ref, *refs):
    first_ref, second_ref, first, second, sems = refs[-5:]
    core = lax.axis_index("core")
    at = 1 - core if theirs else core
    _, size, mid = second.shape
    whole = [in_ref[n].astype(F32) for n in range(in_ref.shape[0])]
    rows = jnp.concatenate([x[:length] for x in whole], axis=0)
    for j in range(13):
        value = rows[j * size : (j + 1) * size]
        for m, k in enumerate((j, 9 + j) if j < 9 else (2 * j, 2 * j + 1)):
            second[k] = value[:, m * mid : (m + 1) * mid]
    value = rows[13 * size : 13 * size + size // 2]
    second[26] = jnp.concatenate([value[:, :mid], value[:, mid:]], axis=0)
    copies = [pltpu.make_async_copy(second, second_ref.at[:, pl.ds(pl.multiple_of(at * size, size), size), :], sems.at[1])]
    copies[0].start()
    _, half, inner = first.shape
    rows = jnp.concatenate([x[length:] for x in whole], axis=0)
    for j in range(7):
        value = rows[j * half : (j + 1) * half]
        for m in range(4):
            c, ab = (j // 2, 4 * (j % 2) + m) if j < 6 else (m, 8)
            if c < 3:
                first[3 * ab + c] = value[:, m * inner : (m + 1) * inner]
    copies.append(
        pltpu.make_async_copy(first, first_ref.at[:, pl.ds(pl.multiple_of(at * half, half), half), :], sems.at[0])
    )
    copies[1].start()
    for copy in copies:
        copy.wait()


def swapped(x, axis, first):
    axes = (axis,) if isinstance(axis, str) else axis
    parts, size = lax.axis_size("dp"), lax.axis_size(axis)
    partner = list(range(parts * size))
    for i in partner:
        part, at = divmod(i, size)
        if first <= at < size - (size - first) % 2:
            partner[i] = part * size + (at - first ^ 1) + first
        elif parts % 2 == 0:
            partner[i] = (part ^ 1) * size + at
    return lax.ppermute(x, ("dp", *axes), list(enumerate(partner)))


def across(x, *moves):
    axes = tuple(axis for axis, _ in moves)
    flip = 0
    for axis, bit in moves:
        flip = flip * lax.axis_size(axis) + bit
    return lax.ppermute(x, axes, [(i, i ^ flip) for i in range(lax.axis_size(axes))])


def scattered(rows, length):
    halves = lax.axis_size("y")
    grad = jnp.pad(rows, ((0, 0), (0, 0), (0, halves * length - rows.shape[2]), (0, 0)))
    grad = lax.psum_scatter(grad, "dp", scatter_dimension=0, tiled=True)
    grad = grad.reshape(1, 2, halves, length, LANES)
    core = lax.axis_index("core")
    return tuple(lax.dynamic_index_in_dim(grad, at, 1, False) for at in (core, 1 - core))


def assembled(own, got, length, size, inner, mid):
    core = lax.axis_index("core")
    both = jnp.stack([own, got]).astype(F32)
    both = jnp.stack([lax.dynamic_index_in_dim(both, at, 0, False) for at in (core, 1 - core)])
    rows = both[:, :, :length].reshape(2, -1, LANES)
    second = [None] * 27
    for j in range(13):
        for m, k in enumerate((j, 9 + j) if j < 9 else (2 * j, 2 * j + 1)):
            second[k] = rows[:, j * size : (j + 1) * size, m * mid : (m + 1) * mid].reshape(2 * size, mid)
    tail = rows[:, 13 * size : 13 * size + size // 2]
    second[26] = jnp.concatenate([tail[:, :, :mid], tail[:, :, mid:]], axis=1).reshape(2 * size, mid)
    rows, half = both[:, :, length:].reshape(2, -1, LANES), size // 2
    first = [None] * 27
    for j in range(7):
        for m in range(4):
            c, ab = (j // 2, 4 * (j % 2) + m) if j < 6 else (m, 8)
            if c < 3:
                value = rows[:, j * half : (j + 1) * half, m * inner : (m + 1) * inner]
                first[3 * ab + c] = value.reshape(size, inner)
    return jnp.stack(first), jnp.stack(second)


def per_device(volume, kernel_first, kernel_second, cotangent):
    _, inner, depth, height, width = volume.shape
    mid, out = kernel_first.shape[1], kernel_second.shape[1]
    cells = height * width
    parts = lax.axis_size("dp")
    k1, k2 = jnp.swapaxes(kernel_first, 1, 2), jnp.swapaxes(kernel_second, 1, 2)
    rows = depth * height

    one, two = swapped(volume[0], "dep", 0), swapped(volume[0], "dep", 1)
    (blank,) = call(blank_kernel, [shape((out, 2 * width), BF)], [], flops=3_000_000_000)
    cot_rows, back = call(
        spread_kernel,
        [
            shape((depth, out, cells), BF),
            shape((depth + 2, mid, cells + 2 * width), F32),
        ],
        [cotangent[0], k2, blank],
        [pltpu.VMEM((out * rows, width), F32)],
        flops=1_100_000_000,
    )
    moved, w1, w1_last, vol = call(
        arrange_kernel,
        [
            shape((depth, 3 * out, cells), BF),
            shape((3 * mid, 8 * inner), BF),
            shape((mid, 3 * inner), BF),
            shape((depth, inner, cells), BF),
        ],
        [cot_rows, k1, volume[0]],
        [pltpu.VMEM((inner * rows, width), F32)],
        flops=500_000_000,
    )
    deep, one, two = call(
        rim_kernel,
        [shape((3 * depth, inner, cells), BF)] + [shape((3 * depth, inner, 2 * width), BF)] * 2,
        [vol, one, two],
        [pltpu.VMEM((inner * rows, width), F32)],
    )
    one, two = swapped(one, HGT, 0), swapped(two, HGT, 1)
    size = mid // parts
    direct = parts == 2 and size % 16 == 0
    halves = lax.axis_size("y")
    length_second, length_first = (-(-units * size // (16 * halves)) * 8 for units in (27, 7))
    rows_in, rows_out = height - 2, 4
    inner_hidden, inner_second, inner_first = call(
        inner_kernel,
        [
            shape((depth + 2, mid, rows_in * width), BF),
            shape((9 * out, 3 * mid), F32),
            shape((9 * inner, 3 * mid), F32),
        ],
        [deep, w1, w1_last, moved, back],
        [pltpu.VMEM((3 * mid, (depth + 2) * rows_in * width), BF)],
        flops=1_500_000_000,
    )
    hidden, first = call(
        outer_kernel,
        [shape((depth + 2, mid, cells + 2 * width), BF), shape((7, mid, LANES), F32)],
        [deep, two, one, w1, w1_last, back, inner_hidden, inner_first],
        [
            pltpu.VMEM((3 * depth, inner, cells + 4 * width), BF),
            pltpu.VMEM((3 * mid, (depth + 2) * rows_out * width), BF),
        ],
        flops=1_000_000_000,
    )
    block = (length_second + length_first, width)
    grads = call(
        functools.partial(second_kernel, direct),
        [shape((parts, halves, *block), kind) for kind in (F32, BF)] if direct else [shape((14, out, LANES), F32)],
        [hidden, moved, inner_second, first],
        flops=4_000_000_000,
    )
    if direct:
        moves = [(1, 0), (0, 1), (1, 1)]
        keep, send = grads
    else:
        moves = [(0, 1)]
        blocks = grads[0].reshape(14, parts, 2, size, LANES).transpose(1, 2, 0, 3, 4)
        tail = blocks[:, :, 13, :, :mid]
        tail = jnp.concatenate([tail[:, :, : size // 2], tail[:, :, size // 2 :]], axis=-1)
        rows_second = jnp.concatenate([blocks[:, :, :13].reshape(parts, 2, 13 * size, LANES), tail], axis=2)
        blocks = first.reshape(7, parts, 2, size // 2, LANES).transpose(1, 2, 0, 3, 4)
        rows_first = blocks.reshape(parts, 2, 7 * (size // 2), LANES)
        pairs = [scattered(rows, n) for rows, n in ((rows_second, length_second), (rows_first, length_first))]
        keep, send = (jnp.concatenate(both, axis=2) for both in zip(*pairs, strict=True))
        send = send.astype(BF)
    kept, *sends = call(
        functools.partial(plane_kernel, moves),
        [shape(block, F32)] + [shape(block, BF)] * len(moves),
        [keep, across(send, ("core", 1))],
    )
    gots = [across(send, ("dp", x), ("y", y)) for send, (x, y) in zip(sends, moves, strict=True)]
    (share,) = call(total_kernel, [shape(block, BF)], [kept, *gots])
    features, token = call(
        features_kernel,
        [shape(cotangent.shape[1:], BF), shape((8, width), F32)],
        [hidden, k2],
        [pltpu.VMEM((out * rows, width), F32)],
        flops=900_000_000,
    )
    gots = [across(share, ("dep", bits)) for bits in (1, 2, 3)]
    (share,) = call(depth_kernel, [shape(block, BF)], [share, *gots, token])
    (own,) = call(order_kernel, [shape((halves, *block), BF)], [share, across(share, ("y", 1))])
    got = across(own, ("core", 1))
    if size % 16 == 0:
        grads = [shape((27, size, inner), F32), shape((27, 2 * size, mid), F32)]
        scratch = [
            pltpu.VMEM((27, size // 2, inner), F32),
            pltpu.VMEM((27, size, mid), F32),
            pltpu.SemaphoreType.DMA((2,)),
        ]
        written = call(functools.partial(unpack_kernel, length_second, False), grads, [own], scratch, far_outs=True)
        grad_first, grad_second = call(
            functools.partial(unpack_kernel, length_second, True),
            grads,
            [got, *written],
            scratch,
            far=(1, 2),
            far_outs=True,
            aliases={1: 0, 2: 1},
        )
    else:
        grad_first, grad_second = assembled(own, got, length_second, size, inner, mid)
    return features[None], grad_first, grad_second


def solution(mesh):
    dp, dep, hgt = (mesh.shape[axis] for axis in ("dp", "dep", "hgt"))
    split = jax.sharding.Mesh(mesh.devices.reshape(dp, dep, hgt // 2, 2), ("dp", "dep", *HGT))
    block = P("dp", None, "dep", HGT, None)
    return jax.shard_map(
        per_device,
        mesh=split,
        in_specs=(block, P(), P(), block),
        out_specs=(block, P(None, "dp", None), P(None, "dp", None)),
        check_vma=False,
    )
```

```python
import functools

import jax
import jax.numpy as jnp
from jax import lax
from jax.experimental import pallas as pl
from jax.experimental.pallas import tpu as pltpu
from jax.sharding import PartitionSpec as P

BF, F32 = jnp.bfloat16, jnp.float32
LANES = 128
HGT = ("y", "core")
VMEM_BYTES = 28 * 2**20


def call(body, outs, args, scratch=(), flops=0, far=(), far_outs=False, aliases=None):
    moved = sum(x.size * x.dtype.itemsize for x in (*outs, *args))
    return pl.pallas_call(
        body,
        out_shape=outs,
        in_specs=[pl.BlockSpec(memory_space=pl.ANY if n in far else pltpu.VMEM) for n in range(len(args))],
        out_specs=[pl.BlockSpec(memory_space=pl.ANY if far_outs else pltpu.VMEM)] * len(outs),
        scratch_shapes=list(scratch),
        input_output_aliases=aliases or {},
        compiler_params=pltpu.CompilerParams(vmem_limit_bytes=VMEM_BYTES),
        cost_estimate=pl.CostEstimate(flops=flops, bytes_accessed=moved, transcendentals=0),
    )(*args)


def shape(dims, dtype):
    return jax.ShapeDtypeStruct(dims, dtype)


def moved_along_width(x, c):
    if c == 0:
        return x
    pieces = []
    for start in range(0, x.shape[1], LANES):
        piece = x[:, start : start + LANES]
        lane = lax.broadcasted_iota(jnp.int32, piece.shape, 1)
        rolled = pltpu.roll(piece, c % LANES, 1)
        pieces.append(jnp.where(lane == (0 if c == 1 else LANES - 1), 0.0, rolled))
    return pieces[0] if len(pieces) == 1 else jnp.concatenate(pieces, axis=1)


def by_rows(ref, scratch, store):
    channels, depth, height, width = ref.shape
    rows = depth * height
    scratch[...] = ref[...].astype(F32).reshape(channels * rows, width)
    for d in range(depth):
        for h in range(height):
            store(d, h, scratch[pl.ds(d * height + h, channels, stride=rows), :])


def odd(axis):
    return lax.rem(lax.axis_index(axis), 2) == 1


def blank_kernel(out_ref):
    out_ref[...] = jnp.zeros(out_ref.shape, BF)


def spread_kernel(cot_ref, k2_ref, blank_ref, cot_rows_ref, back_ref, scratch):
    out, depth, height, _ = cot_ref.shape
    rows = [[None] * height for _ in range(depth)]

    def store(d, h, row):
        rows[d][h] = row.astype(BF)
        cot_rows_ref[d, :, h * LANES : (h + 1) * LANES] = rows[d][h]

    by_rows(cot_ref, scratch, store)
    mid = k2_ref.shape[1]
    none = blank_ref[...]
    padded = [jnp.concatenate([none, *rows[d], none], axis=1) for d in range(depth)]
    for e in range(depth + 2):
        reached = [(d, e - 1 - d) for d in range(depth) if abs(e - 1 - d) <= 1]
        w = jnp.concatenate(
            [
                k2_ref[9 * (a + 1) + 3 * b : 9 * (a + 1) + 3 * b + 3].reshape(3 * mid, out)
                for _, a in reached
                for b in range(3)
            ],
            axis=1,
        )
        for j in range(0, height + 2, 2):
            rhs = jnp.concatenate(
                [padded[d][:, (j + 2 - b) * LANES : (j + 4 - b) * LANES] for d, _ in reached for b in range(3)], axis=0
            )
            y = jnp.dot(w, rhs, preferred_element_type=F32)
            back = sum(moved_along_width(y[n * mid : (n + 1) * mid], n - 1) for n in range(3))
            back_ref[e, :, j * LANES : (j + 2) * LANES] = back


def as_matrix(ref, c):
    stacked = jnp.concatenate([ref[3 * ab + c] for ab in range(9)], axis=0)
    return stacked.astype(F32).T.astype(BF)


def arrange_kernel(cot_rows_ref, k1_ref, vol_ref, moved_ref, w1_ref, own_ref, scratch):
    def store(d, h, row):
        own_ref[d, :, h * LANES : (h + 1) * LANES] = row.astype(BF)

    by_rows(vol_ref, scratch, store)
    depth, out, cells = cot_rows_ref.shape
    for d in range(depth):
        for h in range(0, cells, LANES):
            row = cot_rows_ref[d, :, h : h + LANES]
            for n, c in enumerate((-1, 0, 1)):
                value = row if c == 0 else moved_along_width(row.astype(F32), c).astype(BF)
                moved_ref[d, n * out : (n + 1) * out, h : h + LANES] = value
    mid = k1_ref.shape[2]
    for c in range(3):
        w1_ref[c * mid : (c + 1) * mid, :] = as_matrix(k1_ref, c)


def sides(axis, one, two):
    me, size = lax.axis_index(axis), lax.axis_size(axis)
    is_odd = odd(axis)
    none = jnp.zeros_like(one)
    before = jnp.where(me == 0, none, jnp.where(is_odd, one, two))
    after = jnp.where(me == size - 1, none, jnp.where(is_odd, two, one))
    return before, after


def rim_kernel(own_ref, one_ref, two_ref, deep_ref, send_one_ref, send_two_ref, scratch):
    depth = own_ref.shape[0]
    deep_ref[depth : 2 * depth] = own_ref[...]
    for at, part in zip((0, 2 * depth), sides("dep", one_ref[...], two_ref[...]), strict=True):

        def store(d, h, row, at=at):
            deep_ref[at + d, :, h * LANES : (h + 1) * LANES] = row.astype(BF)

        by_rows(part, scratch, store)
    n, cells = send_one_ref.shape[2], deep_ref.shape[2]
    first, last = deep_ref[:, :, :n], deep_ref[:, :, cells - n :]
    is_odd = odd(HGT)
    send_one_ref[...] = jnp.where(is_odd, first, last)
    send_two_ref[...] = jnp.where(is_odd, last, first)


def widened(deep_ref, one_ref, two_ref):
    left, right = sides(HGT, one_ref[...], two_ref[...])
    return [jnp.concatenate([left[d], deep_ref[d], right[d]], axis=1) for d in range(deep_ref.shape[0])]


def pack(direct, refs, rows_of, blocks):
    if not direct:
        for j, block in enumerate(blocks):
            refs[0][j] = block
        return
    keep_ref, send_ref = refs
    parts, halves, length, _ = keep_ref.shape
    core = lax.axis_index("core") == 1
    for part in range(parts):
        one, two = (jnp.concatenate(rows_of(part, c), axis=0) for c in range(2))
        for half in range(halves):
            at = slice(half * length, (half + 1) * length)
            keep_ref[part, half] = jnp.where(core, two[at], one[at])
            send_ref[part, half] = jnp.where(core, one[at], two[at]).astype(send_ref.dtype)


def folded(tail):
    half = tail.shape[0] // 2
    return jnp.concatenate([tail[:half], tail[half:]], axis=1)


def activated(w1, rhs, d, depth, heights):
    mid = w1.shape[0] // 3
    y = jnp.dot(w1, rhs, preferred_element_type=F32)
    pre = sum(moved_along_width(y[n * mid : (n + 1) * mid], 1 - n) for n in range(3))
    s = 1.0 / (1.0 + jnp.exp(-pre))
    dep, deps = lax.axis_index("dep"), lax.axis_size("dep")
    hgt, hgts = lax.axis_index(HGT), lax.axis_size(HGT)
    results = []
    for n, side in enumerate(heights):
        p, q = (x[:, n * LANES : (n + 1) * LANES] for x in (pre, s))
        value, slope = (p * q).astype(BF), q * (1.0 + p * (1.0 - q))
        outside = []
        if d == 0:
            outside.append(dep == 0)
        if d == depth - 1:
            outside.append(dep == deps - 1)
        if side < 0:
            outside.append(hgt == 0)
        if side > 0:
            outside.append(hgt == hgts - 1)
        for far in outside:
            value = jnp.where(far, jnp.zeros_like(value), value)
            slope = jnp.where(far, jnp.zeros_like(slope), slope)
        results.append((value, slope))
    return results


def neighbours(ref, d, starts, count):
    return jnp.concatenate(
        [
            jnp.concatenate(
                [ref[d + a, :, (start + b) * LANES : (start + b + count) * LANES] for start in starts], axis=1
            )
            for a in range(3)
            for b in range(3)
        ],
        axis=0,
    )


def products(left, right):
    return lax.dot_general(left, right, (((1,), (1,)), ((), ())), preferred_element_type=F32)


def shares(delta, n_channels, ref, at):
    for n in range(3):
        ref[n * n_channels : (n + 1) * n_channels, at : at + LANES] = moved_along_width(delta, n - 1).astype(BF)


def inner_kernel(deep_ref, w1_ref, moved_ref, back_ref, hidden_ref, second_ref, first_ref, delta_ref):
    w1 = w1_ref[...]
    depth, mid, cells = hidden_ref.shape
    height = cells // LANES
    for d in range(depth):
        for h in range(0, height, 2):
            results = activated(w1, neighbours(deep_ref, d, [h], 2), d, depth, (0, 0))
            for n, (value, slope) in enumerate(results):
                at = (h + n) * LANES
                hidden_ref[d, :, at : at + LANES] = value
                back = back_ref[d, :, at + 2 * LANES : at + 3 * LANES]
                shares(back * slope, mid, delta_ref, d * cells + at)
    own = depth - 2
    left = jnp.concatenate(
        [
            jnp.concatenate([moved_ref[d, :, (2 - b) * LANES : (2 - b) * LANES + cells] for d in range(own)], axis=1)
            for b in range(3)
        ],
        axis=0,
    )
    right = jnp.concatenate(
        [jnp.concatenate([hidden_ref[d + a] for a in range(3)], axis=0) for d in range(own)], axis=1
    )
    second_ref[...] = products(left, right)
    right = jnp.concatenate([neighbours(deep_ref, d, [0], height) for d in range(depth)], axis=1)
    first_ref[...] = products(delta_ref[...], right)


def outer_kernel(
    direct, deep_ref, two_ref, one_ref, w1_ref, back_ref, inner_ref, first_ref, hidden_ref, *grad_refs_and_scratch,
):
    *grad_refs, rows_ref, delta_ref = grad_refs_and_scratch
    for d, row in enumerate(widened(deep_ref, one_ref, two_ref)):
        rows_ref[d] = row
    w1 = w1_ref[...]
    depth, mid, cells = hidden_ref.shape
    last = cells // LANES - 2
    for d in range(depth):
        hidden_ref[d, :, 2 * LANES : last * LANES] = inner_ref[d]
        for h, sides_of in ((0, (-1, 0)), (last, (0, 1))):
            results = activated(w1, neighbours(rows_ref, d, [h], 2), d, depth, sides_of)
            for n, (value, slope) in enumerate(results):
                at = (h + n) * LANES
                hidden_ref[d, :, at : at + LANES] = value
                delta = back_ref[d, :, at : at + LANES] * slope
                shares(delta, mid, delta_ref, (4 * d + (2 if h else 0) + n) * LANES)
    right = jnp.concatenate([neighbours(rows_ref, d, [0, last], 2) for d in range(depth)], axis=1)
    total = first_ref[...] + products(delta_ref[...], right)
    inner = rows_ref.shape[1]
    blocks, tails = [], []
    for n in range(3):
        part = total[n * mid : (n + 1) * mid]
        blocks += [part[:, m * LANES : (m + 1) * LANES] for m in range(2)]
        tails.append(part[:, 2 * LANES :])
    tails.append(jnp.zeros((mid, LANES - 3 * inner), F32))
    blocks.append(jnp.concatenate(tails, axis=1))
    size = mid // lax.axis_size("dp")
    half = size // 2

    def rows_of(part, core):
        return [block[part * size + core * half : part * size + (core + 1) * half] for block in blocks]

    pack(direct, grad_refs, rows_of, blocks)


def second_kernel(direct, hidden_ref, moved_ref, second_ref, *grad_refs):
    depth, mid, cells = hidden_ref.shape
    height = cells // LANES
    own = depth - 2
    out = moved_ref.shape[1] // 3
    heads, tails = [], []
    for b in range(3):
        far = [h for h in range(height - 2) if not 2 <= h + b <= height - 3]
        left = jnp.concatenate(
            [moved_ref[d, :, h * LANES : (h + 1) * LANES] for d in range(own) for h in far], axis=1
        )
        right = jnp.concatenate(
            [
                jnp.concatenate([hidden_ref[d + a, :, (h + b) * LANES : (h + b + 1) * LANES] for a in range(3)], axis=0)
                for d in range(own)
                for h in far
            ],
            axis=1,
        )
        total = second_ref[3 * b * out : 3 * (b + 1) * out, :] + products(left, right)
        for c in range(3):
            part = total[c * out : (c + 1) * out]
            heads.append(part[:, :LANES])
            tails.append(part[:, LANES:])
    blocks = heads + [jnp.concatenate(tails[n : n + 2], axis=1) for n in range(0, 8, 2)]
    size = mid // lax.axis_size("dp")

    def rows_of(part, core):
        at = slice((2 * part + core) * size, (2 * part + core + 1) * size)
        return [block[at] for block in blocks] + [folded(tails[8][at])]

    pack(direct, grad_refs, rows_of, [*blocks, jnp.concatenate([tails[8], jnp.zeros_like(tails[8])], axis=1)])


def features_kernel(hidden_ref, k2_ref, out_ref, token_ref, scratch):
    out, depth, height, _ = out_ref.shape
    w2 = jnp.concatenate([as_matrix(k2_ref, c) for c in range(3)], axis=0)
    for d in range(depth):
        for h in range(0, height, 2):
            rhs = jnp.concatenate(
                [
                    hidden_ref[d + a, :, (h + b) * LANES : (h + b + 2) * LANES]
                    for a in range(3)
                    for b in range(3)
                ],
                axis=0,
            )
            y = jnp.dot(w2, rhs, preferred_element_type=F32)
            total = sum(moved_along_width(y[n * out : (n + 1) * out], 1 - n) for n in range(3))
            for r in range(2):
                row = total[:, r * LANES : (r + 1) * LANES]
                scratch[pl.ds(d * height + h + r, out, stride=depth * height), :] = row
    out_ref[...] = scratch[...].reshape(out_ref.shape).astype(BF)
    token_ref[...] = scratch[:8]


def plane_kernel(moves, *refs):
    keep_first, got_first, keep_second, got_second, kept_ref, *send_refs = refs
    part = lax.rem(lax.axis_index("dp"), keep_first.shape[0])
    half = lax.axis_index("y")

    def total(x, y):
        at = 1 - part if x else part, 1 - half if y else half
        return jnp.concatenate([keep_second[at] + got_second[at].astype(F32), keep_first[at] + got_first[at]], axis=0)

    kept_ref[...] = total(0, 0)
    for (x, y), send_ref in zip(moves, send_refs, strict=True):
        send_ref[...] = total(x, y).astype(BF)


def total_kernel(kept_ref, *refs):
    *got_refs, out_ref = refs
    value = kept_ref[...]
    for ref in got_refs:
        value = value + ref[...].astype(F32)
    out_ref[...] = value.astype(BF)


def depth_kernel(a_ref, b_ref, c_ref, d_ref, _, out_ref):
    one = a_ref[...].astype(F32) + b_ref[...].astype(F32)
    two = c_ref[...].astype(F32) + d_ref[...].astype(F32)
    out_ref[...] = (one + two).astype(BF)


def order_kernel(own_ref, got_ref, out_ref):
    mine = lax.axis_index("y")
    out_ref[mine] = own_ref[...]
    out_ref[1 - mine] = got_ref[...]


def unpack_kernel(length, theirs, in_ref, *refs):
    first_ref, second_ref, first, second, sems = refs[-5:]
    core = lax.axis_index("core")
    at = 1 - core if theirs else core
    _, size, mid = second.shape
    whole = [in_ref[n].astype(F32) for n in range(in_ref.shape[0])]
    rows = jnp.concatenate([x[:length] for x in whole], axis=0)
    for j in range(13):
        value = rows[j * size : (j + 1) * size]
        for m, k in enumerate((j, 9 + j) if j < 9 else (2 * j, 2 * j + 1)):
            second[k] = value[:, m * mid : (m + 1) * mid]
    value = rows[13 * size : 13 * size + size // 2]
    second[26] = jnp.concatenate([value[:, :mid], value[:, mid:]], axis=0)
    copies = [pltpu.make_async_copy(second, second_ref.at[:, pl.ds(pl.multiple_of(at * size, size), size), :], sems.at[1])]
    copies[0].start()
    _, half, inner = first.shape
    rows = jnp.concatenate([x[length:] for x in whole], axis=0)
    for j in range(7):
        value = rows[j * half : (j + 1) * half]
        for m in range(4):
            c, ab = (j // 2, 4 * (j % 2) + m) if j < 6 else (m, 8)
            if c < 3:
                first[3 * ab + c] = value[:, m * inner : (m + 1) * inner]
    copies.append(
        pltpu.make_async_copy(first, first_ref.at[:, pl.ds(pl.multiple_of(at * half, half), half), :], sems.at[0])
    )
    copies[1].start()
    for copy in copies:
        copy.wait()


def swapped(x, axis, first):
    axes = (axis,) if isinstance(axis, str) else axis
    parts, size = lax.axis_size("dp"), lax.axis_size(axis)
    partner = list(range(parts * size))
    for i in partner:
        part, at = divmod(i, size)
        if first <= at < size - (size - first) % 2:
            partner[i] = part * size + (at - first ^ 1) + first
        elif parts % 2 == 0:
            partner[i] = (part ^ 1) * size + at
    return lax.ppermute(x, ("dp", *axes), list(enumerate(partner)))


def across(x, *moves):
    axes = tuple(axis for axis, _ in moves)
    flip = 0
    for axis, bit in moves:
        flip = flip * lax.axis_size(axis) + bit
    return lax.ppermute(x, axes, [(i, i ^ flip) for i in range(lax.axis_size(axes))])


def scattered(rows, length):
    halves = lax.axis_size("y")
    grad = jnp.pad(rows, ((0, 0), (0, 0), (0, halves * length - rows.shape[2]), (0, 0)))
    grad = lax.psum_scatter(grad, "dp", scatter_dimension=0, tiled=True)
    grad = grad.reshape(1, 2, halves, length, LANES)
    core = lax.axis_index("core")
    return tuple(lax.dynamic_index_in_dim(grad, at, 1, False) for at in (core, 1 - core))


def assembled(own, got, length, size, inner, mid):
    core = lax.axis_index("core")
    both = jnp.stack([own, got]).astype(F32)
    both = jnp.stack([lax.dynamic_index_in_dim(both, at, 0, False) for at in (core, 1 - core)])
    rows = both[:, :, :length].reshape(2, -1, LANES)
    second = [None] * 27
    for j in range(13):
        for m, k in enumerate((j, 9 + j) if j < 9 else (2 * j, 2 * j + 1)):
            second[k] = rows[:, j * size : (j + 1) * size, m * mid : (m + 1) * mid].reshape(2 * size, mid)
    tail = rows[:, 13 * size : 13 * size + size // 2]
    second[26] = jnp.concatenate([tail[:, :, :mid], tail[:, :, mid:]], axis=1).reshape(2 * size, mid)
    rows, half = both[:, :, length:].reshape(2, -1, LANES), size // 2
    first = [None] * 27
    for j in range(7):
        for m in range(4):
            c, ab = (j // 2, 4 * (j % 2) + m) if j < 6 else (m, 8)
            if c < 3:
                value = rows[:, j * half : (j + 1) * half, m * inner : (m + 1) * inner]
                first[3 * ab + c] = value.reshape(size, inner)
    return jnp.stack(first), jnp.stack(second)


def per_device(volume, kernel_first, kernel_second, cotangent):
    _, inner, depth, height, width = volume.shape
    mid, out = kernel_first.shape[1], kernel_second.shape[1]
    cells = height * width
    parts = lax.axis_size("dp")
    k1, k2 = jnp.swapaxes(kernel_first, 1, 2), jnp.swapaxes(kernel_second, 1, 2)
    rows = depth * height

    one, two = swapped(volume[0], "dep", 0), swapped(volume[0], "dep", 1)
    (blank,) = call(blank_kernel, [shape((out, 2 * width), BF)], [], flops=3_000_000_000)
    cot_rows, back = call(
        spread_kernel,
        [
            shape((depth, out, cells), BF),
            shape((depth + 2, mid, cells + 2 * width), F32),
        ],
        [cotangent[0], k2, blank],
        [pltpu.VMEM((out * rows, width), F32)],
        flops=1_100_000_000,
    )
    moved, w1, vol = call(
        arrange_kernel,
        [
            shape((depth, 3 * out, cells), BF),
            shape((3 * mid, 9 * inner), BF),
            shape((depth, inner, cells), BF),
        ],
        [cot_rows, k1, volume[0]],
        [pltpu.VMEM((inner * rows, width), F32)],
        flops=500_000_000,
    )
    deep, one, two = call(
        rim_kernel,
        [shape((3 * depth, inner, cells), BF)] + [shape((3 * depth, inner, 2 * width), BF)] * 2,
        [vol, one, two],
        [pltpu.VMEM((inner * rows, width), F32)],
    )
    one, two = swapped(one, HGT, 0), swapped(two, HGT, 1)
    size = mid // parts
    direct = parts == 2 and size % 16 == 0
    halves = lax.axis_size("y")
    length_second, length_first = (-(-units * size // (16 * halves)) * 8 for units in (27, 7))
    rows_in, rows_out = height - 2, 4
    inner_hidden, inner_second, inner_first = call(
        inner_kernel,
        [
            shape((depth + 2, mid, rows_in * width), BF),
            shape((9 * out, 3 * mid), F32),
            shape((3 * mid, 9 * inner), F32),
        ],
        [deep, w1, moved, back],
        [pltpu.VMEM((3 * mid, (depth + 2) * rows_in * width), BF)],
        flops=1_500_000_000,
    )
    hidden, *first = call(
        functools.partial(outer_kernel, direct),
        [shape((depth + 2, mid, cells + 2 * width), BF)]
        + ([shape((parts, halves, length_first, width), F32)] * 2 if direct else [shape((7, mid, LANES), F32)]),
        [deep, two, one, w1, back, inner_hidden, inner_first],
        [
            pltpu.VMEM((3 * depth, inner, cells + 4 * width), BF),
            pltpu.VMEM((3 * mid, (depth + 2) * rows_out * width), BF),
        ],
        flops=1_000_000_000,
    )
    second = call(
        functools.partial(second_kernel, direct),
        [shape((parts, halves, length_second, width), kind) for kind in (F32, BF)]
        if direct
        else [shape((14, out, LANES), F32)],
        [hidden, moved, inner_second],
        flops=4_000_000_000,
    )
    if direct:
        moves = [(1, 0), (0, 1), (1, 1)]
    else:
        moves = [(0, 1)]
        blocks = second[0].reshape(14, parts, 2, size, LANES).transpose(1, 2, 0, 3, 4)
        tail = blocks[:, :, 13, :, :mid]
        tail = jnp.concatenate([tail[:, :, : size // 2], tail[:, :, size // 2 :]], axis=-1)
        rows_second = jnp.concatenate([blocks[:, :, :13].reshape(parts, 2, 13 * size, LANES), tail], axis=2)
        second = scattered(rows_second, length_second)
        blocks = first[0].reshape(7, parts, 2, size // 2, LANES).transpose(1, 2, 0, 3, 4)
        first = scattered(blocks.reshape(parts, 2, 7 * (size // 2), LANES), length_first)
    block = (length_second + length_first, width)
    kept, *sends = call(
        functools.partial(plane_kernel, moves),
        [shape(block, F32)] + [shape(block, BF)] * len(moves),
        [x for keep, send in (first, second) for x in (keep, across(send, ("core", 1)))],
    )
    gots = [across(send, ("dp", x), ("y", y)) for send, (x, y) in zip(sends, moves, strict=True)]
    (share,) = call(total_kernel, [shape(block, BF)], [kept, *gots])
    features, token = call(
        features_kernel,
        [shape(cotangent.shape[1:], BF), shape((8, width), F32)],
        [hidden, k2],
        [pltpu.VMEM((out * rows, width), F32)],
        flops=900_000_000,
    )
    gots = [across(share, ("dep", bits)) for bits in (1, 3, 2)]
    (share,) = call(depth_kernel, [shape(block, BF)], [share, *gots, token])
    (own,) = call(order_kernel, [shape((halves, *block), BF)], [share, across(share, ("y", 1))])
    got = across(own, ("core", 1))
    if size % 16 == 0:
        grads = [shape((27, size, inner), F32), shape((27, 2 * size, mid), F32)]
        scratch = [
            pltpu.VMEM((27, size // 2, inner), F32),
            pltpu.VMEM((27, size, mid), F32),
            pltpu.SemaphoreType.DMA((2,)),
        ]
        written = call(functools.partial(unpack_kernel, length_second, False), grads, [own], scratch, far_outs=True)
        grad_first, grad_second = call(
            functools.partial(unpack_kernel, length_second, True),
            grads,
            [got, *written],
            scratch,
            far=(1, 2),
            far_outs=True,
            aliases={1: 0, 2: 1},
        )
    else:
        grad_first, grad_second = assembled(own, got, length_second, size, inner, mid)
    return features[None], grad_first, grad_second


def solution(mesh):
    dp, dep, hgt = (mesh.shape[axis] for axis in ("dp", "dep", "hgt"))
    split = jax.sharding.Mesh(mesh.devices.reshape(dp, dep, hgt // 2, 2), ("dp", "dep", *HGT))
    block = P("dp", None, "dep", HGT, None)
    return jax.shard_map(
        per_device,
        mesh=split,
        in_specs=(block, P(), P(), block),
        out_specs=(block, P(None, "dp", None), P(None, "dp", None)),
        check_vma=False,
    )
```

```python
import functools

import jax
import jax.numpy as jnp
from jax import lax
from jax.experimental import pallas as pl
from jax.experimental.pallas import tpu as pltpu
from jax.sharding import PartitionSpec as P

BF, F32 = jnp.bfloat16, jnp.float32
LANES = 128
HGT = ("y", "core")
VMEM_BYTES = 28 * 2**20


def call(body, outs, args, scratch=(), flops=0, far=(), far_outs=False, aliases=None):
    moved = sum(x.size * x.dtype.itemsize for x in (*outs, *args))
    return pl.pallas_call(
        body,
        out_shape=outs,
        in_specs=[pl.BlockSpec(memory_space=pl.ANY if n in far else pltpu.VMEM) for n in range(len(args))],
        out_specs=[pl.BlockSpec(memory_space=pl.ANY if far_outs else pltpu.VMEM)] * len(outs),
        scratch_shapes=list(scratch),
        input_output_aliases=aliases or {},
        compiler_params=pltpu.CompilerParams(vmem_limit_bytes=VMEM_BYTES),
        cost_estimate=pl.CostEstimate(flops=flops, bytes_accessed=moved, transcendentals=0),
    )(*args)


def shape(dims, dtype):
    return jax.ShapeDtypeStruct(dims, dtype)


def moved_along_width(x, c):
    if c == 0:
        return x
    pieces = []
    for start in range(0, x.shape[1], LANES):
        piece = x[:, start : start + LANES]
        lane = lax.broadcasted_iota(jnp.int32, piece.shape, 1)
        rolled = pltpu.roll(piece, c % LANES, 1)
        pieces.append(jnp.where(lane == (0 if c == 1 else LANES - 1), 0.0, rolled))
    return pieces[0] if len(pieces) == 1 else jnp.concatenate(pieces, axis=1)


def by_rows(ref, scratch, store):
    channels, depth, height, width = ref.shape
    rows = depth * height
    scratch[...] = ref[...].astype(F32).reshape(channels * rows, width)
    for d in range(depth):
        for h in range(height):
            store(d, h, scratch[pl.ds(d * height + h, channels, stride=rows), :])


def odd(axis):
    return lax.rem(lax.axis_index(axis), 2) == 1


def blank_kernel(out_ref):
    out_ref[...] = jnp.zeros(out_ref.shape, BF)


def own_kernel(vol_ref, _, out_ref, scratch):
    def store(d, h, row):
        out_ref[d, :, h * LANES : (h + 1) * LANES] = row.astype(BF)

    by_rows(vol_ref, scratch, store)


def spread_kernel(cot_ref, k2_ref, blank_ref, _, cot_rows_ref, back_ref, scratch):
    out, depth, height, _ = cot_ref.shape
    rows = [[None] * height for _ in range(depth)]

    def store(d, h, row):
        rows[d][h] = row.astype(BF)
        cot_rows_ref[d, :, h * LANES : (h + 1) * LANES] = rows[d][h]

    by_rows(cot_ref, scratch, store)
    mid = k2_ref.shape[1]
    none = blank_ref[...]
    padded = [jnp.concatenate([none, *rows[d], none], axis=1) for d in range(depth)]
    for e in range(depth + 2):
        reached = [(d, e - 1 - d) for d in range(depth) if abs(e - 1 - d) <= 1]
        w = jnp.concatenate(
            [
                k2_ref[9 * (a + 1) + 3 * b : 9 * (a + 1) + 3 * b + 3].reshape(3 * mid, out)
                for _, a in reached
                for b in range(3)
            ],
            axis=1,
        )
        for j in range(0, height + 2, 2):
            rhs = jnp.concatenate(
                [padded[d][:, (j + 2 - b) * LANES : (j + 4 - b) * LANES] for d, _ in reached for b in range(3)], axis=0
            )
            y = jnp.dot(w, rhs, preferred_element_type=F32)
            back = sum(moved_along_width(y[n * mid : (n + 1) * mid], n - 1) for n in range(3))
            back_ref[e, :, j * LANES : (j + 2) * LANES] = back


def as_matrix(ref, c):
    stacked = jnp.concatenate([ref[3 * ab + c] for ab in range(9)], axis=0)
    return stacked.astype(F32).T.astype(BF)


def arrange_kernel(cot_rows_ref, k1_ref, _, moved_ref, w1_ref, w1_last_ref):
    depth, out, cells = cot_rows_ref.shape
    for d in range(depth):
        for h in range(0, cells, LANES):
            row = cot_rows_ref[d, :, h : h + LANES]
            for n, c in enumerate((-1, 0, 1)):
                value = row if c == 0 else moved_along_width(row.astype(F32), c).astype(BF)
                moved_ref[d, n * out : (n + 1) * out, h : h + LANES] = value
    mid = k1_ref.shape[2]
    for c in range(3):
        w = as_matrix(k1_ref, c)
        split = w1_ref.shape[1]
        w1_ref[c * mid : (c + 1) * mid, :] = w[:, :split]
        w1_last_ref[:, c * (w.shape[1] - split) : (c + 1) * (w.shape[1] - split)] = w[:, split:]


def sides(axis, one, two):
    me, size = lax.axis_index(axis), lax.axis_size(axis)
    is_odd = odd(axis)
    none = jnp.zeros_like(one)
    before = jnp.where(me == 0, none, jnp.where(is_odd, one, two))
    after = jnp.where(me == size - 1, none, jnp.where(is_odd, two, one))
    return before, after


def extend(deep_ref, one_ref, two_ref, scratch):
    depth = deep_ref.shape[0] // 3
    for at, part in zip((0, 2 * depth), sides("dep", one_ref[...], two_ref[...]), strict=True):

        def store(d, h, row, at=at):
            deep_ref[at + d, :, h * LANES : (h + 1) * LANES] = row.astype(BF)

        by_rows(part, scratch, store)


def edges(deep_ref, n):
    cells = deep_ref.shape[2]
    return deep_ref[:, :, :n], deep_ref[:, :, cells - n :]


def inside():
    hgt, hgts = lax.axis_index(HGT), lax.axis_size(HGT)
    return jnp.logical_and(hgt > 0, hgt < hgts - 1)


def early_rim_kernel(own_ref, one_ref, two_ref, _, deep_ref, send_ref, scratch):
    depth = own_ref.shape[0]
    deep_ref[depth : 2 * depth] = own_ref[...]
    extend(deep_ref, one_ref, two_ref, scratch)
    first, last = edges(deep_ref, send_ref.shape[2])
    send_ref[...] = jnp.where(odd(HGT), last, first)


def late_rim_kernel(early_ref, one_ref, two_ref, _, deep_ref, send_ref):
    deep_ref[...] = early_ref[...]

    depth = one_ref.shape[0]

    @pl.when(jnp.logical_not(inside()))
    def _():
        deep_ref[:depth], deep_ref[2 * depth :] = sides("dep", one_ref[...], two_ref[...])

    first, last = edges(deep_ref, send_ref.shape[2])
    send_ref[...] = jnp.where(odd(HGT), first, last)


def widened(deep_ref, one_ref, two_ref):
    left, right = sides(HGT, one_ref[...], two_ref[...])
    return [jnp.concatenate([left[d], deep_ref[d], right[d]], axis=1) for d in range(deep_ref.shape[0])]


def pack(keep_ref, send_ref, rows_of):
    parts, halves, _, _ = keep_ref.shape
    core = lax.axis_index("core") == 1
    for part in range(parts):
        one, two = ([jnp.concatenate(rows, axis=0) for rows in rows_of(part, c)] for c in range(2))
        for half in range(halves):

            def quarter(grads, half=half):
                lengths = [grad.shape[0] // halves for grad in grads]
                return jnp.concatenate(
                    [grad[half * n : (half + 1) * n] for grad, n in zip(grads, lengths, strict=True)], axis=0
                )

            a, b = quarter(one), quarter(two)
            keep_ref[part, half] = jnp.where(core, b, a)
            send_ref[part, half] = jnp.where(core, a, b).astype(BF)


def folded(tail):
    half = tail.shape[0] // 2
    return jnp.concatenate([tail[:half], tail[half:]], axis=1)


def activated(weights, ref, d, h, depth, heights):
    w1, w1_last = weights
    mid = w1_last.shape[0]
    rhs = neighbours(ref, d, [h], 2)
    n_last = ref.shape[1]
    y = jnp.dot(w1, rhs[: rhs.shape[0] - n_last], preferred_element_type=F32)
    last = rhs[rhs.shape[0] - n_last :].astype(F32)
    last = jnp.concatenate([moved_along_width(last, 1 - n).astype(BF) for n in range(3)], axis=0)
    pre = jnp.dot(w1_last, last, preferred_element_type=F32)
    pre = sum((moved_along_width(y[n * mid : (n + 1) * mid], 1 - n) for n in range(3)), pre)
    s = 1.0 / (1.0 + jnp.exp(-pre))
    dep, deps = lax.axis_index("dep"), lax.axis_size("dep")
    hgt, hgts = lax.axis_index(HGT), lax.axis_size(HGT)
    results = []
    for n, side in enumerate(heights):
        p, q = (x[:, n * LANES : (n + 1) * LANES] for x in (pre, s))
        value, slope = (p * q).astype(BF), q * (1.0 + p * (1.0 - q))
        outside = []
        if d == 0:
            outside.append(dep == 0)
        if d == depth - 1:
            outside.append(dep == deps - 1)
        if side < 0:
            outside.append(hgt == 0)
        if side > 0:
            outside.append(hgt == hgts - 1)
        for far in outside:
            value = jnp.where(far, jnp.zeros_like(value), value)
            slope = jnp.where(far, jnp.zeros_like(slope), slope)
        results.append((value, slope))
    return results


def neighbours(ref, d, starts, count):
    return jnp.concatenate(
        [
            jnp.concatenate(
                [ref[d + a, :, (start + b) * LANES : (start + b + count) * LANES] for start in starts], axis=1
            )
            for a in range(3)
            for b in range(3)
        ],
        axis=0,
    )


def products(left, right):
    return lax.dot_general(left, right, (((1,), (1,)), ((), ())), preferred_element_type=F32)


def shares(delta, n_channels, ref, at):
    for n in range(3):
        ref[n * n_channels : (n + 1) * n_channels, at : at + LANES] = moved_along_width(delta, n - 1).astype(BF)


def inner_kernel(deep_ref, w1_ref, w1_last_ref, moved_ref, back_ref, hidden_ref, second_ref, first_ref, delta_ref):
    weights = w1_ref[...], w1_last_ref[...]
    depth, mid, cells = hidden_ref.shape
    height = cells // LANES
    for d in range(depth):
        for h in range(0, height, 2):
            results = activated(weights, deep_ref, d, h, depth, (0, 0))
            for n, (value, slope) in enumerate(results):
                at = (h + n) * LANES
                hidden_ref[d, :, at : at + LANES] = value
                back = back_ref[d, :, at + 2 * LANES : at + 3 * LANES]
                shares(back * slope, mid, delta_ref, d * cells + at)
    own = depth - 2
    left = jnp.concatenate(
        [
            jnp.concatenate([moved_ref[d, :, (2 - b) * LANES : (2 - b) * LANES + cells] for d in range(own)], axis=1)
            for b in range(3)
        ],
        axis=0,
    )
    right = jnp.concatenate(
        [jnp.concatenate([hidden_ref[d + a] for a in range(3)], axis=0) for d in range(own)], axis=1
    )
    second_ref[...] = products(left, right)
    right = jnp.concatenate([neighbours(deep_ref, d, [0], height) for d in range(depth)], axis=1)
    first_ref[...] = products(right, delta_ref[...])


def outer_kernel(
    deep_ref, two_ref, one_ref, w1_ref, w1_last_ref, back_ref, inner_ref, first_ref, hidden_ref, blocks_ref, rows_ref, delta_ref,
):
    for d, row in enumerate(widened(deep_ref, one_ref, two_ref)):
        rows_ref[d] = row
    weights = w1_ref[...], w1_last_ref[...]
    depth, mid, cells = hidden_ref.shape
    last = cells // LANES - 2
    for d in range(depth):
        hidden_ref[d, :, 2 * LANES : last * LANES] = inner_ref[d]
        for h, sides_of in ((0, (-1, 0)), (last, (0, 1))):
            results = activated(weights, rows_ref, d, h, depth, sides_of)
            for n, (value, slope) in enumerate(results):
                at = (h + n) * LANES
                hidden_ref[d, :, at : at + LANES] = value
                delta = back_ref[d, :, at : at + LANES] * slope
                shares(delta, mid, delta_ref, (4 * d + (2 if h else 0) + n) * LANES)
    right = jnp.concatenate([neighbours(rows_ref, d, [0, last], 2) for d in range(depth)], axis=1)
    total = (first_ref[...] + products(right, delta_ref[...])).T
    inner = rows_ref.shape[1]
    tails = []
    for n in range(3):
        part = total[n * mid : (n + 1) * mid]
        for m in range(2):
            blocks_ref[2 * n + m] = part[:, m * LANES : (m + 1) * LANES]
        tails.append(part[:, 2 * LANES :])
    tails.append(jnp.zeros((mid, LANES - 3 * inner), F32))
    blocks_ref[6] = jnp.concatenate(tails, axis=1)


def second_kernel(direct, hidden_ref, moved_ref, second_ref, first_ref, *grad_refs):
    depth, mid, cells = hidden_ref.shape
    height = cells // LANES
    own = depth - 2
    out = moved_ref.shape[1] // 3
    heads, tails = [], []
    for b in range(3):
        far = [h for h in range(height - 2) if not 2 <= h + b <= height - 3]
        left = jnp.concatenate(
            [moved_ref[d, :, h * LANES : (h + 1) * LANES] for d in range(own) for h in far], axis=1
        )
        right = jnp.concatenate(
            [
                jnp.concatenate([hidden_ref[d + a, :, (h + b) * LANES : (h + b + 1) * LANES] for a in range(3)], axis=0)
                for d in range(own)
                for h in far
            ],
            axis=1,
        )
        total = second_ref[3 * b * out : 3 * (b + 1) * out, :] + products(left, right)
        for c in range(3):
            part = total[c * out : (c + 1) * out]
            heads.append(part[:, :LANES])
            tails.append(part[:, LANES:])
    blocks = heads + [jnp.concatenate(tails[n : n + 2], axis=1) for n in range(0, 8, 2)]
    size = mid // lax.axis_size("dp")

    if not direct:
        for j, block in enumerate([*blocks, jnp.concatenate([tails[8], jnp.zeros_like(tails[8])], axis=1)]):
            grad_refs[0][j] = block
        return

    def rows_of(part, core):
        at = slice((2 * part + core) * size, (2 * part + core + 1) * size)
        second = [block[at] for block in blocks] + [folded(tails[8][at])]
        start = part * size + core * (size // 2)
        return second, [first_ref[j, start : start + size // 2, :] for j in range(first_ref.shape[0])]

    pack(*grad_refs, rows_of)


def features_kernel(hidden_ref, k2_ref, out_ref, token_ref, scratch):
    out, depth, height, _ = out_ref.shape
    w2 = jnp.concatenate([as_matrix(k2_ref, c) for c in range(3)], axis=0)
    for d in range(depth):
        for h in range(0, height, 2):
            rhs = jnp.concatenate(
                [
                    hidden_ref[d + a, :, (h + b) * LANES : (h + b + 2) * LANES]
                    for a in range(3)
                    for b in range(3)
                ],
                axis=0,
            )
            y = jnp.dot(w2, rhs, preferred_element_type=F32)
            total = sum(moved_along_width(y[n * out : (n + 1) * out], 1 - n) for n in range(3))
            for r in range(2):
                row = total[:, r * LANES : (r + 1) * LANES]
                scratch[pl.ds(d * height + h + r, out, stride=depth * height), :] = row
    out_ref[...] = scratch[...].reshape(out_ref.shape).astype(BF)
    token_ref[...] = scratch[:8]


def plane_kernel(moves, keep_ref, got_ref, kept_ref, *send_refs):
    part = lax.rem(lax.axis_index("dp"), keep_ref.shape[0])
    half = lax.axis_index("y")

    def total(x, y):
        at = 1 - part if x else part, 1 - half if y else half
        return keep_ref[at] + got_ref[at].astype(F32)

    kept_ref[...] = total(0, 0)
    for (x, y), send_ref in zip(moves, send_refs, strict=True):
        send_ref[...] = total(x, y).astype(BF)


def total_kernel(kept_ref, *refs):
    *got_refs, out_ref = refs
    value = kept_ref[...]
    for ref in got_refs:
        value = value + ref[...].astype(F32)
    out_ref[...] = value.astype(BF)


def depth_kernel(a_ref, b_ref, c_ref, d_ref, _, out_ref):
    one = a_ref[...].astype(F32) + b_ref[...].astype(F32)
    two = c_ref[...].astype(F32) + d_ref[...].astype(F32)
    out_ref[...] = (one + two).astype(BF)


def order_kernel(own_ref, got_ref, out_ref):
    mine = lax.axis_index("y")
    out_ref[mine] = own_ref[...]
    out_ref[1 - mine] = got_ref[...]


def unpack_kernel(length, theirs, in_ref, *refs):
    first_ref, second_ref, first, second, sems = refs[-5:]
    core = lax.axis_index("core")
    at = 1 - core if theirs else core
    _, size, mid = second.shape
    whole = [in_ref[n].astype(F32) for n in range(in_ref.shape[0])]
    rows = jnp.concatenate([x[:length] for x in whole], axis=0)
    for j in range(13):
        value = rows[j * size : (j + 1) * size]
        for m, k in enumerate((j, 9 + j) if j < 9 else (2 * j, 2 * j + 1)):
            second[k] = value[:, m * mid : (m + 1) * mid]
    value = rows[13 * size : 13 * size + size // 2]
    second[26] = jnp.concatenate([value[:, :mid], value[:, mid:]], axis=0)
    copies = [pltpu.make_async_copy(second, second_ref.at[:, pl.ds(pl.multiple_of(at * size, size), size), :], sems.at[1])]
    copies[0].start()
    _, half, inner = first.shape
    rows = jnp.concatenate([x[length:] for x in whole], axis=0)
    for j in range(7):
        value = rows[j * half : (j + 1) * half]
        for m in range(4):
            c, ab = (j // 2, 4 * (j % 2) + m) if j < 6 else (m, 8)
            if c < 3:
                first[3 * ab + c] = value[:, m * inner : (m + 1) * inner]
    copies.append(
        pltpu.make_async_copy(first, first_ref.at[:, pl.ds(pl.multiple_of(at * half, half), half), :], sems.at[0])
    )
    copies[1].start()
    for copy in copies:
        copy.wait()


def swapped(x, axis, first):
    axes = (axis,) if isinstance(axis, str) else axis
    parts, size = lax.axis_size("dp"), lax.axis_size(axis)
    partner = list(range(parts * size))
    for i in partner:
        part, at = divmod(i, size)
        if first <= at < size - (size - first) % 2:
            partner[i] = part * size + (at - first ^ 1) + first
        elif parts % 2 == 0:
            partner[i] = (part ^ 1) * size + at
    return lax.ppermute(x, ("dp", *axes), list(enumerate(partner)))


def along_depth(x, first, inner):
    parts, deps, hgts = (lax.axis_size(axis) for axis in ("dp", "dep", HGT))
    partner = list(range(parts * deps * hgts))
    for i in partner:
        part, at = divmod(i, deps * hgts)
        z, h = divmod(at, hgts)
        if (0 < h < hgts - 1) == inner and first <= z < deps - (deps - first) % 2:
            partner[i] = (part * deps + (z - first ^ 1) + first) * hgts + h
        elif parts % 2 == 0:
            partner[i] = ((part ^ 1) * deps + z) * hgts + h
    return lax.ppermute(x, ("dp", "dep", *HGT), list(enumerate(partner)))


def across(x, *moves):
    axes = tuple(axis for axis, _ in moves)
    flip = 0
    for axis, bit in moves:
        flip = flip * lax.axis_size(axis) + bit
    return lax.ppermute(x, axes, [(i, i ^ flip) for i in range(lax.axis_size(axes))])


def scattered(rows, length):
    halves = lax.axis_size("y")
    grad = jnp.pad(rows, ((0, 0), (0, 0), (0, halves * length - rows.shape[2]), (0, 0)))
    grad = lax.psum_scatter(grad, "dp", scatter_dimension=0, tiled=True)
    grad = grad.reshape(1, 2, halves, length, LANES)
    core = lax.axis_index("core")
    return tuple(lax.dynamic_index_in_dim(grad, at, 1, False) for at in (core, 1 - core))


def assembled(own, got, length, size, inner, mid):
    core = lax.axis_index("core")
    both = jnp.stack([own, got]).astype(F32)
    both = jnp.stack([lax.dynamic_index_in_dim(both, at, 0, False) for at in (core, 1 - core)])
    rows = both[:, :, :length].reshape(2, -1, LANES)
    second = [None] * 27
    for j in range(13):
        for m, k in enumerate((j, 9 + j) if j < 9 else (2 * j, 2 * j + 1)):
            second[k] = rows[:, j * size : (j + 1) * size, m * mid : (m + 1) * mid].reshape(2 * size, mid)
    tail = rows[:, 13 * size : 13 * size + size // 2]
    second[26] = jnp.concatenate([tail[:, :, :mid], tail[:, :, mid:]], axis=1).reshape(2 * size, mid)
    rows, half = both[:, :, length:].reshape(2, -1, LANES), size // 2
    first = [None] * 27
    for j in range(7):
        for m in range(4):
            c, ab = (j // 2, 4 * (j % 2) + m) if j < 6 else (m, 8)
            if c < 3:
                value = rows[:, j * half : (j + 1) * half, m * inner : (m + 1) * inner]
                first[3 * ab + c] = value.reshape(size, inner)
    return jnp.stack(first), jnp.stack(second)


def per_device(volume, kernel_first, kernel_second, cotangent):
    _, inner, depth, height, width = volume.shape
    mid, out = kernel_first.shape[1], kernel_second.shape[1]
    cells = height * width
    parts = lax.axis_size("dp")
    k1, k2 = jnp.swapaxes(kernel_first, 1, 2), jnp.swapaxes(kernel_second, 1, 2)
    rows = depth * height

    early = [along_depth(volume[0], first, True) for first in range(2)]
    (blank,) = call(blank_kernel, [shape((out, 2 * width), BF)], [], flops=3_000_000_000)
    (vol,) = call(
        own_kernel,
        [shape((depth, inner, cells), BF)],
        [volume[0], blank],
        [pltpu.VMEM((inner * rows, width), F32)],
    )
    late = [along_depth(vol, first, False) for first in range(2)]
    cot_rows, back = call(
        spread_kernel,
        [
            shape((depth, out, cells), BF),
            shape((depth + 2, mid, cells + 2 * width), F32),
        ],
        [cotangent[0], k2, blank, vol],
        [pltpu.VMEM((out * rows, width), F32)],
        flops=300_000_000,
    )
    extended = shape((3 * depth, inner, cells), BF)
    edge = shape((3 * depth, inner, 2 * width), BF)
    scratch = [pltpu.VMEM((inner * rows, width), F32)]
    deep, two = call(early_rim_kernel, [extended, edge], [vol, *early, cot_rows], scratch)
    moved, w1, w1_last = call(
        arrange_kernel,
        [shape((depth, 3 * out, cells), BF), shape((3 * mid, 8 * inner), BF), shape((mid, 3 * inner), BF)],
        [cot_rows, k1, deep],
        flops=500_000_000,
    )
    two = swapped(two, HGT, 1)
    deep, one = call(late_rim_kernel, [extended, edge], [deep, *late, w1])
    one = swapped(one, HGT, 0)

    size = mid // parts
    direct = parts == 2 and size % 16 == 0
    halves = lax.axis_size("y")
    length_second, length_first = (-(-units * size // (16 * halves)) * 8 for units in (27, 7))
    rows_in, rows_out = height - 2, 4
    inner_hidden, inner_second, inner_first = call(
        inner_kernel,
        [
            shape((depth + 2, mid, rows_in * width), BF),
            shape((9 * out, 3 * mid), F32),
            shape((9 * inner, 3 * mid), F32),
        ],
        [deep, w1, w1_last, moved, back],
        [pltpu.VMEM((3 * mid, (depth + 2) * rows_in * width), BF)],
        flops=1_500_000_000,
    )
    hidden, first = call(
        outer_kernel,
        [shape((depth + 2, mid, cells + 2 * width), BF), shape((7, mid, LANES), F32)],
        [deep, two, one, w1, w1_last, back, inner_hidden, inner_first],
        [
            pltpu.VMEM((3 * depth, inner, cells + 4 * width), BF),
            pltpu.VMEM((3 * mid, (depth + 2) * rows_out * width), BF),
        ],
        flops=1_000_000_000,
    )
    block = (length_second + length_first, width)
    grads = call(
        functools.partial(second_kernel, direct),
        [shape((parts, halves, *block), kind) for kind in (F32, BF)] if direct else [shape((14, out, LANES), F32)],
        [hidden, moved, inner_second, first],
        flops=4_000_000_000,
    )
    if direct:
        moves = [(1, 0), (0, 1), (1, 1)]
        keep, send = grads
    else:
        moves = [(0, 1)]
        blocks = grads[0].reshape(14, parts, 2, size, LANES).transpose(1, 2, 0, 3, 4)
        tail = blocks[:, :, 13, :, :mid]
        tail = jnp.concatenate([tail[:, :, : size // 2], tail[:, :, size // 2 :]], axis=-1)
        rows_second = jnp.concatenate([blocks[:, :, :13].reshape(parts, 2, 13 * size, LANES), tail], axis=2)
        blocks = first.reshape(7, parts, 2, size // 2, LANES).transpose(1, 2, 0, 3, 4)
        rows_first = blocks.reshape(parts, 2, 7 * (size // 2), LANES)
        pairs = [scattered(rows, n) for rows, n in ((rows_second, length_second), (rows_first, length_first))]
        keep, send = (jnp.concatenate(both, axis=2) for both in zip(*pairs, strict=True))
        send = send.astype(BF)
    kept, *sends = call(
        functools.partial(plane_kernel, moves),
        [shape(block, F32)] + [shape(block, BF)] * len(moves),
        [keep, across(send, ("core", 1))],
    )
    gots = [across(send, ("dp", x), ("y", y)) for send, (x, y) in zip(sends, moves, strict=True)]
    (share,) = call(total_kernel, [shape(block, BF)], [kept, *gots])
    features, token = call(
        features_kernel,
        [shape(cotangent.shape[1:], BF), shape((8, width), F32)],
        [hidden, k2],
        [pltpu.VMEM((out * rows, width), F32)],
        flops=900_000_000,
    )
    gots = [across(share, ("dep", bits)) for bits in (1, 2, 3)]
    (share,) = call(depth_kernel, [shape(block, BF)], [share, *gots, token])
    (own,) = call(order_kernel, [shape((halves, *block), BF)], [share, across(share, ("y", 1))])
    got = across(own, ("core", 1))
    if size % 16 == 0:
        grads = [shape((27, size, inner), F32), shape((27, 2 * size, mid), F32)]
        scratch = [
            pltpu.VMEM((27, size // 2, inner), F32),
            pltpu.VMEM((27, size, mid), F32),
            pltpu.SemaphoreType.DMA((2,)),
        ]
        written = call(functools.partial(unpack_kernel, length_second, False), grads, [own], scratch, far_outs=True)
        grad_first, grad_second = call(
            functools.partial(unpack_kernel, length_second, True),
            grads,
            [got, *written],
            scratch,
            far=(1, 2),
            far_outs=True,
            aliases={1: 0, 2: 1},
        )
    else:
        grad_first, grad_second = assembled(own, got, length_second, size, inner, mid)
    return features[None], grad_first, grad_second


def solution(mesh):
    dp, dep, hgt = (mesh.shape[axis] for axis in ("dp", "dep", "hgt"))
    split = jax.sharding.Mesh(mesh.devices.reshape(dp, dep, hgt // 2, 2), ("dp", "dep", *HGT))
    block = P("dp", None, "dep", HGT, None)
    return jax.shard_map(
        per_device,
        mesh=split,
        in_specs=(block, P(), P(), block),
        out_specs=(block, P(None, "dp", None), P(None, "dp", None)),
        check_vma=False,
    )
```

```python
import functools

import jax
import jax.numpy as jnp
from jax import lax
from jax.experimental import pallas as pl
from jax.experimental.pallas import tpu as pltpu
from jax.sharding import PartitionSpec as P

BF, F32 = jnp.bfloat16, jnp.float32
LANES = 128
HGT = ("y", "core")
VMEM_BYTES = 28 * 2**20


def call(body, outs, args, scratch=(), flops=0, far=(), far_outs=(), aliases=None):
    moved = sum(x.size * x.dtype.itemsize for x in (*outs, *args))
    return pl.pallas_call(
        body,
        out_shape=outs,
        in_specs=[pl.BlockSpec(memory_space=pl.ANY if n in far else pltpu.VMEM) for n in range(len(args))],
        out_specs=[pl.BlockSpec(memory_space=pl.ANY if n in far_outs else pltpu.VMEM) for n in range(len(outs))],
        scratch_shapes=list(scratch),
        input_output_aliases=aliases or {},
        compiler_params=pltpu.CompilerParams(vmem_limit_bytes=VMEM_BYTES),
        cost_estimate=pl.CostEstimate(flops=flops, bytes_accessed=moved, transcendentals=0),
    )(*args)


def shape(dims, dtype):
    return jax.ShapeDtypeStruct(dims, dtype)


def moved_along_width(x, c):
    if c == 0:
        return x
    pieces = []
    for start in range(0, x.shape[1], LANES):
        piece = x[:, start : start + LANES]
        lane = lax.broadcasted_iota(jnp.int32, piece.shape, 1)
        rolled = pltpu.roll(piece, c % LANES, 1)
        pieces.append(jnp.where(lane == (0 if c == 1 else LANES - 1), 0.0, rolled))
    return pieces[0] if len(pieces) == 1 else jnp.concatenate(pieces, axis=1)


def by_rows(ref, scratch, store):
    channels, depth, height, width = ref.shape
    rows = depth * height
    scratch[...] = ref[...].astype(F32).reshape(channels * rows, width)
    for d in range(depth):
        for h in range(height):
            store(d, h, scratch[pl.ds(d * height + h, channels, stride=rows), :])


def odd(axis):
    return lax.rem(lax.axis_index(axis), 2) == 1


def blank_kernel(out_ref):
    out_ref[...] = jnp.zeros(out_ref.shape, BF)


def spread_kernel(cot_ref, k2_ref, blank_ref, cot_rows_ref, back_ref, scratch):
    out, depth, height, _ = cot_ref.shape
    rows = [[None] * height for _ in range(depth)]

    def store(d, h, row):
        rows[d][h] = row.astype(BF)
        cot_rows_ref[d, :, h * LANES : (h + 1) * LANES] = rows[d][h]

    by_rows(cot_ref, scratch, store)
    mid = k2_ref.shape[1]
    none = blank_ref[...]
    padded = [jnp.concatenate([none, *rows[d], none], axis=1) for d in range(depth)]
    for e in range(depth + 2):
        reached = [(d, e - 1 - d) for d in range(depth) if abs(e - 1 - d) <= 1]
        w = jnp.concatenate(
            [
                k2_ref[9 * (a + 1) + 3 * b : 9 * (a + 1) + 3 * b + 3].reshape(3 * mid, out)
                for _, a in reached
                for b in range(3)
            ],
            axis=1,
        )
        for j in range(0, height + 2, 2):
            rhs = jnp.concatenate(
                [padded[d][:, (j + 2 - b) * LANES : (j + 4 - b) * LANES] for d, _ in reached for b in range(3)], axis=0
            )
            y = jnp.dot(w, rhs, preferred_element_type=F32)
            back = sum(moved_along_width(y[n * mid : (n + 1) * mid], n - 1) for n in range(3))
            back_ref[e, :, j * LANES : (j + 2) * LANES] = back


def as_matrix(ref, c):
    stacked = jnp.concatenate([ref[3 * ab + c] for ab in range(9)], axis=0)
    return stacked.astype(F32).T.astype(BF)


def arrange_kernel(cot_rows_ref, k1_ref, vol_ref, moved_ref, w1_ref, own_ref, scratch):
    def store(d, h, row):
        own_ref[d, :, h * LANES : (h + 1) * LANES] = row.astype(BF)

    by_rows(vol_ref, scratch, store)
    depth, out, cells = cot_rows_ref.shape
    for d in range(depth):
        for h in range(0, cells, LANES):
            row = cot_rows_ref[d, :, h : h + LANES]
            for n, c in enumerate((-1, 0, 1)):
                value = row if c == 0 else moved_along_width(row.astype(F32), c).astype(BF)
                moved_ref[d, n * out : (n + 1) * out, h : h + LANES] = value
    mid = k1_ref.shape[2]
    for c in range(3):
        w1_ref[c * mid : (c + 1) * mid, :] = as_matrix(k1_ref, c)


def sides(axis, one, two):
    me, size = lax.axis_index(axis), lax.axis_size(axis)
    is_odd = odd(axis)
    none = jnp.zeros_like(one)
    before = jnp.where(me == 0, none, jnp.where(is_odd, one, two))
    after = jnp.where(me == size - 1, none, jnp.where(is_odd, two, one))
    return before, after


def rim_kernel(own_ref, one_ref, two_ref, deep_ref, send_one_ref, send_two_ref, scratch):
    depth = own_ref.shape[0]
    deep_ref[depth : 2 * depth] = own_ref[...]
    for at, part in zip((0, 2 * depth), sides("dep", one_ref[...], two_ref[...]), strict=True):

        def store(d, h, row, at=at):
            deep_ref[at + d, :, h * LANES : (h + 1) * LANES] = row.astype(BF)

        by_rows(part, scratch, store)
    n, cells = send_one_ref.shape[2], deep_ref.shape[2]
    first, last = deep_ref[:, :, :n], deep_ref[:, :, cells - n :]
    is_odd = odd(HGT)
    send_one_ref[...] = jnp.where(is_odd, first, last)
    send_two_ref[...] = jnp.where(is_odd, last, first)


def widened(deep_ref, one_ref, two_ref):
    left, right = sides(HGT, one_ref[...], two_ref[...])
    return [jnp.concatenate([left[d], deep_ref[d], right[d]], axis=1) for d in range(deep_ref.shape[0])]


def pack(direct, refs, rows_of, blocks):
    if not direct:
        for j, block in enumerate(blocks):
            refs[0][j] = block
        return
    keep_ref, send_ref = refs
    parts, halves, length, _ = keep_ref.shape
    core = lax.axis_index("core") == 1

    def filled(rows):
        rest = length - sum(x.shape[0] for x in rows)
        return jnp.concatenate([*rows, jnp.zeros((rest, LANES), F32)] if rest else rows, axis=0)

    for part in range(parts):
        for half in range(halves):
            one, two = (filled(rows_of(part, c)[half]) for c in range(2))
            keep_ref[part, half] = jnp.where(core, two, one)
            send_ref[part, half] = jnp.where(core, one, two).astype(send_ref.dtype)


def folded(tail):
    half = tail.shape[0] // 2
    return jnp.concatenate([tail[:half], tail[half:]], axis=1)


def activated(w1, rhs, d, depth, heights):
    mid = w1.shape[0] // 3
    y = jnp.dot(w1, rhs, preferred_element_type=F32)
    pre = sum(moved_along_width(y[n * mid : (n + 1) * mid], 1 - n) for n in range(3))
    s = 1.0 / (1.0 + jnp.exp(-pre))
    dep, deps = lax.axis_index("dep"), lax.axis_size("dep")
    hgt, hgts = lax.axis_index(HGT), lax.axis_size(HGT)
    results = []
    for n, side in enumerate(heights):
        p, q = (x[:, n * LANES : (n + 1) * LANES] for x in (pre, s))
        value, slope = (p * q).astype(BF), q * (1.0 + p * (1.0 - q))
        outside = []
        if d == 0:
            outside.append(dep == 0)
        if d == depth - 1:
            outside.append(dep == deps - 1)
        if side < 0:
            outside.append(hgt == 0)
        if side > 0:
            outside.append(hgt == hgts - 1)
        for far in outside:
            value = jnp.where(far, jnp.zeros_like(value), value)
            slope = jnp.where(far, jnp.zeros_like(slope), slope)
        results.append((value, slope))
    return results


def neighbours(ref, d, starts, count):
    return jnp.concatenate(
        [
            jnp.concatenate(
                [ref[d + a, :, (start + b) * LANES : (start + b + count) * LANES] for start in starts], axis=1
            )
            for a in range(3)
            for b in range(3)
        ],
        axis=0,
    )


def products(left, right):
    return lax.dot_general(left, right, (((1,), (1,)), ((), ())), preferred_element_type=F32)


def shares(delta, n_channels, ref, at):
    for n in range(3):
        ref[n * n_channels : (n + 1) * n_channels, at : at + LANES] = moved_along_width(delta, n - 1).astype(BF)


def inner_kernel(deep_ref, w1_ref, moved_ref, back_ref, hidden_ref, second_ref, first_ref, delta_ref):
    w1 = w1_ref[...]
    depth, mid, cells = hidden_ref.shape
    height = cells // LANES
    for d in range(depth):
        for h in range(0, height, 2):
            results = activated(w1, neighbours(deep_ref, d, [h], 2), d, depth, (0, 0))
            for n, (value, slope) in enumerate(results):
                at = (h + n) * LANES
                hidden_ref[d, :, at : at + LANES] = value
                back = back_ref[d, :, at + 2 * LANES : at + 3 * LANES]
                shares(back * slope, mid, delta_ref, d * cells + at)
    own = depth - 2
    left = jnp.concatenate(
        [
            jnp.concatenate([moved_ref[d, :, (2 - b) * LANES : (2 - b) * LANES + cells] for d in range(own)], axis=1)
            for b in range(3)
        ],
        axis=0,
    )
    right = jnp.concatenate(
        [jnp.concatenate([hidden_ref[d + a] for a in range(3)], axis=0) for d in range(own)], axis=1
    )
    second_ref[...] = products(left, right)
    right = jnp.concatenate([neighbours(deep_ref, d, [0], height) for d in range(depth)], axis=1)
    first_ref[...] = products(delta_ref[...], right)


def outer_kernel(
    direct, deep_ref, two_ref, one_ref, w1_ref, back_ref, inner_ref, first_ref, hidden_ref, *grad_refs_and_scratch,
):
    *grad_refs, rows_ref, delta_ref = grad_refs_and_scratch
    for d, row in enumerate(widened(deep_ref, one_ref, two_ref)):
        rows_ref[d] = row
    w1 = w1_ref[...]
    depth, mid, cells = hidden_ref.shape
    last = cells // LANES - 2
    for d in range(depth):
        hidden_ref[d, :, 2 * LANES : last * LANES] = inner_ref[d]
        for h, sides_of in ((0, (-1, 0)), (last, (0, 1))):
            results = activated(w1, neighbours(rows_ref, d, [h], 2), d, depth, sides_of)
            for n, (value, slope) in enumerate(results):
                at = (h + n) * LANES
                hidden_ref[d, :, at : at + LANES] = value
                delta = back_ref[d, :, at : at + LANES] * slope
                shares(delta, mid, delta_ref, (4 * d + (2 if h else 0) + n) * LANES)
    right = jnp.concatenate([neighbours(rows_ref, d, [0, last], 2) for d in range(depth)], axis=1)
    total = first_ref[...] + products(delta_ref[...], right)
    inner = rows_ref.shape[1]
    blocks, tails = [], []
    for n in range(3):
        part = total[n * mid : (n + 1) * mid]
        blocks += [part[:, m * LANES : (m + 1) * LANES] for m in range(2)]
        tails.append(part[:, 2 * LANES :])
    tails.append(jnp.zeros((mid, LANES - 3 * inner), F32))
    blocks.append(jnp.concatenate(tails, axis=1))
    size = mid // lax.axis_size("dp")
    half = size // 2

    def rows_of(part, core):
        rows = [block[part * size + core * half : part * size + (core + 1) * half] for block in blocks]
        return rows[:3], rows[3:]

    pack(direct, grad_refs, rows_of, blocks)


def second_kernel(direct, hidden_ref, moved_ref, second_ref, *grad_refs):
    depth, mid, cells = hidden_ref.shape
    height = cells // LANES
    own = depth - 2
    out = moved_ref.shape[1] // 3
    heads, tails = [], []
    for b in range(3):
        far = [h for h in range(height - 2) if not 2 <= h + b <= height - 3]
        left = jnp.concatenate(
            [moved_ref[d, :, h * LANES : (h + 1) * LANES] for d in range(own) for h in far], axis=1
        )
        right = jnp.concatenate(
            [
                jnp.concatenate([hidden_ref[d + a, :, (h + b) * LANES : (h + b + 1) * LANES] for a in range(3)], axis=0)
                for d in range(own)
                for h in far
            ],
            axis=1,
        )
        total = second_ref[3 * b * out : 3 * (b + 1) * out, :] + products(left, right)
        for c in range(3):
            part = total[c * out : (c + 1) * out]
            heads.append(part[:, :LANES])
            tails.append(part[:, LANES:])
    blocks = heads + [jnp.concatenate(tails[n : n + 2], axis=1) for n in range(0, 8, 2)]
    size = mid // lax.axis_size("dp")

    def rows_of(part, core):
        at = slice((2 * part + core) * size, (2 * part + core + 1) * size)
        rows = [block[at] for block in blocks] + [folded(tails[8][at])]
        return rows[:7], rows[7:]

    pack(direct, grad_refs, rows_of, [*blocks, jnp.concatenate([tails[8], jnp.zeros_like(tails[8])], axis=1)])


def features_kernel(hidden_ref, k2_ref, out_ref, token_ref, scratch):
    out, depth, height, _ = out_ref.shape
    w2 = jnp.concatenate([as_matrix(k2_ref, c) for c in range(3)], axis=0)
    for d in range(depth):
        for h in range(0, height, 2):
            rhs = jnp.concatenate(
                [
                    hidden_ref[d + a, :, (h + b) * LANES : (h + b + 2) * LANES]
                    for a in range(3)
                    for b in range(3)
                ],
                axis=0,
            )
            y = jnp.dot(w2, rhs, preferred_element_type=F32)
            total = sum(moved_along_width(y[n * out : (n + 1) * out], 1 - n) for n in range(3))
            for r in range(2):
                row = total[:, r * LANES : (r + 1) * LANES]
                scratch[pl.ds(d * height + h + r, out, stride=depth * height), :] = row
    out_ref[...] = scratch[...].reshape(out_ref.shape).astype(BF)
    token_ref[...] = scratch[:8]


def plane_kernel(moves, cuts, *refs):
    sums, (kept_ref, *send_refs) = refs[: -1 - len(moves)], refs[-1 - len(moves) :]
    part = lax.rem(lax.axis_index("dp"), sums[0].shape[0])
    half = lax.axis_index("y")

    def total(x, y):
        at = 1 - part if x else part, 1 - half if y else half
        values = [keep[at] + got[at].astype(F32) for keep, got in zip(sums[::2], sums[1::2], strict=True)]
        if len(values) == 1:
            return values[0]
        one, two = (jnp.concatenate([v[:n] for v, n in zip(values, cut, strict=True)], axis=0) for cut in cuts)
        return jnp.where(at[1] == 0, one, two)

    kept_ref[...] = total(0, 0)
    for (x, y), send_ref in zip(moves, send_refs, strict=True):
        send_ref[...] = total(x, y).astype(BF)


def total_kernel(kept_ref, *refs):
    *got_refs, out_ref = refs
    value = kept_ref[...]
    for ref in got_refs:
        value = value + ref[...].astype(F32)
    out_ref[...] = value.astype(BF)


def depth_kernel(a_ref, b_ref, c_ref, d_ref, _, out_ref, padded_ref):
    one = a_ref[...].astype(F32) + b_ref[...].astype(F32)
    two = c_ref[...].astype(F32) + d_ref[...].astype(F32)
    out_ref[...] = (one + two).astype(BF)
    rest = jnp.zeros((padded_ref.shape[0] - out_ref.shape[0], LANES), F32)
    padded_ref[...] = jnp.concatenate([one + two, rest], axis=0).astype(BF)


def after_kernel(in_ref, _, out_ref):
    out_ref[...] = in_ref[: out_ref.shape[0]]


def write_kernel(count, wheres, *refs):
    n_scratch = 6
    in_refs = refs[:count]
    out_refs, scratch = refs[: -n_scratch * count], refs[-n_scratch * count :]
    if wheres[0][1]:
        first_ref, second_ref, token_ref = out_refs[-3:]
        token_ref[...] = jnp.zeros(token_ref.shape, F32)
    else:
        first_ref, second_ref = out_refs[-2:]
    core, y = lax.axis_index("core"), lax.axis_index("y")

    def begun(n, half):
        wide, last, low, high, tail, sems = scratch[n_scratch * n : n_scratch * (n + 1)]
        own_core, _ = wheres[n]
        at = core if own_core else 1 - core
        rows = in_refs[n][...].astype(F32)
        _, _, size, mid = wide.shape
        _, small, inner = low.shape
        here = pl.ds(pl.multiple_of(at * size, size), size)
        count = 2 if half else 7
        for j in range(count):
            value = rows[j * size : (j + 1) * size]
            for m in range(2):
                wide[m, j] = value[:, m * mid : (m + 1) * mid]
        pairs = [(wide.at[:, :count], second_ref.at[0:2, 7 * half : 7 * half + count, here, :])]
        row = count * size
        if half:
            for j in range(4):
                value = rows[row : row + size]
                row += size
                for m in range(2):
                    last[2 * j + m] = value[:, m * mid : (m + 1) * mid]
            value = rows[row : row + size // 2]
            row += size // 2
            last[8] = jnp.concatenate([value[:, :mid], value[:, mid:]], axis=0)
            pairs.append((last, second_ref.at[2, :, here, :]))
        copies = [pltpu.make_async_copy(src, dst, sems.at[i]) for i, (src, dst) in enumerate(pairs)]
        for copy in copies:
            copy.start()
        here = pl.ds(pl.multiple_of(at * small, small), small)
        places = [(high, 0, 4), (low, 0, 4), (low, 4, 4), (tail, 0, 3)] if half else [(low, 0, 4), (low, 4, 4), (high, 0, 4)]
        for ref, start, number in places:
            value = rows[row : row + small]
            row += small
            for m in range(number):
                ref[start + m] = value[:, m * inner : (m + 1) * inner]
        if half:
            pairs = [
                (high, first_ref.at[4:8, 1, here, :]),
                (low, first_ref.at[0:8, 2, here, :]),
                (tail, first_ref.at[8, :, here, :]),
            ]
        else:
            pairs = [(low, first_ref.at[0:8, 0, here, :]), (high, first_ref.at[0:4, 1, here, :])]
        more = [pltpu.make_async_copy(src, dst, sems.at[2 + i]) for i, (src, dst) in enumerate(pairs)]
        for copy in more:
            copy.start()
        return copies + more

    for half in range(2):

        @pl.when(y == half)
        def _(half=half):
            copies = []
            for n, (_, own_y) in enumerate(wheres):
                copies += begun(n, half if own_y else 1 - half)
            for copy in copies:
                copy.wait()


def swapped(x, axis, first):
    axes = (axis,) if isinstance(axis, str) else axis
    parts, size = lax.axis_size("dp"), lax.axis_size(axis)
    partner = list(range(parts * size))
    for i in partner:
        part, at = divmod(i, size)
        if first <= at < size - (size - first) % 2:
            partner[i] = part * size + (at - first ^ 1) + first
        elif parts % 2 == 0:
            partner[i] = (part ^ 1) * size + at
    return lax.ppermute(x, ("dp", *axes), list(enumerate(partner)))


def across(x, *moves):
    axes = tuple(axis for axis, _ in moves)
    flip = 0
    for axis, bit in moves:
        flip = flip * lax.axis_size(axis) + bit
    return lax.ppermute(x, axes, [(i, i ^ flip) for i in range(lax.axis_size(axes))])


def scattered(rows, cuts):
    halves = [
        jnp.concatenate([x[:, :, :n] if at == 0 else x[:, :, x.shape[2] - n :] for x, n in zip(rows, cut)], axis=2)
        for at, cut in enumerate(cuts)
    ]
    grad = lax.psum_scatter(jnp.stack(halves, axis=2), "dp", scatter_dimension=0, tiled=True)
    core = lax.axis_index("core")
    return tuple(lax.dynamic_index_in_dim(grad, at, 1, False) for at in (core, 1 - core))


def assembled(quarters, size, inner, mid):
    first, second = ([[None, None] for _ in range(27)] for _ in range(2))
    half = size // 2
    for core in range(2):
        for y in range(2):
            rows, row = quarters[core][y].astype(F32), 0
            for j in range(7) if y == 0 else range(7, 13):
                for m, k in enumerate((j, 9 + j) if j < 9 else (2 * j, 2 * j + 1)):
                    second[k][core] = rows[row : row + size, m * mid : (m + 1) * mid]
                row += size
            if y == 1:
                tail = rows[row : row + half]
                second[26][core] = jnp.concatenate([tail[:, :mid], tail[:, mid:]], axis=0)
                row += half
            for j in range(3) if y == 0 else range(3, 7):
                for m in range(4):
                    c, ab = (j // 2, 4 * (j % 2) + m) if j < 6 else (m, 8)
                    if c < 3:
                        first[3 * ab + c][core] = rows[row : row + half, m * inner : (m + 1) * inner]
                row += half
    return tuple(jnp.stack([jnp.concatenate(both, axis=0) for both in grad]) for grad in (first, second))


def per_device(volume, kernel_first, kernel_second, cotangent):
    _, inner, depth, height, width = volume.shape
    mid, out = kernel_first.shape[1], kernel_second.shape[1]
    cells = height * width
    parts = lax.axis_size("dp")
    k1, k2 = jnp.swapaxes(kernel_first, 1, 2), jnp.swapaxes(kernel_second, 1, 2)
    rows = depth * height

    one, two = swapped(volume[0], "dep", 0), swapped(volume[0], "dep", 1)
    (blank,) = call(blank_kernel, [shape((out, 2 * width), BF)], [], flops=3_000_000_000)
    cot_rows, back = call(
        spread_kernel,
        [
            shape((depth, out, cells), BF),
            shape((depth + 2, mid, cells + 2 * width), F32),
        ],
        [cotangent[0], k2, blank],
        [pltpu.VMEM((out * rows, width), F32)],
        flops=1_100_000_000,
    )
    moved, w1, vol = call(
        arrange_kernel,
        [
            shape((depth, 3 * out, cells), BF),
            shape((3 * mid, 9 * inner), BF),
            shape((depth, inner, cells), BF),
        ],
        [cot_rows, k1, volume[0]],
        [pltpu.VMEM((inner * rows, width), F32)],
        flops=500_000_000,
    )
    deep, one, two = call(
        rim_kernel,
        [shape((3 * depth, inner, cells), BF)] + [shape((3 * depth, inner, 2 * width), BF)] * 2,
        [vol, one, two],
        [pltpu.VMEM((inner * rows, width), F32)],
    )
    one, two = swapped(one, HGT, 0), swapped(two, HGT, 1)
    size = mid // parts
    direct = parts == 2 and size % 16 == 0
    halves = lax.axis_size("y")
    cuts = ((7 * size, 3 * size // 2), (13 * size // 2, 2 * size))
    length_second, length_first = 7 * size, 2 * size
    rows_in, rows_out = height - 2, 4
    inner_hidden, inner_second, inner_first = call(
        inner_kernel,
        [
            shape((depth + 2, mid, rows_in * width), BF),
            shape((9 * out, 3 * mid), F32),
            shape((3 * mid, 9 * inner), F32),
        ],
        [deep, w1, moved, back],
        [pltpu.VMEM((3 * mid, (depth + 2) * rows_in * width), BF)],
        flops=1_500_000_000,
    )
    hidden, *first = call(
        functools.partial(outer_kernel, direct),
        [shape((depth + 2, mid, cells + 2 * width), BF)]
        + ([shape((parts, halves, length_first, width), F32)] * 2 if direct else [shape((7, mid, LANES), F32)]),
        [deep, two, one, w1, back, inner_hidden, inner_first],
        [
            pltpu.VMEM((3 * depth, inner, cells + 4 * width), BF),
            pltpu.VMEM((3 * mid, (depth + 2) * rows_out * width), BF),
        ],
        flops=1_000_000_000,
    )
    second = call(
        functools.partial(second_kernel, direct),
        [shape((parts, halves, length_second, width), kind) for kind in (F32, BF)]
        if direct
        else [shape((14, out, LANES), F32)],
        [hidden, moved, inner_second],
        flops=4_000_000_000,
    )
    if direct:
        moves = [(1, 0), (0, 1), (1, 1)]
        grads = [second, first]
    else:
        moves = [(0, 1)]
        blocks = second[0].reshape(14, parts, 2, size, LANES).transpose(1, 2, 0, 3, 4)
        tail = blocks[:, :, 13, :, :mid]
        tail = jnp.concatenate([tail[:, :, : size // 2], tail[:, :, size // 2 :]], axis=-1)
        rows_second = jnp.concatenate([blocks[:, :, :13].reshape(parts, 2, 13 * size, LANES), tail], axis=2)
        blocks = first[0].reshape(7, parts, 2, size // 2, LANES).transpose(1, 2, 0, 3, 4)
        rows_first = blocks.reshape(parts, 2, 7 * (size // 2), LANES)
        grads = [scattered([rows_second, rows_first], cuts)]
    block = (sum(cuts[0]), width)
    kept, *sends = call(
        functools.partial(plane_kernel, moves, cuts),
        [shape(block, F32)] + [shape(block, BF)] * len(moves),
        [x for keep, send in grads for x in (keep, across(send, ("core", 1)))],
    )
    gots = [across(send, ("dp", x), ("y", y)) for send, (x, y) in zip(sends, moves, strict=True)]
    (share,) = call(total_kernel, [shape(block, BF)], [kept, *gots])
    features, token = call(
        features_kernel,
        [shape(cotangent.shape[1:], BF), shape((8, width), F32)],
        [hidden, k2],
        [pltpu.VMEM((out * rows, width), F32)],
        flops=900_000_000,
    )
    gots = [across(share, ("dep", bits)) for bits in (1, 2, 3)]
    share, for_y = call(depth_kernel, [shape(block, BF), shape((block[0] + 16, width), BF)], [share, *gots, token])
    other, far = across(share, ("core", 1)), across(for_y, ("y", 1))
    if size % 16 == 0:
        outs = [shape((9, 3, size, inner), F32), shape((3, 9, 2 * size, mid), F32)]

        def written(quarters, wheres, before=()):
            scratch = [
                pltpu.VMEM((2, 7, size, mid), F32),
                pltpu.VMEM((9, size, mid), F32),
                pltpu.VMEM((8, size // 2, inner), F32),
                pltpu.VMEM((4, size // 2, inner), F32),
                pltpu.VMEM((3, size // 2, inner), F32),
                pltpu.SemaphoreType.DMA((5,)),
            ]
            count = len(quarters)
            return call(
                functools.partial(write_kernel, count, wheres),
                outs if before else [*outs, shape((8, width), F32)],
                [*quarters, *before],
                scratch * count,
                far=range(count, count + len(before)),
                far_outs=(0, 1),
                aliases={count + n: n for n in range(len(before))},
            )

        *grads, token = written([share, other], [(True, True), (False, True)])
        (far,) = call(after_kernel, [shape(block, BF)], [far, token])
        grads = written([far, across(far, ("core", 1))], [(True, False), (False, False)], grads)
        grad_first, grad_second = (grad.reshape(27, *grad.shape[2:]) for grad in grads)
    else:
        core, y = lax.axis_index("core"), lax.axis_index("y")
        stacked = jnp.stack([jnp.stack([share, far[: block[0]]]), jnp.stack([other, across(far[: block[0]], ("core", 1))])])
        quarters = [
            [stacked[lax.bitwise_xor(core, c), lax.bitwise_xor(y, h)] for h in range(2)] for c in range(2)
        ]
        grad_first, grad_second = assembled(quarters, size, inner, mid)
    return features[None], grad_first, grad_second


def solution(mesh):
    dp, dep, hgt = (mesh.shape[axis] for axis in ("dp", "dep", "hgt"))
    split = jax.sharding.Mesh(mesh.devices.reshape(dp, dep, hgt // 2, 2), ("dp", "dep", *HGT))
    block = P("dp", None, "dep", HGT, None)
    return jax.shard_map(
        per_device,
        mesh=split,
        in_specs=(block, P(), P(), block),
        out_specs=(block, P(None, "dp", None), P(None, "dp", None)),
        check_vma=False,
    )
```

```python
import functools

import jax
import jax.numpy as jnp
from jax import lax
from jax.experimental import pallas as pl
from jax.experimental.pallas import tpu as pltpu
from jax.sharding import PartitionSpec as P

BF, F32 = jnp.bfloat16, jnp.float32
LANES = 128
HGT = ("y", "core")
VMEM_BYTES = 28 * 2**20


def call(body, outs, args, scratch=(), flops=0, far=(), far_outs=False, aliases=None):
    moved = sum(x.size * x.dtype.itemsize for x in (*outs, *args))
    return pl.pallas_call(
        body,
        out_shape=outs,
        in_specs=[pl.BlockSpec(memory_space=pl.ANY if n in far else pltpu.VMEM) for n in range(len(args))],
        out_specs=[pl.BlockSpec(memory_space=pl.ANY if far_outs else pltpu.VMEM)] * len(outs),
        scratch_shapes=list(scratch),
        input_output_aliases=aliases or {},
        compiler_params=pltpu.CompilerParams(vmem_limit_bytes=VMEM_BYTES),
        cost_estimate=pl.CostEstimate(flops=flops, bytes_accessed=moved, transcendentals=0),
    )(*args)


def shape(dims, dtype):
    return jax.ShapeDtypeStruct(dims, dtype)


def moved_along_width(x, c):
    if c == 0:
        return x
    pieces = []
    for start in range(0, x.shape[1], LANES):
        piece = x[:, start : start + LANES]
        lane = lax.broadcasted_iota(jnp.int32, piece.shape, 1)
        rolled = pltpu.roll(piece, c % LANES, 1)
        pieces.append(jnp.where(lane == (0 if c == 1 else LANES - 1), 0.0, rolled))
    return pieces[0] if len(pieces) == 1 else jnp.concatenate(pieces, axis=1)


def by_rows(ref, scratch, store):
    channels, depth, height, width = ref.shape
    rows = depth * height
    scratch[: channels * rows] = ref[...].astype(F32).reshape(channels * rows, width)
    for d in range(depth):
        for h in range(height):
            store(d, h, scratch[pl.ds(d * height + h, channels, stride=rows), :])


def odd(axis):
    return lax.rem(lax.axis_index(axis), 2) == 1


def blank_kernel(out_ref):
    out_ref[...] = jnp.zeros(out_ref.shape, BF)


def spread_kernel(cot_ref, k2_ref, blank_ref, cot_rows_ref, back_ref, scratch):
    out, depth, height, _ = cot_ref.shape
    rows = [[None] * height for _ in range(depth)]

    def store(d, h, row):
        rows[d][h] = row.astype(BF)
        cot_rows_ref[d, :, h * LANES : (h + 1) * LANES] = rows[d][h]

    by_rows(cot_ref, scratch, store)
    mid = k2_ref.shape[1]
    none = blank_ref[...]
    padded = [jnp.concatenate([none, *rows[d], none], axis=1) for d in range(depth)]
    for e in range(depth + 2):
        reached = [(d, e - 1 - d) for d in range(depth) if abs(e - 1 - d) <= 1]
        w = jnp.concatenate(
            [
                k2_ref[9 * (a + 1) + 3 * b : 9 * (a + 1) + 3 * b + 3].reshape(3 * mid, out)
                for _, a in reached
                for b in range(3)
            ],
            axis=1,
        )
        for j in range(0, height + 2, 2):
            rhs = jnp.concatenate(
                [padded[d][:, (j + 2 - b) * LANES : (j + 4 - b) * LANES] for d, _ in reached for b in range(3)], axis=0
            )
            y = jnp.dot(w, rhs, preferred_element_type=F32)
            back = sum(moved_along_width(y[n * mid : (n + 1) * mid], n - 1) for n in range(3))
            back_ref[e, :, j * LANES : (j + 2) * LANES] = back


def as_matrix(ref, c):
    stacked = jnp.concatenate([ref[3 * ab + c] for ab in range(9)], axis=0)
    return stacked.astype(F32).T.astype(BF)


def arrange_kernel(cot_rows_ref, k1_ref, vol_ref, moved_ref, w1_ref, own_ref, scratch):
    def store(d, h, row):
        own_ref[d, :, h * LANES : (h + 1) * LANES] = row.astype(BF)

    by_rows(vol_ref, scratch, store)
    depth, out, cells = cot_rows_ref.shape
    for d in range(depth):
        for h in range(0, cells, LANES):
            row = cot_rows_ref[d, :, h : h + LANES]
            for n, c in enumerate((-1, 0, 1)):
                value = row if c == 0 else moved_along_width(row.astype(F32), c).astype(BF)
                moved_ref[d, n * out : (n + 1) * out, h : h + LANES] = value
    mid = k1_ref.shape[2]
    for c in range(3):
        w1_ref[c * mid : (c + 1) * mid, :] = as_matrix(k1_ref, c)


def sides(axis, one, two):
    me, size = lax.axis_index(axis), lax.axis_size(axis)
    is_odd = odd(axis)
    none = jnp.zeros_like(one)
    before = jnp.where(me == 0, none, jnp.where(is_odd, one, two))
    after = jnp.where(me == size - 1, none, jnp.where(is_odd, two, one))
    return before, after


def rim_kernel(own_ref, one_ref, two_ref, deep_ref, send_one_ref, send_two_ref, scratch):
    depth = own_ref.shape[0]
    deep_ref[depth : 2 * depth] = own_ref[...]
    for at, part in zip((0, 2 * depth), sides("dep", one_ref[...], two_ref[...]), strict=True):

        def store(d, h, row, at=at):
            deep_ref[at + d, :, h * LANES : (h + 1) * LANES] = row.astype(BF)

        by_rows(part, scratch, store)
    n, cells = send_one_ref.shape[2], deep_ref.shape[2]
    first, last = deep_ref[:, :, :n], deep_ref[:, :, cells - n :]
    is_odd = odd(HGT)
    send_one_ref[...] = jnp.where(is_odd, first, last)
    send_two_ref[...] = jnp.where(is_odd, last, first)


def widened(deep_ref, one_ref, two_ref):
    left, right = sides(HGT, one_ref[...], two_ref[...])
    return [jnp.concatenate([left[d], deep_ref[d], right[d]], axis=1) for d in range(deep_ref.shape[0])]


def pack(direct, refs, rows_of, blocks):
    if not direct:
        for j, block in enumerate(blocks):
            refs[0][j] = block
        return
    keep_ref, send_ref = refs
    parts, halves, length, _ = keep_ref.shape
    core = lax.axis_index("core") == 1
    for part in range(parts):
        one, two = (jnp.concatenate(rows_of(part, c), axis=0) for c in range(2))
        for half in range(halves):
            at = slice(half * length, (half + 1) * length)
            keep_ref[part, half] = jnp.where(core, two[at], one[at])
            send_ref[part, half] = jnp.where(core, one[at], two[at]).astype(send_ref.dtype)


def folded(tail):
    half = tail.shape[0] // 2
    return jnp.concatenate([tail[:half], tail[half:]], axis=1)


def activated(w1, rhs, d, depth, heights):
    mid = w1.shape[0] // 3
    y = jnp.dot(w1, rhs, preferred_element_type=F32)
    pre = sum(moved_along_width(y[n * mid : (n + 1) * mid], 1 - n) for n in range(3))
    s = 1.0 / (1.0 + jnp.exp(-pre))
    dep, deps = lax.axis_index("dep"), lax.axis_size("dep")
    hgt, hgts = lax.axis_index(HGT), lax.axis_size(HGT)
    results = []
    for n, side in enumerate(heights):
        p, q = (x[:, n * LANES : (n + 1) * LANES] for x in (pre, s))
        value, slope = (p * q).astype(BF), q * (1.0 + p * (1.0 - q))
        outside = []
        if d == 0:
            outside.append(dep == 0)
        if d == depth - 1:
            outside.append(dep == deps - 1)
        if side < 0:
            outside.append(hgt == 0)
        if side > 0:
            outside.append(hgt == hgts - 1)
        for far in outside:
            value = jnp.where(far, jnp.zeros_like(value), value)
            slope = jnp.where(far, jnp.zeros_like(slope), slope)
        results.append((value, slope))
    return results


def neighbours(ref, d, starts, count):
    return jnp.concatenate(
        [
            jnp.concatenate(
                [ref[d + a, :, (start + b) * LANES : (start + b + count) * LANES] for start in starts], axis=1
            )
            for a in range(3)
            for b in range(3)
        ],
        axis=0,
    )


def products(left, right):
    return lax.dot_general(left, right, (((1,), (1,)), ((), ())), preferred_element_type=F32)


def shares(delta, n_channels, ref, at):
    for n in range(3):
        ref[n * n_channels : (n + 1) * n_channels, at : at + LANES] = moved_along_width(delta, n - 1).astype(BF)


def inner_kernel(deep_ref, w1_ref, moved_ref, back_ref, hidden_ref, second_ref, first_ref, delta_ref):
    w1 = w1_ref[...]
    depth, mid, cells = hidden_ref.shape
    height = cells // LANES
    for d in range(depth):
        for h in range(0, height, 2):
            results = activated(w1, neighbours(deep_ref, d, [h], 2), d, depth, (0, 0))
            for n, (value, slope) in enumerate(results):
                at = (h + n) * LANES
                hidden_ref[d, :, at : at + LANES] = value
                back = back_ref[d, :, at + 2 * LANES : at + 3 * LANES]
                shares(back * slope, mid, delta_ref, d * cells + at)
    own = depth - 2
    left = jnp.concatenate(
        [
            jnp.concatenate([moved_ref[d, :, (2 - b) * LANES : (2 - b) * LANES + cells] for d in range(own)], axis=1)
            for b in range(3)
        ],
        axis=0,
    )
    right = jnp.concatenate(
        [jnp.concatenate([hidden_ref[d + a] for a in range(3)], axis=0) for d in range(own)], axis=1
    )
    second_ref[...] = products(left, right)
    right = jnp.concatenate([neighbours(deep_ref, d, [0], height) for d in range(depth)], axis=1)
    first_ref[...] = products(delta_ref[...], right)


def outer_kernel(
    direct, deep_ref, two_ref, one_ref, w1_ref, back_ref, inner_ref, first_ref, hidden_ref, *grad_refs_and_scratch,
):
    *grad_refs, rows_ref, delta_ref = grad_refs_and_scratch
    for d, row in enumerate(widened(deep_ref, one_ref, two_ref)):
        rows_ref[d] = row
    w1 = w1_ref[...]
    depth, mid, cells = hidden_ref.shape
    last = cells // LANES - 2
    for d in range(depth):
        hidden_ref[d, :, 2 * LANES : last * LANES] = inner_ref[d]
        for h, sides_of in ((0, (-1, 0)), (last, (0, 1))):
            results = activated(w1, neighbours(rows_ref, d, [h], 2), d, depth, sides_of)
            for n, (value, slope) in enumerate(results):
                at = (h + n) * LANES
                hidden_ref[d, :, at : at + LANES] = value
                delta = back_ref[d, :, at : at + LANES] * slope
                shares(delta, mid, delta_ref, (4 * d + (2 if h else 0) + n) * LANES)
    right = jnp.concatenate([neighbours(rows_ref, d, [0, last], 2) for d in range(depth)], axis=1)
    total = first_ref[...] + products(delta_ref[...], right)
    inner = rows_ref.shape[1]
    blocks, tails = [], []
    for n in range(3):
        part = total[n * mid : (n + 1) * mid]
        blocks += [part[:, m * LANES : (m + 1) * LANES] for m in range(2)]
        tails.append(part[:, 2 * LANES :])
    tails.append(jnp.zeros((mid, LANES - 3 * inner), F32))
    blocks.append(jnp.concatenate(tails, axis=1))
    size = mid // lax.axis_size("dp")
    half = size // 2

    def rows_of(part, core):
        return [block[part * size + core * half : part * size + (core + 1) * half] for block in blocks]

    pack(direct, grad_refs, rows_of, blocks)


def second_kernel(direct, hidden_ref, moved_ref, second_ref, *grad_refs):
    depth, mid, cells = hidden_ref.shape
    height = cells // LANES
    own = depth - 2
    out = moved_ref.shape[1] // 3
    heads, tails = [], []
    for b in range(3):
        far = [h for h in range(height - 2) if not 2 <= h + b <= height - 3]
        left = jnp.concatenate(
            [moved_ref[d, :, h * LANES : (h + 1) * LANES] for d in range(own) for h in far], axis=1
        )
        right = jnp.concatenate(
            [
                jnp.concatenate([hidden_ref[d + a, :, (h + b) * LANES : (h + b + 1) * LANES] for a in range(3)], axis=0)
                for d in range(own)
                for h in far
            ],
            axis=1,
        )
        total = second_ref[3 * b * out : 3 * (b + 1) * out, :] + products(left, right)
        for c in range(3):
            part = total[c * out : (c + 1) * out]
            heads.append(part[:, :LANES])
            tails.append(part[:, LANES:])
    blocks = heads + [jnp.concatenate(tails[n : n + 2], axis=1) for n in range(0, 8, 2)]
    size = mid // lax.axis_size("dp")

    def rows_of(part, core):
        at = slice((2 * part + core) * size, (2 * part + core + 1) * size)
        return [block[at] for block in blocks] + [folded(tails[8][at])]

    pack(direct, grad_refs, rows_of, [*blocks, jnp.concatenate([tails[8], jnp.zeros_like(tails[8])], axis=1)])


def features_kernel(hidden_ref, k2_ref, out_ref, token_ref, scratch):
    out, depth, height, _ = out_ref.shape
    w2 = jnp.concatenate([as_matrix(k2_ref, c) for c in range(3)], axis=0)
    for d in range(depth):
        for h in range(0, height, 2):
            rhs = jnp.concatenate(
                [
                    hidden_ref[d + a, :, (h + b) * LANES : (h + b + 2) * LANES]
                    for a in range(3)
                    for b in range(3)
                ],
                axis=0,
            )
            y = jnp.dot(w2, rhs, preferred_element_type=F32)
            total = sum(moved_along_width(y[n * out : (n + 1) * out], 1 - n) for n in range(3))
            for r in range(2):
                row = total[:, r * LANES : (r + 1) * LANES]
                scratch[pl.ds(d * height + h + r, out, stride=depth * height), :] = row
    out_ref[...] = scratch[: out * depth * height].reshape(out_ref.shape).astype(BF)
    token_ref[...] = scratch[:8]


def plane_kernel(moves, *refs):
    keep_first, got_first, keep_second, got_second, kept_ref, *send_refs = refs
    part = lax.rem(lax.axis_index("dp"), keep_first.shape[0])
    half = lax.axis_index("y")

    def total(x, y):
        at = 1 - part if x else part, 1 - half if y else half
        return jnp.concatenate([keep_second[at] + got_second[at].astype(F32), keep_first[at] + got_first[at]], axis=0)

    kept_ref[...] = total(0, 0)
    for (x, y), send_ref in zip(moves, send_refs, strict=True):
        send_ref[...] = total(x, y).astype(BF)


def total_kernel(kept_ref, *refs):
    *got_refs, out_ref = refs
    value = kept_ref[...]
    for ref in got_refs:
        value = value + ref[...].astype(F32)
    out_ref[...] = value.astype(BF)


def depth_kernel(a_ref, b_ref, c_ref, d_ref, _, out_ref):
    one = a_ref[...].astype(F32) + b_ref[...].astype(F32)
    two = c_ref[...].astype(F32) + d_ref[...].astype(F32)
    out_ref[...] = (one + two).astype(BF)


def order_kernel(own_ref, got_ref, out_ref):
    mine = lax.axis_index("y")
    out_ref[mine] = own_ref[...]
    out_ref[1 - mine] = got_ref[...]


def unpack_kernel(length, theirs, in_ref, *refs):
    first_ref, second_ref, first, second, sems = refs[-5:]
    core = lax.axis_index("core")
    at = 1 - core if theirs else core
    _, size, mid = second.shape
    whole = [in_ref[n].astype(F32) for n in range(in_ref.shape[0])]
    rows = jnp.concatenate([x[:length] for x in whole], axis=0)
    for j in range(13):
        value = rows[j * size : (j + 1) * size]
        for m, k in enumerate((j, 9 + j) if j < 9 else (2 * j, 2 * j + 1)):
            second[k] = value[:, m * mid : (m + 1) * mid]
    value = rows[13 * size : 13 * size + size // 2]
    second[26] = jnp.concatenate([value[:, :mid], value[:, mid:]], axis=0)
    copies = [pltpu.make_async_copy(second, second_ref.at[:, pl.ds(pl.multiple_of(at * size, size), size), :], sems.at[1])]
    copies[0].start()
    _, half, inner = first.shape
    rows = jnp.concatenate([x[length:] for x in whole], axis=0)
    for j in range(7):
        value = rows[j * half : (j + 1) * half]
        for m in range(4):
            c, ab = (j // 2, 4 * (j % 2) + m) if j < 6 else (m, 8)
            if c < 3:
                first[3 * ab + c] = value[:, m * inner : (m + 1) * inner]
    copies.append(
        pltpu.make_async_copy(first, first_ref.at[:, pl.ds(pl.multiple_of(at * half, half), half), :], sems.at[0])
    )
    copies[1].start()
    for copy in copies:
        copy.wait()


def swapped(x, axis, first):
    axes = (axis,) if isinstance(axis, str) else axis
    parts, size = lax.axis_size("dp"), lax.axis_size(axis)
    partner = list(range(parts * size))
    for i in partner:
        part, at = divmod(i, size)
        if first <= at < size - (size - first) % 2:
            partner[i] = part * size + (at - first ^ 1) + first
        elif parts % 2 == 0:
            partner[i] = (part ^ 1) * size + at
    return lax.ppermute(x, ("dp", *axes), list(enumerate(partner)))


def across(x, *moves):
    axes = tuple(axis for axis, _ in moves)
    flip = 0
    for axis, bit in moves:
        flip = flip * lax.axis_size(axis) + bit
    return lax.ppermute(x, axes, [(i, i ^ flip) for i in range(lax.axis_size(axes))])


def scattered(rows, length):
    halves = lax.axis_size("y")
    grad = jnp.pad(rows, ((0, 0), (0, 0), (0, halves * length - rows.shape[2]), (0, 0)))
    grad = lax.psum_scatter(grad, "dp", scatter_dimension=0, tiled=True)
    grad = grad.reshape(1, 2, halves, length, LANES)
    core = lax.axis_index("core")
    return tuple(lax.dynamic_index_in_dim(grad, at, 1, False) for at in (core, 1 - core))


def assembled(own, got, length, size, inner, mid):
    core = lax.axis_index("core")
    both = jnp.stack([own, got]).astype(F32)
    both = jnp.stack([lax.dynamic_index_in_dim(both, at, 0, False) for at in (core, 1 - core)])
    rows = both[:, :, :length].reshape(2, -1, LANES)
    second = [None] * 27
    for j in range(13):
        for m, k in enumerate((j, 9 + j) if j < 9 else (2 * j, 2 * j + 1)):
            second[k] = rows[:, j * size : (j + 1) * size, m * mid : (m + 1) * mid].reshape(2 * size, mid)
    tail = rows[:, 13 * size : 13 * size + size // 2]
    second[26] = jnp.concatenate([tail[:, :, :mid], tail[:, :, mid:]], axis=1).reshape(2 * size, mid)
    rows, half = both[:, :, length:].reshape(2, -1, LANES), size // 2
    first = [None] * 27
    for j in range(7):
        for m in range(4):
            c, ab = (j // 2, 4 * (j % 2) + m) if j < 6 else (m, 8)
            if c < 3:
                value = rows[:, j * half : (j + 1) * half, m * inner : (m + 1) * inner]
                first[3 * ab + c] = value.reshape(size, inner)
    return jnp.stack(first), jnp.stack(second)


def per_device(volume, kernel_first, kernel_second, cotangent):
    _, inner, depth, height, width = volume.shape
    mid, out = kernel_first.shape[1], kernel_second.shape[1]
    cells = height * width
    parts = lax.axis_size("dp")
    k1, k2 = jnp.swapaxes(kernel_first, 1, 2), jnp.swapaxes(kernel_second, 1, 2)
    rows = depth * height

    one, two = swapped(volume[0], "dep", 0), swapped(volume[0], "dep", 1)
    (blank,) = call(blank_kernel, [shape((out, 2 * width), BF)], [], flops=3_000_000_000)
    cot_rows, back = call(
        spread_kernel,
        [
            shape((depth, out, cells), BF),
            shape((depth + 2, mid, cells + 2 * width), F32),
        ],
        [cotangent[0], k2, blank],
        [pltpu.VMEM(((out + 1) * rows, width), F32)],
        flops=1_100_000_000,
    )
    moved, w1, vol = call(
        arrange_kernel,
        [
            shape((depth, 3 * out, cells), BF),
            shape((3 * mid, 9 * inner), BF),
            shape((depth, inner, cells), BF),
        ],
        [cot_rows, k1, volume[0]],
        [pltpu.VMEM(((inner + 1) * rows, width), F32)],
        flops=500_000_000,
    )
    deep, one, two = call(
        rim_kernel,
        [shape((3 * depth, inner, cells), BF)] + [shape((3 * depth, inner, 2 * width), BF)] * 2,
        [vol, one, two],
        [pltpu.VMEM(((inner + 1) * rows, width), F32)],
    )
    one, two = swapped(one, HGT, 0), swapped(two, HGT, 1)
    size = mid // parts
    direct = parts == 2 and size % 16 == 0
    halves = lax.axis_size("y")
    length_second, length_first = (-(-units * size // (16 * halves)) * 8 for units in (27, 7))
    rows_in, rows_out = height - 2, 4
    inner_hidden, inner_second, inner_first = call(
        inner_kernel,
        [
            shape((depth + 2, mid, rows_in * width), BF),
            shape((9 * out, 3 * mid), F32),
            shape((3 * mid, 9 * inner), F32),
        ],
        [deep, w1, moved, back],
        [pltpu.VMEM((3 * mid, (depth + 2) * rows_in * width), BF)],
        flops=1_500_000_000,
    )
    hidden, *first = call(
        functools.partial(outer_kernel, direct),
        [shape((depth + 2, mid, cells + 2 * width), BF)]
        + ([shape((parts, halves, length_first, width), F32)] * 2 if direct else [shape((7, mid, LANES), F32)]),
        [deep, two, one, w1, back, inner_hidden, inner_first],
        [
            pltpu.VMEM((3 * depth, inner, cells + 4 * width), BF),
            pltpu.VMEM((3 * mid, (depth + 2) * rows_out * width), BF),
        ],
        flops=1_000_000_000,
    )
    second = call(
        functools.partial(second_kernel, direct),
        [shape((parts, halves, length_second, width), kind) for kind in (F32, BF)]
        if direct
        else [shape((14, out, LANES), F32)],
        [hidden, moved, inner_second],
        flops=4_000_000_000,
    )
    if direct:
        moves = [(1, 0), (0, 1), (1, 1)]
    else:
        moves = [(0, 1)]
        blocks = second[0].reshape(14, parts, 2, size, LANES).transpose(1, 2, 0, 3, 4)
        tail = blocks[:, :, 13, :, :mid]
        tail = jnp.concatenate([tail[:, :, : size // 2], tail[:, :, size // 2 :]], axis=-1)
        rows_second = jnp.concatenate([blocks[:, :, :13].reshape(parts, 2, 13 * size, LANES), tail], axis=2)
        second = scattered(rows_second, length_second)
        blocks = first[0].reshape(7, parts, 2, size // 2, LANES).transpose(1, 2, 0, 3, 4)
        first = scattered(blocks.reshape(parts, 2, 7 * (size // 2), LANES), length_first)
    block = (length_second + length_first, width)
    kept, *sends = call(
        functools.partial(plane_kernel, moves),
        [shape(block, F32)] + [shape(block, BF)] * len(moves),
        [x for keep, send in (first, second) for x in (keep, across(send, ("core", 1)))],
    )
    gots = [across(send, ("dp", x), ("y", y)) for send, (x, y) in zip(sends, moves, strict=True)]
    (share,) = call(total_kernel, [shape(block, BF)], [kept, *gots])
    features, token = call(
        features_kernel,
        [shape(cotangent.shape[1:], BF), shape((8, width), F32)],
        [hidden, k2],
        [pltpu.VMEM(((out + 1) * rows, width), F32)],
        flops=900_000_000,
    )
    gots = [across(share, ("dep", bits)) for bits in (1, 2, 3)]
    (share,) = call(depth_kernel, [shape(block, BF)], [share, *gots, token])
    (own,) = call(order_kernel, [shape((halves, *block), BF)], [share, across(share, ("y", 1))])
    got = across(own, ("core", 1))
    if size % 16 == 0:
        grads = [shape((27, size, inner), F32), shape((27, 2 * size, mid), F32)]
        scratch = [
            pltpu.VMEM((27, size // 2, inner), F32),
            pltpu.VMEM((27, size, mid), F32),
            pltpu.SemaphoreType.DMA((2,)),
        ]
        written = call(functools.partial(unpack_kernel, length_second, False), grads, [own], scratch, far_outs=True)
        grad_first, grad_second = call(
            functools.partial(unpack_kernel, length_second, True),
            grads,
            [got, *written],
            scratch,
            far=(1, 2),
            far_outs=True,
            aliases={1: 0, 2: 1},
        )
    else:
        grad_first, grad_second = assembled(own, got, length_second, size, inner, mid)
    return features[None], grad_first, grad_second


def solution(mesh):
    dp, dep, hgt = (mesh.shape[axis] for axis in ("dp", "dep", "hgt"))
    split = jax.sharding.Mesh(mesh.devices.reshape(dp, dep, hgt // 2, 2), ("dp", "dep", *HGT))
    block = P("dp", None, "dep", HGT, None)
    return jax.shard_map(
        per_device,
        mesh=split,
        in_specs=(block, P(), P(), block),
        out_specs=(block, P(None, "dp", None), P(None, "dp", None)),
        check_vma=False,
    )
```

```python
import functools

import jax
import jax.numpy as jnp
from jax import lax
from jax.experimental import pallas as pl
from jax.experimental.pallas import tpu as pltpu
from jax.sharding import PartitionSpec as P

BF, F32 = jnp.bfloat16, jnp.float32
LANES = 128
HGT = ("y", "core")
VMEM_BYTES = 28 * 2**20


def call(body, outs, args, scratch=(), flops=0, far=(), far_outs=(), aliases=None):
    moved = sum(x.size * x.dtype.itemsize for x in (*outs, *args))
    return pl.pallas_call(
        body,
        out_shape=outs,
        in_specs=[pl.BlockSpec(memory_space=pl.ANY if n in far else pltpu.VMEM) for n in range(len(args))],
        out_specs=[pl.BlockSpec(memory_space=pl.ANY if n in far_outs else pltpu.VMEM) for n in range(len(outs))],
        scratch_shapes=list(scratch),
        input_output_aliases=aliases or {},
        compiler_params=pltpu.CompilerParams(vmem_limit_bytes=VMEM_BYTES),
        cost_estimate=pl.CostEstimate(flops=flops, bytes_accessed=moved, transcendentals=0),
    )(*args)


def shape(dims, dtype):
    return jax.ShapeDtypeStruct(dims, dtype)


def moved_along_width(x, c):
    if c == 0:
        return x
    pieces = []
    for start in range(0, x.shape[1], LANES):
        piece = x[:, start : start + LANES]
        lane = lax.broadcasted_iota(jnp.int32, piece.shape, 1)
        rolled = pltpu.roll(piece, c % LANES, 1)
        pieces.append(jnp.where(lane == (0 if c == 1 else LANES - 1), 0.0, rolled))
    return pieces[0] if len(pieces) == 1 else jnp.concatenate(pieces, axis=1)


def by_rows(ref, scratch, store):
    channels, depth, height, width = ref.shape
    rows = depth * height
    scratch[: channels * rows] = ref[...].astype(F32).reshape(channels * rows, width)
    for d in range(depth):
        for h in range(height):
            store(d, h, scratch[pl.ds(d * height + h, channels, stride=rows), :])


def odd(axis):
    return lax.rem(lax.axis_index(axis), 2) == 1


def blank_kernel(out_ref):
    out_ref[...] = jnp.zeros(out_ref.shape, BF)


def spread_kernel(cot_ref, k2_ref, blank_ref, cot_rows_ref, back_ref, scratch):
    out, depth, height, _ = cot_ref.shape
    rows = [[None] * height for _ in range(depth)]

    def store(d, h, row):
        rows[d][h] = row.astype(BF)
        cot_rows_ref[d, :, h * LANES : (h + 1) * LANES] = rows[d][h]

    by_rows(cot_ref, scratch, store)
    mid = k2_ref.shape[1]
    none = blank_ref[...]
    padded = [jnp.concatenate([none, *rows[d], none], axis=1) for d in range(depth)]
    for e in range(depth + 2):
        reached = [(d, e - 1 - d) for d in range(depth) if abs(e - 1 - d) <= 1]
        w = jnp.concatenate(
            [
                k2_ref[9 * (a + 1) + 3 * b : 9 * (a + 1) + 3 * b + 3].reshape(3 * mid, out)
                for _, a in reached
                for b in range(3)
            ],
            axis=1,
        )
        for j in range(0, height + 2, 2):
            rhs = jnp.concatenate(
                [padded[d][:, (j + 2 - b) * LANES : (j + 4 - b) * LANES] for d, _ in reached for b in range(3)], axis=0
            )
            y = jnp.dot(w, rhs, preferred_element_type=F32)
            back = sum(moved_along_width(y[n * mid : (n + 1) * mid], n - 1) for n in range(3))
            back_ref[e, :, j * LANES : (j + 2) * LANES] = back


def as_matrix(ref, c):
    stacked = jnp.concatenate([ref[3 * ab + c] for ab in range(9)], axis=0)
    return stacked.astype(F32).T.astype(BF)


def arrange_kernel(cot_rows_ref, k1_ref, vol_ref, moved_ref, w1_ref, own_ref, scratch):
    def store(d, h, row):
        own_ref[d, :, h * LANES : (h + 1) * LANES] = row.astype(BF)

    by_rows(vol_ref, scratch, store)
    depth, out, cells = cot_rows_ref.shape
    for d in range(depth):
        for h in range(0, cells, LANES):
            row = cot_rows_ref[d, :, h : h + LANES]
            for n, c in enumerate((-1, 0, 1)):
                value = row if c == 0 else moved_along_width(row.astype(F32), c).astype(BF)
                moved_ref[d, n * out : (n + 1) * out, h : h + LANES] = value
    mid = k1_ref.shape[2]
    for c in range(3):
        w1_ref[c * mid : (c + 1) * mid, :] = as_matrix(k1_ref, c)


def sides(axis, one, two):
    me, size = lax.axis_index(axis), lax.axis_size(axis)
    is_odd = odd(axis)
    none = jnp.zeros_like(one)
    before = jnp.where(me == 0, none, jnp.where(is_odd, one, two))
    after = jnp.where(me == size - 1, none, jnp.where(is_odd, two, one))
    return before, after


def rim_kernel(own_ref, one_ref, two_ref, deep_ref, send_one_ref, send_two_ref, scratch):
    depth = own_ref.shape[0]
    deep_ref[depth : 2 * depth] = own_ref[...]
    for at, part in zip((0, 2 * depth), sides("dep", one_ref[...], two_ref[...]), strict=True):

        def store(d, h, row, at=at):
            deep_ref[at + d, :, h * LANES : (h + 1) * LANES] = row.astype(BF)

        by_rows(part, scratch, store)
    n, cells = send_one_ref.shape[2], deep_ref.shape[2]
    first, last = deep_ref[:, :, :n], deep_ref[:, :, cells - n :]
    is_odd = odd(HGT)
    send_one_ref[...] = jnp.where(is_odd, first, last)
    send_two_ref[...] = jnp.where(is_odd, last, first)


def widened(deep_ref, one_ref, two_ref):
    left, right = sides(HGT, one_ref[...], two_ref[...])
    return [jnp.concatenate([left[d], deep_ref[d], right[d]], axis=1) for d in range(deep_ref.shape[0])]


def pack(direct, refs, rows_of, blocks):
    if not direct:
        for j, block in enumerate(blocks):
            refs[0][j] = block
        return
    keep_ref, send_ref = refs
    parts, halves, length, _ = keep_ref.shape
    core = lax.axis_index("core") == 1

    def filled(rows):
        rest = length - sum(x.shape[0] for x in rows)
        return jnp.concatenate([*rows, jnp.zeros((rest, LANES), F32)] if rest else rows, axis=0)

    for part in range(parts):
        for half in range(halves):
            one, two = (filled(rows_of(part, c)[half]) for c in range(2))
            keep_ref[part, half] = jnp.where(core, two, one)
            send_ref[part, half] = jnp.where(core, one, two).astype(send_ref.dtype)


def folded(tail):
    half = tail.shape[0] // 2
    return jnp.concatenate([tail[:half], tail[half:]], axis=1)


def activated(w1, rhs, d, depth, heights):
    mid = w1.shape[0] // 3
    y = jnp.dot(w1, rhs, preferred_element_type=F32)
    pre = sum(moved_along_width(y[n * mid : (n + 1) * mid], 1 - n) for n in range(3))
    s = 1.0 / (1.0 + jnp.exp(-pre))
    dep, deps = lax.axis_index("dep"), lax.axis_size("dep")
    hgt, hgts = lax.axis_index(HGT), lax.axis_size(HGT)
    results = []
    for n, side in enumerate(heights):
        p, q = (x[:, n * LANES : (n + 1) * LANES] for x in (pre, s))
        value, slope = (p * q).astype(BF), q * (1.0 + p * (1.0 - q))
        outside = []
        if d == 0:
            outside.append(dep == 0)
        if d == depth - 1:
            outside.append(dep == deps - 1)
        if side < 0:
            outside.append(hgt == 0)
        if side > 0:
            outside.append(hgt == hgts - 1)
        for far in outside:
            value = jnp.where(far, jnp.zeros_like(value), value)
            slope = jnp.where(far, jnp.zeros_like(slope), slope)
        results.append((value, slope))
    return results


def neighbours(ref, d, starts, count):
    return jnp.concatenate(
        [
            jnp.concatenate(
                [ref[d + a, :, (start + b) * LANES : (start + b + count) * LANES] for start in starts], axis=1
            )
            for a in range(3)
            for b in range(3)
        ],
        axis=0,
    )


def products(left, right):
    return lax.dot_general(left, right, (((1,), (1,)), ((), ())), preferred_element_type=F32)


def shares(delta, n_channels, ref, at):
    for n in range(3):
        ref[n * n_channels : (n + 1) * n_channels, at : at + LANES] = moved_along_width(delta, n - 1).astype(BF)


def inner_kernel(deep_ref, w1_ref, moved_ref, back_ref, hidden_ref, second_ref, first_ref, delta_ref):
    w1 = w1_ref[...]
    depth, mid, cells = hidden_ref.shape
    height = cells // LANES
    for d in range(depth):
        for h in range(0, height, 2):
            results = activated(w1, neighbours(deep_ref, d, [h], 2), d, depth, (0, 0))
            for n, (value, slope) in enumerate(results):
                at = (h + n) * LANES
                hidden_ref[d, :, at : at + LANES] = value
                back = back_ref[d, :, at + 2 * LANES : at + 3 * LANES]
                shares(back * slope, mid, delta_ref, d * cells + at)
    own = depth - 2
    left = jnp.concatenate(
        [
            jnp.concatenate([moved_ref[d, :, (2 - b) * LANES : (2 - b) * LANES + cells] for d in range(own)], axis=1)
            for b in range(3)
        ],
        axis=0,
    )
    right = jnp.concatenate(
        [jnp.concatenate([hidden_ref[d + a] for a in range(3)], axis=0) for d in range(own)], axis=1
    )
    second_ref[...] = products(left, right)
    right = jnp.concatenate([neighbours(deep_ref, d, [0], height) for d in range(depth)], axis=1)
    first_ref[...] = products(delta_ref[...], right)


def outer_kernel(
    direct, deep_ref, two_ref, one_ref, w1_ref, back_ref, inner_ref, first_ref, hidden_ref, *grad_refs_and_scratch,
):
    *grad_refs, rows_ref, delta_ref = grad_refs_and_scratch
    for d, row in enumerate(widened(deep_ref, one_ref, two_ref)):
        rows_ref[d] = row
    w1 = w1_ref[...]
    depth, mid, cells = hidden_ref.shape
    last = cells // LANES - 2
    for d in range(depth):
        hidden_ref[d, :, 2 * LANES : last * LANES] = inner_ref[d]
        for h, sides_of in ((0, (-1, 0)), (last, (0, 1))):
            results = activated(w1, neighbours(rows_ref, d, [h], 2), d, depth, sides_of)
            for n, (value, slope) in enumerate(results):
                at = (h + n) * LANES
                hidden_ref[d, :, at : at + LANES] = value
                delta = back_ref[d, :, at : at + LANES] * slope
                shares(delta, mid, delta_ref, (4 * d + (2 if h else 0) + n) * LANES)
    right = jnp.concatenate([neighbours(rows_ref, d, [0, last], 2) for d in range(depth)], axis=1)
    total = first_ref[...] + products(delta_ref[...], right)
    inner = rows_ref.shape[1]
    blocks, tails = [], []
    for n in range(3):
        part = total[n * mid : (n + 1) * mid]
        blocks += [part[:, m * LANES : (m + 1) * LANES] for m in range(2)]
        tails.append(part[:, 2 * LANES :])
    tails.append(jnp.zeros((mid, LANES - 3 * inner), F32))
    blocks.append(jnp.concatenate(tails, axis=1))
    size = mid // lax.axis_size("dp")
    half = size // 2

    def rows_of(part, core):
        rows = [block[part * size + core * half : part * size + (core + 1) * half] for block in blocks]
        return rows[:3], rows[3:]

    pack(direct, grad_refs, rows_of, blocks)


def second_kernel(direct, hidden_ref, moved_ref, second_ref, *grad_refs):
    depth, mid, cells = hidden_ref.shape
    height = cells // LANES
    own = depth - 2
    out = moved_ref.shape[1] // 3
    heads, tails = [], []
    for b in range(3):
        far = [h for h in range(height - 2) if not 2 <= h + b <= height - 3]
        left = jnp.concatenate(
            [moved_ref[d, :, h * LANES : (h + 1) * LANES] for d in range(own) for h in far], axis=1
        )
        right = jnp.concatenate(
            [
                jnp.concatenate([hidden_ref[d + a, :, (h + b) * LANES : (h + b + 1) * LANES] for a in range(3)], axis=0)
                for d in range(own)
                for h in far
            ],
            axis=1,
        )
        total = second_ref[3 * b * out : 3 * (b + 1) * out, :] + products(left, right)
        for c in range(3):
            part = total[c * out : (c + 1) * out]
            heads.append(part[:, :LANES])
            tails.append(part[:, LANES:])
    blocks = heads + [jnp.concatenate(tails[n : n + 2], axis=1) for n in range(0, 8, 2)]
    size = mid // lax.axis_size("dp")

    def rows_of(part, core):
        at = slice((2 * part + core) * size, (2 * part + core + 1) * size)
        rows = [block[at] for block in blocks] + [folded(tails[8][at])]
        return rows[:7], rows[7:]

    pack(direct, grad_refs, rows_of, [*blocks, jnp.concatenate([tails[8], jnp.zeros_like(tails[8])], axis=1)])


def features_kernel(hidden_ref, k2_ref, out_ref, token_ref, scratch):
    out, depth, height, _ = out_ref.shape
    w2 = jnp.concatenate([as_matrix(k2_ref, c) for c in range(3)], axis=0)
    for d in range(depth):
        for h in range(0, height, 2):
            rhs = jnp.concatenate(
                [
                    hidden_ref[d + a, :, (h + b) * LANES : (h + b + 2) * LANES]
                    for a in range(3)
                    for b in range(3)
                ],
                axis=0,
            )
            y = jnp.dot(w2, rhs, preferred_element_type=F32)
            total = sum(moved_along_width(y[n * out : (n + 1) * out], 1 - n) for n in range(3))
            for r in range(2):
                row = total[:, r * LANES : (r + 1) * LANES]
                scratch[pl.ds(d * height + h + r, out, stride=depth * height), :] = row
    out_ref[...] = scratch[: out * depth * height].reshape(out_ref.shape).astype(BF)
    token_ref[...] = scratch[:8]


def plane_kernel(moves, cuts, *refs):
    sums, (kept_ref, *send_refs) = refs[: -1 - len(moves)], refs[-1 - len(moves) :]
    part = lax.rem(lax.axis_index("dp"), sums[0].shape[0])
    half = lax.axis_index("y")

    def total(x, y):
        at = 1 - part if x else part, 1 - half if y else half
        values = [keep[at] + got[at].astype(F32) for keep, got in zip(sums[::2], sums[1::2], strict=True)]
        if len(values) == 1:
            return values[0]
        one, two = (jnp.concatenate([v[:n] for v, n in zip(values, cut, strict=True)], axis=0) for cut in cuts)
        return jnp.where(at[1] == 0, one, two)

    kept_ref[...] = total(0, 0)
    for (x, y), send_ref in zip(moves, send_refs, strict=True):
        send_ref[...] = total(x, y).astype(BF)


def total_kernel(kept_ref, *refs):
    *got_refs, out_ref = refs
    value = kept_ref[...]
    for ref in got_refs:
        value = value + ref[...].astype(F32)
    out_ref[...] = value.astype(BF)


def depth_kernel(a_ref, b_ref, c_ref, d_ref, _, out_ref, padded_ref):
    one = a_ref[...].astype(F32) + b_ref[...].astype(F32)
    two = c_ref[...].astype(F32) + d_ref[...].astype(F32)
    out_ref[...] = (one + two).astype(BF)
    rest = jnp.zeros((padded_ref.shape[0] - out_ref.shape[0], LANES), F32)
    padded_ref[...] = jnp.concatenate([one + two, rest], axis=0).astype(BF)


def write_kernel(count, wheres, *refs):
    n_scratch = 6
    in_refs = refs[:count]
    out_refs, scratch = refs[: -n_scratch * count], refs[-n_scratch * count :]
    if wheres[0][1]:
        first_ref, second_ref, token_ref = out_refs[-3:]
        token_ref[...] = jnp.zeros(token_ref.shape, F32)
    else:
        first_ref, second_ref = out_refs[-2:]
    core, y = lax.axis_index("core"), lax.axis_index("y")

    def begun(n, half):
        wide, last, low, high, tail, sems = scratch[n_scratch * n : n_scratch * (n + 1)]
        own_core, _ = wheres[n]
        at = core if own_core else 1 - core
        rows = in_refs[n][...].astype(F32)
        _, _, size, mid = wide.shape
        _, small, inner = low.shape
        here = pl.ds(pl.multiple_of(at * size, size), size)
        count = 2 if half else 7
        for j in range(count):
            value = rows[j * size : (j + 1) * size]
            for m in range(2):
                wide[m, j] = value[:, m * mid : (m + 1) * mid]
        pairs = [(wide.at[:, :count], second_ref.at[0:2, 7 * half : 7 * half + count, here, :])]
        row = count * size
        if half:
            for j in range(4):
                value = rows[row : row + size]
                row += size
                for m in range(2):
                    last[2 * j + m] = value[:, m * mid : (m + 1) * mid]
            value = rows[row : row + size // 2]
            row += size // 2
            last[8] = jnp.concatenate([value[:, :mid], value[:, mid:]], axis=0)
            pairs.append((last, second_ref.at[2, :, here, :]))
        copies = [pltpu.make_async_copy(src, dst, sems.at[i]) for i, (src, dst) in enumerate(pairs)]
        for copy in copies:
            copy.start()
        here = pl.ds(pl.multiple_of(at * small, small), small)
        places = [(high, 0, 4), (low, 0, 4), (low, 4, 4), (tail, 0, 3)] if half else [(low, 0, 4), (low, 4, 4), (high, 0, 4)]
        for ref, start, number in places:
            value = rows[row : row + small]
            row += small
            for m in range(number):
                ref[start + m] = value[:, m * inner : (m + 1) * inner]
        if half:
            pairs = [
                (high, first_ref.at[4:8, 1, here, :]),
                (low, first_ref.at[0:8, 2, here, :]),
                (tail, first_ref.at[8, :, here, :]),
            ]
        else:
            pairs = [(low, first_ref.at[0:8, 0, here, :]), (high, first_ref.at[0:4, 1, here, :])]
        more = [pltpu.make_async_copy(src, dst, sems.at[2 + i]) for i, (src, dst) in enumerate(pairs)]
        for copy in more:
            copy.start()
        return copies + more

    for half in range(2):

        @pl.when(y == half)
        def _(half=half):
            copies = []
            for n, (_, own_y) in enumerate(wheres):
                copies += begun(n, half if own_y else 1 - half)
            for copy in copies:
                copy.wait()


def swapped(x, axis, first):
    axes = (axis,) if isinstance(axis, str) else axis
    parts, size = lax.axis_size("dp"), lax.axis_size(axis)
    partner = list(range(parts * size))
    for i in partner:
        part, at = divmod(i, size)
        if first <= at < size - (size - first) % 2:
            partner[i] = part * size + (at - first ^ 1) + first
        elif parts % 2 == 0:
            partner[i] = (part ^ 1) * size + at
    return lax.ppermute(x, ("dp", *axes), list(enumerate(partner)))


def across(x, *moves):
    axes = tuple(axis for axis, _ in moves)
    flip = 0
    for axis, bit in moves:
        flip = flip * lax.axis_size(axis) + bit
    return lax.ppermute(x, axes, [(i, i ^ flip) for i in range(lax.axis_size(axes))])


def scattered(rows, cuts):
    halves = [
        jnp.concatenate([x[:, :, :n] if at == 0 else x[:, :, x.shape[2] - n :] for x, n in zip(rows, cut)], axis=2)
        for at, cut in enumerate(cuts)
    ]
    grad = lax.psum_scatter(jnp.stack(halves, axis=2), "dp", scatter_dimension=0, tiled=True)
    core = lax.axis_index("core")
    return tuple(lax.dynamic_index_in_dim(grad, at, 1, False) for at in (core, 1 - core))


def assembled(quarters, size, inner, mid):
    first, second = ([[None, None] for _ in range(27)] for _ in range(2))
    half = size // 2
    for core in range(2):
        for y in range(2):
            rows, row = quarters[core][y].astype(F32), 0
            for j in range(7) if y == 0 else range(7, 13):
                for m, k in enumerate((j, 9 + j) if j < 9 else (2 * j, 2 * j + 1)):
                    second[k][core] = rows[row : row + size, m * mid : (m + 1) * mid]
                row += size
            if y == 1:
                tail = rows[row : row + half]
                second[26][core] = jnp.concatenate([tail[:, :mid], tail[:, mid:]], axis=0)
                row += half
            for j in range(3) if y == 0 else range(3, 7):
                for m in range(4):
                    c, ab = (j // 2, 4 * (j % 2) + m) if j < 6 else (m, 8)
                    if c < 3:
                        first[3 * ab + c][core] = rows[row : row + half, m * inner : (m + 1) * inner]
                row += half
    return tuple(jnp.stack([jnp.concatenate(both, axis=0) for both in grad]) for grad in (first, second))


def per_device(volume, kernel_first, kernel_second, cotangent):
    _, inner, depth, height, width = volume.shape
    mid, out = kernel_first.shape[1], kernel_second.shape[1]
    cells = height * width
    parts = lax.axis_size("dp")
    k1, k2 = jnp.swapaxes(kernel_first, 1, 2), jnp.swapaxes(kernel_second, 1, 2)
    rows = depth * height

    one, two = swapped(volume[0], "dep", 0), swapped(volume[0], "dep", 1)
    (blank,) = call(blank_kernel, [shape((out, 2 * width), BF)], [], flops=3_000_000_000)
    cot_rows, back = call(
        spread_kernel,
        [
            shape((depth, out, cells), BF),
            shape((depth + 2, mid, cells + 2 * width), F32),
        ],
        [cotangent[0], k2, blank],
        [pltpu.VMEM(((out + 1) * rows, width), F32)],
        flops=1_100_000_000,
    )
    moved, w1, vol = call(
        arrange_kernel,
        [
            shape((depth, 3 * out, cells), BF),
            shape((3 * mid, 9 * inner), BF),
            shape((depth, inner, cells), BF),
        ],
        [cot_rows, k1, volume[0]],
        [pltpu.VMEM(((inner + 1) * rows, width), F32)],
        flops=500_000_000,
    )
    deep, one, two = call(
        rim_kernel,
        [shape((3 * depth, inner, cells), BF)] + [shape((3 * depth, inner, 2 * width), BF)] * 2,
        [vol, one, two],
        [pltpu.VMEM(((inner + 1) * rows, width), F32)],
    )
    one, two = swapped(one, HGT, 0), swapped(two, HGT, 1)
    size = mid // parts
    direct = parts == 2 and size % 16 == 0
    halves = lax.axis_size("y")
    cuts = ((7 * size, 3 * size // 2), (13 * size // 2, 2 * size))
    length_second, length_first = 7 * size, 2 * size
    rows_in, rows_out = height - 2, 4
    inner_hidden, inner_second, inner_first = call(
        inner_kernel,
        [
            shape((depth + 2, mid, rows_in * width), BF),
            shape((9 * out, 3 * mid), F32),
            shape((3 * mid, 9 * inner), F32),
        ],
        [deep, w1, moved, back],
        [pltpu.VMEM((3 * mid, (depth + 2) * rows_in * width), BF)],
        flops=1_500_000_000,
    )
    hidden, *first = call(
        functools.partial(outer_kernel, direct),
        [shape((depth + 2, mid, cells + 2 * width), BF)]
        + ([shape((parts, halves, length_first, width), F32)] * 2 if direct else [shape((7, mid, LANES), F32)]),
        [deep, two, one, w1, back, inner_hidden, inner_first],
        [
            pltpu.VMEM((3 * depth, inner, cells + 4 * width), BF),
            pltpu.VMEM((3 * mid, (depth + 2) * rows_out * width), BF),
        ],
        flops=1_000_000_000,
    )
    second = call(
        functools.partial(second_kernel, direct),
        [shape((parts, halves, length_second, width), kind) for kind in (F32, BF)]
        if direct
        else [shape((14, out, LANES), F32)],
        [hidden, moved, inner_second],
        flops=4_000_000_000,
    )
    if direct:
        moves = [(1, 0), (0, 1), (1, 1)]
        grads = [second, first]
    else:
        moves = [(0, 1)]
        blocks = second[0].reshape(14, parts, 2, size, LANES).transpose(1, 2, 0, 3, 4)
        tail = blocks[:, :, 13, :, :mid]
        tail = jnp.concatenate([tail[:, :, : size // 2], tail[:, :, size // 2 :]], axis=-1)
        rows_second = jnp.concatenate([blocks[:, :, :13].reshape(parts, 2, 13 * size, LANES), tail], axis=2)
        blocks = first[0].reshape(7, parts, 2, size // 2, LANES).transpose(1, 2, 0, 3, 4)
        rows_first = blocks.reshape(parts, 2, 7 * (size // 2), LANES)
        grads = [scattered([rows_second, rows_first], cuts)]
    block = (sum(cuts[0]), width)
    kept, *sends = call(
        functools.partial(plane_kernel, moves, cuts),
        [shape(block, F32)] + [shape(block, BF)] * len(moves),
        [x for keep, send in grads for x in (keep, across(send, ("core", 1)))],
    )
    gots = [across(send, ("dp", x), ("y", y)) for send, (x, y) in zip(sends, moves, strict=True)]
    (share,) = call(total_kernel, [shape(block, BF)], [kept, *gots])
    features, token = call(
        features_kernel,
        [shape(cotangent.shape[1:], BF), shape((8, width), F32)],
        [hidden, k2],
        [pltpu.VMEM(((out + 1) * rows, width), F32)],
        flops=900_000_000,
    )
    gots = [across(share, ("dep", bits)) for bits in (1, 2, 3)]
    share, for_y = call(depth_kernel, [shape(block, BF), shape((block[0] + 16, width), BF)], [share, *gots, token])
    other, far = across(share, ("core", 1)), across(for_y, ("y", 1))
    far_other = across(for_y, ("y", 1), ("core", 1))
    if size % 16 == 0:
        outs = [shape((9, 3, size, inner), F32), shape((3, 9, 2 * size, mid), F32)]

        def written(quarters, wheres, before=()):
            scratch = [
                pltpu.VMEM((2, 7, size, mid), F32),
                pltpu.VMEM((9, size, mid), F32),
                pltpu.VMEM((8, size // 2, inner), F32),
                pltpu.VMEM((4, size // 2, inner), F32),
                pltpu.VMEM((3, size // 2, inner), F32),
                pltpu.SemaphoreType.DMA((5,)),
            ]
            count = len(quarters)
            return call(
                functools.partial(write_kernel, count, wheres),
                outs if before else [*outs, shape((8, width), F32)],
                [*quarters, *before],
                scratch * count,
                far=range(count, count + len(before)),
                far_outs=(0, 1),
                aliases={count + n: n for n in range(len(before))},
            )

        *grads, _ = written([share, other], [(True, True), (False, True)])
        grads = written([far_other, far], [(False, False), (True, False)], grads)
        grad_first, grad_second = (grad.reshape(27, *grad.shape[2:]) for grad in grads)
    else:
        core, y = lax.axis_index("core"), lax.axis_index("y")
        stacked = jnp.stack([jnp.stack([share, far[: block[0]]]), jnp.stack([other, far_other[: block[0]]])])
        quarters = [
            [stacked[lax.bitwise_xor(core, c), lax.bitwise_xor(y, h)] for h in range(2)] for c in range(2)
        ]
        grad_first, grad_second = assembled(quarters, size, inner, mid)
    return features[None], grad_first, grad_second


def solution(mesh):
    dp, dep, hgt = (mesh.shape[axis] for axis in ("dp", "dep", "hgt"))
    split = jax.sharding.Mesh(mesh.devices.reshape(dp, dep, hgt // 2, 2), ("dp", "dep", *HGT))
    block = P("dp", None, "dep", HGT, None)
    return jax.shard_map(
        per_device,
        mesh=split,
        in_specs=(block, P(), P(), block),
        out_specs=(block, P(None, "dp", None), P(None, "dp", None)),
        check_vma=False,
    )
```

```python
import functools

import jax
import jax.numpy as jnp
from jax import lax
from jax.experimental import pallas as pl
from jax.experimental.pallas import tpu as pltpu
from jax.sharding import PartitionSpec as P

BF, F32 = jnp.bfloat16, jnp.float32
LANES = 128
HGT = ("y", "core")
VMEM_BYTES = 28 * 2**20


def call(body, outs, args, scratch=(), flops=0, far=(), far_outs=(), aliases=None):
    moved = sum(x.size * x.dtype.itemsize for x in (*outs, *args))
    return pl.pallas_call(
        body,
        out_shape=outs,
        in_specs=[pl.BlockSpec(memory_space=pl.ANY if n in far else pltpu.VMEM) for n in range(len(args))],
        out_specs=[pl.BlockSpec(memory_space=pl.ANY if n in far_outs else pltpu.VMEM) for n in range(len(outs))],
        scratch_shapes=list(scratch),
        input_output_aliases=aliases or {},
        compiler_params=pltpu.CompilerParams(vmem_limit_bytes=VMEM_BYTES),
        cost_estimate=pl.CostEstimate(flops=flops, bytes_accessed=moved, transcendentals=0),
    )(*args)


def shape(dims, dtype):
    return jax.ShapeDtypeStruct(dims, dtype)


def moved_along_width(x, c):
    if c == 0:
        return x
    pieces = []
    for start in range(0, x.shape[1], LANES):
        piece = x[:, start : start + LANES]
        lane = lax.broadcasted_iota(jnp.int32, piece.shape, 1)
        rolled = pltpu.roll(piece, c % LANES, 1)
        pieces.append(jnp.where(lane == (0 if c == 1 else LANES - 1), 0.0, rolled))
    return pieces[0] if len(pieces) == 1 else jnp.concatenate(pieces, axis=1)


def by_rows(ref, scratch, store):
    channels, depth, height, width = ref.shape
    rows = depth * height
    scratch[: channels * rows] = ref[...].astype(F32).reshape(channels * rows, width)
    for d in range(depth):
        for h in range(height):
            store(d, h, scratch[pl.ds(d * height + h, channels, stride=rows), :])


def odd(axis):
    return lax.rem(lax.axis_index(axis), 2) == 1


def blank_kernel(out_ref):
    out_ref[...] = jnp.zeros(out_ref.shape, BF)


def spread_kernel(cot_ref, k2_ref, blank_ref, cot_rows_ref, back_ref, scratch):
    out, depth, height, _ = cot_ref.shape
    rows = [[None] * height for _ in range(depth)]

    def store(d, h, row):
        rows[d][h] = row.astype(BF)
        cot_rows_ref[d, :, h * LANES : (h + 1) * LANES] = rows[d][h]

    by_rows(cot_ref, scratch, store)
    mid = k2_ref.shape[1]
    none = blank_ref[...]
    padded = [jnp.concatenate([none, *rows[d], none], axis=1) for d in range(depth)]
    for e in range(depth + 2):
        reached = [(d, e - 1 - d) for d in range(depth) if abs(e - 1 - d) <= 1]
        w = jnp.concatenate(
            [
                k2_ref[9 * (a + 1) + 3 * b : 9 * (a + 1) + 3 * b + 3].reshape(3 * mid, out)
                for _, a in reached
                for b in range(3)
            ],
            axis=1,
        )
        for j in range(0, height + 2, 2):
            rhs = jnp.concatenate(
                [padded[d][:, (j + 2 - b) * LANES : (j + 4 - b) * LANES] for d, _ in reached for b in range(3)], axis=0
            )
            y = jnp.dot(w, rhs, preferred_element_type=F32)
            back = sum(moved_along_width(y[n * mid : (n + 1) * mid], n - 1) for n in range(3))
            back_ref[e, :, j * LANES : (j + 2) * LANES] = back


def as_matrix(ref, c):
    stacked = jnp.concatenate([ref[3 * ab + c] for ab in range(9)], axis=0)
    return stacked.astype(F32).T.astype(BF)


def arrange_kernel(cot_rows_ref, k1_ref, vol_ref, moved_ref, w1_ref, own_ref, scratch):
    def store(d, h, row):
        own_ref[d, :, h * LANES : (h + 1) * LANES] = row.astype(BF)

    by_rows(vol_ref, scratch, store)
    depth, out, cells = cot_rows_ref.shape
    for d in range(depth):
        for h in range(0, cells, LANES):
            row = cot_rows_ref[d, :, h : h + LANES]
            for n, c in enumerate((-1, 0, 1)):
                value = row if c == 0 else moved_along_width(row.astype(F32), c).astype(BF)
                moved_ref[d, n * out : (n + 1) * out, h : h + LANES] = value
    mid = k1_ref.shape[2]
    for c in range(3):
        w1_ref[c * mid : (c + 1) * mid, :] = as_matrix(k1_ref, c)


def sides(axis, one, two):
    me, size = lax.axis_index(axis), lax.axis_size(axis)
    is_odd = odd(axis)
    none = jnp.zeros_like(one)
    before = jnp.where(me == 0, none, jnp.where(is_odd, one, two))
    after = jnp.where(me == size - 1, none, jnp.where(is_odd, two, one))
    return before, after


def rim_kernel(own_ref, one_ref, two_ref, deep_ref, send_one_ref, send_two_ref, scratch):
    depth = own_ref.shape[0]
    deep_ref[depth : 2 * depth] = own_ref[...]
    for at, part in zip((0, 2 * depth), sides("dep", one_ref[...], two_ref[...]), strict=True):

        def store(d, h, row, at=at):
            deep_ref[at + d, :, h * LANES : (h + 1) * LANES] = row.astype(BF)

        by_rows(part, scratch, store)
    n, cells = send_one_ref.shape[2], deep_ref.shape[2]
    first, last = deep_ref[:, :, :n], deep_ref[:, :, cells - n :]
    is_odd = odd(HGT)
    send_one_ref[...] = jnp.where(is_odd, first, last)
    send_two_ref[...] = jnp.where(is_odd, last, first)


def widened(deep_ref, one_ref, two_ref):
    left, right = sides(HGT, one_ref[...], two_ref[...])
    return [jnp.concatenate([left[d], deep_ref[d], right[d]], axis=1) for d in range(deep_ref.shape[0])]


def pack(direct, refs, rows_of, blocks):
    if not direct:
        for j, block in enumerate(blocks):
            refs[0][j] = block
        return
    keep_ref, send_ref = refs
    parts, halves, length, _ = keep_ref.shape
    core = lax.axis_index("core") == 1

    def filled(rows):
        rest = length - sum(x.shape[0] for x in rows)
        return jnp.concatenate([*rows, jnp.zeros((rest, LANES), F32)] if rest else rows, axis=0)

    for part in range(parts):
        for half in range(halves):
            one, two = (filled(rows_of(part, c)[half]) for c in range(2))
            keep_ref[part, half] = jnp.where(core, two, one)
            send_ref[part, half] = jnp.where(core, one, two).astype(send_ref.dtype)


def folded(tail):
    half = tail.shape[0] // 2
    return jnp.concatenate([tail[:half], tail[half:]], axis=1)


def activated(w1, rhs, d, depth, heights):
    mid = w1.shape[0] // 3
    y = jnp.dot(w1, rhs, preferred_element_type=F32)
    pre = sum(moved_along_width(y[n * mid : (n + 1) * mid], 1 - n) for n in range(3))
    s = 1.0 / (1.0 + jnp.exp(-pre))
    dep, deps = lax.axis_index("dep"), lax.axis_size("dep")
    hgt, hgts = lax.axis_index(HGT), lax.axis_size(HGT)
    results = []
    for n, side in enumerate(heights):
        p, q = (x[:, n * LANES : (n + 1) * LANES] for x in (pre, s))
        value, slope = (p * q).astype(BF), q * (1.0 + p * (1.0 - q))
        outside = []
        if d == 0:
            outside.append(dep == 0)
        if d == depth - 1:
            outside.append(dep == deps - 1)
        if side < 0:
            outside.append(hgt == 0)
        if side > 0:
            outside.append(hgt == hgts - 1)
        for far in outside:
            value = jnp.where(far, jnp.zeros_like(value), value)
            slope = jnp.where(far, jnp.zeros_like(slope), slope)
        results.append((value, slope))
    return results


def neighbours(ref, d, starts, count):
    return jnp.concatenate(
        [
            jnp.concatenate(
                [ref[d + a, :, (start + b) * LANES : (start + b + count) * LANES] for start in starts], axis=1
            )
            for a in range(3)
            for b in range(3)
        ],
        axis=0,
    )


def products(left, right):
    return lax.dot_general(left, right, (((1,), (1,)), ((), ())), preferred_element_type=F32)


def shares(delta, n_channels, ref, at):
    for n in range(3):
        ref[n * n_channels : (n + 1) * n_channels, at : at + LANES] = moved_along_width(delta, n - 1).astype(BF)


def inner_kernel(deep_ref, w1_ref, moved_ref, back_ref, hidden_ref, second_ref, first_ref, delta_ref):
    w1 = w1_ref[...]
    depth, mid, cells = hidden_ref.shape
    height = cells // LANES
    for d in range(depth):
        for h in range(0, height, 2):
            results = activated(w1, neighbours(deep_ref, d, [h], 2), d, depth, (0, 0))
            for n, (value, slope) in enumerate(results):
                at = (h + n) * LANES
                hidden_ref[d, :, at : at + LANES] = value
                back = back_ref[d, :, at + 2 * LANES : at + 3 * LANES]
                shares(back * slope, mid, delta_ref, d * cells + at)
    own = depth - 2
    left = jnp.concatenate(
        [
            jnp.concatenate([moved_ref[d, :, (2 - b) * LANES : (2 - b) * LANES + cells] for d in range(own)], axis=1)
            for b in range(3)
        ],
        axis=0,
    )
    right = jnp.concatenate(
        [jnp.concatenate([hidden_ref[d + a] for a in range(3)], axis=0) for d in range(own)], axis=1
    )
    second_ref[...] = products(left, right)
    right = jnp.concatenate([neighbours(deep_ref, d, [0], height) for d in range(depth)], axis=1)
    first_ref[...] = products(delta_ref[...], right)


def outer_kernel(
    direct, deep_ref, two_ref, one_ref, w1_ref, back_ref, inner_ref, first_ref, hidden_ref, *grad_refs_and_scratch,
):
    *grad_refs, rows_ref, delta_ref = grad_refs_and_scratch
    for d, row in enumerate(widened(deep_ref, one_ref, two_ref)):
        rows_ref[d] = row
    w1 = w1_ref[...]
    depth, mid, cells = hidden_ref.shape
    last = cells // LANES - 2
    for d in range(depth):
        hidden_ref[d, :, 2 * LANES : last * LANES] = inner_ref[d]
        for h, sides_of in ((0, (-1, 0)), (last, (0, 1))):
            results = activated(w1, neighbours(rows_ref, d, [h], 2), d, depth, sides_of)
            for n, (value, slope) in enumerate(results):
                at = (h + n) * LANES
                hidden_ref[d, :, at : at + LANES] = value
                delta = back_ref[d, :, at : at + LANES] * slope
                shares(delta, mid, delta_ref, (4 * d + (2 if h else 0) + n) * LANES)
    right = jnp.concatenate([neighbours(rows_ref, d, [0, last], 2) for d in range(depth)], axis=1)
    total = first_ref[...] + products(delta_ref[...], right)
    inner = rows_ref.shape[1]
    blocks, tails = [], []
    for n in range(3):
        part = total[n * mid : (n + 1) * mid]
        blocks += [part[:, m * LANES : (m + 1) * LANES] for m in range(2)]
        tails.append(part[:, 2 * LANES :])
    tails.append(jnp.zeros((mid, LANES - 3 * inner), F32))
    blocks.append(jnp.concatenate(tails, axis=1))
    size = mid // lax.axis_size("dp")
    half = size // 2

    def rows_of(part, core):
        rows = [block[part * size + core * half : part * size + (core + 1) * half] for block in blocks]
        return rows[:3], rows[3:]

    pack(direct, grad_refs, rows_of, blocks)


def second_kernel(direct, hidden_ref, moved_ref, second_ref, *grad_refs):
    depth, mid, cells = hidden_ref.shape
    height = cells // LANES
    own = depth - 2
    out = moved_ref.shape[1] // 3
    heads, tails = [], []
    for b in range(3):
        far = [h for h in range(height - 2) if not 2 <= h + b <= height - 3]
        left = jnp.concatenate(
            [moved_ref[d, :, h * LANES : (h + 1) * LANES] for d in range(own) for h in far], axis=1
        )
        right = jnp.concatenate(
            [
                jnp.concatenate([hidden_ref[d + a, :, (h + b) * LANES : (h + b + 1) * LANES] for a in range(3)], axis=0)
                for d in range(own)
                for h in far
            ],
            axis=1,
        )
        total = second_ref[3 * b * out : 3 * (b + 1) * out, :] + products(left, right)
        for c in range(3):
            part = total[c * out : (c + 1) * out]
            heads.append(part[:, :LANES])
            tails.append(part[:, LANES:])
    blocks = heads + [jnp.concatenate(tails[n : n + 2], axis=1) for n in range(0, 8, 2)]
    size = mid // lax.axis_size("dp")

    def rows_of(part, core):
        at = slice((2 * part + core) * size, (2 * part + core + 1) * size)
        rows = [block[at] for block in blocks] + [folded(tails[8][at])]
        return rows[:7], rows[7:]

    pack(direct, grad_refs, rows_of, [*blocks, jnp.concatenate([tails[8], jnp.zeros_like(tails[8])], axis=1)])


def features_kernel(hidden_ref, k2_ref, out_ref, token_ref, scratch):
    out, depth, height, _ = out_ref.shape
    w2 = jnp.concatenate([as_matrix(k2_ref, c) for c in range(3)], axis=0)
    for d in range(depth):
        for h in range(0, height, 2):
            rhs = jnp.concatenate(
                [
                    hidden_ref[d + a, :, (h + b) * LANES : (h + b + 2) * LANES]
                    for a in range(3)
                    for b in range(3)
                ],
                axis=0,
            )
            y = jnp.dot(w2, rhs, preferred_element_type=F32)
            total = sum(moved_along_width(y[n * out : (n + 1) * out], 1 - n) for n in range(3))
            for r in range(2):
                row = total[:, r * LANES : (r + 1) * LANES]
                scratch[pl.ds(d * height + h + r, out, stride=depth * height), :] = row
    out_ref[...] = scratch[: out * depth * height].reshape(out_ref.shape).astype(BF)
    token_ref[...] = scratch[:8]


def plane_kernel(moves, cuts, *refs):
    sums, (kept_ref, *send_refs) = refs[: -1 - len(moves)], refs[-1 - len(moves) :]
    part = lax.rem(lax.axis_index("dp"), sums[0].shape[0])
    half = lax.axis_index("y")

    def total(x, y):
        at = 1 - part if x else part, 1 - half if y else half
        values = [keep[at] + got[at].astype(F32) for keep, got in zip(sums[::2], sums[1::2], strict=True)]
        if len(values) == 1:
            return values[0]
        one, two = (jnp.concatenate([v[:n] for v, n in zip(values, cut, strict=True)], axis=0) for cut in cuts)
        return jnp.where(at[1] == 0, one, two)

    kept_ref[...] = total(0, 0)
    for (x, y), send_ref in zip(moves, send_refs, strict=True):
        send_ref[...] = total(x, y).astype(BF)


def total_kernel(kept_ref, *refs):
    *got_refs, out_ref = refs
    value = kept_ref[...]
    for ref in got_refs:
        value = value + ref[...].astype(F32)
    out_ref[...] = value.astype(BF)


def depth_kernel(a_ref, b_ref, c_ref, d_ref, _, out_ref, padded_ref):
    one = a_ref[...].astype(F32) + b_ref[...].astype(F32)
    two = c_ref[...].astype(F32) + d_ref[...].astype(F32)
    out_ref[...] = (one + two).astype(BF)
    rest = jnp.zeros((padded_ref.shape[0] - out_ref.shape[0], LANES), F32)
    padded_ref[...] = jnp.concatenate([one + two, rest], axis=0).astype(BF)


def write_kernel(count, wheres, *refs):
    n_scratch = 6
    in_refs = refs[:count]
    out_refs, scratch = refs[: -n_scratch * count], refs[-n_scratch * count :]
    first_ref, second_ref = out_refs[-2:]
    core, y = lax.axis_index("core"), lax.axis_index("y")

    def begun(n, half):
        wide, last, low, high, tail, sems = scratch[n_scratch * n : n_scratch * (n + 1)]
        own_core, _ = wheres[n]
        at = core if own_core else 1 - core
        rows = in_refs[n][...].astype(F32)
        _, _, size, mid = wide.shape
        _, small, inner = low.shape
        here = pl.ds(pl.multiple_of(at * size, size), size)
        count = 2 if half else 7
        for j in range(count):
            value = rows[j * size : (j + 1) * size]
            for m in range(2):
                wide[m, j] = value[:, m * mid : (m + 1) * mid]
        pairs = [(wide.at[:, :count], second_ref.at[0:2, 7 * half : 7 * half + count, here, :])]
        row = count * size
        if half:
            for j in range(4):
                value = rows[row : row + size]
                row += size
                for m in range(2):
                    last[2 * j + m] = value[:, m * mid : (m + 1) * mid]
            value = rows[row : row + size // 2]
            row += size // 2
            last[8] = jnp.concatenate([value[:, :mid], value[:, mid:]], axis=0)
            pairs.append((last, second_ref.at[2, :, here, :]))
        copies = [pltpu.make_async_copy(src, dst, sems.at[i]) for i, (src, dst) in enumerate(pairs)]
        for copy in copies:
            copy.start()
        here = pl.ds(pl.multiple_of(at * small, small), small)
        places = [(high, 0, 4), (low, 0, 4), (low, 4, 4), (tail, 0, 3)] if half else [(low, 0, 4), (low, 4, 4), (high, 0, 4)]
        for ref, start, number in places:
            value = rows[row : row + small]
            row += small
            for m in range(number):
                ref[start + m] = value[:, m * inner : (m + 1) * inner]
        if half:
            pairs = [
                (high, first_ref.at[4:8, 1, here, :]),
                (low, first_ref.at[0:8, 2, here, :]),
                (tail, first_ref.at[8, :, here, :]),
            ]
        else:
            pairs = [(low, first_ref.at[0:8, 0, here, :]), (high, first_ref.at[0:4, 1, here, :])]
        more = [pltpu.make_async_copy(src, dst, sems.at[2 + i]) for i, (src, dst) in enumerate(pairs)]
        for copy in more:
            copy.start()
        return copies + more

    for half in range(2):

        @pl.when(y == half)
        def _(half=half):
            copies = []
            for n, (_, own_y) in enumerate(wheres):
                copies += begun(n, half if own_y else 1 - half)
            for copy in copies:
                copy.wait()


def swapped(x, axis, first):
    axes = (axis,) if isinstance(axis, str) else axis
    parts, size = lax.axis_size("dp"), lax.axis_size(axis)
    partner = list(range(parts * size))
    for i in partner:
        part, at = divmod(i, size)
        if first <= at < size - (size - first) % 2:
            partner[i] = part * size + (at - first ^ 1) + first
        elif parts % 2 == 0:
            partner[i] = (part ^ 1) * size + at
    return lax.ppermute(x, ("dp", *axes), list(enumerate(partner)))


def across(x, *moves):
    axes = tuple(axis for axis, _ in moves)
    flip = 0
    for axis, bit in moves:
        flip = flip * lax.axis_size(axis) + bit
    return lax.ppermute(x, axes, [(i, i ^ flip) for i in range(lax.axis_size(axes))])


def scattered(rows, cuts):
    halves = [
        jnp.concatenate([x[:, :, :n] if at == 0 else x[:, :, x.shape[2] - n :] for x, n in zip(rows, cut)], axis=2)
        for at, cut in enumerate(cuts)
    ]
    grad = lax.psum_scatter(jnp.stack(halves, axis=2), "dp", scatter_dimension=0, tiled=True)
    core = lax.axis_index("core")
    return tuple(lax.dynamic_index_in_dim(grad, at, 1, False) for at in (core, 1 - core))


def assembled(quarters, size, inner, mid):
    first, second = ([[None, None] for _ in range(27)] for _ in range(2))
    half = size // 2
    for core in range(2):
        for y in range(2):
            rows, row = quarters[core][y].astype(F32), 0
            for j in range(7) if y == 0 else range(7, 13):
                for m, k in enumerate((j, 9 + j) if j < 9 else (2 * j, 2 * j + 1)):
                    second[k][core] = rows[row : row + size, m * mid : (m + 1) * mid]
                row += size
            if y == 1:
                tail = rows[row : row + half]
                second[26][core] = jnp.concatenate([tail[:, :mid], tail[:, mid:]], axis=0)
                row += half
            for j in range(3) if y == 0 else range(3, 7):
                for m in range(4):
                    c, ab = (j // 2, 4 * (j % 2) + m) if j < 6 else (m, 8)
                    if c < 3:
                        first[3 * ab + c][core] = rows[row : row + half, m * inner : (m + 1) * inner]
                row += half
    return tuple(jnp.stack([jnp.concatenate(both, axis=0) for both in grad]) for grad in (first, second))


def per_device(volume, kernel_first, kernel_second, cotangent):
    _, inner, depth, height, width = volume.shape
    mid, out = kernel_first.shape[1], kernel_second.shape[1]
    cells = height * width
    parts = lax.axis_size("dp")
    k1, k2 = jnp.swapaxes(kernel_first, 1, 2), jnp.swapaxes(kernel_second, 1, 2)
    rows = depth * height

    one, two = swapped(volume[0], "dep", 0), swapped(volume[0], "dep", 1)
    (blank,) = call(blank_kernel, [shape((out, 2 * width), BF)], [], flops=3_000_000_000)
    cot_rows, back = call(
        spread_kernel,
        [
            shape((depth, out, cells), BF),
            shape((depth + 2, mid, cells + 2 * width), F32),
        ],
        [cotangent[0], k2, blank],
        [pltpu.VMEM(((out + 1) * rows, width), F32)],
        flops=1_100_000_000,
    )
    moved, w1, vol = call(
        arrange_kernel,
        [
            shape((depth, 3 * out, cells), BF),
            shape((3 * mid, 9 * inner), BF),
            shape((depth, inner, cells), BF),
        ],
        [cot_rows, k1, volume[0]],
        [pltpu.VMEM(((inner + 1) * rows, width), F32)],
        flops=500_000_000,
    )
    deep, one, two = call(
        rim_kernel,
        [shape((3 * depth, inner, cells), BF)] + [shape((3 * depth, inner, 2 * width), BF)] * 2,
        [vol, one, two],
        [pltpu.VMEM(((inner + 1) * rows, width), F32)],
    )
    one, two = swapped(one, HGT, 0), swapped(two, HGT, 1)
    size = mid // parts
    direct = parts == 2 and size % 16 == 0
    halves = lax.axis_size("y")
    cuts = ((7 * size, 3 * size // 2), (13 * size // 2, 2 * size))
    length_second, length_first = 7 * size, 2 * size
    rows_in, rows_out = height - 2, 4
    inner_hidden, inner_second, inner_first = call(
        inner_kernel,
        [
            shape((depth + 2, mid, rows_in * width), BF),
            shape((9 * out, 3 * mid), F32),
            shape((3 * mid, 9 * inner), F32),
        ],
        [deep, w1, moved, back],
        [pltpu.VMEM((3 * mid, (depth + 2) * rows_in * width), BF)],
        flops=1_500_000_000,
    )
    hidden, *first = call(
        functools.partial(outer_kernel, direct),
        [shape((depth + 2, mid, cells + 2 * width), BF)]
        + ([shape((parts, halves, length_first, width), F32)] * 2 if direct else [shape((7, mid, LANES), F32)]),
        [deep, two, one, w1, back, inner_hidden, inner_first],
        [
            pltpu.VMEM((3 * depth, inner, cells + 4 * width), BF),
            pltpu.VMEM((3 * mid, (depth + 2) * rows_out * width), BF),
        ],
        flops=1_000_000_000,
    )
    second = call(
        functools.partial(second_kernel, direct),
        [shape((parts, halves, length_second, width), kind) for kind in (F32, BF)]
        if direct
        else [shape((14, out, LANES), F32)],
        [hidden, moved, inner_second],
        flops=4_000_000_000,
    )
    if direct:
        moves = [(1, 0), (0, 1), (1, 1)]
        grads = [second, first]
    else:
        moves = [(0, 1)]
        blocks = second[0].reshape(14, parts, 2, size, LANES).transpose(1, 2, 0, 3, 4)
        tail = blocks[:, :, 13, :, :mid]
        tail = jnp.concatenate([tail[:, :, : size // 2], tail[:, :, size // 2 :]], axis=-1)
        rows_second = jnp.concatenate([blocks[:, :, :13].reshape(parts, 2, 13 * size, LANES), tail], axis=2)
        blocks = first[0].reshape(7, parts, 2, size // 2, LANES).transpose(1, 2, 0, 3, 4)
        rows_first = blocks.reshape(parts, 2, 7 * (size // 2), LANES)
        grads = [scattered([rows_second, rows_first], cuts)]
    block = (sum(cuts[0]), width)
    kept, *sends = call(
        functools.partial(plane_kernel, moves, cuts),
        [shape(block, F32)] + [shape(block, BF)] * len(moves),
        [x for keep, send in grads for x in (keep, across(send, ("core", 1)))],
    )
    gots = [across(send, ("dp", x), ("y", y)) for send, (x, y) in zip(sends, moves, strict=True)]
    (share,) = call(total_kernel, [shape(block, BF)], [kept, *gots])
    features, token = call(
        features_kernel,
        [shape(cotangent.shape[1:], BF), shape((8, width), F32)],
        [hidden, k2],
        [pltpu.VMEM(((out + 1) * rows, width), F32)],
        flops=900_000_000,
    )
    gots = [across(share, ("dep", bits)) for bits in (1, 2, 3)]
    share, for_y = call(depth_kernel, [shape(block, BF), shape((block[0] + 16, width), BF)], [share, *gots, token])
    other, far = across(share, ("core", 1)), across(for_y, ("y", 1))
    far_other = across(for_y, ("y", 1), ("core", 1))
    if size % 16 == 0:
        outs = [shape((9, 3, size, inner), F32), shape((3, 9, 2 * size, mid), F32)]

        def written(quarters, wheres, before=()):
            scratch = [
                pltpu.VMEM((2, 7, size, mid), F32),
                pltpu.VMEM((9, size, mid), F32),
                pltpu.VMEM((8, size // 2, inner), F32),
                pltpu.VMEM((4, size // 2, inner), F32),
                pltpu.VMEM((3, size // 2, inner), F32),
                pltpu.SemaphoreType.DMA((5,)),
            ]
            count = len(quarters)
            return call(
                functools.partial(write_kernel, count, wheres),
                outs,
                [*quarters, *before],
                scratch * count,
                far=range(count, count + len(before)),
                far_outs=(0, 1),
                aliases={count + n: n for n in range(len(before))},
            )

        grads = written([share, other], [(True, True), (False, True)])
        grads = written([far_other, far], [(False, False), (True, False)], grads)
        grad_first, grad_second = (grad.reshape(27, *grad.shape[2:]) for grad in grads)
    else:
        core, y = lax.axis_index("core"), lax.axis_index("y")
        stacked = jnp.stack([jnp.stack([share, far[: block[0]]]), jnp.stack([other, far_other[: block[0]]])])
        quarters = [
            [stacked[lax.bitwise_xor(core, c), lax.bitwise_xor(y, h)] for h in range(2)] for c in range(2)
        ]
        grad_first, grad_second = assembled(quarters, size, inner, mid)
    return features[None], grad_first, grad_second


def solution(mesh):
    dp, dep, hgt = (mesh.shape[axis] for axis in ("dp", "dep", "hgt"))
    split = jax.sharding.Mesh(mesh.devices.reshape(dp, dep, hgt // 2, 2), ("dp", "dep", *HGT))
    block = P("dp", None, "dep", HGT, None)
    return jax.shard_map(
        per_device,
        mesh=split,
        in_specs=(block, P(), P(), block),
        out_specs=(block, P(None, "dp", None), P(None, "dp", None)),
        check_vma=False,
    )
```

```python
import functools

import jax
import jax.numpy as jnp
from jax import lax
from jax.experimental import pallas as pl
from jax.experimental.pallas import tpu as pltpu
from jax.sharding import PartitionSpec as P

BF, F32 = jnp.bfloat16, jnp.float32
LANES = 128
HGT = ("y", "core")
VMEM_BYTES = 28 * 2**20


def call(body, outs, args, scratch=(), flops=0, far=(), far_outs=(), aliases=None):
    moved = sum(x.size * x.dtype.itemsize for x in (*outs, *args))
    return pl.pallas_call(
        body,
        out_shape=outs,
        in_specs=[pl.BlockSpec(memory_space=pl.ANY if n in far else pltpu.VMEM) for n in range(len(args))],
        out_specs=[pl.BlockSpec(memory_space=pl.ANY if n in far_outs else pltpu.VMEM) for n in range(len(outs))],
        scratch_shapes=list(scratch),
        input_output_aliases=aliases or {},
        compiler_params=pltpu.CompilerParams(vmem_limit_bytes=VMEM_BYTES),
        cost_estimate=pl.CostEstimate(flops=flops, bytes_accessed=moved, transcendentals=0),
    )(*args)


def shape(dims, dtype):
    return jax.ShapeDtypeStruct(dims, dtype)


def moved_along_width(x, c):
    if c == 0:
        return x
    pieces = []
    for start in range(0, x.shape[1], LANES):
        piece = x[:, start : start + LANES]
        lane = lax.broadcasted_iota(jnp.int32, piece.shape, 1)
        rolled = pltpu.roll(piece, c % LANES, 1)
        pieces.append(jnp.where(lane == (0 if c == 1 else LANES - 1), 0.0, rolled))
    return pieces[0] if len(pieces) == 1 else jnp.concatenate(pieces, axis=1)


def by_rows(ref, scratch, store):
    channels, depth, height, width = ref.shape
    rows = depth * height
    scratch[: channels * rows] = ref[...].astype(F32).reshape(channels * rows, width)
    for d in range(depth):
        for h in range(height):
            store(d, h, scratch[pl.ds(d * height + h, channels, stride=rows), :])


def odd(axis):
    return lax.rem(lax.axis_index(axis), 2) == 1


def blank_kernel(out_ref):
    out_ref[...] = jnp.zeros(out_ref.shape, BF)


def spread_kernel(cot_ref, k2_ref, blank_ref, cot_rows_ref, back_ref, scratch):
    out, depth, height, _ = cot_ref.shape
    rows = [[None] * height for _ in range(depth)]

    def store(d, h, row):
        rows[d][h] = row.astype(BF)
        cot_rows_ref[d, :, h * LANES : (h + 1) * LANES] = rows[d][h]

    by_rows(cot_ref, scratch, store)
    mid = k2_ref.shape[1]
    none = blank_ref[...]
    padded = [jnp.concatenate([none, *rows[d], none], axis=1) for d in range(depth)]
    for e in range(depth + 2):
        reached = [(d, e - 1 - d) for d in range(depth) if abs(e - 1 - d) <= 1]
        w = jnp.concatenate(
            [
                k2_ref[9 * (a + 1) + 3 * b : 9 * (a + 1) + 3 * b + 3].reshape(3 * mid, out)
                for _, a in reached
                for b in range(3)
            ],
            axis=1,
        )
        for j in range(0, height + 2, 2):
            rhs = jnp.concatenate(
                [padded[d][:, (j + 2 - b) * LANES : (j + 4 - b) * LANES] for d, _ in reached for b in range(3)], axis=0
            )
            y = jnp.dot(w, rhs, preferred_element_type=F32)
            back = sum(moved_along_width(y[n * mid : (n + 1) * mid], n - 1) for n in range(3))
            back_ref[e, :, j * LANES : (j + 2) * LANES] = back


def as_matrix(ref, c):
    stacked = jnp.concatenate([ref[3 * ab + c] for ab in range(9)], axis=0)
    return stacked.astype(F32).T.astype(BF)


def arrange_kernel(cot_rows_ref, k1_ref, vol_ref, moved_ref, w1_ref, own_ref, scratch):
    def store(d, h, row):
        own_ref[d, :, h * LANES : (h + 1) * LANES] = row.astype(BF)

    by_rows(vol_ref, scratch, store)
    depth, out, cells = cot_rows_ref.shape
    for d in range(depth):
        for h in range(0, cells, LANES):
            row = cot_rows_ref[d, :, h : h + LANES]
            for n, c in enumerate((-1, 0, 1)):
                value = row if c == 0 else moved_along_width(row.astype(F32), c).astype(BF)
                moved_ref[d, n * out : (n + 1) * out, h : h + LANES] = value
    mid = k1_ref.shape[2]
    for c in range(3):
        w1_ref[c * mid : (c + 1) * mid, :] = as_matrix(k1_ref, c)


def sides(axis, one, two):
    me, size = lax.axis_index(axis), lax.axis_size(axis)
    is_odd = odd(axis)
    none = jnp.zeros_like(one)
    before = jnp.where(me == 0, none, jnp.where(is_odd, one, two))
    after = jnp.where(me == size - 1, none, jnp.where(is_odd, two, one))
    return before, after


def rim_kernel(own_ref, two_ref, one_ref, deep_ref, send_one_ref, send_two_ref, scratch):
    depth = own_ref.shape[0]
    deep_ref[depth : 2 * depth] = own_ref[...]
    for at, part in zip((0, 2 * depth), sides("dep", one_ref[...], two_ref[...]), strict=True):

        def store(d, h, row, at=at):
            deep_ref[at + d, :, h * LANES : (h + 1) * LANES] = row.astype(BF)

        by_rows(part, scratch, store)
    n, cells = send_one_ref.shape[2], deep_ref.shape[2]
    first, last = deep_ref[:, :, :n], deep_ref[:, :, cells - n :]
    is_odd = odd(HGT)
    send_one_ref[...] = jnp.where(is_odd, first, last)
    send_two_ref[...] = jnp.where(is_odd, last, first)


def widened(deep_ref, one_ref, two_ref):
    left, right = sides(HGT, one_ref[...], two_ref[...])
    return [jnp.concatenate([left[d], deep_ref[d], right[d]], axis=1) for d in range(deep_ref.shape[0])]


def pack(direct, refs, rows_of, blocks):
    if not direct:
        for j, block in enumerate(blocks):
            refs[0][j] = block
        return
    keep_ref, send_ref = refs
    parts, halves, length, _ = keep_ref.shape
    core = lax.axis_index("core") == 1

    def filled(rows):
        rest = length - sum(x.shape[0] for x in rows)
        return jnp.concatenate([*rows, jnp.zeros((rest, LANES), F32)] if rest else rows, axis=0)

    for part in range(parts):
        for half in range(halves):
            one, two = (filled(rows_of(part, c)[half]) for c in range(2))
            keep_ref[part, half] = jnp.where(core, two, one)
            send_ref[part, half] = jnp.where(core, one, two).astype(send_ref.dtype)


def folded(tail):
    half = tail.shape[0] // 2
    return jnp.concatenate([tail[:half], tail[half:]], axis=1)


def activated(w1, rhs, d, depth, heights):
    mid = w1.shape[0] // 3
    y = jnp.dot(w1, rhs, preferred_element_type=F32)
    pre = sum(moved_along_width(y[n * mid : (n + 1) * mid], 1 - n) for n in range(3))
    s = 1.0 / (1.0 + jnp.exp(-pre))
    dep, deps = lax.axis_index("dep"), lax.axis_size("dep")
    hgt, hgts = lax.axis_index(HGT), lax.axis_size(HGT)
    results = []
    for n, side in enumerate(heights):
        p, q = (x[:, n * LANES : (n + 1) * LANES] for x in (pre, s))
        value, slope = (p * q).astype(BF), q * (1.0 + p * (1.0 - q))
        outside = []
        if d == 0:
            outside.append(dep == 0)
        if d == depth - 1:
            outside.append(dep == deps - 1)
        if side < 0:
            outside.append(hgt == 0)
        if side > 0:
            outside.append(hgt == hgts - 1)
        for far in outside:
            value = jnp.where(far, jnp.zeros_like(value), value)
            slope = jnp.where(far, jnp.zeros_like(slope), slope)
        results.append((value, slope))
    return results


def neighbours(ref, d, starts, count):
    return jnp.concatenate(
        [
            jnp.concatenate(
                [ref[d + a, :, (start + b) * LANES : (start + b + count) * LANES] for start in starts], axis=1
            )
            for a in range(3)
            for b in range(3)
        ],
        axis=0,
    )


def products(left, right):
    return lax.dot_general(left, right, (((1,), (1,)), ((), ())), preferred_element_type=F32)


def shares(delta, n_channels, ref, at):
    for n in range(3):
        ref[n * n_channels : (n + 1) * n_channels, at : at + LANES] = moved_along_width(delta, n - 1).astype(BF)


def inner_kernel(deep_ref, w1_ref, moved_ref, back_ref, hidden_ref, second_ref, first_ref, delta_ref):
    w1 = w1_ref[...]
    depth, mid, cells = hidden_ref.shape
    height = cells // LANES
    for d in range(depth):
        for h in range(0, height, 2):
            results = activated(w1, neighbours(deep_ref, d, [h], 2), d, depth, (0, 0))
            for n, (value, slope) in enumerate(results):
                at = (h + n) * LANES
                hidden_ref[d, :, at : at + LANES] = value
                back = back_ref[d, :, at + 2 * LANES : at + 3 * LANES]
                shares(back * slope, mid, delta_ref, d * cells + at)
    own = depth - 2
    left = jnp.concatenate(
        [
            jnp.concatenate([moved_ref[d, :, (2 - b) * LANES : (2 - b) * LANES + cells] for d in range(own)], axis=1)
            for b in range(3)
        ],
        axis=0,
    )
    right = jnp.concatenate(
        [jnp.concatenate([hidden_ref[d + a] for a in range(3)], axis=0) for d in range(own)], axis=1
    )
    second_ref[...] = products(left, right)
    right = jnp.concatenate([neighbours(deep_ref, d, [0], height) for d in range(depth)], axis=1)
    first_ref[...] = products(delta_ref[...], right)


def outer_kernel(
    direct, deep_ref, two_ref, one_ref, w1_ref, back_ref, inner_ref, first_ref, hidden_ref, *grad_refs_and_scratch,
):
    *grad_refs, rows_ref, delta_ref = grad_refs_and_scratch
    for d, row in enumerate(widened(deep_ref, one_ref, two_ref)):
        rows_ref[d] = row
    w1 = w1_ref[...]
    depth, mid, cells = hidden_ref.shape
    last = cells // LANES - 2
    for d in range(depth):
        hidden_ref[d, :, 2 * LANES : last * LANES] = inner_ref[d]
        for h, sides_of in ((0, (-1, 0)), (last, (0, 1))):
            results = activated(w1, neighbours(rows_ref, d, [h], 2), d, depth, sides_of)
            for n, (value, slope) in enumerate(results):
                at = (h + n) * LANES
                hidden_ref[d, :, at : at + LANES] = value
                delta = back_ref[d, :, at : at + LANES] * slope
                shares(delta, mid, delta_ref, (4 * d + (2 if h else 0) + n) * LANES)
    right = jnp.concatenate([neighbours(rows_ref, d, [0, last], 2) for d in range(depth)], axis=1)
    total = first_ref[...] + products(delta_ref[...], right)
    inner = rows_ref.shape[1]
    blocks, tails = [], []
    for n in range(3):
        part = total[n * mid : (n + 1) * mid]
        blocks += [part[:, m * LANES : (m + 1) * LANES] for m in range(2)]
        tails.append(part[:, 2 * LANES :])
    tails.append(jnp.zeros((mid, LANES - 3 * inner), F32))
    blocks.append(jnp.concatenate(tails, axis=1))
    size = mid // lax.axis_size("dp")
    half = size // 2

    def rows_of(part, core):
        rows = [block[part * size + core * half : part * size + (core + 1) * half] for block in blocks]
        return rows[:3], rows[3:]

    pack(direct, grad_refs, rows_of, blocks)


def second_kernel(direct, hidden_ref, moved_ref, second_ref, *grad_refs):
    depth, mid, cells = hidden_ref.shape
    height = cells // LANES
    own = depth - 2
    out = moved_ref.shape[1] // 3
    heads, tails = [], []
    for b in range(3):
        far = [h for h in range(height - 2) if not 2 <= h + b <= height - 3]
        left = jnp.concatenate(
            [moved_ref[d, :, h * LANES : (h + 1) * LANES] for d in range(own) for h in far], axis=1
        )
        right = jnp.concatenate(
            [
                jnp.concatenate([hidden_ref[d + a, :, (h + b) * LANES : (h + b + 1) * LANES] for a in range(3)], axis=0)
                for d in range(own)
                for h in far
            ],
            axis=1,
        )
        total = second_ref[3 * b * out : 3 * (b + 1) * out, :] + products(left, right)
        for c in range(3):
            part = total[c * out : (c + 1) * out]
            heads.append(part[:, :LANES])
            tails.append(part[:, LANES:])
    blocks = heads + [jnp.concatenate(tails[n : n + 2], axis=1) for n in range(0, 8, 2)]
    size = mid // lax.axis_size("dp")

    def rows_of(part, core):
        at = slice((2 * part + core) * size, (2 * part + core + 1) * size)
        rows = [block[at] for block in blocks] + [folded(tails[8][at])]
        return rows[:7], rows[7:]

    pack(direct, grad_refs, rows_of, [*blocks, jnp.concatenate([tails[8], jnp.zeros_like(tails[8])], axis=1)])


def features_kernel(hidden_ref, k2_ref, out_ref, token_ref, scratch):
    out, depth, height, _ = out_ref.shape
    w2 = jnp.concatenate([as_matrix(k2_ref, c) for c in range(3)], axis=0)
    for d in range(depth):
        for h in range(0, height, 2):
            rhs = jnp.concatenate(
                [
                    hidden_ref[d + a, :, (h + b) * LANES : (h + b + 2) * LANES]
                    for a in range(3)
                    for b in range(3)
                ],
                axis=0,
            )
            y = jnp.dot(w2, rhs, preferred_element_type=F32)
            total = sum(moved_along_width(y[n * out : (n + 1) * out], 1 - n) for n in range(3))
            for r in range(2):
                row = total[:, r * LANES : (r + 1) * LANES]
                scratch[pl.ds(d * height + h + r, out, stride=depth * height), :] = row
    out_ref[...] = scratch[: out * depth * height].reshape(out_ref.shape).astype(BF)
    token_ref[...] = scratch[:8]


def plane_kernel(moves, cuts, *refs):
    sums, (kept_ref, *send_refs) = refs[: -1 - len(moves)], refs[-1 - len(moves) :]
    part = lax.rem(lax.axis_index("dp"), sums[0].shape[0])
    half = lax.axis_index("y")

    def total(x, y):
        at = 1 - part if x else part, 1 - half if y else half
        values = [keep[at] + got[at].astype(F32) for keep, got in zip(sums[::2], sums[1::2], strict=True)]
        if len(values) == 1:
            return values[0]
        one, two = (jnp.concatenate([v[:n] for v, n in zip(values, cut, strict=True)], axis=0) for cut in cuts)
        return jnp.where(at[1] == 0, one, two)

    kept_ref[...] = total(0, 0)
    for (x, y), send_ref in zip(moves, send_refs, strict=True):
        send_ref[...] = total(x, y).astype(BF)


def total_kernel(kept_ref, *refs):
    *got_refs, out_ref = refs
    value = kept_ref[...]
    for ref in got_refs:
        value = value + ref[...].astype(F32)
    out_ref[...] = value.astype(BF)


def depth_kernel(a_ref, b_ref, c_ref, d_ref, _, out_ref, padded_ref):
    one = a_ref[...].astype(F32) + b_ref[...].astype(F32)
    two = c_ref[...].astype(F32) + d_ref[...].astype(F32)
    out_ref[...] = (one + two).astype(BF)
    rest = jnp.zeros((padded_ref.shape[0] - out_ref.shape[0], LANES), F32)
    padded_ref[...] = jnp.concatenate([one + two, rest], axis=0).astype(BF)


def write_kernel(count, wheres, *refs):
    n_scratch = 6
    in_refs = refs[:count]
    out_refs, scratch = refs[: -n_scratch * count], refs[-n_scratch * count :]
    first_ref, second_ref = out_refs[-2:]
    core, y = lax.axis_index("core"), lax.axis_index("y")

    def begun(n, half):
        wide, last, low, high, tail, sems = scratch[n_scratch * n : n_scratch * (n + 1)]
        own_core, _ = wheres[n]
        at = core if own_core else 1 - core
        rows = in_refs[n][...].astype(F32)
        _, _, size, mid = wide.shape
        _, small, inner = low.shape
        here = pl.ds(pl.multiple_of(at * size, size), size)
        count = 2 if half else 7
        for j in range(count):
            value = rows[j * size : (j + 1) * size]
            for m in range(2):
                wide[m, j] = value[:, m * mid : (m + 1) * mid]
        pairs = [(wide.at[:, :count], second_ref.at[0:2, 7 * half : 7 * half + count, here, :])]
        row = count * size
        if half:
            for j in range(4):
                value = rows[row : row + size]
                row += size
                for m in range(2):
                    last[2 * j + m] = value[:, m * mid : (m + 1) * mid]
            value = rows[row : row + size // 2]
            row += size // 2
            last[8] = jnp.concatenate([value[:, :mid], value[:, mid:]], axis=0)
            pairs.append((last, second_ref.at[2, :, here, :]))
        copies = [pltpu.make_async_copy(src, dst, sems.at[i]) for i, (src, dst) in enumerate(pairs)]
        for copy in copies:
            copy.start()
        here = pl.ds(pl.multiple_of(at * small, small), small)
        places = [(high, 0, 4), (low, 0, 4), (low, 4, 4), (tail, 0, 3)] if half else [(low, 0, 4), (low, 4, 4), (high, 0, 4)]
        for ref, start, number in places:
            value = rows[row : row + small]
            row += small
            for m in range(number):
                ref[start + m] = value[:, m * inner : (m + 1) * inner]
        if half:
            pairs = [
                (high, first_ref.at[4:8, 1, here, :]),
                (low, first_ref.at[0:8, 2, here, :]),
                (tail, first_ref.at[8, :, here, :]),
            ]
        else:
            pairs = [(low, first_ref.at[0:8, 0, here, :]), (high, first_ref.at[0:4, 1, here, :])]
        more = [pltpu.make_async_copy(src, dst, sems.at[2 + i]) for i, (src, dst) in enumerate(pairs)]
        for copy in more:
            copy.start()
        return copies + more

    for half in range(2):

        @pl.when(y == half)
        def _(half=half):
            copies = []
            for n, (_, own_y) in enumerate(wheres):
                copies += begun(n, half if own_y else 1 - half)
            for copy in copies:
                copy.wait()


def swapped(x, axis, first):
    axes = (axis,) if isinstance(axis, str) else axis
    parts, size = lax.axis_size("dp"), lax.axis_size(axis)
    partner = list(range(parts * size))
    for i in partner:
        part, at = divmod(i, size)
        if first <= at < size - (size - first) % 2:
            partner[i] = part * size + (at - first ^ 1) + first
        elif parts % 2 == 0:
            partner[i] = (part ^ 1) * size + at
    return lax.ppermute(x, ("dp", *axes), list(enumerate(partner)))


def across(x, *moves):
    axes = tuple(axis for axis, _ in moves)
    flip = 0
    for axis, bit in moves:
        flip = flip * lax.axis_size(axis) + bit
    return lax.ppermute(x, axes, [(i, i ^ flip) for i in range(lax.axis_size(axes))])


def scattered(rows, cuts):
    halves = [
        jnp.concatenate([x[:, :, :n] if at == 0 else x[:, :, x.shape[2] - n :] for x, n in zip(rows, cut)], axis=2)
        for at, cut in enumerate(cuts)
    ]
    grad = lax.psum_scatter(jnp.stack(halves, axis=2), "dp", scatter_dimension=0, tiled=True)
    core = lax.axis_index("core")
    return tuple(lax.dynamic_index_in_dim(grad, at, 1, False) for at in (core, 1 - core))


def assembled(quarters, size, inner, mid):
    first, second = ([[None, None] for _ in range(27)] for _ in range(2))
    half = size // 2
    for core in range(2):
        for y in range(2):
            rows, row = quarters[core][y].astype(F32), 0
            for j in range(7) if y == 0 else range(7, 13):
                for m, k in enumerate((j, 9 + j) if j < 9 else (2 * j, 2 * j + 1)):
                    second[k][core] = rows[row : row + size, m * mid : (m + 1) * mid]
                row += size
            if y == 1:
                tail = rows[row : row + half]
                second[26][core] = jnp.concatenate([tail[:, :mid], tail[:, mid:]], axis=0)
                row += half
            for j in range(3) if y == 0 else range(3, 7):
                for m in range(4):
                    c, ab = (j // 2, 4 * (j % 2) + m) if j < 6 else (m, 8)
                    if c < 3:
                        first[3 * ab + c][core] = rows[row : row + half, m * inner : (m + 1) * inner]
                row += half
    return tuple(jnp.stack([jnp.concatenate(both, axis=0) for both in grad]) for grad in (first, second))


def per_device(volume, kernel_first, kernel_second, cotangent):
    _, inner, depth, height, width = volume.shape
    mid, out = kernel_first.shape[1], kernel_second.shape[1]
    cells = height * width
    parts = lax.axis_size("dp")
    k1, k2 = jnp.swapaxes(kernel_first, 1, 2), jnp.swapaxes(kernel_second, 1, 2)
    rows = depth * height

    one, two = swapped(volume[0], "dep", 0), swapped(volume[0], "dep", 1)
    (blank,) = call(blank_kernel, [shape((out, 2 * width), BF)], [], flops=3_000_000_000)
    cot_rows, back = call(
        spread_kernel,
        [
            shape((depth, out, cells), BF),
            shape((depth + 2, mid, cells + 2 * width), F32),
        ],
        [cotangent[0], k2, blank],
        [pltpu.VMEM(((out + 1) * rows, width), F32)],
        flops=1_100_000_000,
    )
    moved, w1, vol = call(
        arrange_kernel,
        [
            shape((depth, 3 * out, cells), BF),
            shape((3 * mid, 9 * inner), BF),
            shape((depth, inner, cells), BF),
        ],
        [cot_rows, k1, volume[0]],
        [pltpu.VMEM(((inner + 1) * rows, width), F32)],
        flops=500_000_000,
    )
    deep, one, two = call(
        rim_kernel,
        [shape((3 * depth, inner, cells), BF)] + [shape((3 * depth, inner, 2 * width), BF)] * 2,
        [vol, two, one],
        [pltpu.VMEM(((inner + 1) * rows, width), F32)],
    )
    one, two = swapped(one, HGT, 0), swapped(two, HGT, 1)
    size = mid // parts
    direct = parts == 2 and size % 16 == 0
    halves = lax.axis_size("y")
    cuts = ((7 * size, 3 * size // 2), (13 * size // 2, 2 * size))
    length_second, length_first = 7 * size, 2 * size
    rows_in, rows_out = height - 2, 4
    inner_hidden, inner_second, inner_first = call(
        inner_kernel,
        [
            shape((depth + 2, mid, rows_in * width), BF),
            shape((9 * out, 3 * mid), F32),
            shape((3 * mid, 9 * inner), F32),
        ],
        [deep, w1, moved, back],
        [pltpu.VMEM((3 * mid, (depth + 2) * rows_in * width), BF)],
        flops=1_500_000_000,
    )
    hidden, *first = call(
        functools.partial(outer_kernel, direct),
        [shape((depth + 2, mid, cells + 2 * width), BF)]
        + ([shape((parts, halves, length_first, width), F32)] * 2 if direct else [shape((7, mid, LANES), F32)]),
        [deep, two, one, w1, back, inner_hidden, inner_first],
        [
            pltpu.VMEM((3 * depth, inner, cells + 4 * width), BF),
            pltpu.VMEM((3 * mid, (depth + 2) * rows_out * width), BF),
        ],
        flops=1_000_000_000,
    )
    second = call(
        functools.partial(second_kernel, direct),
        [shape((parts, halves, length_second, width), kind) for kind in (F32, BF)]
        if direct
        else [shape((14, out, LANES), F32)],
        [hidden, moved, inner_second],
        flops=4_000_000_000,
    )
    if direct:
        moves = [(1, 0), (0, 1), (1, 1)]
        grads = [second, first]
    else:
        moves = [(0, 1)]
        blocks = second[0].reshape(14, parts, 2, size, LANES).transpose(1, 2, 0, 3, 4)
        tail = blocks[:, :, 13, :, :mid]
        tail = jnp.concatenate([tail[:, :, : size // 2], tail[:, :, size // 2 :]], axis=-1)
        rows_second = jnp.concatenate([blocks[:, :, :13].reshape(parts, 2, 13 * size, LANES), tail], axis=2)
        blocks = first[0].reshape(7, parts, 2, size // 2, LANES).transpose(1, 2, 0, 3, 4)
        rows_first = blocks.reshape(parts, 2, 7 * (size // 2), LANES)
        grads = [scattered([rows_second, rows_first], cuts)]
    block = (sum(cuts[0]), width)
    kept, *sends = call(
        functools.partial(plane_kernel, moves, cuts),
        [shape(block, F32)] + [shape(block, BF)] * len(moves),
        [x for keep, send in grads for x in (keep, across(send, ("core", 1)))],
    )
    gots = [across(send, ("dp", x), ("y", y)) for send, (x, y) in zip(sends, moves, strict=True)]
    (share,) = call(total_kernel, [shape(block, BF)], [kept, *gots])
    features, token = call(
        features_kernel,
        [shape(cotangent.shape[1:], BF), shape((8, width), F32)],
        [hidden, k2],
        [pltpu.VMEM(((out + 1) * rows, width), F32)],
        flops=900_000_000,
    )
    gots = [across(share, ("dep", bits)) for bits in (1, 2, 3)]
    share, for_y = call(depth_kernel, [shape(block, BF), shape((block[0] + 16, width), BF)], [share, *gots, token])
    other, far = across(share, ("core", 1)), across(for_y, ("y", 1))
    far_other = across(for_y, ("y", 1), ("core", 1))
    if size % 16 == 0:
        outs = [shape((9, 3, size, inner), F32), shape((3, 9, 2 * size, mid), F32)]

        def written(quarters, wheres, before=()):
            scratch = [
                pltpu.VMEM((2, 7, size, mid), F32),
                pltpu.VMEM((9, size, mid), F32),
                pltpu.VMEM((8, size // 2, inner), F32),
                pltpu.VMEM((4, size // 2, inner), F32),
                pltpu.VMEM((3, size // 2, inner), F32),
                pltpu.SemaphoreType.DMA((5,)),
            ]
            count = len(quarters)
            return call(
                functools.partial(write_kernel, count, wheres),
                outs,
                [*quarters, *before],
                scratch * count,
                far=range(count, count + len(before)),
                far_outs=(0, 1),
                aliases={count + n: n for n in range(len(before))},
            )

        grads = written([share, other], [(True, True), (False, True)])
        grads = written([far_other, far], [(False, False), (True, False)], grads)
        grad_first, grad_second = (grad.reshape(27, *grad.shape[2:]) for grad in grads)
    else:
        core, y = lax.axis_index("core"), lax.axis_index("y")
        stacked = jnp.stack([jnp.stack([share, far[: block[0]]]), jnp.stack([other, far_other[: block[0]]])])
        quarters = [
            [stacked[lax.bitwise_xor(core, c), lax.bitwise_xor(y, h)] for h in range(2)] for c in range(2)
        ]
        grad_first, grad_second = assembled(quarters, size, inner, mid)
    return features[None], grad_first, grad_second


def solution(mesh):
    dp, dep, hgt = (mesh.shape[axis] for axis in ("dp", "dep", "hgt"))
    split = jax.sharding.Mesh(mesh.devices.reshape(dp, dep, hgt // 2, 2), ("dp", "dep", *HGT))
    block = P("dp", None, "dep", HGT, None)
    return jax.shard_map(
        per_device,
        mesh=split,
        in_specs=(block, P(), P(), block),
        out_specs=(block, P(None, "dp", None), P(None, "dp", None)),
        check_vma=False,
    )
```

```python
import functools

import jax
import jax.numpy as jnp
from jax import lax
from jax.experimental import pallas as pl
from jax.experimental.pallas import tpu as pltpu
from jax.sharding import PartitionSpec as P

BF, F32 = jnp.bfloat16, jnp.float32
LANES = 128
HGT = ("y", "core")
VMEM_BYTES = 28 * 2**20


def call(body, outs, args, scratch=(), flops=0, far=(), far_outs=(), aliases=None):
    moved = sum(x.size * x.dtype.itemsize for x in (*outs, *args))
    return pl.pallas_call(
        body,
        out_shape=outs,
        in_specs=[pl.BlockSpec(memory_space=pl.ANY if n in far else pltpu.VMEM) for n in range(len(args))],
        out_specs=[pl.BlockSpec(memory_space=pl.ANY if n in far_outs else pltpu.VMEM) for n in range(len(outs))],
        scratch_shapes=list(scratch),
        input_output_aliases=aliases or {},
        compiler_params=pltpu.CompilerParams(vmem_limit_bytes=VMEM_BYTES),
        cost_estimate=pl.CostEstimate(flops=flops, bytes_accessed=moved, transcendentals=0),
    )(*args)


def shape(dims, dtype):
    return jax.ShapeDtypeStruct(dims, dtype)


def moved_along_width(x, c):
    if c == 0:
        return x
    pieces = []
    for start in range(0, x.shape[1], LANES):
        piece = x[:, start : start + LANES]
        lane = lax.broadcasted_iota(jnp.int32, piece.shape, 1)
        rolled = pltpu.roll(piece, c % LANES, 1)
        pieces.append(jnp.where(lane == (0 if c == 1 else LANES - 1), 0.0, rolled))
    return pieces[0] if len(pieces) == 1 else jnp.concatenate(pieces, axis=1)


def by_rows(ref, scratch, store):
    channels, depth, height, width = ref.shape
    rows = depth * height
    scratch[: channels * rows] = ref[...].astype(F32).reshape(channels * rows, width)
    for d in range(depth):
        for h in range(height):
            store(d, h, scratch[pl.ds(d * height + h, channels, stride=rows), :])


def odd(axis):
    return lax.rem(lax.axis_index(axis), 2) == 1


def blank_kernel(out_ref):
    out_ref[...] = jnp.zeros(out_ref.shape, BF)


def spread_kernel(cot_ref, k2_ref, blank_ref, cot_rows_ref, back_ref, scratch):
    out, depth, height, _ = cot_ref.shape
    rows = [[None] * height for _ in range(depth)]

    def store(d, h, row):
        rows[d][h] = row.astype(BF)
        cot_rows_ref[d, :, h * LANES : (h + 1) * LANES] = rows[d][h]

    by_rows(cot_ref, scratch, store)
    mid = k2_ref.shape[1]
    none = blank_ref[...]
    padded = [jnp.concatenate([none, *rows[d], none], axis=1) for d in range(depth)]
    for e in range(depth + 2):
        reached = [(d, e - 1 - d) for d in range(depth) if abs(e - 1 - d) <= 1]
        w = jnp.concatenate(
            [
                k2_ref[9 * (a + 1) + 3 * b : 9 * (a + 1) + 3 * b + 3].reshape(3 * mid, out)
                for _, a in reached
                for b in range(3)
            ],
            axis=1,
        )
        for j in range(0, height + 2, 2):
            rhs = jnp.concatenate(
                [padded[d][:, (j + 2 - b) * LANES : (j + 4 - b) * LANES] for d, _ in reached for b in range(3)], axis=0
            )
            y = jnp.dot(w, rhs, preferred_element_type=F32)
            back = sum(moved_along_width(y[n * mid : (n + 1) * mid], n - 1) for n in range(3))
            back_ref[e, :, j * LANES : (j + 2) * LANES] = back


def as_matrix(ref, c):
    stacked = jnp.concatenate([ref[3 * ab + c] for ab in range(9)], axis=0)
    return stacked.astype(F32).T.astype(BF)


def arrange_kernel(cot_rows_ref, k1_ref, vol_ref, moved_ref, w1_ref, own_ref, scratch):
    def store(d, h, row):
        own_ref[d, :, h * LANES : (h + 1) * LANES] = row.astype(BF)

    by_rows(vol_ref, scratch, store)
    depth, out, cells = cot_rows_ref.shape
    for d in range(depth):
        for h in range(0, cells, LANES):
            row = cot_rows_ref[d, :, h : h + LANES]
            for n, c in enumerate((-1, 0, 1)):
                value = row if c == 0 else moved_along_width(row.astype(F32), c).astype(BF)
                moved_ref[d, n * out : (n + 1) * out, h : h + LANES] = value
    mid = k1_ref.shape[2]
    for c in range(3):
        w1_ref[c * mid : (c + 1) * mid, :] = as_matrix(k1_ref, c)


def sides(axis, one, two):
    me, size = lax.axis_index(axis), lax.axis_size(axis)
    is_odd = odd(axis)
    none = jnp.zeros_like(one)
    before = jnp.where(me == 0, none, jnp.where(is_odd, one, two))
    after = jnp.where(me == size - 1, none, jnp.where(is_odd, two, one))
    return before, after


def rim_kernel(own_ref, one_ref, two_ref, deep_ref, send_one_ref, send_two_ref, scratch):
    depth = own_ref.shape[0]
    deep_ref[depth : 2 * depth] = own_ref[...]
    for at, part in zip((0, 2 * depth), sides("dep", one_ref[...], two_ref[...]), strict=True):

        def store(d, h, row, at=at):
            deep_ref[at + d, :, h * LANES : (h + 1) * LANES] = row.astype(BF)

        by_rows(part, scratch, store)
    n, cells = send_one_ref.shape[2], deep_ref.shape[2]
    first, last = deep_ref[:, :, :n], deep_ref[:, :, cells - n :]
    is_odd = odd(HGT)
    send_one_ref[...] = jnp.where(is_odd, first, last)
    send_two_ref[...] = jnp.where(is_odd, last, first)


def widened(deep_ref, one_ref, two_ref):
    left, right = sides(HGT, one_ref[...], two_ref[...])
    return [jnp.concatenate([left[d], deep_ref[d], right[d]], axis=1) for d in range(deep_ref.shape[0])]


def pack(direct, refs, rows_of, blocks):
    if not direct:
        for j, block in enumerate(blocks):
            refs[0][j] = block
        return
    keep_ref, send_ref = refs
    parts, halves, length, _ = keep_ref.shape
    core = lax.axis_index("core") == 1

    def filled(rows):
        rest = length - sum(x.shape[0] for x in rows)
        return jnp.concatenate([*rows, jnp.zeros((rest, LANES), F32)] if rest else rows, axis=0)

    for part in range(parts):
        for half in range(halves):
            one, two = (filled(rows_of(part, c)[half]) for c in range(2))
            keep_ref[part, half] = jnp.where(core, two, one)
            send_ref[part, half] = jnp.where(core, one, two).astype(send_ref.dtype)


def folded(tail):
    half = tail.shape[0] // 2
    return jnp.concatenate([tail[:half], tail[half:]], axis=1)


def activated(w1, rhs, d, depth, heights):
    mid = w1.shape[0] // 3
    y = jnp.dot(w1, rhs, preferred_element_type=F32)
    pre = sum(moved_along_width(y[n * mid : (n + 1) * mid], 1 - n) for n in range(3))
    s = 1.0 / (1.0 + jnp.exp(-pre))
    dep, deps = lax.axis_index("dep"), lax.axis_size("dep")
    hgt, hgts = lax.axis_index(HGT), lax.axis_size(HGT)
    results = []
    for n, side in enumerate(heights):
        p, q = (x[:, n * LANES : (n + 1) * LANES] for x in (pre, s))
        value, slope = (p * q).astype(BF), q * (1.0 + p * (1.0 - q))
        outside = []
        if d == 0:
            outside.append(dep == 0)
        if d == depth - 1:
            outside.append(dep == deps - 1)
        if side < 0:
            outside.append(hgt == 0)
        if side > 0:
            outside.append(hgt == hgts - 1)
        for far in outside:
            value = jnp.where(far, jnp.zeros_like(value), value)
            slope = jnp.where(far, jnp.zeros_like(slope), slope)
        results.append((value, slope))
    return results


def neighbours(ref, d, starts, count):
    return jnp.concatenate(
        [
            jnp.concatenate(
                [ref[d + a, :, (start + b) * LANES : (start + b + count) * LANES] for start in starts], axis=1
            )
            for a in range(3)
            for b in range(3)
        ],
        axis=0,
    )


def products(left, right):
    return lax.dot_general(left, right, (((1,), (1,)), ((), ())), preferred_element_type=F32)


def shares(delta, n_channels, ref, at):
    for n in range(3):
        ref[n * n_channels : (n + 1) * n_channels, at : at + LANES] = moved_along_width(delta, n - 1).astype(BF)


def inner_kernel(deep_ref, w1_ref, moved_ref, back_ref, hidden_ref, second_ref, first_ref, delta_ref):
    w1 = w1_ref[...]
    depth, mid, cells = hidden_ref.shape
    height = cells // LANES
    for d in range(depth):
        for h in range(0, height, 2):
            results = activated(w1, neighbours(deep_ref, d, [h], 2), d, depth, (0, 0))
            for n, (value, slope) in enumerate(results):
                at = (h + n) * LANES
                hidden_ref[d, :, at : at + LANES] = value
                back = back_ref[d, :, at + 2 * LANES : at + 3 * LANES]
                shares(back * slope, mid, delta_ref, d * cells + at)
    own = depth - 2
    left = jnp.concatenate(
        [
            jnp.concatenate([moved_ref[d, :, (2 - b) * LANES : (2 - b) * LANES + cells] for d in range(own)], axis=1)
            for b in range(3)
        ],
        axis=0,
    )
    right = jnp.concatenate(
        [jnp.concatenate([hidden_ref[d + a] for a in range(3)], axis=0) for d in range(own)], axis=1
    )
    second_ref[...] = products(left, right)
    right = jnp.concatenate([neighbours(deep_ref, d, [0], height) for d in range(depth)], axis=1)
    first_ref[...] = products(delta_ref[...], right)


def outer_kernel(
    direct, deep_ref, two_ref, one_ref, w1_ref, back_ref, inner_ref, first_ref, hidden_ref, *grad_refs_and_scratch,
):
    *grad_refs, rows_ref, delta_ref = grad_refs_and_scratch
    for d, row in enumerate(widened(deep_ref, one_ref, two_ref)):
        rows_ref[d] = row
    w1 = w1_ref[...]
    depth, mid, cells = hidden_ref.shape
    last = cells // LANES - 2
    for d in range(depth):
        hidden_ref[d, :, 2 * LANES : last * LANES] = inner_ref[d]
        for h, sides_of in ((0, (-1, 0)), (last, (0, 1))):
            results = activated(w1, neighbours(rows_ref, d, [h], 2), d, depth, sides_of)
            for n, (value, slope) in enumerate(results):
                at = (h + n) * LANES
                hidden_ref[d, :, at : at + LANES] = value
                delta = back_ref[d, :, at : at + LANES] * slope
                shares(delta, mid, delta_ref, (4 * d + (2 if h else 0) + n) * LANES)
    right = jnp.concatenate([neighbours(rows_ref, d, [0, last], 2) for d in range(depth)], axis=1)
    total = first_ref[...] + products(delta_ref[...], right)
    inner = rows_ref.shape[1]
    blocks, tails = [], []
    for n in range(3):
        part = total[n * mid : (n + 1) * mid]
        blocks += [part[:, m * LANES : (m + 1) * LANES] for m in range(2)]
        tails.append(part[:, 2 * LANES :])
    tails.append(jnp.zeros((mid, LANES - 3 * inner), F32))
    blocks.append(jnp.concatenate(tails, axis=1))
    size = mid // lax.axis_size("dp")
    half = size // 2

    def rows_of(part, core):
        rows = [block[part * size + core * half : part * size + (core + 1) * half] for block in blocks]
        return rows[:3], rows[3:]

    pack(direct, grad_refs, rows_of, blocks)


def second_kernel(direct, hidden_ref, moved_ref, second_ref, *grad_refs):
    depth, mid, cells = hidden_ref.shape
    height = cells // LANES
    own = depth - 2
    out = moved_ref.shape[1] // 3
    heads, tails = [], []
    for b in range(3):
        far = [h for h in range(height - 2) if not 2 <= h + b <= height - 3]
        left = jnp.concatenate(
            [moved_ref[d, :, h * LANES : (h + 1) * LANES] for d in range(own) for h in far], axis=1
        )
        right = jnp.concatenate(
            [
                jnp.concatenate([hidden_ref[d + a, :, (h + b) * LANES : (h + b + 1) * LANES] for a in range(3)], axis=0)
                for d in range(own)
                for h in far
            ],
            axis=1,
        )
        total = second_ref[3 * b * out : 3 * (b + 1) * out, :] + products(left, right)
        for c in range(3):
            part = total[c * out : (c + 1) * out]
            heads.append(part[:, :LANES])
            tails.append(part[:, LANES:])
    blocks = heads + [jnp.concatenate(tails[n : n + 2], axis=1) for n in range(0, 8, 2)]
    size = mid // lax.axis_size("dp")

    def rows_of(part, core):
        at = slice((2 * part + core) * size, (2 * part + core + 1) * size)
        rows = [block[at] for block in blocks] + [folded(tails[8][at])]
        return rows[:7], rows[7:]

    pack(direct, grad_refs, rows_of, [*blocks, jnp.concatenate([tails[8], jnp.zeros_like(tails[8])], axis=1)])


def features_kernel(hidden_ref, k2_ref, out_ref, token_ref, scratch):
    out, depth, height, _ = out_ref.shape
    w2 = jnp.concatenate([as_matrix(k2_ref, c) for c in range(3)], axis=0)
    for d in range(depth):
        for h in range(0, height, 2):
            rhs = jnp.concatenate(
                [
                    hidden_ref[d + a, :, (h + b) * LANES : (h + b + 2) * LANES]
                    for a in range(3)
                    for b in range(3)
                ],
                axis=0,
            )
            y = jnp.dot(w2, rhs, preferred_element_type=F32)
            total = sum(moved_along_width(y[n * out : (n + 1) * out], 1 - n) for n in range(3))
            for r in range(2):
                row = total[:, r * LANES : (r + 1) * LANES]
                scratch[pl.ds(d * height + h + r, out, stride=depth * height), :] = row
    out_ref[...] = scratch[: out * depth * height].reshape(out_ref.shape).astype(BF)
    token_ref[...] = scratch[:8]


def plane_kernel(moves, cuts, *refs):
    sums, (kept_ref, *send_refs) = refs[: -1 - len(moves)], refs[-1 - len(moves) :]
    part = lax.rem(lax.axis_index("dp"), sums[0].shape[0])
    half = lax.axis_index("y")

    def total(x, y):
        at = 1 - part if x else part, 1 - half if y else half
        values = [keep[at] + got[at].astype(F32) for keep, got in zip(sums[::2], sums[1::2], strict=True)]
        if len(values) == 1:
            return values[0]
        one, two = (jnp.concatenate([v[:n] for v, n in zip(values, cut, strict=True)], axis=0) for cut in cuts)
        return jnp.where(at[1] == 0, one, two)

    kept_ref[...] = total(0, 0)
    for (x, y), send_ref in zip(moves, send_refs, strict=True):
        send_ref[...] = total(x, y).astype(BF)


def total_kernel(kept_ref, *refs):
    *got_refs, out_ref = refs
    value = kept_ref[...]
    for ref in got_refs:
        value = value + ref[...].astype(F32)
    out_ref[...] = value.astype(BF)


def depth_kernel(a_ref, b_ref, c_ref, d_ref, _, out_ref, padded_ref):
    one = a_ref[...].astype(F32) + b_ref[...].astype(F32)
    two = c_ref[...].astype(F32) + d_ref[...].astype(F32)
    out_ref[...] = (one + two).astype(BF)
    rest = jnp.zeros((padded_ref.shape[0] - out_ref.shape[0], LANES), F32)
    padded_ref[...] = jnp.concatenate([one + two, rest], axis=0).astype(BF)


def write_kernel(count, wheres, *refs):
    n_scratch = 6
    in_refs = refs[:count]
    out_refs, scratch = refs[: -n_scratch * count], refs[-n_scratch * count :]
    first_ref, second_ref = out_refs[-2:]
    core, y = lax.axis_index("core"), lax.axis_index("y")

    def begun(n, half):
        wide, last, low, high, tail, sems = scratch[n_scratch * n : n_scratch * (n + 1)]
        own_core, _ = wheres[n]
        at = core if own_core else 1 - core
        rows = in_refs[n][...].astype(F32)
        _, _, size, mid = wide.shape
        _, small, inner = low.shape
        here = pl.ds(pl.multiple_of(at * size, size), size)
        count = 2 if half else 7
        for j in range(count):
            value = rows[j * size : (j + 1) * size]
            for m in range(2):
                wide[m, j] = value[:, m * mid : (m + 1) * mid]
        pairs = [(wide.at[:, :count], second_ref.at[0:2, 7 * half : 7 * half + count, here, :])]
        row = count * size
        if half:
            for j in range(4):
                value = rows[row : row + size]
                row += size
                for m in range(2):
                    last[2 * j + m] = value[:, m * mid : (m + 1) * mid]
            value = rows[row : row + size // 2]
            row += size // 2
            last[8] = jnp.concatenate([value[:, :mid], value[:, mid:]], axis=0)
            pairs.append((last, second_ref.at[2, :, here, :]))
        copies = [pltpu.make_async_copy(src, dst, sems.at[i]) for i, (src, dst) in enumerate(pairs)]
        for copy in copies:
            copy.start()
        here = pl.ds(pl.multiple_of(at * small, small), small)
        places = [(high, 0, 4), (low, 0, 4), (low, 4, 4), (tail, 0, 3)] if half else [(low, 0, 4), (low, 4, 4), (high, 0, 4)]
        for ref, start, number in places:
            value = rows[row : row + small]
            row += small
            for m in range(number):
                ref[start + m] = value[:, m * inner : (m + 1) * inner]
        if half:
            pairs = [
                (high, first_ref.at[4:8, 1, here, :]),
                (low, first_ref.at[0:8, 2, here, :]),
                (tail, first_ref.at[8, :, here, :]),
            ]
        else:
            pairs = [(low, first_ref.at[0:8, 0, here, :]), (high, first_ref.at[0:4, 1, here, :])]
        more = [pltpu.make_async_copy(src, dst, sems.at[2 + i]) for i, (src, dst) in enumerate(pairs)]
        for copy in more:
            copy.start()
        return copies + more

    for half in range(2):

        @pl.when(y == half)
        def _(half=half):
            copies = []
            for n, (_, own_y) in enumerate(wheres):
                copies += begun(n, half if own_y else 1 - half)
            for copy in copies:
                copy.wait()


def swapped(x, axis, first):
    axes = (axis,) if isinstance(axis, str) else axis
    parts, size = lax.axis_size("dp"), lax.axis_size(axis)
    partner = list(range(parts * size))
    for i in partner:
        part, at = divmod(i, size)
        if first <= at < size - (size - first) % 2:
            partner[i] = part * size + (at - first ^ 1) + first
        elif parts % 2 == 0:
            partner[i] = (part ^ 1) * size + at
    return lax.ppermute(x, ("dp", *axes), list(enumerate(partner)))


def across(x, *moves):
    axes = tuple(axis for axis, _ in moves)
    flip = 0
    for axis, bit in moves:
        flip = flip * lax.axis_size(axis) + bit
    return lax.ppermute(x, axes, [(i, i ^ flip) for i in range(lax.axis_size(axes))])


def scattered(rows, cuts):
    halves = [
        jnp.concatenate([x[:, :, :n] if at == 0 else x[:, :, x.shape[2] - n :] for x, n in zip(rows, cut)], axis=2)
        for at, cut in enumerate(cuts)
    ]
    grad = lax.psum_scatter(jnp.stack(halves, axis=2), "dp", scatter_dimension=0, tiled=True)
    core = lax.axis_index("core")
    return tuple(lax.dynamic_index_in_dim(grad, at, 1, False) for at in (core, 1 - core))


def assembled(quarters, size, inner, mid):
    first, second = ([[None, None] for _ in range(27)] for _ in range(2))
    half = size // 2
    for core in range(2):
        for y in range(2):
            rows, row = quarters[core][y].astype(F32), 0
            for j in range(7) if y == 0 else range(7, 13):
                for m, k in enumerate((j, 9 + j) if j < 9 else (2 * j, 2 * j + 1)):
                    second[k][core] = rows[row : row + size, m * mid : (m + 1) * mid]
                row += size
            if y == 1:
                tail = rows[row : row + half]
                second[26][core] = jnp.concatenate([tail[:, :mid], tail[:, mid:]], axis=0)
                row += half
            for j in range(3) if y == 0 else range(3, 7):
                for m in range(4):
                    c, ab = (j // 2, 4 * (j % 2) + m) if j < 6 else (m, 8)
                    if c < 3:
                        first[3 * ab + c][core] = rows[row : row + half, m * inner : (m + 1) * inner]
                row += half
    return tuple(jnp.stack([jnp.concatenate(both, axis=0) for both in grad]) for grad in (first, second))


def per_device(volume, kernel_first, kernel_second, cotangent):
    _, inner, depth, height, width = volume.shape
    mid, out = kernel_first.shape[1], kernel_second.shape[1]
    cells = height * width
    parts = lax.axis_size("dp")
    k1, k2 = jnp.swapaxes(kernel_first, 1, 2), jnp.swapaxes(kernel_second, 1, 2)
    rows = depth * height

    one, two = swapped(volume[0], "dep", 0), swapped(volume[0], "dep", 1)
    (blank,) = call(blank_kernel, [shape((out, 2 * width), BF)], [], flops=3_000_000_000)
    cot_rows, back = call(
        spread_kernel,
        [
            shape((depth, out, cells), BF),
            shape((depth + 2, mid, cells + 2 * width), F32),
        ],
        [cotangent[0], k2, blank],
        [pltpu.VMEM(((out + 1) * rows, width), F32)],
        flops=1_100_000_000,
    )
    moved, w1, vol = call(
        arrange_kernel,
        [
            shape((depth, 3 * out, cells), BF),
            shape((3 * mid, 9 * inner), BF),
            shape((depth, inner, cells), BF),
        ],
        [cot_rows, k1, volume[0]],
        [pltpu.VMEM(((inner + 1) * rows, width), F32)],
        flops=500_000_000,
    )
    deep, one, two = call(
        rim_kernel,
        [shape((3 * depth, inner, cells), BF)] + [shape((3 * depth, inner, 2 * width), BF)] * 2,
        [vol, one, two],
        [pltpu.VMEM(((inner + 1) * rows, width), F32)],
    )
    one, two = swapped(one, HGT, 0), swapped(two, HGT, 1)
    size = mid // parts
    direct = parts == 2 and size % 16 == 0
    halves = lax.axis_size("y")
    cuts = ((7 * size, 3 * size // 2), (13 * size // 2, 2 * size))
    length_second, length_first = 7 * size, 2 * size
    rows_in, rows_out = height - 2, 4
    inner_hidden, inner_second, inner_first = call(
        inner_kernel,
        [
            shape((depth + 2, mid, rows_in * width), BF),
            shape((9 * out, 3 * mid), F32),
            shape((3 * mid, 9 * inner), F32),
        ],
        [deep, w1, moved, back],
        [pltpu.VMEM((3 * mid, (depth + 2) * rows_in * width), BF)],
        flops=1_500_000_000,
    )
    hidden, *first = call(
        functools.partial(outer_kernel, direct),
        [shape((depth + 2, mid, cells + 2 * width), BF)]
        + ([shape((parts, halves, length_first, width), F32)] * 2 if direct else [shape((7, mid, LANES), F32)]),
        [deep, two, one, w1, back, inner_hidden, inner_first],
        [
            pltpu.VMEM((3 * depth, inner, cells + 4 * width), BF),
            pltpu.VMEM((3 * mid, (depth + 2) * rows_out * width), BF),
        ],
        flops=1_000_000_000,
    )
    second = call(
        functools.partial(second_kernel, direct),
        [shape((parts, halves, length_second, width), kind) for kind in (F32, BF)]
        if direct
        else [shape((14, out, LANES), F32)],
        [hidden, moved, inner_second],
        flops=4_000_000_000,
    )
    if direct:
        moves = [(0, 1), (1, 0), (1, 1)]
        grads = [second, first]
    else:
        moves = [(0, 1)]
        blocks = second[0].reshape(14, parts, 2, size, LANES).transpose(1, 2, 0, 3, 4)
        tail = blocks[:, :, 13, :, :mid]
        tail = jnp.concatenate([tail[:, :, : size // 2], tail[:, :, size // 2 :]], axis=-1)
        rows_second = jnp.concatenate([blocks[:, :, :13].reshape(parts, 2, 13 * size, LANES), tail], axis=2)
        blocks = first[0].reshape(7, parts, 2, size // 2, LANES).transpose(1, 2, 0, 3, 4)
        rows_first = blocks.reshape(parts, 2, 7 * (size // 2), LANES)
        grads = [scattered([rows_second, rows_first], cuts)]
    block = (sum(cuts[0]), width)
    kept, *sends = call(
        functools.partial(plane_kernel, moves, cuts),
        [shape(block, F32)] + [shape(block, BF)] * len(moves),
        [x for keep, send in grads for x in (keep, across(send, ("core", 1)))],
    )
    gots = [across(send, ("dp", x), ("y", y)) for send, (x, y) in zip(sends, moves, strict=True)]
    (share,) = call(total_kernel, [shape(block, BF)], [kept, *gots])
    features, token = call(
        features_kernel,
        [shape(cotangent.shape[1:], BF), shape((8, width), F32)],
        [hidden, k2],
        [pltpu.VMEM(((out + 1) * rows, width), F32)],
        flops=900_000_000,
    )
    gots = [across(share, ("dep", bits)) for bits in (1, 2, 3)]
    share, for_y = call(depth_kernel, [shape(block, BF), shape((block[0] + 16, width), BF)], [share, *gots, token])
    other, far = across(share, ("core", 1)), across(for_y, ("y", 1))
    far_other = across(for_y, ("y", 1), ("core", 1))
    if size % 16 == 0:
        outs = [shape((9, 3, size, inner), F32), shape((3, 9, 2 * size, mid), F32)]

        def written(quarters, wheres, before=()):
            scratch = [
                pltpu.VMEM((2, 7, size, mid), F32),
                pltpu.VMEM((9, size, mid), F32),
                pltpu.VMEM((8, size // 2, inner), F32),
                pltpu.VMEM((4, size // 2, inner), F32),
                pltpu.VMEM((3, size // 2, inner), F32),
                pltpu.SemaphoreType.DMA((5,)),
            ]
            count = len(quarters)
            return call(
                functools.partial(write_kernel, count, wheres),
                outs,
                [*quarters, *before],
                scratch * count,
                far=range(count, count + len(before)),
                far_outs=(0, 1),
                aliases={count + n: n for n in range(len(before))},
            )

        grads = written([share, other], [(True, True), (False, True)])
        grads = written([far_other, far], [(False, False), (True, False)], grads)
        grad_first, grad_second = (grad.reshape(27, *grad.shape[2:]) for grad in grads)
    else:
        core, y = lax.axis_index("core"), lax.axis_index("y")
        stacked = jnp.stack([jnp.stack([share, far[: block[0]]]), jnp.stack([other, far_other[: block[0]]])])
        quarters = [
            [stacked[lax.bitwise_xor(core, c), lax.bitwise_xor(y, h)] for h in range(2)] for c in range(2)
        ]
        grad_first, grad_second = assembled(quarters, size, inner, mid)
    return features[None], grad_first, grad_second


def solution(mesh):
    dp, dep, hgt = (mesh.shape[axis] for axis in ("dp", "dep", "hgt"))
    split = jax.sharding.Mesh(mesh.devices.reshape(dp, dep, hgt // 2, 2), ("dp", "dep", *HGT))
    block = P("dp", None, "dep", HGT, None)
    return jax.shard_map(
        per_device,
        mesh=split,
        in_specs=(block, P(), P(), block),
        out_specs=(block, P(None, "dp", None), P(None, "dp", None)),
        check_vma=False,
    )
```

```python
import functools

import jax
import jax.numpy as jnp
from jax import lax
from jax.experimental import pallas as pl
from jax.experimental.pallas import tpu as pltpu
from jax.sharding import PartitionSpec as P

BF, F32 = jnp.bfloat16, jnp.float32
LANES = 128
HGT = ("y", "core")
VMEM_BYTES = 28 * 2**20


def call(body, outs, args, scratch=(), flops=0, far=(), far_outs=(), aliases=None):
    moved = sum(x.size * x.dtype.itemsize for x in (*outs, *args))
    return pl.pallas_call(
        body,
        out_shape=outs,
        in_specs=[pl.BlockSpec(memory_space=pl.ANY if n in far else pltpu.VMEM) for n in range(len(args))],
        out_specs=[pl.BlockSpec(memory_space=pl.ANY if n in far_outs else pltpu.VMEM) for n in range(len(outs))],
        scratch_shapes=list(scratch),
        input_output_aliases=aliases or {},
        compiler_params=pltpu.CompilerParams(vmem_limit_bytes=VMEM_BYTES),
        cost_estimate=pl.CostEstimate(flops=flops, bytes_accessed=moved, transcendentals=0),
    )(*args)


def shape(dims, dtype):
    return jax.ShapeDtypeStruct(dims, dtype)


def moved_along_width(x, c):
    if c == 0:
        return x
    pieces = []
    for start in range(0, x.shape[1], LANES):
        piece = x[:, start : start + LANES]
        lane = lax.broadcasted_iota(jnp.int32, piece.shape, 1)
        rolled = pltpu.roll(piece, c % LANES, 1)
        pieces.append(jnp.where(lane == (0 if c == 1 else LANES - 1), 0.0, rolled))
    return pieces[0] if len(pieces) == 1 else jnp.concatenate(pieces, axis=1)


def by_rows(ref, scratch, store):
    channels, depth, height, width = ref.shape
    rows = depth * height
    scratch[: channels * rows] = ref[...].astype(F32).reshape(channels * rows, width)
    for d in range(depth):
        for h in range(height):
            store(d, h, scratch[pl.ds(d * height + h, channels, stride=rows), :])


def odd(axis):
    return lax.rem(lax.axis_index(axis), 2) == 1


def blank_kernel(out_ref):
    out_ref[...] = jnp.zeros(out_ref.shape, BF)


def spread_kernel(cot_ref, k2_ref, blank_ref, cot_rows_ref, back_ref, scratch):
    out, depth, height, _ = cot_ref.shape
    rows = [[None] * height for _ in range(depth)]

    def store(d, h, row):
        rows[d][h] = row.astype(BF)
        cot_rows_ref[d, :, h * LANES : (h + 1) * LANES] = rows[d][h]

    by_rows(cot_ref, scratch, store)
    mid = k2_ref.shape[1]
    none = blank_ref[...]
    padded = [jnp.concatenate([none, *rows[d], none], axis=1) for d in range(depth)]
    for e in range(depth + 2):
        reached = [(d, e - 1 - d) for d in range(depth) if abs(e - 1 - d) <= 1]
        w = jnp.concatenate(
            [
                k2_ref[9 * (a + 1) + 3 * b : 9 * (a + 1) + 3 * b + 3].reshape(3 * mid, out)
                for _, a in reached
                for b in range(3)
            ],
            axis=1,
        )
        for j in range(0, height + 2, 2):
            rhs = jnp.concatenate(
                [padded[d][:, (j + 2 - b) * LANES : (j + 4 - b) * LANES] for d, _ in reached for b in range(3)], axis=0
            )
            y = jnp.dot(w, rhs, preferred_element_type=F32)
            back = sum(moved_along_width(y[n * mid : (n + 1) * mid], n - 1) for n in range(3))
            back_ref[e, :, j * LANES : (j + 2) * LANES] = back


def as_matrix(ref, c):
    stacked = jnp.concatenate([ref[3 * ab + c] for ab in range(9)], axis=0)
    return stacked.astype(F32).T.astype(BF)


def arrange_kernel(cot_rows_ref, k1_ref, vol_ref, moved_ref, w1_ref, own_ref, scratch):
    def store(d, h, row):
        own_ref[d, :, h * LANES : (h + 1) * LANES] = row.astype(BF)

    by_rows(vol_ref, scratch, store)
    depth, out, cells = cot_rows_ref.shape
    for d in range(depth):
        for h in range(0, cells, LANES):
            row = cot_rows_ref[d, :, h : h + LANES]
            for n, c in enumerate((-1, 0, 1)):
                value = row if c == 0 else moved_along_width(row.astype(F32), c).astype(BF)
                moved_ref[d, n * out : (n + 1) * out, h : h + LANES] = value
    mid = k1_ref.shape[2]
    for c in range(3):
        w1_ref[c * mid : (c + 1) * mid, :] = as_matrix(k1_ref, c)


def sides(axis, one, two):
    me, size = lax.axis_index(axis), lax.axis_size(axis)
    is_odd = odd(axis)
    none = jnp.zeros_like(one)
    before = jnp.where(me == 0, none, jnp.where(is_odd, one, two))
    after = jnp.where(me == size - 1, none, jnp.where(is_odd, two, one))
    return before, after


def rim_kernel(own_ref, one_ref, two_ref, deep_ref, send_one_ref, send_two_ref, scratch):
    depth = own_ref.shape[0]
    deep_ref[depth : 2 * depth] = own_ref[...]
    for at, part in zip((0, 2 * depth), sides("dep", one_ref[...], two_ref[...]), strict=True):

        def store(d, h, row, at=at):
            deep_ref[at + d, :, h * LANES : (h + 1) * LANES] = row.astype(BF)

        by_rows(part, scratch, store)
    n, cells = send_one_ref.shape[2], deep_ref.shape[2]
    first, last = deep_ref[:, :, :n], deep_ref[:, :, cells - n :]
    is_odd = odd(HGT)
    send_one_ref[...] = jnp.where(is_odd, first, last)
    send_two_ref[...] = jnp.where(is_odd, last, first)


def widened(deep_ref, one_ref, two_ref):
    left, right = sides(HGT, one_ref[...], two_ref[...])
    return [jnp.concatenate([left[d], deep_ref[d], right[d]], axis=1) for d in range(deep_ref.shape[0])]


def pack(direct, refs, rows_of, blocks):
    if not direct:
        for j, block in enumerate(blocks):
            refs[0][j] = block
        return
    keep_ref, send_ref = refs
    parts, halves, length, _ = keep_ref.shape
    core = lax.axis_index("core") == 1

    def filled(rows):
        rest = length - sum(x.shape[0] for x in rows)
        return jnp.concatenate([*rows, jnp.zeros((rest, LANES), F32)] if rest else rows, axis=0)

    for part in range(parts):
        for half in range(halves):
            one, two = (filled(rows_of(part, c)[half]) for c in range(2))
            keep_ref[part, half] = jnp.where(core, two, one)
            send_ref[part, half] = jnp.where(core, one, two).astype(send_ref.dtype)


def folded(tail):
    half = tail.shape[0] // 2
    return jnp.concatenate([tail[:half], tail[half:]], axis=1)


def activated(w1, rhs, d, depth, heights):
    mid = w1.shape[0] // 3
    y = jnp.dot(w1, rhs, preferred_element_type=F32)
    pre = sum(moved_along_width(y[n * mid : (n + 1) * mid], 1 - n) for n in range(3))
    s = 1.0 / (1.0 + jnp.exp(-pre))
    dep, deps = lax.axis_index("dep"), lax.axis_size("dep")
    hgt, hgts = lax.axis_index(HGT), lax.axis_size(HGT)
    results = []
    for n, side in enumerate(heights):
        p, q = (x[:, n * LANES : (n + 1) * LANES] for x in (pre, s))
        value, slope = (p * q).astype(BF), q * (1.0 + p * (1.0 - q))
        outside = []
        if d == 0:
            outside.append(dep == 0)
        if d == depth - 1:
            outside.append(dep == deps - 1)
        if side < 0:
            outside.append(hgt == 0)
        if side > 0:
            outside.append(hgt == hgts - 1)
        for far in outside:
            value = jnp.where(far, jnp.zeros_like(value), value)
            slope = jnp.where(far, jnp.zeros_like(slope), slope)
        results.append((value, slope))
    return results


def neighbours(ref, d, starts, count):
    return jnp.concatenate(
        [
            jnp.concatenate(
                [ref[d + a, :, (start + b) * LANES : (start + b + count) * LANES] for start in starts], axis=1
            )
            for a in range(3)
            for b in range(3)
        ],
        axis=0,
    )


def products(left, right):
    return lax.dot_general(left, right, (((1,), (1,)), ((), ())), preferred_element_type=F32)


def shares(delta, n_channels, ref, at):
    for n in range(3):
        ref[n * n_channels : (n + 1) * n_channels, at : at + LANES] = moved_along_width(delta, n - 1).astype(BF)


def inner_kernel(deep_ref, w1_ref, moved_ref, back_ref, hidden_ref, second_ref, first_ref, delta_ref):
    w1 = w1_ref[...]
    depth, mid, cells = hidden_ref.shape
    height = cells // LANES
    for d in range(depth):
        for h in range(0, height, 2):
            results = activated(w1, neighbours(deep_ref, d, [h], 2), d, depth, (0, 0))
            for n, (value, slope) in enumerate(results):
                at = (h + n) * LANES
                hidden_ref[d, :, at : at + LANES] = value
                back = back_ref[d, :, at + 2 * LANES : at + 3 * LANES]
                shares(back * slope, mid, delta_ref, d * cells + at)
    own = depth - 2
    left = jnp.concatenate(
        [
            jnp.concatenate([moved_ref[d, :, (2 - b) * LANES : (2 - b) * LANES + cells] for d in range(own)], axis=1)
            for b in range(3)
        ],
        axis=0,
    )
    right = jnp.concatenate(
        [jnp.concatenate([hidden_ref[d + a] for a in range(3)], axis=0) for d in range(own)], axis=1
    )
    second_ref[...] = products(left, right)
    right = jnp.concatenate([neighbours(deep_ref, d, [0], height) for d in range(depth)], axis=1)
    first_ref[...] = products(delta_ref[...], right)


def outer_kernel(
    direct, deep_ref, two_ref, one_ref, w1_ref, back_ref, inner_ref, first_ref, hidden_ref, *grad_refs_and_scratch,
):
    *grad_refs, rows_ref, delta_ref = grad_refs_and_scratch
    for d, row in enumerate(widened(deep_ref, one_ref, two_ref)):
        rows_ref[d] = row
    w1 = w1_ref[...]
    depth, mid, cells = hidden_ref.shape
    last = cells // LANES - 2
    for d in range(depth):
        hidden_ref[d, :, 2 * LANES : last * LANES] = inner_ref[d]
        for h, sides_of in ((0, (-1, 0)), (last, (0, 1))):
            results = activated(w1, neighbours(rows_ref, d, [h], 2), d, depth, sides_of)
            for n, (value, slope) in enumerate(results):
                at = (h + n) * LANES
                hidden_ref[d, :, at : at + LANES] = value
                delta = back_ref[d, :, at : at + LANES] * slope
                shares(delta, mid, delta_ref, (4 * d + (2 if h else 0) + n) * LANES)
    right = jnp.concatenate([neighbours(rows_ref, d, [0, last], 2) for d in range(depth)], axis=1)
    total = first_ref[...] + products(delta_ref[...], right)
    inner = rows_ref.shape[1]
    blocks, tails = [], []
    for n in range(3):
        part = total[n * mid : (n + 1) * mid]
        blocks += [part[:, m * LANES : (m + 1) * LANES] for m in range(2)]
        tails.append(part[:, 2 * LANES :])
    tails.append(jnp.zeros((mid, LANES - 3 * inner), F32))
    blocks.append(jnp.concatenate(tails, axis=1))
    size = mid // lax.axis_size("dp")
    half = size // 2

    def rows_of(part, core):
        rows = [block[part * size + core * half : part * size + (core + 1) * half] for block in blocks]
        return rows[:3], rows[3:]

    pack(direct, grad_refs, rows_of, blocks)


def second_kernel(direct, hidden_ref, moved_ref, second_ref, *grad_refs):
    depth, mid, cells = hidden_ref.shape
    height = cells // LANES
    own = depth - 2
    out = moved_ref.shape[1] // 3
    heads, tails = [], []
    for b in range(3):
        far = [h for h in range(height - 2) if not 2 <= h + b <= height - 3]
        left = jnp.concatenate(
            [moved_ref[d, :, h * LANES : (h + 1) * LANES] for d in range(own) for h in far], axis=1
        )
        right = jnp.concatenate(
            [
                jnp.concatenate([hidden_ref[d + a, :, (h + b) * LANES : (h + b + 1) * LANES] for a in range(3)], axis=0)
                for d in range(own)
                for h in far
            ],
            axis=1,
        )
        total = second_ref[3 * b * out : 3 * (b + 1) * out, :] + products(left, right)
        for c in range(3):
            part = total[c * out : (c + 1) * out]
            heads.append(part[:, :LANES])
            tails.append(part[:, LANES:])
    blocks = heads + [jnp.concatenate(tails[n : n + 2], axis=1) for n in range(0, 8, 2)]
    size = mid // lax.axis_size("dp")

    def rows_of(part, core):
        at = slice((2 * part + core) * size, (2 * part + core + 1) * size)
        rows = [block[at] for block in blocks] + [folded(tails[8][at])]
        return rows[:7], rows[7:]

    pack(direct, grad_refs, rows_of, [*blocks, jnp.concatenate([tails[8], jnp.zeros_like(tails[8])], axis=1)])


def features_kernel(hidden_ref, k2_ref, out_ref, token_ref, scratch):
    out, depth, height, _ = out_ref.shape
    w2 = jnp.concatenate([as_matrix(k2_ref, c) for c in range(3)], axis=0)
    for d in range(depth):
        for h in range(0, height, 2):
            rhs = jnp.concatenate(
                [
                    hidden_ref[d + a, :, (h + b) * LANES : (h + b + 2) * LANES]
                    for a in range(3)
                    for b in range(3)
                ],
                axis=0,
            )
            y = jnp.dot(w2, rhs, preferred_element_type=F32)
            total = sum(moved_along_width(y[n * out : (n + 1) * out], 1 - n) for n in range(3))
            for r in range(2):
                row = total[:, r * LANES : (r + 1) * LANES]
                scratch[pl.ds(d * height + h + r, out, stride=depth * height), :] = row
    out_ref[...] = scratch[: out * depth * height].reshape(out_ref.shape).astype(BF)
    token_ref[...] = scratch[:8]


def plane_kernel(moves, cuts, *refs):
    sums, (kept_ref, *send_refs) = refs[: -1 - len(moves)], refs[-1 - len(moves) :]
    part = lax.rem(lax.axis_index("dp"), sums[0].shape[0])
    half = lax.axis_index("y")

    def total(x, y):
        at = 1 - part if x else part, 1 - half if y else half
        values = [keep[at] + got[at].astype(F32) for keep, got in zip(sums[::2], sums[1::2], strict=True)]
        if len(values) == 1:
            return values[0]
        one, two = (jnp.concatenate([v[:n] for v, n in zip(values, cut, strict=True)], axis=0) for cut in cuts)
        return jnp.where(at[1] == 0, one, two)

    kept_ref[...] = total(0, 0)
    for (x, y), send_ref in zip(moves, send_refs, strict=True):
        send_ref[...] = total(x, y).astype(BF)


def total_kernel(kept_ref, *refs):
    *got_refs, out_ref = refs
    value = kept_ref[...]
    for ref in got_refs:
        value = value + ref[...].astype(F32)
    out_ref[...] = value.astype(BF)


def depth_kernel(a_ref, b_ref, c_ref, d_ref, _, out_ref, padded_ref):
    one = a_ref[...].astype(F32) + b_ref[...].astype(F32)
    two = c_ref[...].astype(F32) + d_ref[...].astype(F32)
    out_ref[...] = (one + two).astype(BF)
    rest = jnp.zeros((padded_ref.shape[0] - out_ref.shape[0], LANES), F32)
    padded_ref[...] = jnp.concatenate([one + two, rest], axis=0).astype(BF)


def write_kernel(count, wheres, *refs):
    n_scratch = 6
    in_refs = refs[:count]
    out_refs, scratch = refs[: -n_scratch * count], refs[-n_scratch * count :]
    first_ref, second_ref = out_refs[-2:]
    core, y = lax.axis_index("core"), lax.axis_index("y")

    def begun(n, half):
        wide, last, low, high, tail, sems = scratch[n_scratch * n : n_scratch * (n + 1)]
        own_core, _ = wheres[n]
        at = core if own_core else 1 - core
        rows = in_refs[n][...].astype(F32)
        _, _, size, mid = wide.shape
        _, small, inner = low.shape
        here = pl.ds(pl.multiple_of(at * size, size), size)
        count = 2 if half else 7
        for j in range(count):
            value = rows[j * size : (j + 1) * size]
            for m in range(2):
                wide[m, j] = value[:, m * mid : (m + 1) * mid]
        pairs = [(wide.at[:, :count], second_ref.at[0:2, 7 * half : 7 * half + count, here, :])]
        row = count * size
        if half:
            for j in range(4):
                value = rows[row : row + size]
                row += size
                for m in range(2):
                    last[2 * j + m] = value[:, m * mid : (m + 1) * mid]
            value = rows[row : row + size // 2]
            row += size // 2
            last[8] = jnp.concatenate([value[:, :mid], value[:, mid:]], axis=0)
            pairs.append((last, second_ref.at[2, :, here, :]))
        copies = [pltpu.make_async_copy(src, dst, sems.at[i]) for i, (src, dst) in enumerate(pairs)]
        for copy in copies:
            copy.start()
        here = pl.ds(pl.multiple_of(at * small, small), small)
        places = [(high, 0, 4), (low, 0, 4), (low, 4, 4), (tail, 0, 3)] if half else [(low, 0, 4), (low, 4, 4), (high, 0, 4)]
        for ref, start, number in places:
            value = rows[row : row + small]
            row += small
            for m in range(number):
                ref[start + m] = value[:, m * inner : (m + 1) * inner]
        if half:
            pairs = [
                (high, first_ref.at[4:8, 1, here, :]),
                (low, first_ref.at[0:8, 2, here, :]),
                (tail, first_ref.at[8, :, here, :]),
            ]
        else:
            pairs = [(low, first_ref.at[0:8, 0, here, :]), (high, first_ref.at[0:4, 1, here, :])]
        more = [pltpu.make_async_copy(src, dst, sems.at[2 + i]) for i, (src, dst) in enumerate(pairs)]
        for copy in more:
            copy.start()
        return copies + more

    for half in range(2):

        @pl.when(y == half)
        def _(half=half):
            copies = []
            for n, (_, own_y) in enumerate(wheres):
                copies += begun(n, half if own_y else 1 - half)
            for copy in copies:
                copy.wait()


def swapped(x, axis, first):
    axes = (axis,) if isinstance(axis, str) else axis
    parts, size = lax.axis_size("dp"), lax.axis_size(axis)
    partner = list(range(parts * size))
    for i in partner:
        part, at = divmod(i, size)
        if first <= at < size - (size - first) % 2:
            partner[i] = part * size + (at - first ^ 1) + first
        elif parts % 2 == 0:
            partner[i] = (part ^ 1) * size + at
    return lax.ppermute(x, ("dp", *axes), list(enumerate(partner)))


def across(x, *moves):
    axes = tuple(axis for axis, _ in moves)
    flip = 0
    for axis, bit in moves:
        flip = flip * lax.axis_size(axis) + bit
    return lax.ppermute(x, axes, [(i, i ^ flip) for i in range(lax.axis_size(axes))])


def scattered(rows, cuts):
    halves = [
        jnp.concatenate([x[:, :, :n] if at == 0 else x[:, :, x.shape[2] - n :] for x, n in zip(rows, cut)], axis=2)
        for at, cut in enumerate(cuts)
    ]
    grad = lax.psum_scatter(jnp.stack(halves, axis=2), "dp", scatter_dimension=0, tiled=True)
    core = lax.axis_index("core")
    return tuple(lax.dynamic_index_in_dim(grad, at, 1, False) for at in (core, 1 - core))


def assembled(quarters, size, inner, mid):
    first, second = ([[None, None] for _ in range(27)] for _ in range(2))
    half = size // 2
    for core in range(2):
        for y in range(2):
            rows, row = quarters[core][y].astype(F32), 0
            for j in range(7) if y == 0 else range(7, 13):
                for m, k in enumerate((j, 9 + j) if j < 9 else (2 * j, 2 * j + 1)):
                    second[k][core] = rows[row : row + size, m * mid : (m + 1) * mid]
                row += size
            if y == 1:
                tail = rows[row : row + half]
                second[26][core] = jnp.concatenate([tail[:, :mid], tail[:, mid:]], axis=0)
                row += half
            for j in range(3) if y == 0 else range(3, 7):
                for m in range(4):
                    c, ab = (j // 2, 4 * (j % 2) + m) if j < 6 else (m, 8)
                    if c < 3:
                        first[3 * ab + c][core] = rows[row : row + half, m * inner : (m + 1) * inner]
                row += half
    return tuple(jnp.stack([jnp.concatenate(both, axis=0) for both in grad]) for grad in (first, second))


def per_device(volume, kernel_first, kernel_second, cotangent):
    _, inner, depth, height, width = volume.shape
    mid, out = kernel_first.shape[1], kernel_second.shape[1]
    cells = height * width
    parts = lax.axis_size("dp")
    k1, k2 = jnp.swapaxes(kernel_first, 1, 2), jnp.swapaxes(kernel_second, 1, 2)
    rows = depth * height

    one, two = swapped(volume[0], "dep", 0), swapped(volume[0], "dep", 1)
    (blank,) = call(blank_kernel, [shape((out, 2 * width), BF)], [], flops=3_000_000_000)
    cot_rows, back = call(
        spread_kernel,
        [
            shape((depth, out, cells), BF),
            shape((depth + 2, mid, cells + 2 * width), F32),
        ],
        [cotangent[0], k2, blank],
        [pltpu.VMEM(((out + 1) * rows, width), F32)],
        flops=1_100_000_000,
    )
    moved, w1, vol = call(
        arrange_kernel,
        [
            shape((depth, 3 * out, cells), BF),
            shape((3 * mid, 9 * inner), BF),
            shape((depth, inner, cells), BF),
        ],
        [cot_rows, k1, volume[0]],
        [pltpu.VMEM(((inner + 1) * rows, width), F32)],
        flops=500_000_000,
    )
    deep, one, two = call(
        rim_kernel,
        [shape((3 * depth, inner, cells), BF)] + [shape((3 * depth, inner, 2 * width), BF)] * 2,
        [vol, one, two],
        [pltpu.VMEM(((inner + 1) * rows, width), F32)],
    )
    one, two = swapped(one, HGT, 0), swapped(two, HGT, 1)
    size = mid // parts
    direct = parts == 2 and size % 16 == 0
    halves = lax.axis_size("y")
    cuts = ((7 * size, 3 * size // 2), (13 * size // 2, 2 * size))
    length_second, length_first = 7 * size, 4 * size
    rows_in, rows_out = height - 2, 4
    inner_hidden, inner_second, inner_first = call(
        inner_kernel,
        [
            shape((depth + 2, mid, rows_in * width), BF),
            shape((9 * out, 3 * mid), F32),
            shape((3 * mid, 9 * inner), F32),
        ],
        [deep, w1, moved, back],
        [pltpu.VMEM((3 * mid, (depth + 2) * rows_in * width), BF)],
        flops=1_500_000_000,
    )
    hidden, *first = call(
        functools.partial(outer_kernel, direct),
        [shape((depth + 2, mid, cells + 2 * width), BF)]
        + ([shape((parts, halves, length_first, width), F32)] * 2 if direct else [shape((7, mid, LANES), F32)]),
        [deep, two, one, w1, back, inner_hidden, inner_first],
        [
            pltpu.VMEM((3 * depth, inner, cells + 4 * width), BF),
            pltpu.VMEM((3 * mid, (depth + 2) * rows_out * width), BF),
        ],
        flops=1_000_000_000,
    )
    second = call(
        functools.partial(second_kernel, direct),
        [shape((parts, halves, length_second, width), kind) for kind in (F32, BF)]
        if direct
        else [shape((14, out, LANES), F32)],
        [hidden, moved, inner_second],
        flops=4_000_000_000,
    )
    if direct:
        moves = [(1, 0), (0, 1), (1, 1)]
        grads = [second, first]
    else:
        moves = [(0, 1)]
        blocks = second[0].reshape(14, parts, 2, size, LANES).transpose(1, 2, 0, 3, 4)
        tail = blocks[:, :, 13, :, :mid]
        tail = jnp.concatenate([tail[:, :, : size // 2], tail[:, :, size // 2 :]], axis=-1)
        rows_second = jnp.concatenate([blocks[:, :, :13].reshape(parts, 2, 13 * size, LANES), tail], axis=2)
        blocks = first[0].reshape(7, parts, 2, size // 2, LANES).transpose(1, 2, 0, 3, 4)
        rows_first = blocks.reshape(parts, 2, 7 * (size // 2), LANES)
        grads = [scattered([rows_second, rows_first], cuts)]
    block = (sum(cuts[0]), width)
    kept, *sends = call(
        functools.partial(plane_kernel, moves, cuts),
        [shape(block, F32)] + [shape(block, BF)] * len(moves),
        [x for keep, send in grads for x in (keep, across(send, ("core", 1)))],
    )
    gots = [across(send, ("dp", x), ("y", y)) for send, (x, y) in zip(sends, moves, strict=True)]
    (share,) = call(total_kernel, [shape(block, BF)], [kept, *gots])
    features, token = call(
        features_kernel,
        [shape(cotangent.shape[1:], BF), shape((8, width), F32)],
        [hidden, k2],
        [pltpu.VMEM(((out + 1) * rows, width), F32)],
        flops=900_000_000,
    )
    gots = [across(share, ("dep", bits)) for bits in (1, 2, 3)]
    share, for_y = call(depth_kernel, [shape(block, BF), shape((block[0] + 16, width), BF)], [share, *gots, token])
    other, far = across(share, ("core", 1)), across(for_y, ("y", 1))
    far_other = across(for_y, ("y", 1), ("core", 1))
    if size % 16 == 0:
        outs = [shape((9, 3, size, inner), F32), shape((3, 9, 2 * size, mid), F32)]

        def written(quarters, wheres, before=()):
            scratch = [
                pltpu.VMEM((2, 7, size, mid), F32),
                pltpu.VMEM((9, size, mid), F32),
                pltpu.VMEM((8, size // 2, inner), F32),
                pltpu.VMEM((4, size // 2, inner), F32),
                pltpu.VMEM((3, size // 2, inner), F32),
                pltpu.SemaphoreType.DMA((5,)),
            ]
            count = len(quarters)
            return call(
                functools.partial(write_kernel, count, wheres),
                outs,
                [*quarters, *before],
                scratch * count,
                far=range(count, count + len(before)),
                far_outs=(0, 1),
                aliases={count + n: n for n in range(len(before))},
            )

        grads = written([share, other], [(True, True), (False, True)])
        grads = written([far_other, far], [(False, False), (True, False)], grads)
        grad_first, grad_second = (grad.reshape(27, *grad.shape[2:]) for grad in grads)
    else:
        core, y = lax.axis_index("core"), lax.axis_index("y")
        stacked = jnp.stack([jnp.stack([share, far[: block[0]]]), jnp.stack([other, far_other[: block[0]]])])
        quarters = [
            [stacked[lax.bitwise_xor(core, c), lax.bitwise_xor(y, h)] for h in range(2)] for c in range(2)
        ]
        grad_first, grad_second = assembled(quarters, size, inner, mid)
    return features[None], grad_first, grad_second


def solution(mesh):
    dp, dep, hgt = (mesh.shape[axis] for axis in ("dp", "dep", "hgt"))
    split = jax.sharding.Mesh(mesh.devices.reshape(dp, dep, hgt // 2, 2), ("dp", "dep", *HGT))
    block = P("dp", None, "dep", HGT, None)
    return jax.shard_map(
        per_device,
        mesh=split,
        in_specs=(block, P(), P(), block),
        out_specs=(block, P(None, "dp", None), P(None, "dp", None)),
        check_vma=False,
    )
```

```python
import functools

import jax
import jax.numpy as jnp
from jax import lax
from jax.experimental import pallas as pl
from jax.experimental.pallas import tpu as pltpu
from jax.sharding import PartitionSpec as P

BF, F32 = jnp.bfloat16, jnp.float32
LANES = 128
HGT = ("y", "core")
VMEM_BYTES = 28 * 2**20


def call(body, outs, args, scratch=(), flops=0, far=(), far_outs=(), aliases=None):
    moved = sum(x.size * x.dtype.itemsize for x in (*outs, *args))
    return pl.pallas_call(
        body,
        out_shape=outs,
        in_specs=[pl.BlockSpec(memory_space=pl.ANY if n in far else pltpu.VMEM) for n in range(len(args))],
        out_specs=[pl.BlockSpec(memory_space=pl.ANY if n in far_outs else pltpu.VMEM) for n in range(len(outs))],
        scratch_shapes=list(scratch),
        input_output_aliases=aliases or {},
        compiler_params=pltpu.CompilerParams(vmem_limit_bytes=VMEM_BYTES),
        cost_estimate=pl.CostEstimate(flops=flops, bytes_accessed=moved, transcendentals=0),
    )(*args)


def shape(dims, dtype):
    return jax.ShapeDtypeStruct(dims, dtype)


def moved_along_width(x, c):
    if c == 0:
        return x
    pieces = []
    for start in range(0, x.shape[1], LANES):
        piece = x[:, start : start + LANES]
        lane = lax.broadcasted_iota(jnp.int32, piece.shape, 1)
        rolled = pltpu.roll(piece, c % LANES, 1)
        pieces.append(jnp.where(lane == (0 if c == 1 else LANES - 1), 0.0, rolled))
    return pieces[0] if len(pieces) == 1 else jnp.concatenate(pieces, axis=1)


def by_rows(ref, scratch, store):
    channels, depth, height, width = ref.shape
    rows = depth * height
    scratch[: channels * rows] = ref[...].astype(F32).reshape(channels * rows, width)
    for d in range(depth):
        for h in range(height):
            store(d, h, scratch[pl.ds(d * height + h, channels, stride=rows), :])


def odd(axis):
    return lax.rem(lax.axis_index(axis), 2) == 1


def blank_kernel(out_ref):
    out_ref[...] = jnp.zeros(out_ref.shape, BF)


def spread_kernel(cot_ref, k2_ref, blank_ref, cot_rows_ref, back_ref, scratch):
    out, depth, height, _ = cot_ref.shape
    rows = [[None] * height for _ in range(depth)]

    def store(d, h, row):
        rows[d][h] = row.astype(BF)
        cot_rows_ref[d, :, h * LANES : (h + 1) * LANES] = rows[d][h]

    by_rows(cot_ref, scratch, store)
    mid = k2_ref.shape[1]
    none = blank_ref[...]
    padded = [jnp.concatenate([none, *rows[d], none], axis=1) for d in range(depth)]
    for e in range(depth + 2):
        reached = [(d, e - 1 - d) for d in range(depth) if abs(e - 1 - d) <= 1]
        w = jnp.concatenate(
            [
                k2_ref[9 * (a + 1) + 3 * b : 9 * (a + 1) + 3 * b + 3].reshape(3 * mid, out)
                for _, a in reached
                for b in range(3)
            ],
            axis=1,
        )
        for j in range(0, height + 2, 2):
            rhs = jnp.concatenate(
                [padded[d][:, (j + 2 - b) * LANES : (j + 4 - b) * LANES] for d, _ in reached for b in range(3)], axis=0
            )
            y = jnp.dot(w, rhs, preferred_element_type=F32)
            back = sum(moved_along_width(y[n * mid : (n + 1) * mid], n - 1) for n in range(3))
            back_ref[e, :, j * LANES : (j + 2) * LANES] = back


def as_matrix(ref, c):
    stacked = jnp.concatenate([ref[3 * ab + c] for ab in range(9)], axis=0)
    return stacked.astype(F32).T.astype(BF)


def arrange_kernel(cot_rows_ref, k1_ref, vol_ref, moved_ref, w1_ref, own_ref, scratch):
    def store(d, h, row):
        own_ref[d, :, h * LANES : (h + 1) * LANES] = row.astype(BF)

    by_rows(vol_ref, scratch, store)
    depth, out, cells = cot_rows_ref.shape
    for d in range(depth):
        for h in range(0, cells, LANES):
            row = cot_rows_ref[d, :, h : h + LANES]
            for n, c in enumerate((-1, 0, 1)):
                value = row if c == 0 else moved_along_width(row.astype(F32), c).astype(BF)
                moved_ref[d, n * out : (n + 1) * out, h : h + LANES] = value
    mid = k1_ref.shape[2]
    for c in range(3):
        w1_ref[c * mid : (c + 1) * mid, :] = as_matrix(k1_ref, c)


def sides(axis, one, two):
    me, size = lax.axis_index(axis), lax.axis_size(axis)
    is_odd = odd(axis)
    none = jnp.zeros_like(one)
    before = jnp.where(me == 0, none, jnp.where(is_odd, one, two))
    after = jnp.where(me == size - 1, none, jnp.where(is_odd, two, one))
    return before, after


def rim_kernel(own_ref, one_ref, two_ref, deep_ref, send_one_ref, send_two_ref, scratch):
    depth = own_ref.shape[0]
    deep_ref[depth : 2 * depth] = own_ref[...]
    for at, part in zip((0, 2 * depth), sides("dep", one_ref[...], two_ref[...]), strict=True):

        def store(d, h, row, at=at):
            deep_ref[at + d, :, h * LANES : (h + 1) * LANES] = row.astype(BF)

        by_rows(part, scratch, store)
    n, cells = send_one_ref.shape[2], deep_ref.shape[2]
    first, last = deep_ref[:, :, :n], deep_ref[:, :, cells - n :]
    is_odd = odd(HGT)
    send_one_ref[...] = jnp.where(is_odd, first, last)
    send_two_ref[...] = jnp.where(is_odd, last, first)


def widened(deep_ref, one_ref, two_ref):
    left, right = sides(HGT, one_ref[...], two_ref[...])
    return [jnp.concatenate([left[d], deep_ref[d], right[d]], axis=1) for d in range(deep_ref.shape[0])]


def pack(direct, refs, rows_of, blocks):
    if not direct:
        for j, block in enumerate(blocks):
            refs[0][j] = block
        return
    keep_ref, send_ref = refs
    parts, halves, length, _ = keep_ref.shape
    core = lax.axis_index("core") == 1

    def filled(rows):
        rest = length - sum(x.shape[0] for x in rows)
        return jnp.concatenate([*rows, jnp.zeros((rest, LANES), F32)] if rest else rows, axis=0)

    for part in range(parts):
        for half in range(halves):
            one, two = (filled(rows_of(part, c)[half]) for c in range(2))
            keep_ref[part, half] = jnp.where(core, two, one)
            send_ref[part, half] = jnp.where(core, one, two).astype(send_ref.dtype)


def folded(tail):
    half = tail.shape[0] // 2
    return jnp.concatenate([tail[:half], tail[half:]], axis=1)


def activated(w1, rhs, d, depth, heights):
    mid = w1.shape[0] // 3
    y = jnp.dot(w1, rhs, preferred_element_type=F32)
    pre = sum(moved_along_width(y[n * mid : (n + 1) * mid], 1 - n) for n in range(3))
    s = 1.0 / (1.0 + jnp.exp(-pre))
    dep, deps = lax.axis_index("dep"), lax.axis_size("dep")
    hgt, hgts = lax.axis_index(HGT), lax.axis_size(HGT)
    results = []
    for n, side in enumerate(heights):
        p, q = (x[:, n * LANES : (n + 1) * LANES] for x in (pre, s))
        value, slope = (p * q).astype(BF), q * (1.0 + p * (1.0 - q))
        outside = []
        if d == 0:
            outside.append(dep == 0)
        if d == depth - 1:
            outside.append(dep == deps - 1)
        if side < 0:
            outside.append(hgt == 0)
        if side > 0:
            outside.append(hgt == hgts - 1)
        for far in outside:
            value = jnp.where(far, jnp.zeros_like(value), value)
            slope = jnp.where(far, jnp.zeros_like(slope), slope)
        results.append((value, slope))
    return results


def neighbours(ref, d, starts, count):
    return jnp.concatenate(
        [
            jnp.concatenate(
                [ref[d + a, :, (start + b) * LANES : (start + b + count) * LANES] for start in starts], axis=1
            )
            for a in range(3)
            for b in range(3)
        ],
        axis=0,
    )


def products(left, right):
    return lax.dot_general(left, right, (((1,), (1,)), ((), ())), preferred_element_type=F32)


def shares(delta, n_channels, ref, at):
    for n in range(3):
        ref[n * n_channels : (n + 1) * n_channels, at : at + LANES] = moved_along_width(delta, n - 1).astype(BF)


def inner_kernel(deep_ref, w1_ref, moved_ref, back_ref, hidden_ref, second_ref, first_ref, delta_ref):
    w1 = w1_ref[...]
    depth, mid, cells = hidden_ref.shape
    height = cells // LANES
    for d in range(depth):
        for h in range(0, height, 2):
            results = activated(w1, neighbours(deep_ref, d, [h], 2), d, depth, (0, 0))
            for n, (value, slope) in enumerate(results):
                at = (h + n) * LANES
                hidden_ref[d, :, at : at + LANES] = value
                back = back_ref[d, :, at + 2 * LANES : at + 3 * LANES]
                shares(back * slope, mid, delta_ref, d * cells + at)
    own = depth - 2
    left = jnp.concatenate(
        [
            jnp.concatenate([moved_ref[d, :, (2 - b) * LANES : (2 - b) * LANES + cells] for d in range(own)], axis=1)
            for b in range(3)
        ],
        axis=0,
    )
    right = jnp.concatenate(
        [jnp.concatenate([hidden_ref[d + a] for a in range(3)], axis=0) for d in range(own)], axis=1
    )
    second_ref[...] = products(left, right)
    right = jnp.concatenate([neighbours(deep_ref, d, [0], height) for d in range(depth)], axis=1)
    first_ref[...] = products(delta_ref[...], right)


def outer_kernel(
    direct, deep_ref, two_ref, one_ref, w1_ref, back_ref, inner_ref, first_ref, hidden_ref, *grad_refs_and_scratch,
):
    *grad_refs, rows_ref, delta_ref = grad_refs_and_scratch
    for d, row in enumerate(widened(deep_ref, one_ref, two_ref)):
        rows_ref[d] = row
    w1 = w1_ref[...]
    depth, mid, cells = hidden_ref.shape
    last = cells // LANES - 2
    for d in range(depth):
        hidden_ref[d, :, 2 * LANES : last * LANES] = inner_ref[d]
        for h, sides_of in ((0, (-1, 0)), (last, (0, 1))):
            results = activated(w1, neighbours(rows_ref, d, [h], 2), d, depth, sides_of)
            for n, (value, slope) in enumerate(results):
                at = (h + n) * LANES
                hidden_ref[d, :, at : at + LANES] = value
                delta = back_ref[d, :, at : at + LANES] * slope
                shares(delta, mid, delta_ref, (4 * d + (2 if h else 0) + n) * LANES)
    right = jnp.concatenate([neighbours(rows_ref, d, [0, last], 2) for d in range(depth)], axis=1)
    total = first_ref[...] + products(delta_ref[...], right)
    inner = rows_ref.shape[1]
    blocks, tails = [], []
    for n in range(3):
        part = total[n * mid : (n + 1) * mid]
        blocks += [part[:, m * LANES : (m + 1) * LANES] for m in range(2)]
        tails.append(part[:, 2 * LANES :])
    tails.append(jnp.zeros((mid, LANES - 3 * inner), F32))
    blocks.append(jnp.concatenate(tails, axis=1))
    size = mid // lax.axis_size("dp")
    half = size // 2

    def rows_of(part, core):
        rows = [block[part * size + core * half : part * size + (core + 1) * half] for block in blocks]
        return rows[:3], rows[3:]

    pack(direct, grad_refs, rows_of, blocks)


def second_kernel(direct, hidden_ref, moved_ref, second_ref, *grad_refs):
    depth, mid, cells = hidden_ref.shape
    height = cells // LANES
    own = depth - 2
    out = moved_ref.shape[1] // 3
    heads, tails = [], []
    for b in range(3):
        far = [h for h in range(height - 2) if not 2 <= h + b <= height - 3]
        left = jnp.concatenate(
            [moved_ref[d, :, h * LANES : (h + 1) * LANES] for d in range(own) for h in far], axis=1
        )
        right = jnp.concatenate(
            [
                jnp.concatenate([hidden_ref[d + a, :, (h + b) * LANES : (h + b + 1) * LANES] for a in range(3)], axis=0)
                for d in range(own)
                for h in far
            ],
            axis=1,
        )
        total = second_ref[3 * b * out : 3 * (b + 1) * out, :] + products(left, right)
        for c in range(3):
            part = total[c * out : (c + 1) * out]
            heads.append(part[:, :LANES])
            tails.append(part[:, LANES:])
    blocks = heads + [jnp.concatenate(tails[n : n + 2], axis=1) for n in range(0, 8, 2)]
    size = mid // lax.axis_size("dp")

    def rows_of(part, core):
        at = slice((2 * part + core) * size, (2 * part + core + 1) * size)
        rows = [block[at] for block in blocks] + [folded(tails[8][at])]
        return rows[:7], rows[7:]

    pack(direct, grad_refs, rows_of, [*blocks, jnp.concatenate([tails[8], jnp.zeros_like(tails[8])], axis=1)])


def features_kernel(hidden_ref, k2_ref, out_ref, token_ref, scratch):
    out, depth, height, _ = out_ref.shape
    w2 = jnp.concatenate([as_matrix(k2_ref, c) for c in range(3)], axis=0)
    for d in range(depth):
        for h in range(0, height, 2):
            rhs = jnp.concatenate(
                [
                    hidden_ref[d + a, :, (h + b) * LANES : (h + b + 2) * LANES]
                    for a in range(3)
                    for b in range(3)
                ],
                axis=0,
            )
            y = jnp.dot(w2, rhs, preferred_element_type=F32)
            total = sum(moved_along_width(y[n * out : (n + 1) * out], 1 - n) for n in range(3))
            for r in range(2):
                row = total[:, r * LANES : (r + 1) * LANES]
                scratch[pl.ds(d * height + h + r, out, stride=depth * height), :] = row
    out_ref[...] = scratch[: out * depth * height].reshape(out_ref.shape).astype(BF)
    token_ref[...] = scratch[:8]


def plane_kernel(moves, cuts, *refs):
    sums, (kept_ref, *send_refs) = refs[: -1 - len(moves)], refs[-1 - len(moves) :]
    part = lax.rem(lax.axis_index("dp"), sums[0].shape[0])
    half = lax.axis_index("y")

    def total(x, y):
        at = 1 - part if x else part, 1 - half if y else half
        values = [keep[at] + got[at].astype(F32) for keep, got in zip(sums[::2], sums[1::2], strict=True)]
        if len(values) == 1:
            return values[0]
        one, two = (jnp.concatenate([v[:n] for v, n in zip(values, cut, strict=True)], axis=0) for cut in cuts)
        return jnp.where(at[1] == 0, one, two)

    kept_ref[...] = total(0, 0)
    core = lax.axis_index("core") == 1
    for (one, two), send_ref in zip(moves, send_refs, strict=True):
        send_ref[...] = jnp.where(core, total(*two), total(*one)).astype(BF)


def total_kernel(kept_ref, *refs):
    *got_refs, out_ref = refs
    value = kept_ref[...]
    for ref in got_refs:
        value = value + ref[...].astype(F32)
    out_ref[...] = value.astype(BF)


def depth_kernel(a_ref, b_ref, c_ref, d_ref, _, out_ref, padded_ref):
    one = a_ref[...].astype(F32) + b_ref[...].astype(F32)
    two = c_ref[...].astype(F32) + d_ref[...].astype(F32)
    out_ref[...] = (one + two).astype(BF)
    rest = jnp.zeros((padded_ref.shape[0] - out_ref.shape[0], LANES), F32)
    padded_ref[...] = jnp.concatenate([one + two, rest], axis=0).astype(BF)


def write_kernel(count, wheres, *refs):
    n_scratch = 6
    in_refs = refs[:count]
    out_refs, scratch = refs[: -n_scratch * count], refs[-n_scratch * count :]
    first_ref, second_ref = out_refs[-2:]
    core, y = lax.axis_index("core"), lax.axis_index("y")

    def begun(n, half):
        wide, last, low, high, tail, sems = scratch[n_scratch * n : n_scratch * (n + 1)]
        own_core, _ = wheres[n]
        at = core if own_core else 1 - core
        rows = in_refs[n][...].astype(F32)
        _, _, size, mid = wide.shape
        _, small, inner = low.shape
        here = pl.ds(pl.multiple_of(at * size, size), size)
        count = 2 if half else 7
        for j in range(count):
            value = rows[j * size : (j + 1) * size]
            for m in range(2):
                wide[m, j] = value[:, m * mid : (m + 1) * mid]
        pairs = [(wide.at[:, :count], second_ref.at[0:2, 7 * half : 7 * half + count, here, :])]
        row = count * size
        if half:
            for j in range(4):
                value = rows[row : row + size]
                row += size
                for m in range(2):
                    last[2 * j + m] = value[:, m * mid : (m + 1) * mid]
            value = rows[row : row + size // 2]
            row += size // 2
            last[8] = jnp.concatenate([value[:, :mid], value[:, mid:]], axis=0)
            pairs.append((last, second_ref.at[2, :, here, :]))
        copies = [pltpu.make_async_copy(src, dst, sems.at[i]) for i, (src, dst) in enumerate(pairs)]
        for copy in copies:
            copy.start()
        here = pl.ds(pl.multiple_of(at * small, small), small)
        places = [(high, 0, 4), (low, 0, 4), (low, 4, 4), (tail, 0, 3)] if half else [(low, 0, 4), (low, 4, 4), (high, 0, 4)]
        for ref, start, number in places:
            value = rows[row : row + small]
            row += small
            for m in range(number):
                ref[start + m] = value[:, m * inner : (m + 1) * inner]
        if half:
            pairs = [
                (high, first_ref.at[4:8, 1, here, :]),
                (low, first_ref.at[0:8, 2, here, :]),
                (tail, first_ref.at[8, :, here, :]),
            ]
        else:
            pairs = [(low, first_ref.at[0:8, 0, here, :]), (high, first_ref.at[0:4, 1, here, :])]
        more = [pltpu.make_async_copy(src, dst, sems.at[2 + i]) for i, (src, dst) in enumerate(pairs)]
        for copy in more:
            copy.start()
        return copies + more

    for half in range(2):

        @pl.when(y == half)
        def _(half=half):
            copies = []
            for n, (_, own_y) in enumerate(wheres):
                copies += begun(n, half if own_y else 1 - half)
            for copy in copies:
                copy.wait()


def swapped(x, axis, first):
    axes = (axis,) if isinstance(axis, str) else axis
    parts, size = lax.axis_size("dp"), lax.axis_size(axis)
    partner = list(range(parts * size))
    for i in partner:
        part, at = divmod(i, size)
        if first <= at < size - (size - first) % 2:
            partner[i] = part * size + (at - first ^ 1) + first
        elif parts % 2 == 0:
            partner[i] = (part ^ 1) * size + at
    return lax.ppermute(x, ("dp", *axes), list(enumerate(partner)))


def across_plane(x, move):
    parts, halves = lax.axis_size("dp"), lax.axis_size("y")
    partner = [
        ((part ^ move[core][0]) * halves + (y ^ move[core][1])) * 2 + core
        for part in range(parts)
        for y in range(halves)
        for core in range(2)
    ]
    return lax.ppermute(x, ("dp", "y", "core"), list(enumerate(partner)))


def across(x, *moves):
    axes = tuple(axis for axis, _ in moves)
    flip = 0
    for axis, bit in moves:
        flip = flip * lax.axis_size(axis) + bit
    return lax.ppermute(x, axes, [(i, i ^ flip) for i in range(lax.axis_size(axes))])


def scattered(rows, cuts):
    halves = [
        jnp.concatenate([x[:, :, :n] if at == 0 else x[:, :, x.shape[2] - n :] for x, n in zip(rows, cut)], axis=2)
        for at, cut in enumerate(cuts)
    ]
    grad = lax.psum_scatter(jnp.stack(halves, axis=2), "dp", scatter_dimension=0, tiled=True)
    core = lax.axis_index("core")
    return tuple(lax.dynamic_index_in_dim(grad, at, 1, False) for at in (core, 1 - core))


def assembled(quarters, size, inner, mid):
    first, second = ([[None, None] for _ in range(27)] for _ in range(2))
    half = size // 2
    for core in range(2):
        for y in range(2):
            rows, row = quarters[core][y].astype(F32), 0
            for j in range(7) if y == 0 else range(7, 13):
                for m, k in enumerate((j, 9 + j) if j < 9 else (2 * j, 2 * j + 1)):
                    second[k][core] = rows[row : row + size, m * mid : (m + 1) * mid]
                row += size
            if y == 1:
                tail = rows[row : row + half]
                second[26][core] = jnp.concatenate([tail[:, :mid], tail[:, mid:]], axis=0)
                row += half
            for j in range(3) if y == 0 else range(3, 7):
                for m in range(4):
                    c, ab = (j // 2, 4 * (j % 2) + m) if j < 6 else (m, 8)
                    if c < 3:
                        first[3 * ab + c][core] = rows[row : row + half, m * inner : (m + 1) * inner]
                row += half
    return tuple(jnp.stack([jnp.concatenate(both, axis=0) for both in grad]) for grad in (first, second))


def per_device(volume, kernel_first, kernel_second, cotangent):
    _, inner, depth, height, width = volume.shape
    mid, out = kernel_first.shape[1], kernel_second.shape[1]
    cells = height * width
    parts = lax.axis_size("dp")
    k1, k2 = jnp.swapaxes(kernel_first, 1, 2), jnp.swapaxes(kernel_second, 1, 2)
    rows = depth * height

    one, two = swapped(volume[0], "dep", 0), swapped(volume[0], "dep", 1)
    (blank,) = call(blank_kernel, [shape((out, 2 * width), BF)], [], flops=3_000_000_000)
    cot_rows, back = call(
        spread_kernel,
        [
            shape((depth, out, cells), BF),
            shape((depth + 2, mid, cells + 2 * width), F32),
        ],
        [cotangent[0], k2, blank],
        [pltpu.VMEM(((out + 1) * rows, width), F32)],
        flops=1_100_000_000,
    )
    moved, w1, vol = call(
        arrange_kernel,
        [
            shape((depth, 3 * out, cells), BF),
            shape((3 * mid, 9 * inner), BF),
            shape((depth, inner, cells), BF),
        ],
        [cot_rows, k1, volume[0]],
        [pltpu.VMEM(((inner + 1) * rows, width), F32)],
        flops=500_000_000,
    )
    deep, one, two = call(
        rim_kernel,
        [shape((3 * depth, inner, cells), BF)] + [shape((3 * depth, inner, 2 * width), BF)] * 2,
        [vol, one, two],
        [pltpu.VMEM(((inner + 1) * rows, width), F32)],
    )
    one, two = swapped(one, HGT, 0), swapped(two, HGT, 1)
    size = mid // parts
    direct = parts == 2 and size % 16 == 0
    halves = lax.axis_size("y")
    cuts = ((7 * size, 3 * size // 2), (13 * size // 2, 2 * size))
    length_second, length_first = 7 * size, 2 * size
    rows_in, rows_out = height - 2, 4
    inner_hidden, inner_second, inner_first = call(
        inner_kernel,
        [
            shape((depth + 2, mid, rows_in * width), BF),
            shape((9 * out, 3 * mid), F32),
            shape((3 * mid, 9 * inner), F32),
        ],
        [deep, w1, moved, back],
        [pltpu.VMEM((3 * mid, (depth + 2) * rows_in * width), BF)],
        flops=1_500_000_000,
    )
    hidden, *first = call(
        functools.partial(outer_kernel, direct),
        [shape((depth + 2, mid, cells + 2 * width), BF)]
        + ([shape((parts, halves, length_first, width), F32)] * 2 if direct else [shape((7, mid, LANES), F32)]),
        [deep, two, one, w1, back, inner_hidden, inner_first],
        [
            pltpu.VMEM((3 * depth, inner, cells + 4 * width), BF),
            pltpu.VMEM((3 * mid, (depth + 2) * rows_out * width), BF),
        ],
        flops=1_000_000_000,
    )
    second = call(
        functools.partial(second_kernel, direct),
        [shape((parts, halves, length_second, width), kind) for kind in (F32, BF)]
        if direct
        else [shape((14, out, LANES), F32)],
        [hidden, moved, inner_second],
        flops=4_000_000_000,
    )
    if direct:
        moves = [((0, 1), (1, 0)), ((1, 0), (0, 1)), ((1, 1), (1, 1))]
        grads = [second, first]
    else:
        moves = [((0, 1), (0, 1))]
        blocks = second[0].reshape(14, parts, 2, size, LANES).transpose(1, 2, 0, 3, 4)
        tail = blocks[:, :, 13, :, :mid]
        tail = jnp.concatenate([tail[:, :, : size // 2], tail[:, :, size // 2 :]], axis=-1)
        rows_second = jnp.concatenate([blocks[:, :, :13].reshape(parts, 2, 13 * size, LANES), tail], axis=2)
        blocks = first[0].reshape(7, parts, 2, size // 2, LANES).transpose(1, 2, 0, 3, 4)
        rows_first = blocks.reshape(parts, 2, 7 * (size // 2), LANES)
        grads = [scattered([rows_second, rows_first], cuts)]
    block = (sum(cuts[0]), width)
    kept, *sends = call(
        functools.partial(plane_kernel, moves, cuts),
        [shape(block, F32)] + [shape(block, BF)] * len(moves),
        [x for keep, send in grads for x in (keep, across(send, ("core", 1)))],
    )
    gots = [across_plane(send, move) for send, move in zip(sends, moves, strict=True)]
    (share,) = call(total_kernel, [shape(block, BF)], [kept, *gots])
    features, token = call(
        features_kernel,
        [shape(cotangent.shape[1:], BF), shape((8, width), F32)],
        [hidden, k2],
        [pltpu.VMEM(((out + 1) * rows, width), F32)],
        flops=900_000_000,
    )
    gots = [across(share, ("dep", bits)) for bits in (1, 2, 3)]
    share, for_y = call(depth_kernel, [shape(block, BF), shape((block[0] + 16, width), BF)], [share, *gots, token])
    other, far = across(share, ("core", 1)), across(for_y, ("y", 1))
    far_other = across(for_y, ("y", 1), ("core", 1))
    if size % 16 == 0:
        outs = [shape((9, 3, size, inner), F32), shape((3, 9, 2 * size, mid), F32)]

        def written(quarters, wheres, before=()):
            scratch = [
                pltpu.VMEM((2, 7, size, mid), F32),
                pltpu.VMEM((9, size, mid), F32),
                pltpu.VMEM((8, size // 2, inner), F32),
                pltpu.VMEM((4, size // 2, inner), F32),
                pltpu.VMEM((3, size // 2, inner), F32),
                pltpu.SemaphoreType.DMA((5,)),
            ]
            count = len(quarters)
            return call(
                functools.partial(write_kernel, count, wheres),
                outs,
                [*quarters, *before],
                scratch * count,
                far=range(count, count + len(before)),
                far_outs=(0, 1),
                aliases={count + n: n for n in range(len(before))},
            )

        grads = written([share, other], [(True, True), (False, True)])
        grads = written([far_other, far], [(False, False), (True, False)], grads)
        grad_first, grad_second = (grad.reshape(27, *grad.shape[2:]) for grad in grads)
    else:
        core, y = lax.axis_index("core"), lax.axis_index("y")
        stacked = jnp.stack([jnp.stack([share, far[: block[0]]]), jnp.stack([other, far_other[: block[0]]])])
        quarters = [
            [stacked[lax.bitwise_xor(core, c), lax.bitwise_xor(y, h)] for h in range(2)] for c in range(2)
        ]
        grad_first, grad_second = assembled(quarters, size, inner, mid)
    return features[None], grad_first, grad_second


def solution(mesh):
    dp, dep, hgt = (mesh.shape[axis] for axis in ("dp", "dep", "hgt"))
    split = jax.sharding.Mesh(mesh.devices.reshape(dp, dep, hgt // 2, 2), ("dp", "dep", *HGT))
    block = P("dp", None, "dep", HGT, None)
    return jax.shard_map(
        per_device,
        mesh=split,
        in_specs=(block, P(), P(), block),
        out_specs=(block, P(None, "dp", None), P(None, "dp", None)),
        check_vma=False,
    )
```

```python
import functools

import jax
import jax.numpy as jnp
from jax import lax
from jax.experimental import pallas as pl
from jax.experimental.pallas import tpu as pltpu
from jax.sharding import PartitionSpec as P

BF, F32 = jnp.bfloat16, jnp.float32
LANES = 128
HGT = ("y", "core")
VMEM_BYTES = 28 * 2**20


def call(body, outs, args, scratch=(), flops=0, far=(), far_outs=(), aliases=None):
    moved = sum(x.size * x.dtype.itemsize for x in (*outs, *args))
    return pl.pallas_call(
        body,
        out_shape=outs,
        in_specs=[pl.BlockSpec(memory_space=pl.ANY if n in far else pltpu.VMEM) for n in range(len(args))],
        out_specs=[pl.BlockSpec(memory_space=pl.ANY if n in far_outs else pltpu.VMEM) for n in range(len(outs))],
        scratch_shapes=list(scratch),
        input_output_aliases=aliases or {},
        compiler_params=pltpu.CompilerParams(vmem_limit_bytes=VMEM_BYTES),
        cost_estimate=pl.CostEstimate(flops=flops, bytes_accessed=moved, transcendentals=0),
    )(*args)


def shape(dims, dtype):
    return jax.ShapeDtypeStruct(dims, dtype)


def moved_along_width(x, c):
    if c == 0:
        return x
    pieces = []
    for start in range(0, x.shape[1], LANES):
        piece = x[:, start : start + LANES]
        lane = lax.broadcasted_iota(jnp.int32, piece.shape, 1)
        rolled = pltpu.roll(piece, c % LANES, 1)
        pieces.append(jnp.where(lane == (0 if c == 1 else LANES - 1), 0.0, rolled))
    return pieces[0] if len(pieces) == 1 else jnp.concatenate(pieces, axis=1)


def by_rows(ref, scratch, store):
    channels, depth, height, width = ref.shape
    rows = depth * height
    scratch[: channels * rows] = ref[...].astype(F32).reshape(channels * rows, width)
    for d in range(depth):
        for h in range(height):
            store(d, h, scratch[pl.ds(d * height + h, channels, stride=rows), :])


def odd(axis):
    return lax.rem(lax.axis_index(axis), 2) == 1


def blank_kernel(out_ref):
    out_ref[...] = jnp.zeros(out_ref.shape, BF)


def spread_kernel(cot_ref, k2_ref, blank_ref, cot_rows_ref, back_ref, scratch):
    out, depth, height, _ = cot_ref.shape
    rows = [[None] * height for _ in range(depth)]

    def store(d, h, row):
        rows[d][h] = row.astype(BF)
        cot_rows_ref[d, :, h * LANES : (h + 1) * LANES] = rows[d][h]

    by_rows(cot_ref, scratch, store)
    mid = k2_ref.shape[1]
    none = blank_ref[...]
    padded = [jnp.concatenate([none, *rows[d], none], axis=1) for d in range(depth)]
    for e in range(depth + 2):
        reached = [(d, e - 1 - d) for d in range(depth) if abs(e - 1 - d) <= 1]
        w = jnp.concatenate(
            [
                k2_ref[9 * (a + 1) + 3 * b : 9 * (a + 1) + 3 * b + 3].reshape(3 * mid, out)
                for _, a in reached
                for b in range(3)
            ],
            axis=1,
        )
        for j in range(0, height + 2, 2):
            rhs = jnp.concatenate(
                [padded[d][:, (j + 2 - b) * LANES : (j + 4 - b) * LANES] for d, _ in reached for b in range(3)], axis=0
            )
            y = jnp.dot(w, rhs, preferred_element_type=F32)
            back = sum(moved_along_width(y[n * mid : (n + 1) * mid], n - 1) for n in range(3))
            back_ref[e, :, j * LANES : (j + 2) * LANES] = back


def as_matrix(ref, c):
    stacked = jnp.concatenate([ref[3 * ab + c] for ab in range(9)], axis=0)
    return stacked.astype(F32).T.astype(BF)


def arrange_kernel(cot_rows_ref, k1_ref, vol_ref, moved_ref, w1_ref, own_ref, scratch):
    def store(d, h, row):
        own_ref[d, :, h * LANES : (h + 1) * LANES] = row.astype(BF)

    by_rows(vol_ref, scratch, store)
    depth, out, cells = cot_rows_ref.shape
    for d in range(depth):
        for h in range(0, cells, LANES):
            row = cot_rows_ref[d, :, h : h + LANES]
            for n, c in enumerate((-1, 0, 1)):
                value = row if c == 0 else moved_along_width(row.astype(F32), c).astype(BF)
                moved_ref[d, n * out : (n + 1) * out, h : h + LANES] = value
    mid = k1_ref.shape[2]
    for c in range(3):
        w1_ref[c * mid : (c + 1) * mid, :] = as_matrix(k1_ref, c)


def sides(axis, one, two):
    me, size = lax.axis_index(axis), lax.axis_size(axis)
    is_odd = odd(axis)
    none = jnp.zeros_like(one)
    before = jnp.where(me == 0, none, jnp.where(is_odd, one, two))
    after = jnp.where(me == size - 1, none, jnp.where(is_odd, two, one))
    return before, after


def rim_kernel(own_ref, one_ref, two_ref, deep_ref, send_one_ref, send_two_ref, scratch):
    depth = own_ref.shape[0]
    deep_ref[depth : 2 * depth] = own_ref[...]
    for at, part in zip((0, 2 * depth), sides("dep", one_ref[...], two_ref[...]), strict=True):

        def store(d, h, row, at=at):
            deep_ref[at + d, :, h * LANES : (h + 1) * LANES] = row.astype(BF)

        by_rows(part, scratch, store)
    n, cells = send_one_ref.shape[2], deep_ref.shape[2]
    first, last = deep_ref[:, :, :n], deep_ref[:, :, cells - n :]
    is_odd = odd(HGT)
    send_one_ref[...] = jnp.where(is_odd, first, last)
    send_two_ref[...] = jnp.where(is_odd, last, first)


def widened(deep_ref, one_ref, two_ref):
    left, right = sides(HGT, one_ref[...], two_ref[...])
    return [jnp.concatenate([left[d], deep_ref[d], right[d]], axis=1) for d in range(deep_ref.shape[0])]


def pack(direct, refs, rows_of, blocks):
    if not direct:
        for j, block in enumerate(blocks):
            refs[0][j] = block
        return
    keep_ref, send_ref = refs
    parts, halves, length, _ = keep_ref.shape
    core = lax.axis_index("core") == 1

    def filled(rows):
        rest = length - sum(x.shape[0] for x in rows)
        return jnp.concatenate([*rows, jnp.zeros((rest, LANES), F32)] if rest else rows, axis=0)

    for part in range(parts):
        for half in range(halves):
            one, two = (filled(rows_of(part, c)[half]) for c in range(2))
            keep_ref[part, half] = jnp.where(core, two, one)
            send_ref[part, half] = jnp.where(core, one, two).astype(send_ref.dtype)


def folded(tail):
    half = tail.shape[0] // 2
    return jnp.concatenate([tail[:half], tail[half:]], axis=1)


def activated(w1, rhs, d, depth, heights):
    mid = w1.shape[0] // 3
    y = jnp.dot(w1, rhs, preferred_element_type=F32)
    pre = sum(moved_along_width(y[n * mid : (n + 1) * mid], 1 - n) for n in range(3))
    s = 1.0 / (1.0 + jnp.exp(-pre))
    dep, deps = lax.axis_index("dep"), lax.axis_size("dep")
    hgt, hgts = lax.axis_index(HGT), lax.axis_size(HGT)
    results = []
    for n, side in enumerate(heights):
        p, q = (x[:, n * LANES : (n + 1) * LANES] for x in (pre, s))
        value, slope = (p * q).astype(BF), q * (1.0 + p * (1.0 - q))
        outside = []
        if d == 0:
            outside.append(dep == 0)
        if d == depth - 1:
            outside.append(dep == deps - 1)
        if side < 0:
            outside.append(hgt == 0)
        if side > 0:
            outside.append(hgt == hgts - 1)
        for far in outside:
            value = jnp.where(far, jnp.zeros_like(value), value)
            slope = jnp.where(far, jnp.zeros_like(slope), slope)
        results.append((value, slope))
    return results


def neighbours(ref, d, starts, count):
    return jnp.concatenate(
        [
            jnp.concatenate(
                [ref[d + a, :, (start + b) * LANES : (start + b + count) * LANES] for start in starts], axis=1
            )
            for a in range(3)
            for b in range(3)
        ],
        axis=0,
    )


def products(left, right):
    return lax.dot_general(left, right, (((1,), (1,)), ((), ())), preferred_element_type=F32)


def shares(delta, n_channels, ref, at):
    for n in range(3):
        ref[n * n_channels : (n + 1) * n_channels, at : at + LANES] = moved_along_width(delta, n - 1).astype(BF)


def inner_kernel(deep_ref, w1_ref, moved_ref, back_ref, hidden_ref, second_ref, first_ref, delta_ref):
    w1 = w1_ref[...]
    depth, mid, cells = hidden_ref.shape
    height = cells // LANES
    for d in range(depth):
        for h in range(0, height, 2):
            results = activated(w1, neighbours(deep_ref, d, [h], 2), d, depth, (0, 0))
            for n, (value, slope) in enumerate(results):
                at = (h + n) * LANES
                hidden_ref[d, :, at : at + LANES] = value
                back = back_ref[d, :, at + 2 * LANES : at + 3 * LANES]
                shares(back * slope, mid, delta_ref, d * cells + at)
    own = depth - 2
    left = jnp.concatenate(
        [
            jnp.concatenate([moved_ref[d, :, (2 - b) * LANES : (2 - b) * LANES + cells] for d in range(own)], axis=1)
            for b in range(3)
        ],
        axis=0,
    )
    right = jnp.concatenate(
        [jnp.concatenate([hidden_ref[d + a] for a in range(3)], axis=0) for d in range(own)], axis=1
    )
    second_ref[...] = products(left, right)
    right = jnp.concatenate([neighbours(deep_ref, d, [0], height) for d in range(depth)], axis=1)
    first_ref[...] = products(delta_ref[...], right)


def outer_kernel(
    direct, deep_ref, two_ref, one_ref, w1_ref, back_ref, inner_ref, first_ref, hidden_ref, *grad_refs_and_scratch,
):
    *grad_refs, rows_ref, delta_ref = grad_refs_and_scratch
    for d, row in enumerate(widened(deep_ref, one_ref, two_ref)):
        rows_ref[d] = row
    w1 = w1_ref[...]
    depth, mid, cells = hidden_ref.shape
    last = cells // LANES - 2
    for d in range(depth):
        hidden_ref[d, :, 2 * LANES : last * LANES] = inner_ref[d]
        for h, sides_of in ((0, (-1, 0)), (last, (0, 1))):
            results = activated(w1, neighbours(rows_ref, d, [h], 2), d, depth, sides_of)
            for n, (value, slope) in enumerate(results):
                at = (h + n) * LANES
                hidden_ref[d, :, at : at + LANES] = value
                delta = back_ref[d, :, at : at + LANES] * slope
                shares(delta, mid, delta_ref, (4 * d + (2 if h else 0) + n) * LANES)
    right = jnp.concatenate([neighbours(rows_ref, d, [0, last], 2) for d in range(depth)], axis=1)
    total = first_ref[...] + products(delta_ref[...], right)
    inner = rows_ref.shape[1]
    blocks, tails = [], []
    for n in range(3):
        part = total[n * mid : (n + 1) * mid]
        blocks += [part[:, m * LANES : (m + 1) * LANES] for m in range(2)]
        tails.append(part[:, 2 * LANES :])
    tails.append(jnp.zeros((mid, LANES - 3 * inner), F32))
    blocks.append(jnp.concatenate(tails, axis=1))
    size = mid // lax.axis_size("dp")
    half = size // 2

    def rows_of(part, core):
        rows = [block[part * size + core * half : part * size + (core + 1) * half] for block in blocks]
        return rows[:3], rows[3:]

    pack(direct, grad_refs, rows_of, blocks)


def second_kernel(direct, hidden_ref, moved_ref, second_ref, *grad_refs):
    depth, mid, cells = hidden_ref.shape
    height = cells // LANES
    own = depth - 2
    out = moved_ref.shape[1] // 3
    heads, tails = [], []
    for b in range(3):
        far = [h for h in range(height - 2) if not 2 <= h + b <= height - 3]
        left = jnp.concatenate(
            [moved_ref[d, :, h * LANES : (h + 1) * LANES] for d in range(own) for h in far], axis=1
        )
        right = jnp.concatenate(
            [
                jnp.concatenate([hidden_ref[d + a, :, (h + b) * LANES : (h + b + 1) * LANES] for a in range(3)], axis=0)
                for d in range(own)
                for h in far
            ],
            axis=1,
        )
        total = second_ref[3 * b * out : 3 * (b + 1) * out, :] + products(left, right)
        for c in range(3):
            part = total[c * out : (c + 1) * out]
            heads.append(part[:, :LANES])
            tails.append(part[:, LANES:])
    blocks = heads + [jnp.concatenate(tails[n : n + 2], axis=1) for n in range(0, 8, 2)]
    size = mid // lax.axis_size("dp")

    def rows_of(part, core):
        at = slice((2 * part + core) * size, (2 * part + core + 1) * size)
        rows = [block[at] for block in blocks] + [folded(tails[8][at])]
        return rows[:7], rows[7:]

    pack(direct, grad_refs, rows_of, [*blocks, jnp.concatenate([tails[8], jnp.zeros_like(tails[8])], axis=1)])


def features_kernel(hidden_ref, k2_ref, out_ref, token_ref, scratch):
    out, depth, height, _ = out_ref.shape
    w2 = jnp.concatenate([as_matrix(k2_ref, c) for c in range(3)], axis=0)
    for d in range(depth):
        for h in range(0, height, 2):
            rhs = jnp.concatenate(
                [
                    hidden_ref[d + a, :, (h + b) * LANES : (h + b + 2) * LANES]
                    for a in range(3)
                    for b in range(3)
                ],
                axis=0,
            )
            y = jnp.dot(w2, rhs, preferred_element_type=F32)
            total = sum(moved_along_width(y[n * out : (n + 1) * out], 1 - n) for n in range(3))
            for r in range(2):
                row = total[:, r * LANES : (r + 1) * LANES]
                scratch[pl.ds(d * height + h + r, out, stride=depth * height), :] = row
    out_ref[...] = scratch[: out * depth * height].reshape(out_ref.shape).astype(BF)
    token_ref[...] = scratch[:8]


def plane_kernel(moves, cuts, *refs):
    sums, (kept_ref, *send_refs) = refs[: -1 - len(moves)], refs[-1 - len(moves) :]
    part = lax.rem(lax.axis_index("dp"), sums[0].shape[0])
    half = lax.axis_index("y")

    def total(x, y):
        at = 1 - part if x else part, 1 - half if y else half
        values = [keep[at] + got[at].astype(F32) for keep, got in zip(sums[::2], sums[1::2], strict=True)]
        if len(values) == 1:
            return values[0]
        one, two = (jnp.concatenate([v[:n] for v, n in zip(values, cut, strict=True)], axis=0) for cut in cuts)
        return jnp.where(at[1] == 0, one, two)

    kept_ref[...] = total(0, 0)
    for (x, y), send_ref in zip(moves, send_refs, strict=True):
        send_ref[...] = total(x, y).astype(BF)


def total_kernel(kept_ref, *refs):
    *got_refs, out_ref = refs
    value = kept_ref[...]
    for ref in got_refs:
        value = value + ref[...].astype(F32)
    out_ref[...] = value.astype(BF)


def depth_kernel(a_ref, b_ref, c_ref, d_ref, _, out_ref, padded_ref):
    one = a_ref[...].astype(F32) + b_ref[...].astype(F32)
    two = c_ref[...].astype(F32) + d_ref[...].astype(F32)
    out_ref[...] = (one + two).astype(BF)
    rest = jnp.zeros((padded_ref.shape[0] - out_ref.shape[0], LANES), F32)
    padded_ref[...] = jnp.concatenate([one + two, rest], axis=0).astype(BF)


def write_kernel(count, wheres, *refs):
    n_scratch = 6
    in_refs = refs[:count]
    out_refs, scratch = refs[: -n_scratch * count], refs[-n_scratch * count :]
    first_ref, second_ref = out_refs[-2:]
    core, y = lax.axis_index("core"), lax.axis_index("y")

    def begun(n, half):
        wide, last, low, high, tail, sems = scratch[n_scratch * n : n_scratch * (n + 1)]
        own_core, _ = wheres[n]
        at = core if own_core else 1 - core
        rows = in_refs[n][...].astype(F32)
        _, _, size, mid = wide.shape
        _, small, inner = low.shape
        here = pl.ds(pl.multiple_of(at * size, size), size)
        count = 2 if half else 7
        for j in range(count):
            value = rows[j * size : (j + 1) * size]
            for m in range(2):
                wide[m, j] = value[:, m * mid : (m + 1) * mid]
        pairs = [(wide.at[:, :count], second_ref.at[0:2, 7 * half : 7 * half + count, here, :])]
        row = count * size
        if half:
            for j in range(4):
                value = rows[row : row + size]
                row += size
                for m in range(2):
                    last[2 * j + m] = value[:, m * mid : (m + 1) * mid]
            value = rows[row : row + size // 2]
            row += size // 2
            last[8] = jnp.concatenate([value[:, :mid], value[:, mid:]], axis=0)
            pairs.append((last, second_ref.at[2, :, here, :]))
        copies = [pltpu.make_async_copy(src, dst, sems.at[i]) for i, (src, dst) in enumerate(pairs)]
        for copy in copies:
            copy.start()
        here = pl.ds(pl.multiple_of(at * small, small), small)
        places = [(high, 0, 4), (low, 0, 4), (low, 4, 4), (tail, 0, 3)] if half else [(low, 0, 4), (low, 4, 4), (high, 0, 4)]
        for ref, start, number in places:
            value = rows[row : row + small]
            row += small
            for m in range(number):
                ref[start + m] = value[:, m * inner : (m + 1) * inner]
        if half:
            pairs = [
                (high, first_ref.at[4:8, 1, here, :]),
                (low, first_ref.at[0:8, 2, here, :]),
                (tail, first_ref.at[8, :, here, :]),
            ]
        else:
            pairs = [(low, first_ref.at[0:8, 0, here, :]), (high, first_ref.at[0:4, 1, here, :])]
        more = [pltpu.make_async_copy(src, dst, sems.at[2 + i]) for i, (src, dst) in enumerate(pairs)]
        for copy in more:
            copy.start()
        return copies + more

    for half in range(2):

        @pl.when(y == half)
        def _(half=half):
            copies = []
            for n, (_, own_y) in enumerate(wheres):
                copies += begun(n, half if own_y else 1 - half)
            for copy in copies:
                copy.wait()


def swapped(x, axis, first):
    axes = (axis,) if isinstance(axis, str) else axis
    parts, size = lax.axis_size("dp"), lax.axis_size(axis)
    partner = list(range(parts * size))
    for i in partner:
        part, at = divmod(i, size)
        if first <= at < size - (size - first) % 2:
            partner[i] = part * size + (at - first ^ 1) + first
        elif parts % 2 == 0:
            partner[i] = (part ^ 1) * size + at
    return lax.ppermute(x, ("dp", *axes), list(enumerate(partner)))


def across(x, *moves):
    axes = tuple(axis for axis, _ in moves)
    flip = 0
    for axis, bit in moves:
        flip = flip * lax.axis_size(axis) + bit
    return lax.ppermute(x, axes, [(i, i ^ flip) for i in range(lax.axis_size(axes))])


def scattered(rows, cuts):
    halves = [
        jnp.concatenate([x[:, :, :n] if at == 0 else x[:, :, x.shape[2] - n :] for x, n in zip(rows, cut)], axis=2)
        for at, cut in enumerate(cuts)
    ]
    grad = lax.psum_scatter(jnp.stack(halves, axis=2), "dp", scatter_dimension=0, tiled=True)
    core = lax.axis_index("core")
    return tuple(lax.dynamic_index_in_dim(grad, at, 1, False) for at in (core, 1 - core))


def assembled(quarters, size, inner, mid):
    first, second = ([[None, None] for _ in range(27)] for _ in range(2))
    half = size // 2
    for core in range(2):
        for y in range(2):
            rows, row = quarters[core][y].astype(F32), 0
            for j in range(7) if y == 0 else range(7, 13):
                for m, k in enumerate((j, 9 + j) if j < 9 else (2 * j, 2 * j + 1)):
                    second[k][core] = rows[row : row + size, m * mid : (m + 1) * mid]
                row += size
            if y == 1:
                tail = rows[row : row + half]
                second[26][core] = jnp.concatenate([tail[:, :mid], tail[:, mid:]], axis=0)
                row += half
            for j in range(3) if y == 0 else range(3, 7):
                for m in range(4):
                    c, ab = (j // 2, 4 * (j % 2) + m) if j < 6 else (m, 8)
                    if c < 3:
                        first[3 * ab + c][core] = rows[row : row + half, m * inner : (m + 1) * inner]
                row += half
    return tuple(jnp.stack([jnp.concatenate(both, axis=0) for both in grad]) for grad in (first, second))


def per_device(volume, kernel_first, kernel_second, cotangent):
    _, inner, depth, height, width = volume.shape
    mid, out = kernel_first.shape[1], kernel_second.shape[1]
    cells = height * width
    parts = lax.axis_size("dp")
    k1, k2 = jnp.swapaxes(kernel_first, 1, 2), jnp.swapaxes(kernel_second, 1, 2)
    rows = depth * height

    one, two = swapped(volume[0], "dep", 0), swapped(volume[0], "dep", 1)
    (blank,) = call(blank_kernel, [shape((out, 2 * width), BF)], [], flops=3_000_000_000)
    cot_rows, back = call(
        spread_kernel,
        [
            shape((depth, out, cells), BF),
            shape((depth + 2, mid, cells + 2 * width), F32),
        ],
        [cotangent[0], k2, blank],
        [pltpu.VMEM(((out + 1) * rows, width), F32)],
        flops=1_100_000_000,
    )
    moved, w1, vol = call(
        arrange_kernel,
        [
            shape((depth, 3 * out, cells), BF),
            shape((3 * mid, 9 * inner), BF),
            shape((depth, inner, cells), BF),
        ],
        [cot_rows, k1, volume[0]],
        [pltpu.VMEM(((inner + 1) * rows, width), F32)],
        flops=500_000_000,
    )
    deep, one, two = call(
        rim_kernel,
        [shape((3 * depth, inner, cells), BF)] + [shape((3 * depth, inner, 2 * width), BF)] * 2,
        [vol, one, two],
        [pltpu.VMEM(((inner + 1) * rows, width), F32)],
    )
    one, two = swapped(one, HGT, 0), swapped(two, HGT, 1)
    size = mid // parts
    direct = parts == 2 and size % 16 == 0
    halves = lax.axis_size("y")
    cuts = ((7 * size, 3 * size // 2), (13 * size // 2, 2 * size))
    length_second, length_first = 7 * size, 2 * size
    rows_in, rows_out = height - 2, 4
    inner_hidden, inner_second, inner_first = call(
        inner_kernel,
        [
            shape((depth + 2, mid, rows_in * width), BF),
            shape((9 * out, 3 * mid), F32),
            shape((3 * mid, 9 * inner), F32),
        ],
        [deep, w1, moved, back],
        [pltpu.VMEM((3 * mid, (depth + 2) * rows_in * width), BF)],
        flops=1_500_000_000,
    )
    hidden, *first = call(
        functools.partial(outer_kernel, direct),
        [shape((depth + 2, mid, cells + 2 * width), BF)]
        + ([shape((parts, halves, length_first, width), F32)] * 2 if direct else [shape((7, mid, LANES), F32)]),
        [deep, two, one, w1, back, inner_hidden, inner_first],
        [
            pltpu.VMEM((3 * depth, inner, cells + 4 * width), BF),
            pltpu.VMEM((3 * mid, (depth + 2) * rows_out * width), BF),
        ],
        flops=1_000_000_000,
    )
    second = call(
        functools.partial(second_kernel, direct),
        [shape((parts, halves, length_second, width), kind) for kind in (F32, BF)]
        if direct
        else [shape((14, out, LANES), F32)],
        [hidden, moved, inner_second],
        flops=4_000_000_000,
    )
    if direct:
        moves = [(1, 0), (0, 1), (1, 1)]
        grads = [second, first]
    else:
        moves = [(0, 1)]
        blocks = second[0].reshape(14, parts, 2, size, LANES).transpose(1, 2, 0, 3, 4)
        tail = blocks[:, :, 13, :, :mid]
        tail = jnp.concatenate([tail[:, :, : size // 2], tail[:, :, size // 2 :]], axis=-1)
        rows_second = jnp.concatenate([blocks[:, :, :13].reshape(parts, 2, 13 * size, LANES), tail], axis=2)
        blocks = first[0].reshape(7, parts, 2, size // 2, LANES).transpose(1, 2, 0, 3, 4)
        rows_first = blocks.reshape(parts, 2, 7 * (size // 2), LANES)
        grads = [scattered([rows_second, rows_first], cuts)]
    block = (sum(cuts[0]), width)
    kept, *sends = call(
        functools.partial(plane_kernel, moves, cuts),
        [shape(block, F32)] + [shape(block, BF)] * len(moves),
        [x for keep, send in grads for x in (keep, across(send, ("core", 1)))],
    )
    gots = [across(send, ("dp", x), ("y", y)) for send, (x, y) in zip(sends, moves, strict=True)]
    (share,) = call(total_kernel, [shape(block, BF)], [kept, *gots])
    features, token = call(
        features_kernel,
        [shape(cotangent.shape[1:], BF), shape((8, width), F32)],
        [hidden, k2],
        [pltpu.VMEM(((out + 1) * rows, width), F32)],
        flops=900_000_000,
    )
    gots = [across(share, ("dep", bits)) for bits in (1, 3, 2)]
    share, for_y = call(depth_kernel, [shape(block, BF), shape((block[0] + 16, width), BF)], [share, *gots, token])
    other, far = across(share, ("core", 1)), across(for_y, ("y", 1))
    far_other = across(for_y, ("y", 1), ("core", 1))
    if size % 16 == 0:
        outs = [shape((9, 3, size, inner), F32), shape((3, 9, 2 * size, mid), F32)]

        def written(quarters, wheres, before=()):
            scratch = [
                pltpu.VMEM((2, 7, size, mid), F32),
                pltpu.VMEM((9, size, mid), F32),
                pltpu.VMEM((8, size // 2, inner), F32),
                pltpu.VMEM((4, size // 2, inner), F32),
                pltpu.VMEM((3, size // 2, inner), F32),
                pltpu.SemaphoreType.DMA((5,)),
            ]
            count = len(quarters)
            return call(
                functools.partial(write_kernel, count, wheres),
                outs,
                [*quarters, *before],
                scratch * count,
                far=range(count, count + len(before)),
                far_outs=(0, 1),
                aliases={count + n: n for n in range(len(before))},
            )

        grads = written([share, other], [(True, True), (False, True)])
        grads = written([far_other, far], [(False, False), (True, False)], grads)
        grad_first, grad_second = (grad.reshape(27, *grad.shape[2:]) for grad in grads)
    else:
        core, y = lax.axis_index("core"), lax.axis_index("y")
        stacked = jnp.stack([jnp.stack([share, far[: block[0]]]), jnp.stack([other, far_other[: block[0]]])])
        quarters = [
            [stacked[lax.bitwise_xor(core, c), lax.bitwise_xor(y, h)] for h in range(2)] for c in range(2)
        ]
        grad_first, grad_second = assembled(quarters, size, inner, mid)
    return features[None], grad_first, grad_second


def solution(mesh):
    dp, dep, hgt = (mesh.shape[axis] for axis in ("dp", "dep", "hgt"))
    split = jax.sharding.Mesh(mesh.devices.reshape(dp, dep, hgt // 2, 2), ("dp", "dep", *HGT))
    block = P("dp", None, "dep", HGT, None)
    return jax.shard_map(
        per_device,
        mesh=split,
        in_specs=(block, P(), P(), block),
        out_specs=(block, P(None, "dp", None), P(None, "dp", None)),
        check_vma=False,
    )
```
